32 devices in a mesh: groups: 2 (over y), dp: 4 (over z), tensor: 4 (over x, core).
Axes of the slice: x: 2, y: 2, z: 4, core: 2. Of those that a mesh axis runs over, the one named last changes fastest.
Arguments:
- prompt_kv: bfloat16 [2, 1024, 1024], P(None, ('groups', 'dp'), 'tensor'), parts along dimension 1, may hold values from -8 to 8
- resp_q: bfloat16 [8192, 5120], P(('groups', 'dp'), 'tensor'), parts along dimension 0, may hold values from -8 to 8
- resp_kv: bfloat16 [2, 8192, 1024], P(None, ('groups', 'dp'), 'tensor'), parts along dimension 1, may hold values from -6 to 6
- out_grad: bfloat16 [8192, 5120], P(('groups', 'dp'), 'tensor'), parts along dimension 0, may hold values from -6 to 6
- rewards: float32 [128], P(('groups', 'dp')), parts along dimension 0, may hold values from -12 to 12
- resp_prompt: int32 [128], P('groups'), parts along dimension 0, may hold values from 0 to 3, as said below
- resp_len: int32 [128], P(('groups', 'dp')), parts along dimension 0, may hold values from 16 to 64
Outputs:
- q_grad: bfloat16 [8192, 5120], P(('groups', 'dp'), 'tensor'), parts along dimension 0
- self_kv_grad: bfloat16 [2, 8192, 1024], P(None, ('groups', 'dp'), 'tensor'), parts along dimension 1
- prefix_kv_grad: bfloat16 [2, 1024, 1024], P(None, ('groups', 'dp'), 'tensor'), parts along dimension 1
The draws below stay inside these ranges and needn't reach their ends.
There are 2 independent parts, one for each index of `groups`. The reference program is written for one: setup_inputs(seed, part) draws one part's arguments, and reference() takes and returns one part's arrays. A program takes and returns all parts, laid end to end along the dimension named above; each array names one. Nothing has to cross between parts.
Inputs may be any that keep to these rules, and one draw needn't show every extreme that they name: `resp_prompt`: responses r = i * 16 onward lie on index i of dp, and prompt p on index p of dp. Each prompt has exactly 16 responses, and one index of dp holds at most 4 responses of one prompt.
All inputs are finite; a program needn't handle non-finite values.
Results may differ from the reference program's by a relative error of at most 0.0081.
Values may be sent and summed in bfloat16 or wider, within the bound.
No kernel may reach another device: no remote copies, remote signals or barrier semaphores. Data moves between devices by JAX's collectives and lax.ppermute only.
A program may use at most 128 MiB of HBM per device.

```python
import math
import jax
import jax.numpy as jnp
from jax import lax

QH = 40
KVH = 8
HD = 128
PLEN = 128
RLEN = 64
RESP_DEV = 16
SLOT = 4
RESP = 64
RTOK = 4096
PTOK = 512
N_DP = 4


def draw_resp_prompt(key, part):
    key = jax.random.fold_in(key, 11)
    key_offsets, key_placed, key_orders = jax.random.split(key, 3)
    offsets = jax.random.permutation(key_offsets, N_DP * SLOT)[:RESP_DEV] // SLOT
    placed = jax.random.permutation(key_placed, N_DP)
    orders = jax.vmap(lambda subkey: jax.random.permutation(subkey, RESP_DEV))(jax.random.split(key_orders, N_DP))
    prompts = (placed[:, None] + offsets[orders]) % N_DP
    return prompts.reshape(-1).astype(jnp.int32)


def draw_rewards(key, part):
    key = jax.random.fold_in(key, 12)
    rising = 1.0 + 2.0 * jnp.arange(RESP, dtype=jnp.float32) / max(RESP - 1, 1)
    drawn = jnp.clip(jax.random.normal(key, (RESP,), jnp.float32), -4.0, 4.0) * rising
    return drawn.astype(jnp.float32)


def draw_resp_q(key, part):
    key = jax.random.fold_in(key, 13)
    drawn = jnp.clip(jax.random.normal(key, (RTOK, QH * HD), jnp.float32), -6.0, 6.0)
    return drawn.astype(jnp.bfloat16)


def draw_prompt_kv(key, part):
    key = jax.random.fold_in(key, 14)
    drawn = jnp.clip(jax.random.normal(key, (2, PTOK, KVH * HD), jnp.float32), -6.0, 6.0)
    return drawn.astype(jnp.bfloat16)


def set_ends(entries, key, low, top_value):
    index_at = [jax.random.randint(jax.random.fold_in(key, axis), (), 0, length) for axis, length in enumerate(entries.shape)]
    main_axis = entries.shape.index(max(entries.shape))
    beside = index_at[:main_axis] + [(index_at[main_axis] + 1) % entries.shape[main_axis]] + index_at[main_axis + 1:]
    return entries.at[tuple(index_at)].set(low).at[tuple(beside)].set(top_value)


def block_levels(rng, dims, pieces, least, top_value):
    gain, own = 1.0, jax.random.fold_in(rng, 6)
    for position, parts in pieces:
        heights = jnp.exp(jax.random.uniform(jax.random.fold_in(own, position), (parts,), jnp.float32, least / len(pieces), top_value / len(pieces)))
        gain = gain * jnp.repeat(heights, dims[position] // parts).reshape([-1 if axis == position else 1 for axis in range(len(dims))])
    return gain


def gaussian(rng, shape, spread, limit, pieces=(), kind=jnp.bfloat16):
    values = jax.random.normal(rng, shape, jnp.float32) * spread
    if len(pieces) > 0:
        values = block_levels(rng, shape, pieces, -0.22, 0.18) * values
    return jnp.clip(values, min=-limit, max=limit).astype(kind)


def setup_inputs(seed: int = 0, part: int = 0) -> dict:
    key_list = jax.random.split(jax.random.key(seed), 8)
    part_keys = jax.random.split(jax.random.fold_in(key_list[7], part), 8)
    prompt_kv = draw_prompt_kv(jax.random.fold_in(jax.random.fold_in(key_list[7], part), 71), part)
    resp_q = draw_resp_q(jax.random.fold_in(jax.random.fold_in(key_list[7], part), 71), part)
    resp_kv = gaussian(part_keys[2], (2, RTOK, KVH * HD), 1.0, 6.0, ((1, 4), (2, 4)))
    out_grad = gaussian(part_keys[3], (RTOK, QH * HD), 1.0, 6.0, ((0, 4), (1, 4)))
    rewards = draw_rewards(jax.random.fold_in(jax.random.fold_in(key_list[7], part), 71), part)
    resp_prompt = draw_resp_prompt(jax.random.fold_in(jax.random.fold_in(key_list[7], part), 71), part)
    resp_len = set_ends(jax.random.randint(part_keys[6], (RESP,), RLEN // 4, RLEN + 1), jax.random.fold_in(part_keys[6], 1), RLEN // 4, RLEN).astype(jnp.int32)
    return {"prompt_kv": prompt_kv, "resp_q": resp_q, "resp_kv": resp_kv, "out_grad": out_grad, "rewards": rewards, "resp_prompt": resp_prompt, "resp_len": resp_len}


def attention_grads(queries, all_keys, all_values, scaled):
    score_scale = 1.0 / math.sqrt(HD)
    query_f = queries.astype(jnp.float32)
    key_f = all_keys.astype(jnp.float32)
    value_f = all_values.astype(jnp.float32)
    scaled_f = scaled.astype(jnp.float32)
    scores = jnp.einsum('rtkgd,rskd->rkgts', query_f, key_f) * score_scale
    row_pos = jnp.arange(scores.shape[3], dtype=jnp.int32)[:, None]
    col_pos = jnp.arange(scores.shape[4], dtype=jnp.int32)[None, :]
    allowed = (col_pos < PLEN) | (col_pos - PLEN <= row_pos)
    scores = jnp.where(allowed, scores, -1e+30)
    row_max = lax.optimization_barrier(jnp.max(scores, axis=-1, keepdims=True))
    exp_scores = jnp.exp(scores - row_max)
    weights = exp_scores / lax.optimization_barrier(jnp.sum(exp_scores, axis=-1, keepdims=True))
    rounded = weights.astype(jnp.bfloat16).astype(jnp.float32)
    attended = jnp.einsum('rkgts,rskd->rtkgd', rounded, value_f)
    delta_rows = lax.optimization_barrier(jnp.sum(scaled_f * attended, axis=-1))
    delta_rows = jnp.transpose(delta_rows, (0, 2, 3, 1))[..., None]
    grad_weights = jnp.einsum('rtkgd,rskd->rkgts', scaled_f, value_f)
    grad_scores = (weights * (grad_weights - delta_rows) * score_scale).astype(jnp.bfloat16).astype(jnp.float32)
    query_grad = jnp.einsum('rkgts,rskd->rtkgd', grad_scores, key_f).astype(jnp.bfloat16)
    key_grad = jnp.einsum('rkgts,rtkgd->rskd', grad_scores, query_f).astype(jnp.bfloat16)
    value_grad = jnp.einsum('rkgts,rtkgd->rskd', rounded, scaled_f).astype(jnp.bfloat16)
    return (query_grad, key_grad, value_grad)

def reference(prompt_kv, resp_q, resp_kv, out_grad, rewards, resp_prompt, resp_len):
    group_size = QH // KVH
    kv_width = KVH * HD
    owners = jnp.arange(N_DP, dtype=jnp.int32)
    member = (resp_prompt[:, None] == owners[None, :]).astype(jnp.float32)
    totals = lax.optimization_barrier(jnp.sum(member * rewards[:, None], axis=0))
    advantage = rewards - lax.optimization_barrier(jnp.sum(member * totals[None, :], axis=1)) / RESP_DEV
    positions = jnp.arange(RLEN, dtype=jnp.int32)
    valid_rows = (positions[None, :] < resp_len[:, None]).astype(jnp.float32)
    factor = advantage[:, None] * (RLEN / resp_len.astype(jnp.float32))[:, None] * valid_rows
    scaled = (out_grad.reshape(RESP, RLEN, QH * HD).astype(jnp.float32) * factor[:, :, None]).astype(jnp.bfloat16)
    prompts_all = prompt_kv.reshape(2, N_DP, PLEN, kv_width)
    blocks = (resp_q.reshape(N_DP, RESP_DEV, RLEN, KVH, group_size, HD), jnp.moveaxis(resp_kv.reshape(2, N_DP, RESP_DEV, RLEN, KVH, HD), 1, 0), scaled.reshape(N_DP, RESP_DEV, RLEN, KVH, group_size, HD), resp_prompt.reshape(N_DP, RESP_DEV))

    def one_block(summed, block_args):
        queries, self_kv, scaled_heads, block_prompts = block_args
        picked = jnp.take(prompts_all, block_prompts, axis=1).reshape(2, RESP_DEV, PLEN, KVH, HD)
        joined = jnp.concatenate([picked, self_kv], axis=2)
        query_grad, key_grad, value_grad = attention_grads(queries, joined[0], joined[1], scaled_heads)
        per_resp = jnp.stack([key_grad[:, :PLEN], value_grad[:, :PLEN]], axis=1).astype(jnp.float32)
        route = (block_prompts[:, None] == owners[None, :]).astype(jnp.float32)
        summed = summed + jnp.einsum('rn,rxpkd->nxpkd', route, per_resp)
        return (summed, (query_grad, key_grad[:, PLEN:], value_grad[:, PLEN:]))
    start = jnp.zeros((N_DP, 2, PLEN, KVH, HD), jnp.float32)
    summed, outs = lax.scan(one_block, start, blocks)
    query_grads, key_grads, value_grads = outs
    q_grad = query_grads.reshape(RTOK, QH * HD)
    self_kv_grad = jnp.stack([key_grads, value_grads], axis=0).reshape(2, RTOK, kv_width)
    prefix_kv_grad = jnp.moveaxis(summed, 1, 0).reshape(2, PTOK, kv_width).astype(jnp.bfloat16)
    return (q_grad, self_kv_grad, prefix_kv_grad)
```

```python
import functools
import math

import jax
import jax.numpy as jnp
from jax import lax
from jax.experimental import pallas as pl
from jax.experimental.pallas import tpu as pltpu
from jax.sharding import PartitionSpec as P

HD = 128
NEG = -1e30
F32 = jnp.float32
BF16 = jnp.bfloat16


def dot(a, b, dims):
    return lax.dot_general(a, b, (dims, ((), ())), preferred_element_type=F32)


NN = ((1,), (0,))
NT = ((1,), (1,))
TN = ((0,), (0,))


def softmax_grads(scores_p, scores_s, gw_p, gw_s, factor, mask, scale):
    c = scale * math.log2(math.e)
    scores_s = jnp.where(mask, scores_s, NEG)
    top = jnp.maximum(
        jnp.max(scores_p, axis=0, keepdims=True), jnp.max(scores_s, axis=0, keepdims=True)
    )
    e_p = jnp.exp2((scores_p - top) * c)
    e_s = jnp.exp2((scores_s - top) * c)
    total = jnp.sum(e_p, axis=0, keepdims=True) + jnp.sum(e_s, axis=0, keepdims=True)
    weighted = jnp.sum(e_p * gw_p, axis=0, keepdims=True) + jnp.sum(
        e_s * gw_s, axis=0, keepdims=True
    )
    inverse = 1.0 / total
    delta = weighted * inverse
    gain = inverse * factor
    w_p, w_s = e_p * gain, e_s * gain
    return (
        w_p.astype(BF16),
        w_s.astype(BF16),
        (w_p * (gw_p - delta)).astype(BF16),
        (w_s * (gw_s - delta)).astype(BF16),
    )


def lane_masks(tokens, lanes):
    lane = lax.broadcasted_iota(jnp.int32, (1, lanes), 1)
    return lane, lax.rem(lane, tokens)


def causal(tokens, lanes):
    key = lax.broadcasted_iota(jnp.int32, (tokens, lanes), 0)
    lane = lax.broadcasted_iota(jnp.int32, (tokens, lanes), 1)
    return key <= lax.rem(lane, tokens)


def attend_group(slots, base, group_size, kv_heads, tokens, prefix_len, q, og, kv, prefix, lens, factors, out, self_out, prefix_out):
    scale = 1.0 / math.sqrt(HD)
    whole = group_size - group_size % 2
    wide = whole * tokens
    pairs = [(j, j + 1) if j + 1 < slots else (j, None) for j in range(0, slots, 2)]

    def head(k, h):
        at = (k * group_size + h) * HD
        return slice(at, at + HD)

    def rows(ref, k, blocks):
        return jnp.concatenate([ref[base + j, :, head(k, h)] for j, h in blocks], axis=0)

    def row_factor(j, lanes):
        _, t = lane_masks(tokens, lanes)
        return jnp.where(t < lens[j], factors[j], 0.0)

    for k in range(kv_heads):
        cols = slice(k * HD, (k + 1) * HD)
        key_p, value_p = prefix[0, :, cols], prefix[1, :, cols]
        key_pt = key_p.T
        key_acc = jnp.zeros((prefix_len, HD), F32)
        value_acc = jnp.zeros((prefix_len, HD), F32)
        for pair in pairs:
            members = [j for j in pair if j is not None]
            key_s = {j: kv[base + j, 0, :, cols] for j in members}
            value_s = {j: kv[base + j, 1, :, cols] for j in members}
            second = members[-1]
            key_pair = jnp.concatenate([key_s[pair[0]], key_s[second]], axis=0)
            value_pair = jnp.concatenate([value_s[pair[0]], value_s[second]], axis=0)
            key_t = jnp.concatenate([key_pt, key_pair.T], axis=1)
            key_self = {}
            value_self = {}
            empty = jnp.zeros((tokens, wide), BF16)
            for place, j in enumerate(members):
                blocks = [(j, h) for h in range(whole)]
                q_rows, g_rows = rows(q, k, blocks), rows(og, k, blocks)
                scores = dot(jnp.concatenate([key_p, key_s[j]], axis=0), q_rows, NT)
                gw = dot(jnp.concatenate([value_p, value_s[j]], axis=0), g_rows, NT)
                w_p, w_s, d_p, d_s = softmax_grads(
                    scores[:prefix_len],
                    scores[prefix_len:],
                    gw[:prefix_len],
                    gw[prefix_len:],
                    row_factor(j, wide),
                    causal(tokens, wide),
                    scale,
                )
                d_wide = jnp.concatenate(
                    [d_p, d_s, empty] if place == 0 else [d_p, empty, d_s], axis=0
                )
                q_grad = (dot(key_t, d_wide, NN) * scale).astype(BF16).T
                for n, (_, h) in enumerate(blocks):
                    out[base + j, :, head(k, h)] = q_grad[n * tokens : (n + 1) * tokens]
                kg = dot(jnp.concatenate([d_p, d_s], axis=0), q_rows, NN)
                vg = dot(jnp.concatenate([w_p, w_s], axis=0), g_rows, NN)
                key_acc += kg[:prefix_len]
                value_acc += vg[:prefix_len]
                key_self[j] = kg[prefix_len:]
                value_self[j] = vg[prefix_len:]
            if group_size % 2:
                blocks = [(pair[0], group_size - 1), (second, group_size - 1)]
                q_rows, g_rows = rows(q, k, blocks), rows(og, k, blocks)
                lanes = 2 * tokens
                lane, t = lane_masks(tokens, lanes)
                left = lane < tokens
                length = jnp.where(left, lens[pair[0]], lens[second] if len(members) > 1 else 0)
                gain = jnp.where(left, factors[pair[0]], factors[second])
                factor = jnp.where(t < length, gain, 0.0)
                scores = dot(jnp.concatenate([key_p, key_pair], axis=0), q_rows, NT)
                gw = dot(jnp.concatenate([value_p, value_pair], axis=0), g_rows, NT)

                def own(both):
                    return jnp.where(left, both[:tokens], both[tokens:])

                w_p, w_s, d_p, d_s = softmax_grads(
                    scores[:prefix_len],
                    own(scores[prefix_len:]),
                    gw[:prefix_len],
                    own(gw[prefix_len:]),
                    factor,
                    causal(tokens, lanes),
                    scale,
                )

                def spread(part):
                    none = jnp.zeros_like(part)
                    return jnp.concatenate(
                        [jnp.where(left, part, none), jnp.where(left, none, part)], axis=0
                    )

                d_all = jnp.concatenate([d_p, spread(d_s)], axis=0)
                w_all = jnp.concatenate([w_p, spread(w_s)], axis=0)
                q_grad = (dot(key_t, d_all, NN) * scale).astype(BF16).T
                for n, j in enumerate(members):
                    out[base + j, :, head(k, group_size - 1)] = q_grad[n * tokens : (n + 1) * tokens]
                kg = dot(d_all, q_rows, NN)
                vg = dot(w_all, g_rows, NN)
                key_acc += kg[:prefix_len]
                value_acc += vg[:prefix_len]
                for n, j in enumerate(members):
                    at = prefix_len + n * tokens
                    key_self[j] += kg[at : at + tokens]
                    value_self[j] += vg[at : at + tokens]
            for j in members:
                self_out[base + j, 0, :, cols] = (key_self[j] * scale).astype(BF16)
                self_out[base + j, 1, :, cols] = value_self[j].astype(BF16)
        prefix_out[0, :, cols] = (key_acc * scale).astype(BF16)
        prefix_out[1, :, cols] = value_acc.astype(BF16)


def attention_kernel(dims, *refs):
    n_dp, count, slots, kv_heads, group_size, tokens, prefix_len, near = dims
    groups = count // slots
    n_prompts = n_dp if near else 1
    refs = list(refs)
    resp_prompt, resp_len = refs[:2]
    rewards = refs[2 : 2 + n_prompts]
    q_hbm, og_hbm, kv_hbm = refs[2 + n_prompts : 5 + n_prompts]
    prompts = refs[5 + n_prompts : 5 + 2 * n_prompts]
    q_out, self_out = refs[5 + 2 * n_prompts : 7 + 2 * n_prompts]
    n_out = groups if near else 1
    prefix_outs = refs[7 + 2 * n_prompts : 7 + 2 * n_prompts + n_out]
    (order, seen, totals, lens, factors, q, og, kv, prefix, out, own, grads, sem_in, sem_prefix, sem_out, sem_grads) = refs[
        7 + 2 * n_prompts + n_out :
    ]
    me = lax.axis_index("dp")
    width = kv_heads * HD

    for p in range(n_dp):
        seen[p] = 0
        totals[p] = 0.0

    def place(i, _):
        prompt = resp_prompt[me * count + i]
        if near:
            turn = lax.rem(prompt - me + n_dp, n_dp)
            order[turn * slots + seen[turn]] = i
            seen[turn] = seen[turn] + 1
        else:
            order[i] = i
        return 0

    lax.fori_loop(0, count, place, 0)

    def at_rows(slot):
        return pl.ds(pl.multiple_of(order[slot] * tokens, tokens), tokens)

    def copies_in(slot):
        rows = at_rows(slot)
        return (
            pltpu.make_async_copy(q_hbm.at[rows], q.at[slot], sem_in.at[slot, 0]),
            pltpu.make_async_copy(og_hbm.at[rows], og.at[slot], sem_in.at[slot, 1]),
            pltpu.make_async_copy(kv_hbm.at[0, rows], kv.at[slot, 0], sem_in.at[slot, 2]),
            pltpu.make_async_copy(kv_hbm.at[1, rows], kv.at[slot, 1], sem_in.at[slot, 3]),
        )

    def prefix_copy(g):
        if near:
            return pltpu.make_async_copy(prompts[g], prefix.at[g], sem_prefix.at[g])
        prompt = resp_prompt[me * count + g]
        return pltpu.make_async_copy(prompts[0].at[prompt], prefix.at[g], sem_prefix.at[g])

    def copies_out(slot):
        rows = at_rows(slot)
        return (
            pltpu.make_async_copy(out.at[slot], q_out.at[rows], sem_out.at[slot, 0]),
            pltpu.make_async_copy(own.at[slot, 0], self_out.at[0, rows], sem_out.at[slot, 1]),
            pltpu.make_async_copy(own.at[slot, 1], self_out.at[1, rows], sem_out.at[slot, 2]),
        )

    def grads_copy(g):
        target = prefix_outs[g] if near else prefix_outs[0].at[g]
        return pltpu.make_async_copy(grads.at[g], target, sem_grads.at[g])

    for g in range(groups):
        prefix_copy(g).start()

        def start(n, _):
            for copy in copies_in(g * slots + n):
                copy.start()
            return 0

        lax.fori_loop(0, slots, start, 0)

    if near:
        for s in range(n_dp):
            source = lax.rem(me + s, n_dp)

            def add(i, _):
                prompt = resp_prompt[source * count + i]
                totals[prompt] = totals[prompt] + rewards[s][i]
                return 0

            lax.fori_loop(0, count, add, 0)
    else:

        def add_one(i, _):
            prompt = resp_prompt[i]
            totals[prompt] = totals[prompt] + rewards[0][i]
            return 0

        lax.fori_loop(0, n_dp * count, add_one, 0)

    own_rewards = rewards[0]

    def find_factor(slot, _):
        i = order[slot]
        length = resp_len[i]
        reward = own_rewards[i] if near else own_rewards[me * count + i]
        advantage = reward - totals[resp_prompt[me * count + i]] / count
        lens[slot] = length
        factors[slot] = advantage * (tokens / length.astype(F32))
        return 0

    lax.fori_loop(0, count, find_factor, 0)

    def one_group(g, _):
        base = g * slots

        def wait(n, _):
            for copy in copies_in(base + n):
                copy.wait()
            return 0

        lax.fori_loop(0, slots, wait, 0)
        attend_group(
            slots, base, group_size, kv_heads, tokens, prefix_len, q, og, kv, prefix.at[g],
            [lens[base + j] for j in range(slots)], [factors[base + j] for j in range(slots)],
            out, own, grads.at[g],
        )

        def send(n, _):
            for copy in copies_out(base + n):
                copy.start()
            return 0

        lax.fori_loop(0, slots, send, 0)
        return 0

    for g in range(groups):
        prefix_copy(g).wait()
    lax.fori_loop(0, groups, one_group, 0)
    for g in range(groups):
        grads_copy(g).start()

    def finish(slot, _):
        for copy in copies_out(slot):
            copy.wait()
        return 0

    lax.fori_loop(0, count, finish, 0)
    for g in range(groups):
        grads_copy(g).wait()


def shards(prompt_kv, resp_q, resp_kv, out_grad, rewards, resp_prompt, resp_len):
    n_dp = lax.axis_size("dp")
    count = rewards.shape[0]
    tokens = resp_q.shape[0] // count
    prefix_len, width = prompt_kv.shape[1:]
    kv_heads = width // HD
    group_size = resp_q.shape[1] // width
    slots = (count + n_dp - 1) // n_dp
    groups = count // slots
    near = groups == n_dp

    if near:
        def from_ahead(x, s):
            return lax.ppermute(x, "dp", [((i + s) % n_dp, i) for i in range(n_dp)])

        reward_parts = [rewards] + [from_ahead(rewards, s) for s in range(1, n_dp)]
        prompt_parts = [prompt_kv] + [from_ahead(prompt_kv, s) for s in range(1, n_dp)]
        prefix_shapes = [jax.ShapeDtypeStruct(prompt_kv.shape, BF16)] * groups
    else:
        reward_parts = [lax.all_gather(rewards, "dp", axis=0, tiled=True)]
        prompt_parts = [lax.all_gather(prompt_kv, "dp", axis=0)]
        prefix_shapes = [jax.ShapeDtypeStruct((groups,) + prompt_kv.shape, BF16)]

    dims = (n_dp, count, slots, kv_heads, group_size, tokens, prefix_len, near)
    smem = pl.BlockSpec(memory_space=pltpu.SMEM)
    anywhere = pl.BlockSpec(memory_space=pl.ANY)
    results = pl.pallas_call(
        functools.partial(attention_kernel, dims),
        out_shape=[
            jax.ShapeDtypeStruct(resp_q.shape, BF16),
            jax.ShapeDtypeStruct(resp_kv.shape, BF16),
        ]
        + prefix_shapes,
        in_specs=[smem] * (2 + len(reward_parts)) + [anywhere] * (3 + len(prompt_parts)),
        out_specs=[anywhere] * (2 + len(prefix_shapes)),
        scratch_shapes=[
            pltpu.SMEM((count,), jnp.int32),
            pltpu.SMEM((n_dp,), jnp.int32),
            pltpu.SMEM((n_dp,), F32),
            pltpu.SMEM((count,), jnp.int32),
            pltpu.SMEM((count,), F32),
            pltpu.VMEM((count, tokens, resp_q.shape[1]), BF16),
            pltpu.VMEM((count, tokens, resp_q.shape[1]), BF16),
            pltpu.VMEM((count, 2, tokens, width), BF16),
            pltpu.VMEM((groups, 2, prefix_len, width), BF16),
            pltpu.VMEM((count, tokens, resp_q.shape[1]), BF16),
            pltpu.VMEM((count, 2, tokens, width), BF16),
            pltpu.VMEM((groups, 2, prefix_len, width), BF16),
            pltpu.SemaphoreType.DMA((count, 4)),
            pltpu.SemaphoreType.DMA((groups,)),
            pltpu.SemaphoreType.DMA((count, 3)),
            pltpu.SemaphoreType.DMA((groups,)),
        ],
        compiler_params=pltpu.CompilerParams(vmem_limit_bytes=48 * 1024 * 1024),
        cost_estimate=pl.CostEstimate(
            flops=2 * 5 * count * tokens * group_size * kv_heads * (prefix_len + tokens) * HD,
            bytes_accessed=2 * (3 * resp_q.size + 2 * resp_kv.size),
            transcendentals=0,
        ),
        name="attention_grads",
    )(resp_prompt, resp_len, *reward_parts, resp_q, out_grad, resp_kv, *prompt_parts)
    q_out, self_out = results[:2]

    if near:
        arrived = [results[2]] + [
            lax.ppermute(results[2 + s], "dp", [(i, (i + s) % n_dp) for i in range(n_dp)])
            for s in range(1, n_dp)
        ]
        prefix_out = sum(part.astype(F32) for part in arrived).astype(BF16)
    else:
        mine = lax.dynamic_slice_in_dim(resp_prompt, lax.axis_index("dp") * count, count)
        route = (jnp.arange(n_dp, dtype=jnp.int32)[:, None] == mine[None, :]).astype(BF16)
        outgoing = jnp.dot(
            route, results[2].reshape(groups, -1), preferred_element_type=F32
        ).astype(BF16)
        outgoing = outgoing.reshape((n_dp,) + prompt_kv.shape)
        incoming = lax.all_to_all(outgoing, "dp", split_axis=0, concat_axis=0, tiled=True)
        prefix_out = jnp.sum(incoming, axis=0, dtype=F32).astype(BF16)
    return (q_out, self_out, prefix_out)


def solution(mesh):
    in_specs = (
        P(None, ("groups", "dp"), "tensor"),
        P(("groups", "dp"), "tensor"),
        P(None, ("groups", "dp"), "tensor"),
        P(("groups", "dp"), "tensor"),
        P(("groups", "dp")),
        P("groups"),
        P(("groups", "dp")),
    )
    out_specs = (
        P(("groups", "dp"), "tensor"),
        P(None, ("groups", "dp"), "tensor"),
        P(None, ("groups", "dp"), "tensor"),
    )
    return jax.shard_map(shards, mesh=mesh, in_specs=in_specs, out_specs=out_specs, check_vma=False)
```

```python
import functools
import math

import jax
import jax.numpy as jnp
from jax import lax
from jax.experimental import pallas as pl
from jax.experimental.pallas import tpu as pltpu
from jax.sharding import PartitionSpec as P

HD = 128
NEG = -1e30
TAIL = 16
FIRST = 1
F32 = jnp.float32
BF16 = jnp.bfloat16


def dot(a, b, dims):
    return lax.dot_general(a, b, (dims, ((), ())), preferred_element_type=F32)


NN = ((1,), (0,))
NT = ((1,), (1,))
TN = ((0,), (0,))


def softmax_grads(scores_p, scores_s, gw_p, gw_s, factor, mask, scale):
    c = scale * math.log2(math.e)
    scores_s = jnp.where(mask, scores_s, NEG)
    top = jnp.maximum(
        jnp.max(scores_p, axis=0, keepdims=True), jnp.max(scores_s, axis=0, keepdims=True)
    )
    e_p = jnp.exp2((scores_p - top) * c)
    e_s = jnp.exp2((scores_s - top) * c)
    total = jnp.sum(e_p, axis=0, keepdims=True) + jnp.sum(e_s, axis=0, keepdims=True)
    weighted = jnp.sum(e_p * gw_p, axis=0, keepdims=True) + jnp.sum(
        e_s * gw_s, axis=0, keepdims=True
    )
    inverse = 1.0 / total
    delta = weighted * inverse
    gain = inverse * factor
    w_p, w_s = e_p * gain, e_s * gain
    return (
        w_p.astype(BF16),
        w_s.astype(BF16),
        (w_p * (gw_p - delta)).astype(BF16),
        (w_s * (gw_s - delta)).astype(BF16),
    )


def lane_masks(tokens, lanes):
    lane = lax.broadcasted_iota(jnp.int32, (1, lanes), 1)
    return lane, lax.rem(lane, tokens)


def causal(tokens, lanes):
    key = lax.broadcasted_iota(jnp.int32, (tokens, lanes), 0)
    lane = lax.broadcasted_iota(jnp.int32, (tokens, lanes), 1)
    return key <= lax.rem(lane, tokens)


def attend_group(slots, base, group_size, kv_heads, tokens, prefix_len, q, og, kv, prefix, lens, factors, out, self_out, prefix_out):
    scale = 1.0 / math.sqrt(HD)
    whole = group_size - group_size % 2
    wide = whole * tokens
    pairs = [(j, j + 1) if j + 1 < slots else (j, None) for j in range(0, slots, 2)]

    def head(k, h):
        at = (k * group_size + h) * HD
        return slice(at, at + HD)

    def rows(ref, k, blocks):
        return jnp.concatenate([ref[base + j, :, head(k, h)] for j, h in blocks], axis=0)

    def row_factor(j, lanes):
        _, t = lane_masks(tokens, lanes)
        return jnp.where(t < lens[j], factors[j], 0.0)

    for k in range(kv_heads):
        cols = slice(k * HD, (k + 1) * HD)
        key_p, value_p = prefix[0, :, cols], prefix[1, :, cols]
        key_pt = key_p.T
        key_acc = jnp.zeros((prefix_len, HD), F32)
        value_acc = jnp.zeros((prefix_len, HD), F32)
        for pair in pairs:
            members = [j for j in pair if j is not None]
            key_s = {j: kv[base + j, 0, :, cols] for j in members}
            value_s = {j: kv[base + j, 1, :, cols] for j in members}
            second = members[-1]
            key_pair = jnp.concatenate([key_s[pair[0]], key_s[second]], axis=0)
            value_pair = jnp.concatenate([value_s[pair[0]], value_s[second]], axis=0)
            key_t = jnp.concatenate([key_pt, key_pair.T], axis=1)
            key_self = {}
            value_self = {}
            empty = jnp.zeros((tokens, wide), BF16)
            for place, j in enumerate(members):
                blocks = [(j, h) for h in range(whole)]
                q_rows, g_rows = rows(q, k, blocks), rows(og, k, blocks)
                scores = dot(jnp.concatenate([key_p, key_s[j]], axis=0), q_rows, NT)
                gw = dot(jnp.concatenate([value_p, value_s[j]], axis=0), g_rows, NT)
                w_p, w_s, d_p, d_s = softmax_grads(
                    scores[:prefix_len],
                    scores[prefix_len:],
                    gw[:prefix_len],
                    gw[prefix_len:],
                    row_factor(j, wide),
                    causal(tokens, wide),
                    scale,
                )
                d_wide = jnp.concatenate(
                    [d_p, d_s, empty] if place == 0 else [d_p, empty, d_s], axis=0
                )
                q_grad = (dot(key_t, d_wide, NN) * scale).astype(BF16).T
                for n, (_, h) in enumerate(blocks):
                    out[base + j, :, head(k, h)] = q_grad[n * tokens : (n + 1) * tokens]
                kg = dot(jnp.concatenate([d_p, d_s], axis=0), q_rows, NN)
                vg = dot(jnp.concatenate([w_p, w_s], axis=0), g_rows, NN)
                key_acc += kg[:prefix_len]
                value_acc += vg[:prefix_len]
                key_self[j] = kg[prefix_len:]
                value_self[j] = vg[prefix_len:]
            if group_size % 2:
                blocks = [(pair[0], group_size - 1), (second, group_size - 1)]
                q_rows, g_rows = rows(q, k, blocks), rows(og, k, blocks)
                lanes = 2 * tokens
                lane, t = lane_masks(tokens, lanes)
                left = lane < tokens
                length = jnp.where(left, lens[pair[0]], lens[second] if len(members) > 1 else 0)
                gain = jnp.where(left, factors[pair[0]], factors[second])
                factor = jnp.where(t < length, gain, 0.0)
                scores = dot(jnp.concatenate([key_p, key_pair], axis=0), q_rows, NT)
                gw = dot(jnp.concatenate([value_p, value_pair], axis=0), g_rows, NT)

                def own(both):
                    return jnp.where(left, both[:tokens], both[tokens:])

                w_p, w_s, d_p, d_s = softmax_grads(
                    scores[:prefix_len],
                    own(scores[prefix_len:]),
                    gw[:prefix_len],
                    own(gw[prefix_len:]),
                    factor,
                    causal(tokens, lanes),
                    scale,
                )

                def spread(part):
                    none = jnp.zeros_like(part)
                    return jnp.concatenate(
                        [jnp.where(left, part, none), jnp.where(left, none, part)], axis=0
                    )

                d_all = jnp.concatenate([d_p, spread(d_s)], axis=0)
                w_all = jnp.concatenate([w_p, spread(w_s)], axis=0)
                q_grad = (dot(key_t, d_all, NN) * scale).astype(BF16).T
                for n, j in enumerate(members):
                    out[base + j, :, head(k, group_size - 1)] = q_grad[n * tokens : (n + 1) * tokens]
                kg = dot(d_all, q_rows, NN)
                vg = dot(w_all, g_rows, NN)
                key_acc += kg[:prefix_len]
                value_acc += vg[:prefix_len]
                for n, j in enumerate(members):
                    at = prefix_len + n * tokens
                    key_self[j] += kg[at : at + tokens]
                    value_self[j] += vg[at : at + tokens]
            for j in members:
                self_out[base + j, 0, :, cols] = (key_self[j] * scale).astype(BF16)
                self_out[base + j, 1, :, cols] = value_self[j].astype(BF16)
        prefix_out[0, :, cols] = (key_acc * scale).astype(BF16)
        prefix_out[1, :, cols] = value_acc.astype(BF16)


def group_kernel(turn, dims, refs):
    n_dp, count, slots, kv_heads, group_size, tokens, prefix_len = dims
    refs = list(refs)
    small_hbm = refs[:3]
    payloads = refs[3 : 3 + n_dp]
    q_hbm, og_hbm, kv_hbm = refs[3 + n_dp : 6 + n_dp]
    refs = refs[6 + n_dp + (2 if turn != FIRST else 0) :]
    q_out, self_out, grads_out = refs[:3]
    (resp_prompt, resp_len, rewards, order, q, og, kv, prefix, tails, out, own, grads,
     sem_small, sem_prefix, sem_in, sem_out) = refs[3:]
    me = lax.axis_index("dp")
    prompt = lax.rem(me + turn, n_dp)

    small = [
        pltpu.make_async_copy(src, dst, sem_small.at[n])
        for n, (src, dst) in enumerate(zip(small_hbm, (resp_prompt, resp_len, rewards)))
    ]
    for copy in small:
        copy.start()
    own_rows = [
        pltpu.make_async_copy(payloads[s].at[0, pl.ds(prefix_len, TAIL)], tails.at[s], sem_small.at[3 + s])
        for s in range(n_dp)
    ]
    prefix_copies = [
        pltpu.make_async_copy(payloads[turn].at[n, pl.ds(0, prefix_len)], prefix.at[n], sem_prefix.at[n])
        for n in range(2)
    ]
    for copy in own_rows + prefix_copies:
        copy.start()
    small[0].wait()
    found = 0
    for i in range(count):
        order[found] = i
        found = found + (resp_prompt[me * count + i] == prompt).astype(jnp.int32)

    picked = [order[j] for j in range(slots)]
    rows = [pl.ds(pl.multiple_of(i * tokens, tokens), tokens) for i in picked]
    copies_in, copies_out = [], []
    for j in range(slots):
        copies_in += [
            pltpu.make_async_copy(q_hbm.at[rows[j]], q.at[j], sem_in.at[j, 0]),
            pltpu.make_async_copy(og_hbm.at[rows[j]], og.at[j], sem_in.at[j, 1]),
            pltpu.make_async_copy(kv_hbm.at[0, rows[j]], kv.at[j, 0], sem_in.at[j, 2]),
            pltpu.make_async_copy(kv_hbm.at[1, rows[j]], kv.at[j, 1], sem_in.at[j, 3]),
        ]
        copies_out += [
            pltpu.make_async_copy(out.at[j], q_out.at[rows[j]], sem_out.at[j, 0]),
            pltpu.make_async_copy(own.at[j, 0], self_out.at[0, rows[j]], sem_out.at[j, 1]),
            pltpu.make_async_copy(own.at[j, 1], self_out.at[1, rows[j]], sem_out.at[j, 2]),
        ]
    for copy in copies_in:
        copy.start()

    for copy in small[1:] + own_rows:
        copy.wait()
    member = jnp.zeros((1, tails.shape[2]), F32)
    for s in range(n_dp):
        tail = tails[s].astype(F32)
        reward = tail[0:1] + tail[1:2] + tail[2:3]
        member += jnp.where(tail[3:4] == prompt.astype(F32), reward, 0.0)
    total = jnp.sum(member, axis=1, keepdims=True)
    lens = [resp_len[i] for i in picked]
    factors = [
        (rewards[i] - total / count) * (tokens / length.astype(F32))
        for i, length in zip(picked, lens)
    ]
    for copy in prefix_copies + copies_in:
        copy.wait()
    attend_group(
        slots, 0, group_size, kv_heads, tokens, prefix_len, q, og, kv, prefix, lens, factors, out, own, grads
    )
    last = pltpu.make_async_copy(grads, grads_out, sem_prefix.at[0])
    last.start()
    for copy in copies_out:
        copy.start()
    for copy in copies_out + [last]:
        copy.wait()


def near_grads(turn, dims, small, payloads, resp_q, out_grad, resp_kv, earlier):
    n_dp, count, slots, kv_heads, group_size, tokens, prefix_len = dims
    width = kv_heads * HD
    anywhere = pl.BlockSpec(memory_space=pl.ANY)
    operands = [*small, *payloads, resp_q, out_grad, resp_kv, *earlier]
    lanes = resp_q.shape[1]
    return pl.pallas_call(
        lambda *refs: group_kernel(turn, dims, refs),
        out_shape=[
            jax.ShapeDtypeStruct(resp_q.shape, BF16),
            jax.ShapeDtypeStruct(resp_kv.shape, BF16),
            jax.ShapeDtypeStruct((2, prefix_len, width), BF16),
        ],
        in_specs=[anywhere] * len(operands),
        out_specs=[anywhere] * 3,
        input_output_aliases={len(operands) - 2: 0, len(operands) - 1: 1} if earlier else {},
        scratch_shapes=[
            pltpu.SMEM(small[0].shape, jnp.int32),
            pltpu.SMEM(small[1].shape, jnp.int32),
            pltpu.SMEM(small[2].shape, F32),
            pltpu.SMEM((slots + 1,), jnp.int32),
            pltpu.VMEM((slots, tokens, lanes), BF16),
            pltpu.VMEM((slots, tokens, lanes), BF16),
            pltpu.VMEM((slots, 2, tokens, width), BF16),
            pltpu.VMEM((2, prefix_len, width), BF16),
            pltpu.VMEM((n_dp, TAIL, width), BF16),
            pltpu.VMEM((slots, tokens, lanes), BF16),
            pltpu.VMEM((slots, 2, tokens, width), BF16),
            pltpu.VMEM((2, prefix_len, width), BF16),
            pltpu.SemaphoreType.DMA((3 + n_dp,)),
            pltpu.SemaphoreType.DMA((2,)),
            pltpu.SemaphoreType.DMA((slots, 4)),
            pltpu.SemaphoreType.DMA((slots, 3)),
        ],
        compiler_params=pltpu.CompilerParams(vmem_limit_bytes=48 * 1024 * 1024),
        cost_estimate=pl.CostEstimate(
            flops=2 * 5 * slots * tokens * group_size * kv_heads * (prefix_len + tokens) * HD,
            bytes_accessed=2 * slots * tokens * (3 * lanes + 4 * width),
            transcendentals=0,
        ),
        name="group_grads",
    )(*operands)


def make_payload(prompt_kv, rewards, my_prompts):
    high = lax.reduce_precision(rewards, 8, 7)
    middle = lax.reduce_precision(rewards - high, 8, 7)
    low = rewards - high - middle
    rows = jnp.stack([high, middle, low, my_prompts.astype(F32)]).astype(BF16)
    rows = jnp.pad(
        rows,
        ((0, TAIL - rows.shape[0]), (0, prompt_kv.shape[2] - rows.shape[1])),
        constant_values=-1,
    )
    return jnp.concatenate([prompt_kv, jnp.broadcast_to(rows, (2,) + rows.shape)], axis=1)


def far_kernel(dims, *refs):
    n_dp, count, slots, kv_heads, group_size, tokens, prefix_len = dims
    groups = count
    (resp_prompt, resp_len, rewards, q_hbm, og_hbm, kv_hbm, prompts, q_out, self_out, prefix_outs,
     totals, lens, factors, q, og, kv, prefix, out, own, grads, sem_in, sem_prefix, sem_out, sem_grads) = refs
    me = lax.axis_index("dp")
    width = kv_heads * HD

    for p in range(n_dp):
        totals[p] = 0.0

    def at_rows(slot):
        return pl.ds(pl.multiple_of(slot * tokens, tokens), tokens)

    def copies_in(slot):
        rows = at_rows(slot)
        return (
            pltpu.make_async_copy(q_hbm.at[rows], q.at[slot], sem_in.at[slot, 0]),
            pltpu.make_async_copy(og_hbm.at[rows], og.at[slot], sem_in.at[slot, 1]),
            pltpu.make_async_copy(kv_hbm.at[0, rows], kv.at[slot, 0], sem_in.at[slot, 2]),
            pltpu.make_async_copy(kv_hbm.at[1, rows], kv.at[slot, 1], sem_in.at[slot, 3]),
        )

    def prefix_copy(g):
        prompt = resp_prompt[me * count + g]
        return pltpu.make_async_copy(prompts.at[prompt], prefix.at[g], sem_prefix.at[g])

    def copies_out(slot):
        rows = at_rows(slot)
        return (
            pltpu.make_async_copy(out.at[slot], q_out.at[rows], sem_out.at[slot, 0]),
            pltpu.make_async_copy(own.at[slot, 0], self_out.at[0, rows], sem_out.at[slot, 1]),
            pltpu.make_async_copy(own.at[slot, 1], self_out.at[1, rows], sem_out.at[slot, 2]),
        )

    def grads_copy(g):
        return pltpu.make_async_copy(grads.at[g], prefix_outs.at[g], sem_grads.at[g])

    for g in range(groups):
        prefix_copy(g).start()

        def start(n, _):
            for copy in copies_in(g * slots + n):
                copy.start()
            return 0

        lax.fori_loop(0, slots, start, 0)

    def add(i, _):
        prompt = resp_prompt[i]
        totals[prompt] = totals[prompt] + rewards[i]
        return 0

    lax.fori_loop(0, n_dp * count, add, 0)

    def find_factor(slot, _):
        length = resp_len[slot]
        place = me * count + slot
        advantage = rewards[place] - totals[resp_prompt[place]] / count
        lens[slot] = length
        factors[slot] = advantage * (tokens / length.astype(F32))
        return 0

    lax.fori_loop(0, count, find_factor, 0)

    def one_group(g, _):
        base = g * slots

        def wait(n, _):
            for copy in copies_in(base + n):
                copy.wait()
            return 0

        lax.fori_loop(0, slots, wait, 0)
        attend_group(
            slots, base, group_size, kv_heads, tokens, prefix_len, q, og, kv, prefix.at[g],
            [lens[base + j] for j in range(slots)], [factors[base + j] for j in range(slots)],
            out, own, grads.at[g],
        )

        def send(n, _):
            for copy in copies_out(base + n):
                copy.start()
            return 0

        lax.fori_loop(0, slots, send, 0)
        return 0

    for g in range(groups):
        prefix_copy(g).wait()
    lax.fori_loop(0, groups, one_group, 0)
    for g in range(groups):
        grads_copy(g).start()

    def finish(slot, _):
        for copy in copies_out(slot):
            copy.wait()
        return 0

    lax.fori_loop(0, count, finish, 0)
    for g in range(groups):
        grads_copy(g).wait()


def far_shards(dims, prompt_kv, resp_q, resp_kv, out_grad, rewards, resp_prompt, resp_len, my_prompts):
    n_dp, count, slots, kv_heads, group_size, tokens, prefix_len = dims
    assert slots == 1
    width = kv_heads * HD
    lanes = resp_q.shape[1]
    smem = pl.BlockSpec(memory_space=pltpu.SMEM)
    anywhere = pl.BlockSpec(memory_space=pl.ANY)
    q_out, self_out, per_resp = pl.pallas_call(
        functools.partial(far_kernel, dims),
        out_shape=[
            jax.ShapeDtypeStruct(resp_q.shape, BF16),
            jax.ShapeDtypeStruct(resp_kv.shape, BF16),
            jax.ShapeDtypeStruct((count, 2, prefix_len, width), BF16),
        ],
        in_specs=[smem] * 3 + [anywhere] * 4,
        out_specs=[anywhere] * 3,
        scratch_shapes=[
            pltpu.SMEM((n_dp,), F32),
            pltpu.SMEM((count,), jnp.int32),
            pltpu.SMEM((count,), F32),
            pltpu.VMEM((count, tokens, lanes), BF16),
            pltpu.VMEM((count, tokens, lanes), BF16),
            pltpu.VMEM((count, 2, tokens, width), BF16),
            pltpu.VMEM((count, 2, prefix_len, width), BF16),
            pltpu.VMEM((count, tokens, lanes), BF16),
            pltpu.VMEM((count, 2, tokens, width), BF16),
            pltpu.VMEM((count, 2, prefix_len, width), BF16),
            pltpu.SemaphoreType.DMA((count, 4)),
            pltpu.SemaphoreType.DMA((count,)),
            pltpu.SemaphoreType.DMA((count, 3)),
            pltpu.SemaphoreType.DMA((count,)),
        ],
        compiler_params=pltpu.CompilerParams(vmem_limit_bytes=48 * 1024 * 1024),
        name="far_grads",
    )(
        resp_prompt,
        resp_len,
        lax.all_gather(rewards, "dp", axis=0, tiled=True),
        resp_q,
        out_grad,
        resp_kv,
        lax.all_gather(prompt_kv, "dp", axis=0),
    )
    route = (jnp.arange(n_dp, dtype=jnp.int32)[:, None] == my_prompts[None, :]).astype(BF16)
    outgoing = jnp.dot(route, per_resp.reshape(count, -1), preferred_element_type=F32).astype(BF16)
    outgoing = outgoing.reshape((n_dp,) + prompt_kv.shape)
    incoming = lax.all_to_all(outgoing, "dp", split_axis=0, concat_axis=0, tiled=True)
    prefix_out = jnp.sum(incoming, axis=0, dtype=F32).astype(BF16)
    return (q_out, self_out, prefix_out)


def shards(prompt_kv, resp_q, resp_kv, out_grad, rewards, resp_prompt, resp_len):
    n_dp = lax.axis_size("dp")
    count = rewards.shape[0]
    tokens = resp_q.shape[0] // count
    prefix_len, width = prompt_kv.shape[1:]
    kv_heads = width // HD
    group_size = resp_q.shape[1] // width
    slots = (count + n_dp - 1) // n_dp
    dims = (n_dp, count, slots, kv_heads, group_size, tokens, prefix_len)
    my_prompts = lax.dynamic_slice_in_dim(resp_prompt, lax.axis_index("dp") * count, count)
    if count // slots != n_dp:
        return far_shards(dims, prompt_kv, resp_q, resp_kv, out_grad, rewards, resp_prompt, resp_len, my_prompts)

    payload = make_payload(prompt_kv, rewards, my_prompts)
    payloads = [payload] + [
        lax.ppermute(payload, "dp", [((i + s) % n_dp, i) for i in range(n_dp)])
        for s in range(1, n_dp)
    ]
    earlier = ()
    arrived = []
    for turn in [*range(FIRST, n_dp), *range(FIRST)]:
        *earlier, grads = near_grads(
            turn, dims, (resp_prompt, resp_len, rewards), payloads, resp_q, out_grad, resp_kv, earlier
        )
        if turn:
            grads = lax.ppermute(grads, "dp", [(i, (i + turn) % n_dp) for i in range(n_dp)])
        arrived.append(grads)
    prefix_out = sum(part.astype(F32) for part in arrived).astype(BF16)
    return (*earlier, prefix_out)


def solution(mesh):
    in_specs = (
        P(None, ("groups", "dp"), "tensor"),
        P(("groups", "dp"), "tensor"),
        P(None, ("groups", "dp"), "tensor"),
        P(("groups", "dp"), "tensor"),
        P(("groups", "dp")),
        P("groups"),
        P(("groups", "dp")),
    )
    out_specs = (
        P(("groups", "dp"), "tensor"),
        P(None, ("groups", "dp"), "tensor"),
        P(None, ("groups", "dp"), "tensor"),
    )
    return jax.shard_map(shards, mesh=mesh, in_specs=in_specs, out_specs=out_specs, check_vma=False)
```

```python
import functools
import math

import jax
import jax.numpy as jnp
from jax import lax
from jax.experimental import pallas as pl
from jax.experimental.pallas import tpu as pltpu
from jax.sharding import PartitionSpec as P

HD = 128
NEG = -1e30
FIRST = 1
F32 = jnp.float32
BF16 = jnp.bfloat16


def dot(a, b, dims):
    return lax.dot_general(a, b, (dims, ((), ())), preferred_element_type=F32)


NN = ((1,), (0,))
NT = ((1,), (1,))
TN = ((0,), (0,))


def attend_group(slots, base, group_size, kv_heads, tokens, prefix_len, q, og, kv, prefix, lens, factors, out, self_out, prefix_out):
    scale = 1.0 / math.sqrt(HD)
    log_scale = scale * math.log2(math.e)
    whole = group_size - group_size % 2
    pairs = [(j, j + 1) if j + 1 < slots else (j, j) for j in range(0, slots, 2)]
    most = max(whole, 2) * tokens
    assert tokens & (tokens - 1) == 0
    lane = lax.broadcasted_iota(jnp.int32, (1, most), 1)
    token = lane & (tokens - 1)
    key = lax.broadcasted_iota(jnp.int32, (tokens, most), 0)
    causal = key <= (lax.broadcasted_iota(jnp.int32, (tokens, most), 1) & (tokens - 1))
    left = lane[:, : 2 * tokens] < tokens

    def head(k, h):
        at = (k * group_size + h) * HD
        return slice(at, at + HD)

    def rows(ref, k, blocks):
        return jnp.concatenate([ref[base + j, :, head(k, h)] for j, h in blocks], axis=0)

    class Heads:
        pass

    heads, chunks = [], []
    for k in range(kv_heads):
        t = Heads()
        t.cols = slice(k * HD, (k + 1) * HD)
        t.key_p, t.value_p = prefix[0, :, t.cols], prefix[1, :, t.cols]
        t.key_pt = t.key_p.T
        t.key_acc = t.value_acc = None
        t.key_self, t.value_self, t.left_over = {}, {}, 0
        heads.append(t)
        for pair in pairs:
            p = Heads()
            p.keys = [kv[base + j, 0, :, t.cols] for j in pair]
            p.values = [kv[base + j, 1, :, t.cols] for j in pair]
            p.key_pair = jnp.concatenate(p.keys, axis=0)
            p.value_pair = jnp.concatenate(p.values, axis=0)
            p.key_t = jnp.concatenate([t.key_pt, p.key_pair.T], axis=1)
            for n in range(2 if pair[0] != pair[1] else 1):
                c = Heads()
                c.k, c.t, c.p, c.pair, c.place = k, t, p, pair, n
                c.blocks = [(pair[n], h) for h in range(whole)]
                c.shared = False
                chunks.append(c)
            if group_size % 2:
                c = Heads()
                c.k, c.t, c.p, c.pair = k, t, p, pair
                c.blocks = [(j, group_size - 1) for j in pair]
                c.shared = True
                chunks.append(c)
        t.left_over = len([c for c in chunks if c.t is t])

    def own(both):
        return jnp.where(left, both[:tokens], both[tokens:])

    def spread(part):
        none = jnp.zeros_like(part)
        return jnp.concatenate([jnp.where(left, part, none), jnp.where(left, none, part)], axis=0)

    def products(c):
        t, p = c.t, c.p
        c.q_rows, c.g_rows = rows(q, c.k, c.blocks), rows(og, c.k, c.blocks)
        key_s, value_s = (
            (p.key_pair, p.value_pair) if c.shared else (p.keys[c.place], p.values[c.place])
        )
        c.scores = dot(jnp.concatenate([t.key_p, key_s], axis=0), c.q_rows, NT)
        c.gw = dot(jnp.concatenate([t.value_p, value_s], axis=0), c.g_rows, NT)

    def weigh(c):
        lanes = len(c.blocks) * tokens
        scores_p, scores_s = c.scores[:prefix_len], c.scores[prefix_len:]
        c.gw_p, c.gw_s = c.gw[:prefix_len], c.gw[prefix_len:]
        if c.shared:
            scores_s, c.gw_s = own(scores_s), own(c.gw_s)
        scores_s = jnp.where(causal[:, :lanes], scores_s, NEG)
        top = jnp.maximum(
            jnp.max(scores_p, axis=0, keepdims=True), jnp.max(scores_s, axis=0, keepdims=True)
        )
        c.e_p = jnp.exp2((scores_p - top) * log_scale)
        c.e_s = jnp.exp2((scores_s - top) * log_scale)
        total = jnp.sum(c.e_p, axis=0, keepdims=True) + jnp.sum(c.e_s, axis=0, keepdims=True)
        weighted = jnp.sum(c.e_p * c.gw_p, axis=0, keepdims=True) + jnp.sum(
            c.e_s * c.gw_s, axis=0, keepdims=True
        )
        if c.shared:
            first, second = c.pair
            length = jnp.where(left, lens[first], lens[second] if first != second else 0)
            gain = jnp.where(left, factors[first], factors[second])
        else:
            length, gain = lens[c.pair[c.place]], factors[c.pair[c.place]]
        inverse = 1.0 / total
        c.delta = weighted * inverse
        c.gain = inverse * jnp.where(token[:, :lanes] < length, gain, 0.0)

    def gradients(c):
        w_p, w_s = c.e_p * c.gain, c.e_s * c.gain
        d_p = (w_p * (c.gw_p - c.delta)).astype(BF16)
        d_s = (w_s * (c.gw_s - c.delta)).astype(BF16)
        w_p, w_s = w_p.astype(BF16), w_s.astype(BF16)
        if c.shared:
            d_s, w_s = spread(d_s), spread(w_s)
            c.d_all = c.d_wide = jnp.concatenate([d_p, d_s], axis=0)
        else:
            c.d_all = jnp.concatenate([d_p, d_s], axis=0)
            empty = jnp.zeros_like(d_s)
            c.d_wide = jnp.concatenate([d_p, d_s, empty] if c.place == 0 else [d_p, empty, d_s], axis=0)
        c.w_all = jnp.concatenate([w_p, w_s], axis=0)

    def outgoing(c):
        t = c.t
        q_grad = (dot(c.p.key_t, c.d_wide, NN) * scale).astype(BF16).T
        kg = dot(c.d_all, c.q_rows, NN)
        vg = dot(c.w_all, c.g_rows, NN)
        targets = list(dict.fromkeys(c.pair)) if c.shared else [c.pair[c.place]]
        for n, (j, h) in enumerate(c.blocks):
            if not c.shared or n < len(targets):
                out[base + j, :, head(c.k, h)] = q_grad[n * tokens : (n + 1) * tokens]
        t.key_acc = kg[:prefix_len] if t.key_acc is None else t.key_acc + kg[:prefix_len]
        t.value_acc = vg[:prefix_len] if t.value_acc is None else t.value_acc + vg[:prefix_len]
        for n, j in enumerate(targets):
            at = slice(prefix_len + n * tokens, prefix_len + (n + 1) * tokens)
            t.key_self.setdefault(j, []).append(kg[at])
            t.value_self.setdefault(j, []).append(vg[at])
        t.left_over -= 1
        if t.left_over == 0:
            for j in range(slots):
                self_out[base + j, 0, :, t.cols] = (sum(t.key_self[j]) * scale).astype(BF16)
                self_out[base + j, 1, :, t.cols] = sum(t.value_self[j]).astype(BF16)
            prefix_out[0, :, t.cols] = (t.key_acc * scale).astype(BF16)
            prefix_out[1, :, t.cols] = t.value_acc.astype(BF16)

    stages = (products, weigh, gradients, outgoing)
    for step in range(len(chunks) + len(stages) - 1):
        for late, stage in enumerate(stages):
            if 0 <= step - late < len(chunks):
                stage(chunks[step - late])


def group_kernel(turn, dims, refs):
    n_dp, count, slots, kv_heads, group_size, tokens, prefix_len = dims
    refs = list(refs)
    n_small = 2 + n_dp
    small_hbm = refs[:n_small]
    prompt_hbm, q_hbm, og_hbm, kv_hbm = refs[n_small : n_small + 4]
    refs = refs[n_small + 4 + (2 if turn != FIRST else 0) :]
    q_out, self_out, grads_out = refs[:3]
    resp_prompt, resp_len, *rewards = refs[3 : 3 + n_small]
    order, q, og, kv, prefix, out, own, grads, sem_small, sem_prefix, sem_in, sem_out = refs[3 + n_small :]
    me = lax.axis_index("dp")
    prompt = lax.rem(me + turn, n_dp)

    small = [
        pltpu.make_async_copy(src, dst, sem_small.at[n])
        for n, (src, dst) in enumerate(zip(small_hbm, (resp_prompt, resp_len, *rewards)))
    ]
    prefix_copy = pltpu.make_async_copy(prompt_hbm, prefix, sem_prefix.at[0])
    for copy in small + [prefix_copy]:
        copy.start()
    small[0].wait()
    found = 0
    for i in range(count):
        order[found] = i
        found = found + (resp_prompt[me * count + i] == prompt).astype(jnp.int32)

    picked = [order[j] for j in range(slots)]
    rows = [pl.ds(pl.multiple_of(i * tokens, tokens), tokens) for i in picked]
    copies_in, copies_out = [], []
    for j in range(slots):
        copies_in += [
            pltpu.make_async_copy(q_hbm.at[rows[j]], q.at[j], sem_in.at[j, 0]),
            pltpu.make_async_copy(og_hbm.at[rows[j]], og.at[j], sem_in.at[j, 1]),
            pltpu.make_async_copy(kv_hbm.at[0, rows[j]], kv.at[j, 0], sem_in.at[j, 2]),
            pltpu.make_async_copy(kv_hbm.at[1, rows[j]], kv.at[j, 1], sem_in.at[j, 3]),
        ]
        copies_out += [
            pltpu.make_async_copy(out.at[j], q_out.at[rows[j]], sem_out.at[j, 0]),
            pltpu.make_async_copy(own.at[j, 0], self_out.at[0, rows[j]], sem_out.at[j, 1]),
            pltpu.make_async_copy(own.at[j, 1], self_out.at[1, rows[j]], sem_out.at[j, 2]),
        ]
    for copy in copies_in:
        copy.start()

    for copy in small[1:]:
        copy.wait()
    total = jnp.float32(0.0)
    for away in range(n_dp):
        source = lax.rem(me + away, n_dp) * count
        for i in range(count):
            total += jnp.where(resp_prompt[source + i] == prompt, rewards[away][i], 0.0)
    lens = [resp_len[i] for i in picked]
    factors = [
        (rewards[0][i] - total / count) * (tokens / length.astype(F32))
        for i, length in zip(picked, lens)
    ]
    for copy in [prefix_copy] + copies_in:
        copy.wait()
    attend_group(
        slots, 0, group_size, kv_heads, tokens, prefix_len, q, og, kv, prefix, lens, factors, out, own, grads
    )
    last = pltpu.make_async_copy(grads, grads_out, sem_prefix.at[0])
    last.start()
    for copy in copies_out:
        copy.start()
    for copy in copies_out + [last]:
        copy.wait()


def near_grads(turn, dims, small, prompt, resp_q, out_grad, resp_kv, earlier):
    n_dp, count, slots, kv_heads, group_size, tokens, prefix_len = dims
    width = kv_heads * HD
    anywhere = pl.BlockSpec(memory_space=pltpu.HBM)
    operands = [*small, prompt, resp_q, out_grad, resp_kv, *earlier]
    lanes = resp_q.shape[1]
    return pl.pallas_call(
        lambda *refs: group_kernel(turn, dims, refs),
        out_shape=[
            jax.ShapeDtypeStruct(resp_q.shape, BF16),
            jax.ShapeDtypeStruct(resp_kv.shape, BF16),
            jax.ShapeDtypeStruct((2, prefix_len, width), BF16),
        ],
        in_specs=[anywhere] * len(operands),
        out_specs=[anywhere] * 3,
        input_output_aliases={len(operands) - 2: 0, len(operands) - 1: 1} if earlier else {},
        scratch_shapes=[
            *[pltpu.SMEM(x.shape, x.dtype) for x in small],
            pltpu.SMEM((slots + 1,), jnp.int32),
            pltpu.VMEM((slots, tokens, lanes), BF16),
            pltpu.VMEM((slots, tokens, lanes), BF16),
            pltpu.VMEM((slots, 2, tokens, width), BF16),
            pltpu.VMEM((2, prefix_len, width), BF16),
            pltpu.VMEM((slots, tokens, lanes), BF16),
            pltpu.VMEM((slots, 2, tokens, width), BF16),
            pltpu.VMEM((2, prefix_len, width), BF16),
            pltpu.SemaphoreType.DMA((len(small),)),
            pltpu.SemaphoreType.DMA((2,)),
            pltpu.SemaphoreType.DMA((slots, 4)),
            pltpu.SemaphoreType.DMA((slots, 3)),
        ],
        compiler_params=pltpu.CompilerParams(vmem_limit_bytes=48 * 1024 * 1024),
        cost_estimate=pl.CostEstimate(
            flops=2 * 5 * slots * tokens * group_size * kv_heads * (prefix_len + tokens) * HD,
            bytes_accessed=2 * slots * tokens * (3 * lanes + 4 * width),
            transcendentals=0,
        ),
        name="group_grads",
    )(*operands)


def far_kernel(dims, *refs):
    n_dp, count, slots, kv_heads, group_size, tokens, prefix_len = dims
    groups = count
    (resp_prompt, resp_len, rewards, q_hbm, og_hbm, kv_hbm, prompts, q_out, self_out, prefix_outs,
     totals, lens, factors, q, og, kv, prefix, out, own, grads, sem_in, sem_prefix, sem_out, sem_grads) = refs
    me = lax.axis_index("dp")
    width = kv_heads * HD

    for p in range(n_dp):
        totals[p] = 0.0

    def at_rows(slot):
        return pl.ds(pl.multiple_of(slot * tokens, tokens), tokens)

    def copies_in(slot):
        rows = at_rows(slot)
        return (
            pltpu.make_async_copy(q_hbm.at[rows], q.at[slot], sem_in.at[slot, 0]),
            pltpu.make_async_copy(og_hbm.at[rows], og.at[slot], sem_in.at[slot, 1]),
            pltpu.make_async_copy(kv_hbm.at[0, rows], kv.at[slot, 0], sem_in.at[slot, 2]),
            pltpu.make_async_copy(kv_hbm.at[1, rows], kv.at[slot, 1], sem_in.at[slot, 3]),
        )

    def prefix_copy(g):
        prompt = resp_prompt[me * count + g]
        return pltpu.make_async_copy(prompts.at[prompt], prefix.at[g], sem_prefix.at[g])

    def copies_out(slot):
        rows = at_rows(slot)
        return (
            pltpu.make_async_copy(out.at[slot], q_out.at[rows], sem_out.at[slot, 0]),
            pltpu.make_async_copy(own.at[slot, 0], self_out.at[0, rows], sem_out.at[slot, 1]),
            pltpu.make_async_copy(own.at[slot, 1], self_out.at[1, rows], sem_out.at[slot, 2]),
        )

    def grads_copy(g):
        return pltpu.make_async_copy(grads.at[g], prefix_outs.at[g], sem_grads.at[g])

    for g in range(groups):
        prefix_copy(g).start()

        def start(n, _):
            for copy in copies_in(g * slots + n):
                copy.start()
            return 0

        lax.fori_loop(0, slots, start, 0)

    def add(i, _):
        prompt = resp_prompt[i]
        totals[prompt] = totals[prompt] + rewards[i]
        return 0

    lax.fori_loop(0, n_dp * count, add, 0)

    def find_factor(slot, _):
        length = resp_len[slot]
        place = me * count + slot
        advantage = rewards[place] - totals[resp_prompt[place]] / count
        lens[slot] = length
        factors[slot] = advantage * (tokens / length.astype(F32))
        return 0

    lax.fori_loop(0, count, find_factor, 0)

    def one_group(g, _):
        base = g * slots

        def wait(n, _):
            for copy in copies_in(base + n):
                copy.wait()
            return 0

        lax.fori_loop(0, slots, wait, 0)
        attend_group(
            slots, base, group_size, kv_heads, tokens, prefix_len, q, og, kv, prefix.at[g],
            [lens[base + j] for j in range(slots)], [factors[base + j] for j in range(slots)],
            out, own, grads.at[g],
        )

        def send(n, _):
            for copy in copies_out(base + n):
                copy.start()
            return 0

        lax.fori_loop(0, slots, send, 0)
        return 0

    for g in range(groups):
        prefix_copy(g).wait()
    lax.fori_loop(0, groups, one_group, 0)
    for g in range(groups):
        grads_copy(g).start()

    def finish(slot, _):
        for copy in copies_out(slot):
            copy.wait()
        return 0

    lax.fori_loop(0, count, finish, 0)
    for g in range(groups):
        grads_copy(g).wait()


def far_shards(dims, prompt_kv, resp_q, resp_kv, out_grad, rewards, resp_prompt, resp_len, my_prompts):
    n_dp, count, slots, kv_heads, group_size, tokens, prefix_len = dims
    assert slots == 1
    width = kv_heads * HD
    lanes = resp_q.shape[1]
    smem = pl.BlockSpec(memory_space=pltpu.SMEM)
    anywhere = pl.BlockSpec(memory_space=pl.ANY)
    q_out, self_out, per_resp = pl.pallas_call(
        functools.partial(far_kernel, dims),
        out_shape=[
            jax.ShapeDtypeStruct(resp_q.shape, BF16),
            jax.ShapeDtypeStruct(resp_kv.shape, BF16),
            jax.ShapeDtypeStruct((count, 2, prefix_len, width), BF16),
        ],
        in_specs=[smem] * 3 + [anywhere] * 4,
        out_specs=[anywhere] * 3,
        scratch_shapes=[
            pltpu.SMEM((n_dp,), F32),
            pltpu.SMEM((count,), jnp.int32),
            pltpu.SMEM((count,), F32),
            pltpu.VMEM((count, tokens, lanes), BF16),
            pltpu.VMEM((count, tokens, lanes), BF16),
            pltpu.VMEM((count, 2, tokens, width), BF16),
            pltpu.VMEM((count, 2, prefix_len, width), BF16),
            pltpu.VMEM((count, tokens, lanes), BF16),
            pltpu.VMEM((count, 2, tokens, width), BF16),
            pltpu.VMEM((count, 2, prefix_len, width), BF16),
            pltpu.SemaphoreType.DMA((count, 4)),
            pltpu.SemaphoreType.DMA((count,)),
            pltpu.SemaphoreType.DMA((count, 3)),
            pltpu.SemaphoreType.DMA((count,)),
        ],
        compiler_params=pltpu.CompilerParams(vmem_limit_bytes=48 * 1024 * 1024),
        name="far_grads",
    )(
        resp_prompt,
        resp_len,
        lax.all_gather(rewards, "dp", axis=0, tiled=True),
        resp_q,
        out_grad,
        resp_kv,
        lax.all_gather(prompt_kv, "dp", axis=0),
    )
    route = (jnp.arange(n_dp, dtype=jnp.int32)[:, None] == my_prompts[None, :]).astype(BF16)
    outgoing = jnp.dot(route, per_resp.reshape(count, -1), preferred_element_type=F32).astype(BF16)
    outgoing = outgoing.reshape((n_dp,) + prompt_kv.shape)
    incoming = lax.all_to_all(outgoing, "dp", split_axis=0, concat_axis=0, tiled=True)
    prefix_out = jnp.sum(incoming, axis=0, dtype=F32).astype(BF16)
    return (q_out, self_out, prefix_out)


def shards(prompt_kv, resp_q, resp_kv, out_grad, rewards, resp_prompt, resp_len):
    n_dp = lax.axis_size("dp")
    count = rewards.shape[0]
    tokens = resp_q.shape[0] // count
    prefix_len, width = prompt_kv.shape[1:]
    kv_heads = width // HD
    group_size = resp_q.shape[1] // width
    slots = (count + n_dp - 1) // n_dp
    dims = (n_dp, count, slots, kv_heads, group_size, tokens, prefix_len)
    my_prompts = lax.dynamic_slice_in_dim(resp_prompt, lax.axis_index("dp") * count, count)
    if count // slots != n_dp:
        return far_shards(dims, prompt_kv, resp_q, resp_kv, out_grad, rewards, resp_prompt, resp_len, my_prompts)

    def from_ahead(x, s):
        return lax.ppermute(x, "dp", [((i + s) % n_dp, i) for i in range(n_dp)])

    all_rewards = [rewards] + [from_ahead(rewards, s) for s in range(1, n_dp)]
    prompts = [prompt_kv] + [from_ahead(prompt_kv, s) for s in range(1, n_dp)]
    earlier = ()
    arrived = []
    for turn in [*range(FIRST, n_dp), *range(FIRST)]:
        *earlier, grads = near_grads(
            turn, dims, (resp_prompt, resp_len, *all_rewards), prompts[turn], resp_q, out_grad, resp_kv, earlier
        )
        if turn:
            grads = lax.ppermute(grads, "dp", [(i, (i + turn) % n_dp) for i in range(n_dp)])
        arrived.append(grads)
    prefix_out = sum(part.astype(F32) for part in arrived).astype(BF16)
    return (*earlier, prefix_out)


def solution(mesh):
    in_specs = (
        P(None, ("groups", "dp"), "tensor"),
        P(("groups", "dp"), "tensor"),
        P(None, ("groups", "dp"), "tensor"),
        P(("groups", "dp"), "tensor"),
        P(("groups", "dp")),
        P("groups"),
        P(("groups", "dp")),
    )
    out_specs = (
        P(("groups", "dp"), "tensor"),
        P(None, ("groups", "dp"), "tensor"),
        P(None, ("groups", "dp"), "tensor"),
    )
    return jax.shard_map(shards, mesh=mesh, in_specs=in_specs, out_specs=out_specs, check_vma=False)
```

```python
import functools
import math
from typing import NamedTuple

import jax
import jax.numpy as jnp
from jax import lax
from jax.experimental import pallas as pl
from jax.experimental.pallas import tpu as pltpu
from jax.sharding import PartitionSpec as P

HD = 128
NEG = -1e30
TAIL = 16
F32 = jnp.float32
BF16 = jnp.bfloat16
VMEM_BYTES = 63 * 1024 * 1024
ANYWHERE = pl.BlockSpec(memory_space=pl.ANY)


class Sizes(NamedTuple):
    n_dp: int
    count: int
    slots: int
    kv_heads: int
    group_size: int
    tokens: int
    prefix_len: int

    @property
    def width(self):
        return self.kv_heads * HD

    @property
    def lanes(self):
        return self.kv_heads * self.group_size * HD


def dot(a, b, dims):
    return lax.dot_general(a, b, (dims, ((), ())), preferred_element_type=F32)


NN = ((1,), (0,))
NT = ((1,), (1,))


class Bag:
    pass


def attend_pair(z, at, q, og, kv, prefix, lens, factors, out, own_out, sink, apart):
    tokens, prefix_len, group_size = z.tokens, z.prefix_len, z.group_size
    scale = 1.0 / math.sqrt(HD)
    log_scale = scale * math.log2(math.e)
    whole = group_size - group_size % 2
    single = len(at) == 1
    members = range(len(at))
    sides = (0, 0) if single else (0, 1)
    most = max(whole, 2) * tokens
    assert tokens & (tokens - 1) == 0
    token = lax.broadcasted_iota(jnp.int32, (1, most), 1) & (tokens - 1)
    key = lax.broadcasted_iota(jnp.int32, (tokens, most), 0)
    causal = key <= (lax.broadcasted_iota(jnp.int32, (tokens, most), 1) & (tokens - 1))
    left = lax.broadcasted_iota(jnp.int32, (1, 2 * tokens), 1) < tokens

    def head(k, h):
        start = (k * group_size + h) * HD
        return slice(start, start + HD)

    def rows(ref, k, blocks):
        return jnp.concatenate([ref[at[n], :, head(k, h)] for n, h in blocks], axis=0)

    def halves(part):
        none = jnp.zeros_like(part)
        return [jnp.where(left, part, none), jnp.where(left, none, part)]

    chunks = []
    for k in range(z.kv_heads):
        t = Bag()
        t.cols = slice(k * HD, (k + 1) * HD)
        t.key_p, t.value_p = prefix[0, :, t.cols], prefix[1, :, t.cols]
        t.keys = [kv[at[n], 0, :, t.cols] for n in sides]
        t.values = [kv[at[n], 1, :, t.cols] for n in sides]
        t.key_pair = jnp.concatenate(t.keys, axis=0)
        t.value_pair = jnp.concatenate(t.values, axis=0)
        t.key_t = jnp.concatenate([t.key_p.T, t.key_pair.T], axis=1)
        t.prefix_sums = {n: [] for n in members}
        t.self_sums = {n: [] for n in members}
        mine = []
        for n in members:
            c = Bag()
            c.k, c.t, c.side, c.blocks = k, t, n, [(n, h) for h in range(whole)]
            mine.append(c)
        if group_size % 2:
            c = Bag()
            c.k, c.t, c.side, c.blocks = k, t, None, [(n, group_size - 1) for n in sides]
            mine.append(c)
        t.left_over = len(mine)
        chunks += mine

    def products(c):
        t = c.t
        c.q_rows, c.g_rows = rows(q, c.k, c.blocks), rows(og, c.k, c.blocks)
        if c.side is None:
            key_s, value_s = t.key_pair, t.value_pair
        else:
            key_s, value_s = t.keys[c.side], t.values[c.side]
        c.scores = dot(jnp.concatenate([t.key_p, key_s], axis=0), c.q_rows, NT)
        c.gw = dot(jnp.concatenate([t.value_p, value_s], axis=0), c.g_rows, NT)

    def weigh(c):
        lanes = len(c.blocks) * tokens
        scores_p, scores_s = c.scores[:prefix_len], c.scores[prefix_len:]
        c.gw_p, c.gw_s = c.gw[:prefix_len], c.gw[prefix_len:]
        if c.side is None:
            scores_s = jnp.where(left, scores_s[:tokens], scores_s[tokens:])
            c.gw_s = jnp.where(left, c.gw_s[:tokens], c.gw_s[tokens:])
        scores_s = jnp.where(causal[:, :lanes], scores_s, NEG)
        top = jnp.maximum(
            jnp.max(scores_p, axis=0, keepdims=True), jnp.max(scores_s, axis=0, keepdims=True)
        )
        c.e_p = jnp.exp2((scores_p - top) * log_scale)
        c.e_s = jnp.exp2((scores_s - top) * log_scale)
        total = jnp.sum(c.e_p, axis=0, keepdims=True) + jnp.sum(c.e_s, axis=0, keepdims=True)
        weighted = jnp.sum(c.e_p * c.gw_p, axis=0, keepdims=True) + jnp.sum(
            c.e_s * c.gw_s, axis=0, keepdims=True
        )
        if c.side is None:
            length = jnp.where(left, lens[0], 0 if single else lens[1])
            gain = jnp.where(left, factors[0], factors[-1])
        else:
            length, gain = lens[c.side], factors[c.side]
        inverse = 1.0 / total
        c.delta = weighted * inverse
        c.gain = inverse * jnp.where(token[:, :lanes] < length, gain, 0.0)

    def gradients(c):
        w_p, w_s = c.e_p * c.gain, c.e_s * c.gain
        d_p = (w_p * (c.gw_p - c.delta)).astype(BF16)
        d_s = (w_s * (c.gw_s - c.delta)).astype(BF16)
        w_p, w_s = w_p.astype(BF16), w_s.astype(BF16)
        if c.side is None:
            d_s, w_s = halves(d_s), halves(w_s)
            c.d_wide = jnp.concatenate([d_p, *d_s], axis=0)
            c.d_all = jnp.concatenate([*halves(d_p), *d_s], axis=0) if apart else c.d_wide
            c.w_all = jnp.concatenate([*(halves(w_p) if apart else [w_p]), *w_s], axis=0)
        else:
            empty = jnp.zeros_like(d_s)
            c.d_wide = jnp.concatenate([d_p, empty, d_s] if c.side else [d_p, d_s, empty], axis=0)
            c.d_all = jnp.concatenate([d_p, d_s], axis=0)
            c.w_all = jnp.concatenate([w_p, w_s], axis=0)

    def outgoing(c):
        t = c.t
        q_grad = (dot(t.key_t, c.d_wide, NN) * scale).astype(BF16).T
        kg = dot(c.d_all, c.q_rows, NN)
        vg = dot(c.w_all, c.g_rows, NN)
        targets = members if c.side is None else [c.side]
        for place, (n, h) in enumerate(c.blocks):
            if c.side is not None or place < len(targets):
                out[at[n], :, head(c.k, h)] = q_grad[place * tokens : (place + 1) * tokens]
        many = 2 if c.side is None and apart else 1
        for place, n in enumerate(targets):
            if place < many:
                rows_p = slice(place * prefix_len, (place + 1) * prefix_len)
                t.prefix_sums[n if apart else 0].append((kg[rows_p], vg[rows_p]))
            start = many * prefix_len + place * tokens
            rows_s = slice(start, start + tokens)
            t.self_sums[n].append((kg[rows_s], vg[rows_s]))
        t.left_over -= 1
        if t.left_over == 0:
            for n in members:
                keys, values = zip(*t.self_sums[n])
                own_out[at[n], 0, :, t.cols] = (sum(keys) * scale).astype(BF16)
                own_out[at[n], 1, :, t.cols] = sum(values).astype(BF16)
                if apart or n == 0:
                    keys, values = zip(*t.prefix_sums[n])
                    sink(n, t.cols, sum(keys) * scale, sum(values))

    stages = (products, weigh, gradients, outgoing)
    for step in range(len(chunks) + len(stages) - 1):
        for late, stage in enumerate(stages):
            if 0 <= step - late < len(chunks):
                stage(chunks[step - late])


def token_rows(z, i):
    return pl.ds(pl.multiple_of(i * z.tokens, z.tokens), z.tokens)


def find_responses(z, me, turns, resp_prompt, order):
    for t, turn in enumerate(turns):
        prompt = lax.rem(me + turn, z.n_dp)
        found = t * z.slots
        for i in range(z.count):
            order[found] = i
            found = found + (resp_prompt[me * z.count + i] == prompt).astype(jnp.int32)


def prompt_total(z, prompt, tails):
    sums = jnp.zeros((1, tails.shape[2]), F32)
    for s in range(z.n_dp):
        tail = tails[s].astype(F32)
        sums += tail[0:1] + tail[1:2] + tail[2:3]
    lane = lax.broadcasted_iota(jnp.int32, sums.shape, 1)
    return jnp.sum(jnp.where(lane == prompt, sums, 0.0))


def reward_factor(z, reward, total, length):
    return (reward - total / z.count) * (z.tokens / length.astype(F32))


def pack_kernel(z, prompt_hbm, rewards_hbm, resp_prompt_hbm, payload, rewards, resp_prompt, tail, sems):
    me = lax.axis_index("dp")
    small = [
        pltpu.make_async_copy(rewards_hbm, rewards, sems.at[0]),
        pltpu.make_async_copy(resp_prompt_hbm, resp_prompt, sems.at[1]),
    ]
    large = [
        pltpu.make_async_copy(
            prompt_hbm.at[n], payload.at[pl.ds(n * z.prefix_len, z.prefix_len)], sems.at[2 + n]
        )
        for n in range(2)
    ]
    for copy in small + large:
        copy.start()
    for copy in small:
        copy.wait()
    lane = lax.broadcasted_iota(jnp.int32, (1, z.width), 1)
    sums = jnp.zeros((1, z.width), F32)
    for i in range(z.count):
        sums += jnp.where(lane == resp_prompt[me * z.count + i], rewards[i], 0.0)
    high = sums.astype(BF16).astype(F32)
    middle = (sums - high).astype(BF16).astype(F32)
    low = sums - high - middle
    row = lax.broadcasted_iota(jnp.int32, (TAIL, z.width), 0)
    pieces = jnp.where(row == 0, high, jnp.where(row == 1, middle, jnp.where(row == 2, low, 0.0)))
    tail[...] = pieces.astype(BF16)
    last = pltpu.make_async_copy(tail, payload.at[pl.ds(2 * z.prefix_len, TAIL)], sems.at[0])
    last.start()
    for copy in large + [last]:
        copy.wait()


def tail_copies(z, payloads, tails, sems):
    return [
        pltpu.make_async_copy(payloads[s].at[pl.ds(2 * z.prefix_len, TAIL)], tails.at[s], sems.at[s])
        for s in range(z.n_dp)
    ]


def near_kernel(z, turns, raw, aliased, *refs):
    refs = list(refs)
    small_hbm = refs[:3]
    q_hbm, og_hbm, kv_hbm = refs[3:6]
    n_payloads = 1 if raw else z.n_dp
    payloads = refs[6 : 6 + n_payloads]
    refs = refs[6 + n_payloads + aliased :]
    n_grads = 1 if raw else len(turns)
    q_out, self_out = refs[:2]
    grads_out = refs[2 : 2 + n_grads]
    (resp_prompt, resp_len, rewards, order, lens, factors, q, og, kv, prefix, tails, acc, out, own, grads,
     sem_small, sem_prefix, sem_in, sem_out, sem_grads) = refs[2 + n_grads :]
    me = lax.axis_index("dp")
    n_slots = len(turns) * z.slots
    per_unit = 2 - z.slots % 2
    units = n_slots // per_unit

    small = [
        pltpu.make_async_copy(src, dst, sem_small.at[n])
        for n, (src, dst) in enumerate(zip(small_hbm, (resp_prompt, resp_len, rewards)))
    ]
    for copy in small:
        copy.start()
    prefix_copies = [
        pltpu.make_async_copy(
            payloads[0 if raw else turn].at[pl.ds(n * z.prefix_len, z.prefix_len)],
            prefix.at[t, n],
            sem_prefix.at[t, n],
        )
        for t, turn in enumerate(turns)
        for n in range(2)
    ]
    late = [] if raw else tail_copies(z, payloads, tails, sem_grads)
    for copy in prefix_copies + late:
        copy.start()
    small[0].wait()
    find_responses(z, me, turns, resp_prompt, order)

    def copies_in(slot):
        rows = token_rows(z, order[slot])
        return (
            pltpu.make_async_copy(q_hbm.at[rows], q.at[slot], sem_in.at[slot, 0]),
            pltpu.make_async_copy(og_hbm.at[rows], og.at[slot], sem_in.at[slot, 1]),
            pltpu.make_async_copy(kv_hbm.at[0, rows], kv.at[slot, 0], sem_in.at[slot, 2]),
            pltpu.make_async_copy(kv_hbm.at[1, rows], kv.at[slot, 1], sem_in.at[slot, 3]),
        )

    def copies_out(slot):
        rows = token_rows(z, order[slot])
        return (
            pltpu.make_async_copy(out.at[slot], q_out.at[rows], sem_out.at[slot, 0]),
            pltpu.make_async_copy(own.at[slot, 0], self_out.at[0, rows], sem_out.at[slot, 1]),
            pltpu.make_async_copy(own.at[slot, 1], self_out.at[1, rows], sem_out.at[slot, 2]),
        )

    for slot in range(n_slots):
        for copy in copies_in(slot):
            copy.start()
    for copy in small[1:] + late:
        copy.wait()
    for t, turn in enumerate(turns):
        total = None if raw else prompt_total(z, lax.rem(me + turn, z.n_dp), tails)
        for slot in range(t * z.slots, (t + 1) * z.slots):
            i = order[slot]
            lens[slot] = resp_len[i]
            factors[slot] = 1.0 if raw else reward_factor(z, rewards[i], total, resp_len[i])
    if not raw:
        acc[...] = jnp.zeros(acc.shape, F32)
    for copy in prefix_copies:
        copy.wait()

    def unit(u, _):
        at = [u * per_unit + n for n in range(per_unit)]
        t = u // (z.slots // per_unit)
        for slot in at:
            for copy in copies_in(slot):
                copy.wait()

        def sink(n, cols, key_grad, value_grad):
            if raw:
                grads[at[n], 0, :, cols] = key_grad.astype(BF16)
                grads[at[n], 1, :, cols] = value_grad.astype(BF16)
            else:
                acc[t, 0, :, cols] += key_grad
                acc[t, 1, :, cols] += value_grad

        attend_pair(
            z, at, q, og, kv, prefix.at[t], [lens[n] for n in at], [factors[n] for n in at], out, own, sink, raw
        )
        for slot in at:
            for copy in copies_out(slot):
                copy.start()
        return 0

    lax.fori_loop(0, units, unit, 0)
    if raw:
        last = [pltpu.make_async_copy(grads, grads_out[0], sem_grads.at[0])]
    else:
        grads[...] = acc[...].astype(BF16)
        last = [
            pltpu.make_async_copy(grads.at[t], grads_out[t], sem_grads.at[t]) for t in range(len(turns))
        ]
    for copy in last:
        copy.start()
    for slot in range(n_slots):
        for copy in copies_out(slot):
            copy.wait()
    for copy in last:
        copy.wait()


def near_grads(z, turns, raw, small, resp_q, out_grad, resp_kv, payloads, earlier):
    n_slots = len(turns) * z.slots
    operands = [*small, resp_q, out_grad, resp_kv, *payloads, *earlier]
    one = (2, z.prefix_len, z.width)
    grads_shapes = [(z.slots,) + one] if raw else [one] * len(turns)
    return pl.pallas_call(
        functools.partial(near_kernel, z, turns, raw, len(earlier)),
        out_shape=[
            jax.ShapeDtypeStruct(resp_q.shape, BF16),
            jax.ShapeDtypeStruct(resp_kv.shape, BF16),
            *[jax.ShapeDtypeStruct(shape, BF16) for shape in grads_shapes],
        ],
        in_specs=[ANYWHERE] * len(operands),
        out_specs=[ANYWHERE] * (2 + len(grads_shapes)),
        input_output_aliases={len(operands) - 2: 0, len(operands) - 1: 1} if earlier else {},
        scratch_shapes=[
            *[pltpu.SMEM(x.shape, x.dtype) for x in small],
            pltpu.SMEM((n_slots + 1,), jnp.int32),
            pltpu.SMEM((n_slots,), jnp.int32),
            pltpu.SMEM((n_slots,), F32),
            pltpu.VMEM((n_slots, z.tokens, z.lanes), BF16),
            pltpu.VMEM((n_slots, z.tokens, z.lanes), BF16),
            pltpu.VMEM((n_slots, 2, z.tokens, z.width), BF16),
            pltpu.VMEM((len(turns),) + one, BF16),
            pltpu.VMEM((z.n_dp, TAIL, z.width), BF16),
            pltpu.VMEM((len(turns),) + one, F32),
            pltpu.VMEM((n_slots, z.tokens, z.lanes), BF16),
            pltpu.VMEM((n_slots, 2, z.tokens, z.width), BF16),
            pltpu.VMEM(grads_shapes[0] if raw else (len(turns),) + one, BF16),
            pltpu.SemaphoreType.DMA((len(small),)),
            pltpu.SemaphoreType.DMA((len(turns), 2)),
            pltpu.SemaphoreType.DMA((n_slots, 4)),
            pltpu.SemaphoreType.DMA((n_slots, 3)),
            pltpu.SemaphoreType.DMA((z.n_dp,)),
        ],
        compiler_params=pltpu.CompilerParams(vmem_limit_bytes=VMEM_BYTES),
        cost_estimate=pl.CostEstimate(flops=0, bytes_accessed=0, transcendentals=0),
        name="raw_grads" if raw else "group_grads",
    )(*operands)


def finish_kernel(z, *refs):
    refs = list(refs)
    small_hbm, payloads = refs[:3], refs[3 : 3 + z.n_dp]
    per_resp_hbm = refs[3 + z.n_dp]
    q_out, self_out, grads_out = refs[6 + z.n_dp : 9 + z.n_dp]
    (resp_prompt, resp_len, rewards, order, tails, q, own, per_resp, grads, sem_small, sem_in, sem_out) = refs[
        9 + z.n_dp :
    ]
    me = lax.axis_index("dp")
    small = [
        pltpu.make_async_copy(src, dst, sem_small.at[n])
        for n, (src, dst) in enumerate(zip(small_hbm, (resp_prompt, resp_len, rewards)))
    ]
    late = tail_copies(z, payloads, tails, sem_small.at[pl.ds(3, z.n_dp)])
    late.append(pltpu.make_async_copy(per_resp_hbm, per_resp, sem_small.at[3 + z.n_dp]))
    for copy in small + late:
        copy.start()
    small[0].wait()
    find_responses(z, me, (0,), resp_prompt, order)

    def moves(slot, back):
        rows = token_rows(z, order[slot])
        ends = [(q_out.at[rows], q.at[slot])]
        ends += [(self_out.at[n, rows], own.at[slot, n]) for n in range(2)]
        sems = sem_out if back else sem_in
        return [
            pltpu.make_async_copy(*(reversed(pair) if back else pair), sems.at[slot, n])
            for n, pair in enumerate(ends)
        ]

    for slot in range(z.slots):
        for copy in moves(slot, False):
            copy.start()
    for copy in small[1:] + late:
        copy.wait()
    total = prompt_total(z, me, tails)
    factors = [
        reward_factor(z, rewards[order[slot]], total, resp_len[order[slot]]) for slot in range(z.slots)
    ]
    summed = per_resp[0].astype(F32) * factors[0]
    for slot in range(1, z.slots):
        summed += per_resp[slot].astype(F32) * factors[slot]
    grads[...] = summed.astype(BF16)
    last = pltpu.make_async_copy(grads, grads_out, sem_small.at[0])
    last.start()
    for slot in range(z.slots):
        for copy in moves(slot, False):
            copy.wait()
        q[slot] = (q[slot].astype(F32) * factors[slot]).astype(BF16)
        own[slot] = (own[slot].astype(F32) * factors[slot]).astype(BF16)
        for copy in moves(slot, True):
            copy.start()
    for slot in range(z.slots):
        for copy in moves(slot, True):
            copy.wait()
    last.wait()


def finish(z, small, payloads, per_resp, q_out, self_out):
    operands = [*small, *payloads, per_resp, q_out, self_out]
    one = (2, z.prefix_len, z.width)
    return pl.pallas_call(
        functools.partial(finish_kernel, z),
        out_shape=[
            jax.ShapeDtypeStruct(q_out.shape, BF16),
            jax.ShapeDtypeStruct(self_out.shape, BF16),
            jax.ShapeDtypeStruct(one, BF16),
        ],
        in_specs=[ANYWHERE] * len(operands),
        out_specs=[ANYWHERE] * 3,
        input_output_aliases={len(operands) - 2: 0, len(operands) - 1: 1},
        scratch_shapes=[
            *[pltpu.SMEM(x.shape, x.dtype) for x in small],
            pltpu.SMEM((z.slots + 1,), jnp.int32),
            pltpu.VMEM((z.n_dp, TAIL, z.width), BF16),
            pltpu.VMEM((z.slots, z.tokens, z.lanes), BF16),
            pltpu.VMEM((z.slots, 2, z.tokens, z.width), BF16),
            pltpu.VMEM((z.slots,) + one, BF16),
            pltpu.VMEM(one, BF16),
            pltpu.SemaphoreType.DMA((len(small) + z.n_dp + 1,)),
            pltpu.SemaphoreType.DMA((z.slots, 3)),
            pltpu.SemaphoreType.DMA((z.slots, 3)),
        ],
        compiler_params=pltpu.CompilerParams(vmem_limit_bytes=VMEM_BYTES),
        cost_estimate=pl.CostEstimate(flops=0, bytes_accessed=0, transcendentals=0),
        name="finish_own",
    )(*operands)


def near_shards(z, prompt_kv, resp_q, resp_kv, out_grad, rewards, resp_prompt, resp_len):
    n_dp = z.n_dp
    small = (resp_prompt, resp_len, rewards)
    payload = pl.pallas_call(
        functools.partial(pack_kernel, z),
        out_shape=jax.ShapeDtypeStruct((2 * z.prefix_len + TAIL, z.width), BF16),
        in_specs=[ANYWHERE] * 3,
        out_specs=ANYWHERE,
        scratch_shapes=[
            pltpu.SMEM(rewards.shape, F32),
            pltpu.SMEM(resp_prompt.shape, jnp.int32),
            pltpu.VMEM((TAIL, z.width), BF16),
            pltpu.SemaphoreType.DMA((4,)),
        ],
        compiler_params=pltpu.CompilerParams(vmem_limit_bytes=VMEM_BYTES),
        name="pack",
    )(prompt_kv, rewards, resp_prompt)

    away = sorted(range(1, n_dp), key=lambda s: -min(s, n_dp - s))
    payloads = {0: payload}
    for s in away:
        payloads[s] = lax.ppermute(payload, "dp", [((i + s) % n_dp, i) for i in range(n_dp)])
    everyone = [payloads[s] for s in range(n_dp)]

    *written, per_resp = near_grads(z, (0,), True, small, resp_q, out_grad, resp_kv, [payload], ())
    first = len(away) // 2
    arrived = []
    for turns in (tuple(away[:first]), tuple(away[first:])):
        if not turns:
            continue
        results = near_grads(z, turns, False, small, resp_q, out_grad, resp_kv, everyone, written)
        written = results[:2]
        for turn, grads in zip(turns, results[2:]):
            arrived.append(lax.ppermute(grads, "dp", [(i, (i + turn) % n_dp) for i in range(n_dp)]))
    q_out, self_out, own_grads = finish(z, small, everyone, per_resp, *written)
    prefix_out = sum(part.astype(F32) for part in [own_grads, *arrived]).astype(BF16)
    return (q_out, self_out, prefix_out)


def far_kernel(z, *refs):
    (resp_prompt, resp_len, rewards, q_hbm, og_hbm, kv_hbm, prompts, q_out, self_out, prefix_outs,
     totals, lens, factors, q, og, kv, prefix, out, own, grads, sem_in, sem_prefix, sem_out) = refs
    me = lax.axis_index("dp")

    for p in range(z.n_dp):
        totals[p] = 0.0

    def copies_in(slot):
        rows = token_rows(z, slot)
        prompt = resp_prompt[me * z.count + slot]
        return (
            pltpu.make_async_copy(q_hbm.at[rows], q.at[slot], sem_in.at[slot, 0]),
            pltpu.make_async_copy(og_hbm.at[rows], og.at[slot], sem_in.at[slot, 1]),
            pltpu.make_async_copy(kv_hbm.at[0, rows], kv.at[slot, 0], sem_in.at[slot, 2]),
            pltpu.make_async_copy(kv_hbm.at[1, rows], kv.at[slot, 1], sem_in.at[slot, 3]),
            pltpu.make_async_copy(prompts.at[prompt], prefix.at[slot], sem_prefix.at[slot]),
        )

    def copies_out(slot):
        rows = token_rows(z, slot)
        return (
            pltpu.make_async_copy(out.at[slot], q_out.at[rows], sem_out.at[slot, 0]),
            pltpu.make_async_copy(own.at[slot, 0], self_out.at[0, rows], sem_out.at[slot, 1]),
            pltpu.make_async_copy(own.at[slot, 1], self_out.at[1, rows], sem_out.at[slot, 2]),
            pltpu.make_async_copy(grads.at[slot], prefix_outs.at[slot], sem_out.at[slot, 3]),
        )

    def start(slot, _):
        for copy in copies_in(slot):
            copy.start()
        return 0

    lax.fori_loop(0, z.count, start, 0)

    def add(i, _):
        prompt = resp_prompt[i]
        totals[prompt] = totals[prompt] + rewards[i]
        return 0

    lax.fori_loop(0, z.n_dp * z.count, add, 0)

    def find_factor(slot, _):
        place = me * z.count + slot
        lens[slot] = resp_len[slot]
        factors[slot] = reward_factor(z, rewards[place], totals[resp_prompt[place]], resp_len[slot])
        return 0

    lax.fori_loop(0, z.count, find_factor, 0)

    def unit(slot, _):
        for copy in copies_in(slot):
            copy.wait()

        def sink(_, cols, key_grad, value_grad):
            grads[slot, 0, :, cols] = key_grad.astype(BF16)
            grads[slot, 1, :, cols] = value_grad.astype(BF16)

        attend_pair(
            z, [slot], q, og, kv, prefix.at[slot], [lens[slot]], [factors[slot]], out, own, sink, True
        )
        for copy in copies_out(slot):
            copy.start()
        return 0

    lax.fori_loop(0, z.count, unit, 0)

    def end(slot, _):
        for copy in copies_out(slot):
            copy.wait()
        return 0

    lax.fori_loop(0, z.count, end, 0)


def far_shards(z, prompt_kv, resp_q, resp_kv, out_grad, rewards, resp_prompt, resp_len):
    assert z.slots == 1
    count, n_dp = z.count, z.n_dp
    one = (2, z.prefix_len, z.width)
    smem = pl.BlockSpec(memory_space=pltpu.SMEM)
    q_out, self_out, per_resp = pl.pallas_call(
        functools.partial(far_kernel, z),
        out_shape=[
            jax.ShapeDtypeStruct(resp_q.shape, BF16),
            jax.ShapeDtypeStruct(resp_kv.shape, BF16),
            jax.ShapeDtypeStruct((count,) + one, BF16),
        ],
        in_specs=[smem] * 3 + [ANYWHERE] * 4,
        out_specs=[ANYWHERE] * 3,
        scratch_shapes=[
            pltpu.SMEM((n_dp,), F32),
            pltpu.SMEM((count,), jnp.int32),
            pltpu.SMEM((count,), F32),
            pltpu.VMEM((count, z.tokens, z.lanes), BF16),
            pltpu.VMEM((count, z.tokens, z.lanes), BF16),
            pltpu.VMEM((count, 2, z.tokens, z.width), BF16),
            pltpu.VMEM((count,) + one, BF16),
            pltpu.VMEM((count, z.tokens, z.lanes), BF16),
            pltpu.VMEM((count, 2, z.tokens, z.width), BF16),
            pltpu.VMEM((count,) + one, BF16),
            pltpu.SemaphoreType.DMA((count, 4)),
            pltpu.SemaphoreType.DMA((count,)),
            pltpu.SemaphoreType.DMA((count, 4)),
        ],
        compiler_params=pltpu.CompilerParams(vmem_limit_bytes=VMEM_BYTES),
        name="far_grads",
    )(
        resp_prompt,
        resp_len,
        lax.all_gather(rewards, "dp", axis=0, tiled=True),
        resp_q,
        out_grad,
        resp_kv,
        lax.all_gather(prompt_kv, "dp", axis=0),
    )
    my_prompts = lax.dynamic_slice_in_dim(resp_prompt, lax.axis_index("dp") * count, count)
    route = (jnp.arange(n_dp, dtype=jnp.int32)[:, None] == my_prompts[None, :]).astype(BF16)
    outgoing = jnp.dot(route, per_resp.reshape(count, -1), preferred_element_type=F32).astype(BF16)
    outgoing = outgoing.reshape((n_dp,) + one)
    incoming = lax.all_to_all(outgoing, "dp", split_axis=0, concat_axis=0, tiled=True)
    prefix_out = jnp.sum(incoming, axis=0, dtype=F32).astype(BF16)
    return (q_out, self_out, prefix_out)


def shards(prompt_kv, resp_q, resp_kv, out_grad, rewards, resp_prompt, resp_len):
    n_dp = lax.axis_size("dp")
    count = rewards.shape[0]
    prefix_len, width = prompt_kv.shape[1:]
    slots = (count + n_dp - 1) // n_dp
    z = Sizes(
        n_dp, count, slots, width // HD, resp_q.shape[1] // width, resp_q.shape[0] // count, prefix_len
    )
    part = near_shards if count // slots == n_dp else far_shards
    return part(z, prompt_kv, resp_q, resp_kv, out_grad, rewards, resp_prompt, resp_len)


def solution(mesh):
    in_specs = (
        P(None, ("groups", "dp"), "tensor"),
        P(("groups", "dp"), "tensor"),
        P(None, ("groups", "dp"), "tensor"),
        P(("groups", "dp"), "tensor"),
        P(("groups", "dp")),
        P("groups"),
        P(("groups", "dp")),
    )
    out_specs = (
        P(("groups", "dp"), "tensor"),
        P(None, ("groups", "dp"), "tensor"),
        P(None, ("groups", "dp"), "tensor"),
    )
    return jax.shard_map(shards, mesh=mesh, in_specs=in_specs, out_specs=out_specs, check_vma=False)
```

```python
import functools
import math
from typing import NamedTuple

import jax
import jax.numpy as jnp
from jax import lax
from jax.experimental import pallas as pl
from jax.experimental.pallas import tpu as pltpu
from jax.sharding import PartitionSpec as P

HD = 128
NEG = -1e30
TAIL = 16
F32 = jnp.float32
BF16 = jnp.bfloat16
PAIR = 2
VMEM_BYTES = 63 * 1024 * 1024
ANYWHERE = pl.BlockSpec(memory_space=pl.ANY)
IN_SMEM = pl.BlockSpec(memory_space=pltpu.SMEM)


class Sizes(NamedTuple):
    n_dp: int
    count: int
    slots: int
    kv_heads: int
    group_size: int
    tokens: int
    prefix_len: int

    @property
    def width(self):
        return self.kv_heads * HD

    @property
    def lanes(self):
        return self.kv_heads * self.group_size * HD


def dot(a, b, dims):
    return lax.dot_general(a, b, (dims, ((), ())), preferred_element_type=F32)


NN = ((1,), (0,))
NT = ((1,), (1,))


class Bag:
    pass


def attend_pair(z, at, places, q, og, kv, prefix, lens, factors, out, own_out, sink, apart):
    tokens, prefix_len, group_size = z.tokens, z.prefix_len, z.group_size
    scale = 1.0 / math.sqrt(HD)
    log_scale = scale * math.log2(math.e)
    whole = group_size - group_size % 2
    single = len(at) == 1
    members = range(len(at))
    sides = (0, 0) if single else (0, 1)
    two = 2 * tokens
    assert tokens & (tokens - 1) == 0
    token = lax.broadcasted_iota(jnp.int32, (1, two), 1) & (tokens - 1)
    key = lax.broadcasted_iota(jnp.int32, (tokens, two), 0)
    causal = key <= (lax.broadcasted_iota(jnp.int32, (tokens, two), 1) & (tokens - 1))
    left = lax.broadcasted_iota(jnp.int32, (1, two), 1) < tokens

    def head(k, h):
        start = (k * group_size + h) * HD
        return slice(start, start + HD)

    def rows(ref, k, blocks):
        return jnp.concatenate([ref[at[n], head(k, h)] for n, h in blocks], axis=0)

    def halves(part):
        none = jnp.zeros_like(part)
        return [jnp.where(left, part, none), jnp.where(left, none, part)]

    chunks = []
    for k in range(z.kv_heads):
        t = Bag()
        t.cols = slice(k * HD, (k + 1) * HD)
        t.key_p, t.value_p = prefix[0, :, t.cols], prefix[1, :, t.cols]
        t.keys = [kv[0, at[n], t.cols] for n in sides]
        t.values = [kv[1, at[n], t.cols] for n in sides]
        t.key_pair = jnp.concatenate(t.keys, axis=0)
        t.value_pair = jnp.concatenate(t.values, axis=0)
        t.key_t = jnp.concatenate([t.key_p.T, t.key_pair.T], axis=1)
        t.prefix_sums = {n: [] for n in members}
        t.self_sums = {n: [] for n in members}
        mine = []
        for n in members:
            c = Bag()
            c.k, c.t, c.side, c.blocks = k, t, n, [(n, h) for h in range(whole)]
            mine.append(c)
        if group_size % 2:
            c = Bag()
            c.k, c.t, c.side, c.blocks = k, t, None, [(n, group_size - 1) for n in sides]
            mine.append(c)
        t.left_over = len(mine)
        chunks += mine

    def products(c):
        t = c.t
        c.q_rows, c.g_rows = rows(q, c.k, c.blocks), rows(og, c.k, c.blocks)
        if c.side is None:
            key_s, value_s = t.key_pair, t.value_pair
        else:
            key_s, value_s = t.keys[c.side], t.values[c.side]
        c.scores = dot(jnp.concatenate([t.key_p, key_s], axis=0), c.q_rows, NT)
        c.gw = dot(jnp.concatenate([t.value_p, value_s], axis=0), c.g_rows, NT)

    def weigh(c, scores, gw, keep):
        scores_p, scores_s = scores[:prefix_len], scores[prefix_len:]
        gw_p, gw_s = gw[:prefix_len], gw[prefix_len:]
        if c.side is None:
            scores_s = jnp.where(left, scores_s[:tokens], scores_s[tokens:])
            gw_s = jnp.where(left, gw_s[:tokens], gw_s[tokens:])
        scores_s = jnp.where(causal, scores_s, NEG)
        top = jnp.maximum(
            jnp.max(scores_p, axis=0, keepdims=True), jnp.max(scores_s, axis=0, keepdims=True)
        )
        e_p = jnp.exp2((scores_p - top) * log_scale)
        e_s = jnp.exp2((scores_s - top) * log_scale)
        total = jnp.sum(e_p, axis=0, keepdims=True) + jnp.sum(e_s, axis=0, keepdims=True)
        weighted = jnp.sum(e_p * gw_p, axis=0, keepdims=True) + jnp.sum(
            e_s * gw_s, axis=0, keepdims=True
        )
        inverse = 1.0 / total
        delta = weighted * inverse
        gain = inverse * keep
        w_p, w_s = e_p * gain, e_s * gain
        d_p = (w_p * (gw_p - delta)).astype(BF16)
        d_s = (w_s * (gw_s - delta)).astype(BF16)
        return w_p.astype(BF16), w_s.astype(BF16), d_p, d_s

    def gradients(c):
        if c.side is None:
            length = jnp.where(left, lens[0], 0 if single else lens[1])
            gain = jnp.where(left, factors[0], factors[-1])
        else:
            length, gain = lens[c.side], factors[c.side]
        keep = jnp.where(token < length, gain, 0.0)
        parts = []
        for n in range(0, len(c.blocks), 2):
            at_lanes = slice(n * tokens, (n + 2) * tokens)
            parts.append(weigh(c, c.scores[:, at_lanes], c.gw[:, at_lanes], keep))
        w_p, w_s, d_p, d_s = (jnp.concatenate(part, axis=1) for part in zip(*parts))
        if c.side is None:
            d_s, w_s = halves(d_s), halves(w_s)
            c.d_wide = jnp.concatenate([d_p, *d_s], axis=0)
            c.d_all = jnp.concatenate([*halves(d_p), *d_s], axis=0) if apart else c.d_wide
            c.w_all = jnp.concatenate([*(halves(w_p) if apart else [w_p]), *w_s], axis=0)
        else:
            empty = jnp.zeros_like(d_s)
            c.d_wide = jnp.concatenate([d_p, empty, d_s] if c.side else [d_p, d_s, empty], axis=0)
            c.d_all = jnp.concatenate([d_p, d_s], axis=0)
            c.w_all = jnp.concatenate([w_p, w_s], axis=0)

    def outgoing(c):
        t = c.t
        q_grad = (dot(t.key_t, c.d_wide, NN) * scale).astype(BF16).T
        kg = dot(c.d_all, c.q_rows, NN)
        vg = dot(c.w_all, c.g_rows, NN)
        targets = members if c.side is None else [c.side]
        for place, (n, h) in enumerate(c.blocks):
            if c.side is not None or place < len(targets):
                out[places[n], :, head(c.k, h)] = q_grad[place * tokens : (place + 1) * tokens]
        many = 2 if c.side is None and apart else 1
        for place, n in enumerate(targets):
            if place < many:
                rows_p = slice(place * prefix_len, (place + 1) * prefix_len)
                t.prefix_sums[n if apart else 0].append((kg[rows_p], vg[rows_p]))
            start = many * prefix_len + place * tokens
            rows_s = slice(start, start + tokens)
            t.self_sums[n].append((kg[rows_s], vg[rows_s]))
        t.left_over -= 1
        if t.left_over == 0:
            for n in members:
                keys, values = zip(*t.self_sums[n])
                own_out[places[n], 0, :, t.cols] = (sum(keys) * scale).astype(BF16)
                own_out[places[n], 1, :, t.cols] = sum(values).astype(BF16)
                if apart or n == 0:
                    keys, values = zip(*t.prefix_sums[n])
                    sink(n, t.cols, sum(keys) * scale, sum(values))

    stages = (products, gradients, outgoing)
    for step in range(len(chunks) + len(stages) - 1):
        for late, stage in enumerate(stages):
            if 0 <= step - late < len(chunks):
                stage(chunks[step - late])


def token_rows(z, i):
    return pl.ds(pl.multiple_of(i * z.tokens, z.tokens), z.tokens)


def make_plan(z, me, resp_prompt, resp_len, rewards, places, order, lens, gains):
    for t in range(z.n_dp):
        places[t] = t * z.slots
    for i in range(z.count):
        turn = lax.rem(resp_prompt[me * z.count + i] - me + z.n_dp, z.n_dp)
        slot = places[turn]
        places[turn] = slot + 1
        order[slot] = i
        lens[slot] = resp_len[i]
        gains[slot] = rewards[i]


def prompt_total(z, prompt, tails):
    sums = jnp.zeros((1, tails.shape[2]), F32)
    for s in range(z.n_dp):
        tail = tails[s].astype(F32)
        sums += tail[0:1] + tail[1:2] + tail[2:3]
    lane = lax.broadcasted_iota(jnp.int32, sums.shape, 1)
    return jnp.sum(jnp.where(lane == prompt, sums, 0.0))


def reward_factor(z, reward, total, length):
    return (reward - total / z.count) * (z.tokens / length.astype(F32))


def pack_kernel(z, prompt_hbm, rewards_hbm, resp_prompt_hbm, payload, rewards, resp_prompt, staged, sems):
    me = lax.axis_index("dp")
    small = [
        pltpu.make_async_copy(rewards_hbm, rewards, sems.at[0]),
        pltpu.make_async_copy(resp_prompt_hbm, resp_prompt, sems.at[1]),
    ]
    large = [
        pltpu.make_async_copy(
            prompt_hbm.at[n], staged.at[pl.ds(n * z.prefix_len, z.prefix_len)], sems.at[2 + n]
        )
        for n in range(2)
    ]
    for copy in small + large:
        copy.start()
    for copy in small:
        copy.wait()
    lane = lax.broadcasted_iota(jnp.int32, (1, z.width), 1)
    sums = jnp.zeros((1, z.width), F32)
    for i in range(z.count):
        sums += jnp.where(lane == resp_prompt[me * z.count + i], rewards[i], 0.0)
    high = sums.astype(BF16).astype(F32)
    middle = (sums - high).astype(BF16).astype(F32)
    low = sums - high - middle
    row = lax.broadcasted_iota(jnp.int32, (TAIL, z.width), 0)
    pieces = jnp.where(row == 0, high, jnp.where(row == 1, middle, jnp.where(row == 2, low, 0.0)))
    staged[2 * z.prefix_len :, :] = pieces.astype(BF16)
    for copy in large:
        copy.wait()
    last = pltpu.make_async_copy(staged, payload, sems.at[0])
    last.start()
    last.wait()


def tail_copies(z, payloads, tails, sems):
    return [
        pltpu.make_async_copy(payloads[s].at[pl.ds(2 * z.prefix_len, TAIL)], tails.at[s], sems.at[s])
        for s in range(z.n_dp)
    ]


def row_copies(z, here, there, at_here, at_there, sems):
    (q0, og0, kv0), (q1, og1, kv1) = here, there
    return (
        pltpu.make_async_copy(q0.at[at_here], q1.at[at_there], sems.at[0]),
        pltpu.make_async_copy(og0.at[at_here], og1.at[at_there], sems.at[1]),
        pltpu.make_async_copy(kv0.at[0, at_here], kv1.at[0, at_there], sems.at[2]),
        pltpu.make_async_copy(kv0.at[1, at_here], kv1.at[1, at_there], sems.at[3]),
    )


def result_copies(z, out, own, q_out, self_out, place, at, sems):
    return (
        pltpu.make_async_copy(out.at[place], q_out.at[at], sems.at[place, 0]),
        pltpu.make_async_copy(own.at[place, 0], self_out.at[0, at], sems.at[place, 1]),
        pltpu.make_async_copy(own.at[place, 1], self_out.at[1, at], sems.at[place, 2]),
    )


def raw_kernel(z, *refs):
    small_hbm, given, payload = refs[:3], refs[3:6], refs[6]
    plan, sorted_out, (q_out, self_out, grads_out) = refs[7:10], refs[10:13], refs[13:16]
    (resp_prompt, resp_len, rewards, places, q, og, kv, prefix, out, own, grads,
     sem_small, sem_in, sem_sorted, sem_out) = refs[16:]
    order, lens, gains = plan
    held = (q, og, kv)
    me = lax.axis_index("dp")
    small = [
        pltpu.make_async_copy(src, dst, sem_small.at[n])
        for n, (src, dst) in enumerate(zip(small_hbm, (resp_prompt, resp_len, rewards)))
    ]
    small += [
        pltpu.make_async_copy(payload.at[pl.ds(n * z.prefix_len, z.prefix_len)], prefix.at[n], sem_small.at[3 + n])
        for n in range(2)
    ]
    for copy in small:
        copy.start()
    for copy in small[:3]:
        copy.wait()
    make_plan(z, me, resp_prompt, resp_len, rewards, places, order, lens, gains)

    def copies_in(slot):
        return row_copies(
            z, given, held, token_rows(z, order[slot]), token_rows(z, slot), sem_in.at[slot]
        )

    def copies_sorted(slot):
        return row_copies(
            z, held, sorted_out, token_rows(z, slot), token_rows(z, slot - z.slots), sem_sorted.at[slot - z.slots]
        )

    def start_in(slot, _):
        for copy in copies_in(slot):
            copy.start()
        return 0

    lax.fori_loop(0, z.count, start_in, 0)
    for copy in small[3:]:
        copy.wait()

    def unit(u, _):
        at = [u * PAIR + n for n in range(PAIR)]
        for slot in at:
            for copy in copies_in(slot):
                copy.wait()

        def sink(n, cols, key_grad, value_grad):
            grads[at[n], 0, :, cols] = key_grad.astype(BF16)
            grads[at[n], 1, :, cols] = value_grad.astype(BF16)

        attend_pair(
            z, [token_rows(z, n) for n in at], at, q, og, kv, prefix, [lens[n] for n in at], [1.0] * PAIR, out, own,
            sink, True,
        )
        return 0

    lax.fori_loop(0, z.slots // PAIR, unit, 0)
    last = [
        pltpu.make_async_copy(src, dst, sem_out.at[n])
        for n, (src, dst) in enumerate([(out, q_out), (own, self_out), (grads, grads_out)])
    ]
    for copy in last:
        copy.start()

    def start_sorted(slot, _):
        for copy in copies_in(slot):
            copy.wait()
        for copy in copies_sorted(slot):
            copy.start()
        return 0

    def end_sorted(slot, _):
        for copy in copies_sorted(slot):
            copy.wait()
        return 0

    lax.fori_loop(z.slots, z.count, start_sorted, 0)
    lax.fori_loop(z.slots, z.count, end_sorted, 0)
    for copy in last:
        copy.wait()


def group_kernel(z, turns, aliased, *refs):
    plan_hbm, given, payloads = refs[:3], refs[3:6], refs[6 : 6 + z.n_dp]
    refs = refs[6 + z.n_dp + aliased :]
    (q_out, self_out), grads_out = refs[:2], refs[2 : 2 + len(turns)]
    (order, lens, gains, factors, q, og, kv, prefix, tails, acc, out, own, grads,
     sem_plan, sem_prefix, sem_in, sem_out, sem_grads) = refs[2 + len(turns) :]
    me = lax.axis_index("dp")
    n_slots = len(turns) * z.slots
    starts = [(turn - 1) * z.slots * z.tokens for turn in turns]
    span = z.slots * z.tokens

    first = [pltpu.make_async_copy(src, dst, sem_plan.at[n]) for n, (src, dst) in enumerate(zip(plan_hbm, (order, lens, gains)))]
    first += tail_copies(z, payloads, tails, sem_grads)
    second = [
        [
            pltpu.make_async_copy(
                payloads[turn].at[pl.ds(n * z.prefix_len, z.prefix_len)], prefix.at[t, n], sem_prefix.at[t, n]
            )
            for n in range(2)
        ]
        + list(
            row_copies(z, given, (q, og, kv), pl.ds(starts[t], span), pl.ds(t * span, span), sem_in.at[t])
        )
        for t, turn in enumerate(turns)
    ]
    for copy in [*first, *sum(second, [])]:
        copy.start()
    for copy in first:
        copy.wait()
    slots = [turn * z.slots + n for turn in turns for n in range(z.slots)]
    for t, turn in enumerate(turns):
        total = prompt_total(z, lax.rem(me + turn, z.n_dp), tails)
        for place in range(t * z.slots, (t + 1) * z.slots):
            slot = slots[place]
            factors[place] = reward_factor(z, gains[slot], total, lens[slot])
    order_of, lens_of = [order[slot] for slot in slots], [lens[slot] for slot in slots]
    for place in range(n_slots):
        order[place] = order_of[place]
        lens[place] = lens_of[place]
    acc[...] = jnp.zeros(acc.shape, F32)
    for copy in sum(second, []):
        copy.wait()

    def copies_out(place):
        return result_copies(z, out, own, q_out, self_out, place, token_rows(z, order[place]), sem_out)

    def unit(u, _):
        at = [u * PAIR + n for n in range(PAIR)]
        t = u // (z.slots // PAIR)

        def sink(_, cols, key_grad, value_grad):
            acc[t, 0, :, cols] += key_grad
            acc[t, 1, :, cols] += value_grad

        attend_pair(
            z, [token_rows(z, n) for n in at], at, q, og, kv, prefix.at[t], [lens[n] for n in at],
            [factors[n] for n in at], out, own, sink, False,
        )
        for place in at:
            for copy in copies_out(place):
                copy.start()
        return 0

    lax.fori_loop(0, n_slots // PAIR, unit, 0)
    grads[...] = acc[...].astype(BF16)
    last = [pltpu.make_async_copy(grads.at[t], grads_out[t], sem_grads.at[t]) for t in range(len(turns))]
    for copy in last:
        copy.start()
    for place in range(n_slots):
        for copy in copies_out(place):
            copy.wait()
    for copy in last:
        copy.wait()


def finish_kernel(z, *refs):
    plan_hbm, payloads, raw_hbm = refs[:3], refs[3 : 3 + z.n_dp], refs[3 + z.n_dp : 7 + z.n_dp]
    q_out, self_out, grads_out = refs[9 + z.n_dp : 12 + z.n_dp]
    order, lens, gains, tails, out, own, per_resp, come, grads, sem_small, sem_tails, sem_out = refs[12 + z.n_dp :]
    copies = [
        pltpu.make_async_copy(src, dst, sem_small.at[n])
        for n, (src, dst) in enumerate(zip([*plan_hbm, *raw_hbm], (order, lens, gains, out, own, per_resp, come)))
    ]
    copies += tail_copies(z, payloads, tails, sem_tails)
    for copy in copies:
        copy.start()
    for copy in copies:
        copy.wait()
    total = prompt_total(z, lax.axis_index("dp"), tails)
    results = []
    summed = come[...].astype(F32)
    for slot in range(z.slots):
        factor = reward_factor(z, gains[slot], total, lens[slot])
        out[slot] = (out[slot].astype(F32) * factor).astype(BF16)
        own[slot] = (own[slot].astype(F32) * factor).astype(BF16)
        results.append(result_copies(z, out, own, q_out, self_out, slot, token_rows(z, order[slot]), sem_out))
        for copy in results[-1]:
            copy.start()
        summed += per_resp[slot].astype(F32) * factor
    grads[...] = summed
    last = pltpu.make_async_copy(grads, grads_out, sem_small.at[0])
    last.start()
    for copy in sum(results, ()):
        copy.wait()
    last.wait()


def near_shards(z, prompt_kv, resp_q, resp_kv, out_grad, rewards, resp_prompt, resp_len):
    n_dp = z.n_dp
    assert z.slots % PAIR == 0
    shape = jax.ShapeDtypeStruct
    one = (2, z.prefix_len, z.width)
    params = pltpu.CompilerParams(vmem_limit_bytes=VMEM_BYTES)
    cost = pl.CostEstimate(flops=0, bytes_accessed=0, transcendentals=0)
    small = (resp_prompt, resp_len, rewards)
    payload = pl.pallas_call(
        functools.partial(pack_kernel, z),
        out_shape=jax.ShapeDtypeStruct((2 * z.prefix_len + TAIL, z.width), BF16),
        in_specs=[ANYWHERE] * 3,
        out_specs=ANYWHERE,
        scratch_shapes=[
            pltpu.SMEM(rewards.shape, F32),
            pltpu.SMEM(resp_prompt.shape, jnp.int32),
            pltpu.VMEM((2 * z.prefix_len + TAIL, z.width), BF16),
            pltpu.SemaphoreType.DMA((4,)),
        ],
        compiler_params=pltpu.CompilerParams(vmem_limit_bytes=VMEM_BYTES),
        name="pack",
    )(prompt_kv, rewards, resp_prompt)

    away = sorted(range(1, n_dp), key=lambda s: -min(s, n_dp - s))
    payloads = {0: payload}
    for s in away:
        payloads[s] = lax.ppermute(payload, "dp", [((i + s) % n_dp, i) for i in range(n_dp)])
    everyone = [payloads[s] for s in range(n_dp)]

    given = (resp_q, out_grad, resp_kv)
    slots, count, rest = z.slots, z.count, (z.count - z.slots) * z.tokens
    plan_smem = [pltpu.SMEM((count,), kind) for kind in (jnp.int32, jnp.int32, F32)]
    results = pl.pallas_call(
        functools.partial(raw_kernel, z),
        out_shape=[
            shape((count,), jnp.int32),
            shape((count,), jnp.int32),
            shape((count,), F32),
            shape((rest, z.lanes), BF16),
            shape((rest, z.lanes), BF16),
            shape((2, rest, z.width), BF16),
            shape((slots, z.tokens, z.lanes), BF16),
            shape((slots, 2, z.tokens, z.width), BF16),
            shape((slots,) + one, BF16),
        ],
        in_specs=[ANYWHERE] * 7,
        out_specs=[IN_SMEM] * 3 + [ANYWHERE] * 6,
        scratch_shapes=[
            *[pltpu.SMEM(x.shape, x.dtype) for x in small],
            pltpu.SMEM((n_dp,), jnp.int32),
            pltpu.VMEM(resp_q.shape, BF16),
            pltpu.VMEM(resp_q.shape, BF16),
            pltpu.VMEM(resp_kv.shape, BF16),
            pltpu.VMEM(one, BF16),
            pltpu.VMEM((slots, z.tokens, z.lanes), BF16),
            pltpu.VMEM((slots, 2, z.tokens, z.width), BF16),
            pltpu.VMEM((slots,) + one, BF16),
            pltpu.SemaphoreType.DMA((5,)),
            pltpu.SemaphoreType.DMA((count, 4)),
            pltpu.SemaphoreType.DMA((count - slots, 4)),
            pltpu.SemaphoreType.DMA((3,)),
        ],
        compiler_params=params,
        cost_estimate=cost,
        name="raw_grads",
    )(*small, *given, payload)
    plan, in_order, raw = results[:3], results[3:6], results[6:]

    first = len(away) // 2
    written = ()
    arrived = []
    for turns in (tuple(away[:first]), tuple(away[first:])):
        if not turns:
            continue
        n_slots = len(turns) * slots
        operands = [*plan, *in_order, *everyone, *written]
        results = pl.pallas_call(
            functools.partial(group_kernel, z, turns, len(written)),
            out_shape=[shape(resp_q.shape, BF16), shape(resp_kv.shape, BF16)] + [shape(one, BF16)] * len(turns),
            in_specs=[ANYWHERE] * len(operands),
            out_specs=[ANYWHERE] * (2 + len(turns)),
            input_output_aliases={len(operands) - 2: 0, len(operands) - 1: 1} if written else {},
            scratch_shapes=[
                *plan_smem,
                pltpu.SMEM((n_slots,), F32),
                pltpu.VMEM((n_slots * z.tokens, z.lanes), BF16),
                pltpu.VMEM((n_slots * z.tokens, z.lanes), BF16),
                pltpu.VMEM((2, n_slots * z.tokens, z.width), BF16),
                pltpu.VMEM((len(turns),) + one, BF16),
                pltpu.VMEM((n_dp, TAIL, z.width), BF16),
                pltpu.VMEM((len(turns),) + one, F32),
                pltpu.VMEM((n_slots, z.tokens, z.lanes), BF16),
                pltpu.VMEM((n_slots, 2, z.tokens, z.width), BF16),
                pltpu.VMEM((len(turns),) + one, BF16),
                pltpu.SemaphoreType.DMA((3,)),
                pltpu.SemaphoreType.DMA((len(turns), 2)),
                pltpu.SemaphoreType.DMA((len(turns), 4)),
                pltpu.SemaphoreType.DMA((n_slots, 3)),
                pltpu.SemaphoreType.DMA((n_dp,)),
            ],
            compiler_params=params,
            cost_estimate=cost,
            name="group_grads",
        )(*operands)
        written = results[:2]
        for turn, grads in zip(turns, results[2:]):
            arrived.append(lax.ppermute(grads, "dp", [(i, (i + turn) % n_dp) for i in range(n_dp)]))
    operands = [*plan, *everyone, *raw, arrived[0], *written]
    q_out, self_out, own_grads = pl.pallas_call(
        functools.partial(finish_kernel, z),
        out_shape=[shape(resp_q.shape, BF16), shape(resp_kv.shape, BF16), shape(one, F32)],
        in_specs=[ANYWHERE] * len(operands),
        out_specs=[ANYWHERE] * 3,
        input_output_aliases={len(operands) - 2: 0, len(operands) - 1: 1},
        scratch_shapes=[
            *plan_smem,
            pltpu.VMEM((n_dp, TAIL, z.width), BF16),
            pltpu.VMEM((slots, z.tokens, z.lanes), BF16),
            pltpu.VMEM((slots, 2, z.tokens, z.width), BF16),
            pltpu.VMEM((slots,) + one, BF16),
            pltpu.VMEM(one, BF16),
            pltpu.VMEM(one, F32),
            pltpu.SemaphoreType.DMA((7,)),
            pltpu.SemaphoreType.DMA((n_dp,)),
            pltpu.SemaphoreType.DMA((slots, 3)),
        ],
        compiler_params=params,
        cost_estimate=cost,
        name="finish_own",
    )(*operands)
    prefix_out = sum(part.astype(F32) for part in [own_grads, *arrived[1:]]).astype(BF16)
    return (q_out, self_out, prefix_out)


def far_kernel(z, *refs):
    (resp_prompt, resp_len, rewards, q_hbm, og_hbm, kv_hbm, prompts, q_out, self_out, prefix_outs,
     totals, lens, factors, q, og, kv, prefix, out, own, grads, sem_in, sem_prefix, sem_out) = refs
    me = lax.axis_index("dp")

    for p in range(z.n_dp):
        totals[p] = 0.0

    def copies_in(slot):
        rows = token_rows(z, slot)
        prompt = resp_prompt[me * z.count + slot]
        return (
            *row_copies(z, (q_hbm, og_hbm, kv_hbm), (q, og, kv), rows, rows, sem_in.at[slot]),
            pltpu.make_async_copy(prompts.at[prompt], prefix.at[slot], sem_prefix.at[slot]),
        )

    def copies_out(slot):
        rows = token_rows(z, slot)
        return (
            *result_copies(z, out, own, q_out, self_out, slot, rows, sem_out),
            pltpu.make_async_copy(grads.at[slot], prefix_outs.at[slot], sem_out.at[slot, 3]),
        )

    def start(slot, _):
        for copy in copies_in(slot):
            copy.start()
        return 0

    lax.fori_loop(0, z.count, start, 0)

    def add(i, _):
        prompt = resp_prompt[i]
        totals[prompt] = totals[prompt] + rewards[i]
        return 0

    lax.fori_loop(0, z.n_dp * z.count, add, 0)

    def find_factor(slot, _):
        place = me * z.count + slot
        lens[slot] = resp_len[slot]
        factors[slot] = reward_factor(z, rewards[place], totals[resp_prompt[place]], resp_len[slot])
        return 0

    lax.fori_loop(0, z.count, find_factor, 0)

    def unit(slot, _):
        for copy in copies_in(slot):
            copy.wait()

        def sink(_, cols, key_grad, value_grad):
            grads[slot, 0, :, cols] = key_grad.astype(BF16)
            grads[slot, 1, :, cols] = value_grad.astype(BF16)

        attend_pair(
            z, [token_rows(z, slot)], [slot], q, og, kv, prefix.at[slot], [lens[slot]], [factors[slot]], out, own, sink, True
        )
        for copy in copies_out(slot):
            copy.start()
        return 0

    lax.fori_loop(0, z.count, unit, 0)

    def end(slot, _):
        for copy in copies_out(slot):
            copy.wait()
        return 0

    lax.fori_loop(0, z.count, end, 0)


def far_shards(z, prompt_kv, resp_q, resp_kv, out_grad, rewards, resp_prompt, resp_len):
    assert z.slots == 1
    count, n_dp = z.count, z.n_dp
    one = (2, z.prefix_len, z.width)
    smem = pl.BlockSpec(memory_space=pltpu.SMEM)
    q_out, self_out, per_resp = pl.pallas_call(
        functools.partial(far_kernel, z),
        out_shape=[
            jax.ShapeDtypeStruct(resp_q.shape, BF16),
            jax.ShapeDtypeStruct(resp_kv.shape, BF16),
            jax.ShapeDtypeStruct((count,) + one, BF16),
        ],
        in_specs=[smem] * 3 + [ANYWHERE] * 4,
        out_specs=[ANYWHERE] * 3,
        scratch_shapes=[
            pltpu.SMEM((n_dp,), F32),
            pltpu.SMEM((count,), jnp.int32),
            pltpu.SMEM((count,), F32),
            pltpu.VMEM(resp_q.shape, BF16),
            pltpu.VMEM(resp_q.shape, BF16),
            pltpu.VMEM(resp_kv.shape, BF16),
            pltpu.VMEM((count,) + one, BF16),
            pltpu.VMEM((count, z.tokens, z.lanes), BF16),
            pltpu.VMEM((count, 2, z.tokens, z.width), BF16),
            pltpu.VMEM((count,) + one, BF16),
            pltpu.SemaphoreType.DMA((count, 4)),
            pltpu.SemaphoreType.DMA((count,)),
            pltpu.SemaphoreType.DMA((count, 4)),
        ],
        compiler_params=pltpu.CompilerParams(vmem_limit_bytes=VMEM_BYTES),
        name="far_grads",
    )(
        resp_prompt,
        resp_len,
        lax.all_gather(rewards, "dp", axis=0, tiled=True),
        resp_q,
        out_grad,
        resp_kv,
        lax.all_gather(prompt_kv, "dp", axis=0),
    )
    my_prompts = lax.dynamic_slice_in_dim(resp_prompt, lax.axis_index("dp") * count, count)
    route = (jnp.arange(n_dp, dtype=jnp.int32)[:, None] == my_prompts[None, :]).astype(BF16)
    outgoing = jnp.dot(route, per_resp.reshape(count, -1), preferred_element_type=F32).astype(BF16)
    outgoing = outgoing.reshape((n_dp,) + one)
    incoming = lax.all_to_all(outgoing, "dp", split_axis=0, concat_axis=0, tiled=True)
    prefix_out = jnp.sum(incoming, axis=0, dtype=F32).astype(BF16)
    return (q_out, self_out, prefix_out)


def shards(prompt_kv, resp_q, resp_kv, out_grad, rewards, resp_prompt, resp_len):
    n_dp = lax.axis_size("dp")
    count = rewards.shape[0]
    prefix_len, width = prompt_kv.shape[1:]
    slots = (count + n_dp - 1) // n_dp
    z = Sizes(
        n_dp, count, slots, width // HD, resp_q.shape[1] // width, resp_q.shape[0] // count, prefix_len
    )
    part = near_shards if count // slots == n_dp else far_shards
    return part(z, prompt_kv, resp_q, resp_kv, out_grad, rewards, resp_prompt, resp_len)


def solution(mesh):
    in_specs = (
        P(None, ("groups", "dp"), "tensor"),
        P(("groups", "dp"), "tensor"),
        P(None, ("groups", "dp"), "tensor"),
        P(("groups", "dp"), "tensor"),
        P(("groups", "dp")),
        P("groups"),
        P(("groups", "dp")),
    )
    out_specs = (
        P(("groups", "dp"), "tensor"),
        P(None, ("groups", "dp"), "tensor"),
        P(None, ("groups", "dp"), "tensor"),
    )
    return jax.shard_map(shards, mesh=mesh, in_specs=in_specs, out_specs=out_specs, check_vma=False)
```

```python
import functools
import math
from typing import NamedTuple

import jax
import jax.numpy as jnp
from jax import lax
from jax.experimental import pallas as pl
from jax.experimental.pallas import tpu as pltpu
from jax.sharding import PartitionSpec as P

HD = 128
NEG = -1e30
TAIL = 16
F32 = jnp.float32
BF16 = jnp.bfloat16
PAIR = 2
FAR = 3
VMEM_BYTES = 63 * 1024 * 1024
ANYWHERE = pl.BlockSpec(memory_space=pl.ANY)


class Sizes(NamedTuple):
    n_dp: int
    count: int
    slots: int
    kv_heads: int
    group_size: int
    tokens: int
    prefix_len: int

    @property
    def width(self):
        return self.kv_heads * HD

    @property
    def lanes(self):
        return self.kv_heads * self.group_size * HD


def dot(a, b, dims):
    return lax.dot_general(a, b, (dims, ((), ())), preferred_element_type=F32)


NN = ((1,), (0,))
NT = ((1,), (1,))


class Bag:
    pass


def attend_pair(z, at, places, q, og, kv, prefix, lens, factors, out, own_out, sink, apart):
    tokens, prefix_len, group_size = z.tokens, z.prefix_len, z.group_size
    scale = 1.0 / math.sqrt(HD)
    log_scale = scale * math.log2(math.e)
    whole = group_size - group_size % 2
    single = len(at) == 1
    members = range(len(at))
    sides = (0, 0) if single else (0, 1)
    most = max(whole, 2) * tokens
    assert tokens & (tokens - 1) == 0
    token = lax.broadcasted_iota(jnp.int32, (1, most), 1) & (tokens - 1)
    key = lax.broadcasted_iota(jnp.int32, (tokens, most), 0)
    causal = key <= (lax.broadcasted_iota(jnp.int32, (tokens, most), 1) & (tokens - 1))
    left = lax.broadcasted_iota(jnp.int32, (1, 2 * tokens), 1) < tokens

    def head(k, h):
        start = (k * group_size + h) * HD
        return slice(start, start + HD)

    def rows(ref, k, blocks):
        return jnp.concatenate([ref[at[n], head(k, h)] for n, h in blocks], axis=0)

    def halves(part):
        none = jnp.zeros_like(part)
        return [jnp.where(left, part, none), jnp.where(left, none, part)]

    def own_half(both):
        return jnp.where(left, both[:tokens], both[tokens:])

    def rounded(*parts):
        return jnp.concatenate([part.astype(BF16) for part in parts], axis=0)

    chunks = []
    for k in range(z.kv_heads):
        t = Bag()
        t.cols = slice(k * HD, (k + 1) * HD)
        t.key_p, t.value_p = prefix[0, :, t.cols], prefix[1, :, t.cols]
        t.keys = [kv[0, at[n], t.cols] for n in sides]
        t.values = [kv[1, at[n], t.cols] for n in sides]
        t.key_pair = jnp.concatenate(t.keys, axis=0)
        t.value_pair = jnp.concatenate(t.values, axis=0)
        t.key_t = jnp.concatenate([t.key_p.T, t.key_pair.T], axis=1)
        t.prefix_sums = {n: [] for n in members}
        t.self_sums = {n: [] for n in members}
        mine = []
        for n in members:
            c = Bag()
            c.k, c.t, c.side, c.blocks = k, t, n, [(n, h) for h in range(whole)]
            mine.append(c)
        if group_size % 2:
            c = Bag()
            c.k, c.t, c.side, c.blocks = k, t, None, [(n, group_size - 1) for n in sides]
            mine.append(c)
        t.left_over = len(mine)
        chunks += mine

    def products(c):
        t = c.t
        c.q_rows, c.g_rows = rows(q, c.k, c.blocks), rows(og, c.k, c.blocks)
        if c.side is None:
            key_s, value_s = t.key_pair, t.value_pair
        else:
            key_s, value_s = t.keys[c.side], t.values[c.side]
        c.scores = dot(jnp.concatenate([t.key_p, key_s], axis=0), c.q_rows, NT)
        c.gw = dot(jnp.concatenate([t.value_p, value_s], axis=0), c.g_rows, NT)

    def weigh(c):
        scores_p, scores_s = c.scores[:prefix_len], c.scores[prefix_len:]
        c.gw_p, c.gw_s = c.gw[:prefix_len], c.gw[prefix_len:]
        if c.side is None:
            scores_s, c.gw_s = own_half(scores_s), own_half(c.gw_s)
        scores_s = jnp.where(causal[:, : scores_s.shape[1]], scores_s, NEG)
        top = jnp.maximum(
            jnp.max(scores_p, axis=0, keepdims=True), jnp.max(scores_s, axis=0, keepdims=True)
        )
        c.e_p = jnp.exp2((scores_p - top) * log_scale)
        c.e_s = jnp.exp2((scores_s - top) * log_scale)
        total = jnp.sum(c.e_p, axis=0, keepdims=True) + jnp.sum(c.e_s, axis=0, keepdims=True)
        weighted = jnp.sum(c.e_p * c.gw_p, axis=0, keepdims=True) + jnp.sum(
            c.e_s * c.gw_s, axis=0, keepdims=True
        )
        if c.side is None:
            length = jnp.where(left, lens[0], 0 if single else lens[1])
            gain = jnp.where(left, factors[0], factors[-1])
        else:
            length, gain = lens[c.side], factors[c.side]
        inverse = 1.0 / total
        c.delta = weighted * inverse
        c.gain = inverse * jnp.where(token[:, : total.shape[1]] < length, gain, 0.0)

    def gradients(c):
        w_p, w_s = c.e_p * c.gain, c.e_s * c.gain
        d_p, d_s = w_p * (c.gw_p - c.delta), w_s * (c.gw_s - c.delta)
        if c.side is None:
            d_s, w_s = halves(d_s), halves(w_s)
            c.d_wide = rounded(d_p, *d_s)
            c.d_all = rounded(*halves(d_p), *d_s) if apart else c.d_wide
            c.w_all = rounded(*(halves(w_p) if apart else [w_p]), *w_s)
        else:
            empty = jnp.zeros_like(d_s)
            c.d_wide = rounded(*([d_p, empty, d_s] if c.side else [d_p, d_s, empty]))
            c.d_all = rounded(d_p, d_s)
            c.w_all = rounded(w_p, w_s)

    def outgoing(c):
        t = c.t
        q_grad = (dot(t.key_t, c.d_wide, NN) * scale).astype(BF16).T
        kg = dot(c.d_all, c.q_rows, NN)
        vg = dot(c.w_all, c.g_rows, NN)
        targets = members if c.side is None else [c.side]
        for place, (n, h) in enumerate(c.blocks):
            if c.side is not None or place < len(targets):
                out[places[n], :, head(c.k, h)] = q_grad[place * tokens : (place + 1) * tokens]
        many = 2 if c.side is None and apart else 1
        for place, n in enumerate(targets):
            if place < many:
                rows_p = slice(place * prefix_len, (place + 1) * prefix_len)
                t.prefix_sums[n if apart else 0].append((kg[rows_p], vg[rows_p]))
            start = many * prefix_len + place * tokens
            rows_s = slice(start, start + tokens)
            t.self_sums[n].append((kg[rows_s], vg[rows_s]))
        t.left_over -= 1
        if t.left_over == 0:
            for n in members:
                keys, values = zip(*t.self_sums[n])
                own_out[places[n], 0, :, t.cols] = (sum(keys) * scale).astype(BF16)
                own_out[places[n], 1, :, t.cols] = sum(values).astype(BF16)
                if apart or n == 0:
                    keys, values = zip(*t.prefix_sums[n])
                    sink(n, t.cols, sum(keys) * scale, sum(values))

    stages = (products, weigh, gradients, outgoing)
    for step in range(len(chunks) + len(stages) - 1):
        for late, stage in enumerate(stages):
            if 0 <= step - late < len(chunks):
                stage(chunks[step - late])


def token_rows(z, i):
    return pl.ds(pl.multiple_of(i * z.tokens, z.tokens), z.tokens)


def find_responses(z, me, turns, resp_prompt, order):
    for t, turn in enumerate(turns):
        prompt = me ^ turn
        found = t * z.slots
        for i in range(z.count):
            order[found] = i
            found = found + (resp_prompt[me * z.count + i] == prompt).astype(jnp.int32)


def prompt_total(z, me, prompt, resp_prompt, tails, far_rewards):
    sums = jnp.zeros((1, z.width), F32)
    for s in range(tails.shape[0]):
        tail = tails[s].astype(F32)
        sums += tail[0:1] + tail[1:2] + tail[2:3]
    lane = lax.broadcasted_iota(jnp.int32, sums.shape, 1)
    total = jnp.sum(jnp.where(lane == prompt, sums, 0.0))
    for i in range(z.count):
        total += jnp.where(resp_prompt[(me ^ FAR) * z.count + i] == prompt, far_rewards[i], 0.0)
    return total


def reward_factor(z, reward, total, length):
    return (reward - total / z.count) * (z.tokens / length.astype(F32))


def pack_kernel(z, prompt_hbm, rewards_hbm, resp_prompt_hbm, payload, rewards, resp_prompt, staged, sems):
    me = lax.axis_index("dp")
    small = [
        pltpu.make_async_copy(rewards_hbm, rewards, sems.at[0]),
        pltpu.make_async_copy(resp_prompt_hbm, resp_prompt, sems.at[1]),
    ]
    large = [
        pltpu.make_async_copy(
            prompt_hbm.at[n], staged.at[pl.ds(n * z.prefix_len, z.prefix_len)], sems.at[2 + n]
        )
        for n in range(2)
    ]
    for copy in small + large:
        copy.start()
    for copy in small:
        copy.wait()
    lane = lax.broadcasted_iota(jnp.int32, (1, z.width), 1)
    sums = jnp.zeros((1, z.width), F32)
    for i in range(z.count):
        sums += jnp.where(lane == resp_prompt[me * z.count + i], rewards[i], 0.0)
    high = sums.astype(BF16).astype(F32)
    middle = (sums - high).astype(BF16).astype(F32)
    low = sums - high - middle
    row = lax.broadcasted_iota(jnp.int32, (TAIL, z.width), 0)
    pieces = jnp.where(row == 0, high, jnp.where(row == 1, middle, jnp.where(row == 2, low, 0.0)))
    staged[2 * z.prefix_len :, :] = pieces.astype(BF16)
    for copy in large:
        copy.wait()
    last = pltpu.make_async_copy(staged, payload, sems.at[0])
    last.start()
    last.wait()


def tail_copies(z, payloads, tails, sems):
    return [
        pltpu.make_async_copy(payload.at[pl.ds(2 * z.prefix_len, TAIL)], tails.at[n], sems.at[n])
        for n, payload in enumerate(payloads)
    ]


def row_copies(here, there, at_here, at_there, sems):
    (q0, og0, kv0), (q1, og1, kv1) = here, there
    return (
        pltpu.make_async_copy(q0.at[at_here], q1.at[at_there], sems.at[0]),
        pltpu.make_async_copy(og0.at[at_here], og1.at[at_there], sems.at[1]),
        pltpu.make_async_copy(kv0.at[0, at_here], kv1.at[0, at_there], sems.at[2]),
        pltpu.make_async_copy(kv0.at[1, at_here], kv1.at[1, at_there], sems.at[3]),
    )


def result_copies(out, own, q_out, self_out, place, at, sems, back=False):
    pairs = [
        (out.at[place], q_out.at[at]),
        (own.at[place, 0], self_out.at[0, at]),
        (own.at[place, 1], self_out.at[1, at]),
    ]
    return [
        pltpu.make_async_copy(*(reversed(pair) if back else pair), sems.at[place, n])
        for n, pair in enumerate(pairs)
    ]


def group_kernel(z, turns, raw, n_tails, aliased, *refs):
    small_hbm, given = refs[:4], refs[4:7]
    tail_hbm, prompts = refs[7 : 7 + n_tails], refs[7 + n_tails : 7 + n_tails + len(turns)]
    refs = refs[7 + n_tails + len(turns) + aliased :]
    (q_out, self_out), grads_out = refs[:2], refs[2 : 2 + len(turns)]
    (resp_prompt, resp_len, rewards, far_rewards, order, lens, factors, q, og, kv, prefix, tails, acc, out, own, grads,
     sem_small, sem_tails, sem_prefix, sem_in, sem_out, sem_grads) = refs[2 + len(turns) :]
    me = lax.axis_index("dp")
    n_slots = len(turns) * z.slots

    small = [
        pltpu.make_async_copy(src, dst, sem_small.at[n])
        for n, (src, dst) in enumerate(zip(small_hbm, (resp_prompt, resp_len, rewards, far_rewards)))
    ]
    prefix_copies = [
        pltpu.make_async_copy(
            prompts[t].at[pl.ds(n * z.prefix_len, z.prefix_len)], prefix.at[t, n], sem_prefix.at[t, n]
        )
        for t in range(len(turns))
        for n in range(2)
    ]
    late = tail_copies(z, tail_hbm, tails, sem_tails)
    for copy in small + prefix_copies + late:
        copy.start()
    small[0].wait()
    find_responses(z, me, turns, resp_prompt, order)

    def copies_in(slot):
        return row_copies(
            given, (q, og, kv), token_rows(z, order[slot]), token_rows(z, slot), sem_in.at[slot]
        )

    def copies_out(slot):
        return result_copies(out, own, q_out, self_out, slot, token_rows(z, order[slot]), sem_out)

    for slot in range(n_slots):
        for copy in copies_in(slot):
            copy.start()
    for copy in small[1:] + late:
        copy.wait()
    for t, turn in enumerate(turns):
        total = None if raw else prompt_total(z, me, me ^ turn, resp_prompt, tails, far_rewards)
        for slot in range(t * z.slots, (t + 1) * z.slots):
            i = order[slot]
            lens[slot] = resp_len[i]
            factors[slot] = 1.0 if raw else reward_factor(z, rewards[i], total, resp_len[i])
    if not raw:
        acc[...] = jnp.zeros(acc.shape, F32)
    for copy in prefix_copies:
        copy.wait()

    def unit(u, _):
        at = [u * PAIR + n for n in range(PAIR)]
        t = u // (z.slots // PAIR)
        for slot in at:
            for copy in copies_in(slot):
                copy.wait()

        def sink(n, cols, key_grad, value_grad):
            if raw:
                grads[at[n], 0, :, cols] = key_grad.astype(BF16)
                grads[at[n], 1, :, cols] = value_grad.astype(BF16)
            else:
                acc[t, 0, :, cols] += key_grad
                acc[t, 1, :, cols] += value_grad

        attend_pair(
            z, [token_rows(z, n) for n in at], at, q, og, kv, prefix.at[t], [lens[n] for n in at],
            [factors[n] for n in at], out, own, sink, raw,
        )
        for slot in at:
            for copy in copies_out(slot):
                copy.start()
        return 0

    lax.fori_loop(0, n_slots // PAIR, unit, 0)
    if raw:
        last = [pltpu.make_async_copy(grads, grads_out[0], sem_grads.at[0])]
    else:
        grads[...] = acc[...].astype(BF16)
        last = [
            pltpu.make_async_copy(grads.at[t], grads_out[t], sem_grads.at[t]) for t in range(len(turns))
        ]
    for copy in last:
        copy.start()
    for slot in range(n_slots):
        for copy in copies_out(slot):
            copy.wait()
    for copy in last:
        copy.wait()


def finish_kernel(z, n_tails, n_come, *refs):
    small_hbm, tail_hbm = refs[:4], refs[4 : 4 + n_tails]
    per_resp_hbm, come_hbm = refs[4 + n_tails], refs[5 + n_tails : 5 + n_tails + n_come]
    q_out, self_out, grads_out = refs[7 + n_tails + n_come : 10 + n_tails + n_come]
    (resp_prompt, resp_len, rewards, far_rewards, order, tails, out, own, per_resp, come, grads,
     sem_small, sem_tails, sem_come, sem_in, sem_out) = refs[10 + n_tails + n_come :]
    me = lax.axis_index("dp")
    small = [
        pltpu.make_async_copy(src, dst, sem_small.at[n])
        for n, (src, dst) in enumerate(zip(small_hbm, (resp_prompt, resp_len, rewards, far_rewards)))
    ]
    late = tail_copies(z, tail_hbm, tails, sem_tails)
    late += [pltpu.make_async_copy(src, come.at[n], sem_come.at[n]) for n, src in enumerate(come_hbm)]
    late += [pltpu.make_async_copy(per_resp_hbm, per_resp, sem_come.at[n_come])]
    for copy in small + late:
        copy.start()
    small[0].wait()
    find_responses(z, me, (0,), resp_prompt, order)

    def moves(slot, back):
        sems = sem_in if back else sem_out
        return result_copies(out, own, q_out, self_out, slot, token_rows(z, order[slot]), sems, back)

    for slot in range(z.slots):
        for copy in moves(slot, True):
            copy.start()
    for copy in small[1:] + late:
        copy.wait()
    total = prompt_total(z, me, me, resp_prompt, tails, far_rewards)
    summed = come[0].astype(F32)
    for n in range(1, n_come):
        summed += come[n].astype(F32)
    factors = [reward_factor(z, rewards[order[n]], total, resp_len[order[n]]) for n in range(z.slots)]
    for slot in range(z.slots):
        summed += per_resp[slot].astype(F32) * factors[slot]
    grads[...] = summed
    last = pltpu.make_async_copy(grads, grads_out, sem_small.at[0])
    last.start()
    for slot in range(z.slots):
        for copy in moves(slot, True):
            copy.wait()
        out[slot] = (out[slot].astype(F32) * factors[slot]).astype(BF16)
        own[slot] = (own[slot].astype(F32) * factors[slot]).astype(BF16)
        for copy in moves(slot, False):
            copy.start()
    for slot in range(z.slots):
        for copy in moves(slot, False):
            copy.wait()
    last.wait()


def near_shards(z, prompt_kv, resp_q, resp_kv, out_grad, rewards, resp_prompt, resp_len):
    n_dp = z.n_dp
    assert z.slots % PAIR == 0
    shape = jax.ShapeDtypeStruct
    one = (2, z.prefix_len, z.width)
    params = pltpu.CompilerParams(vmem_limit_bytes=VMEM_BYTES)
    cost = pl.CostEstimate(flops=0, bytes_accessed=0, transcendentals=0)
    payload = pl.pallas_call(
        functools.partial(pack_kernel, z),
        out_shape=jax.ShapeDtypeStruct((2 * z.prefix_len + TAIL, z.width), BF16),
        in_specs=[ANYWHERE] * 3,
        out_specs=ANYWHERE,
        scratch_shapes=[
            pltpu.SMEM(rewards.shape, F32),
            pltpu.SMEM(resp_prompt.shape, jnp.int32),
            pltpu.VMEM((2 * z.prefix_len + TAIL, z.width), BF16),
            pltpu.SemaphoreType.DMA((4,)),
        ],
        compiler_params=pltpu.CompilerParams(vmem_limit_bytes=VMEM_BYTES),
        name="pack",
    )(prompt_kv, rewards, resp_prompt)

    assert n_dp == FAR + 1

    def swap(x, s):
        return lax.ppermute(x, "dp", [(i, i ^ s) for i in range(n_dp)])

    payloads = {0: payload, 2: swap(payload, 2), 1: swap(payload, 1)}
    tails = [payloads[s] for s in range(FAR)]
    small = (resp_prompt, resp_len, rewards)
    far_rewards = swap(rewards, FAR)
    smem = [pltpu.SMEM(x.shape, x.dtype) for x in (*small, rewards)]
    slots = z.slots

    def grads_of(turns, raw, written):
        n_slots, n_turns = len(turns) * slots, len(turns)
        used_tails = [] if raw else tails
        used_small = (*small, rewards if raw else far_rewards)
        prompts = [payloads[turn] for turn in turns]
        operands = [*used_small, resp_q, out_grad, resp_kv, *used_tails, *prompts, *written]
        grads_shapes = [(slots,) + one] if raw else [one] * n_turns
        return pl.pallas_call(
            functools.partial(group_kernel, z, turns, raw, len(used_tails), len(written)),
            out_shape=[shape(resp_q.shape, BF16), shape(resp_kv.shape, BF16)]
            + [shape(x, BF16) for x in grads_shapes],
            in_specs=[ANYWHERE] * len(operands),
            out_specs=[ANYWHERE] * (2 + len(grads_shapes)),
            input_output_aliases={len(operands) - 2: 0, len(operands) - 1: 1} if written else {},
            scratch_shapes=[
                *smem,
                pltpu.SMEM((n_slots + 1,), jnp.int32),
                pltpu.SMEM((n_slots,), jnp.int32),
                pltpu.SMEM((n_slots,), F32),
                pltpu.VMEM((n_slots * z.tokens, z.lanes), BF16),
                pltpu.VMEM((n_slots * z.tokens, z.lanes), BF16),
                pltpu.VMEM((2, n_slots * z.tokens, z.width), BF16),
                pltpu.VMEM((n_turns,) + one, BF16),
                pltpu.VMEM((FAR, TAIL, z.width), BF16),
                pltpu.VMEM((n_turns,) + one, F32),
                pltpu.VMEM((n_slots, z.tokens, z.lanes), BF16),
                pltpu.VMEM((n_slots, 2, z.tokens, z.width), BF16),
                pltpu.VMEM(grads_shapes[0] if raw else (n_turns,) + one, BF16),
                pltpu.SemaphoreType.DMA((len(smem),)),
                pltpu.SemaphoreType.DMA((FAR,)),
                pltpu.SemaphoreType.DMA((n_turns, 2)),
                pltpu.SemaphoreType.DMA((n_slots, 4)),
                pltpu.SemaphoreType.DMA((n_slots, 3)),
                pltpu.SemaphoreType.DMA((n_turns,)),
            ],
            compiler_params=params,
            cost_estimate=cost,
            name="raw_grads" if raw else "group_grads",
        )(*operands)

    *written, per_resp = grads_of((0,), True, ())
    onward, per_resp, far_rewards = lax.optimization_barrier((payloads[2], per_resp, far_rewards))
    payloads[FAR] = swap(onward, 1)
    *written, for_2, for_1 = grads_of((2, 1), False, written)
    come = [swap(for_2, 2), swap(for_1, 1)]
    *written, for_far = grads_of((FAR,), False, written)
    last = swap(for_far, FAR)
    operands = [*small, far_rewards, *tails, per_resp, *come, *written]
    q_out, self_out, own_grads = pl.pallas_call(
        functools.partial(finish_kernel, z, len(tails), len(come)),
        out_shape=[shape(resp_q.shape, BF16), shape(resp_kv.shape, BF16), shape(one, F32)],
        in_specs=[ANYWHERE] * len(operands),
        out_specs=[ANYWHERE] * 3,
        input_output_aliases={len(operands) - 2: 0, len(operands) - 1: 1},
        scratch_shapes=[
            *smem,
            pltpu.SMEM((slots + 1,), jnp.int32),
            pltpu.VMEM((FAR, TAIL, z.width), BF16),
            pltpu.VMEM((slots, z.tokens, z.lanes), BF16),
            pltpu.VMEM((slots, 2, z.tokens, z.width), BF16),
            pltpu.VMEM((slots,) + one, BF16),
            pltpu.VMEM((len(come),) + one, BF16),
            pltpu.VMEM(one, F32),
            pltpu.SemaphoreType.DMA((len(smem),)),
            pltpu.SemaphoreType.DMA((FAR,)),
            pltpu.SemaphoreType.DMA((len(come) + 1,)),
            pltpu.SemaphoreType.DMA((slots, 3)),
            pltpu.SemaphoreType.DMA((slots, 3)),
        ],
        compiler_params=params,
        cost_estimate=cost,
        name="finish_own",
    )(*operands)
    prefix_out = (own_grads + last.astype(F32)).astype(BF16)
    return (q_out, self_out, prefix_out)


def far_kernel(z, *refs):
    (resp_prompt, resp_len, rewards, q_hbm, og_hbm, kv_hbm, prompts, q_out, self_out, prefix_outs,
     totals, lens, factors, q, og, kv, prefix, out, own, grads, sem_in, sem_prefix, sem_out) = refs
    me = lax.axis_index("dp")

    for p in range(z.n_dp):
        totals[p] = 0.0

    def copies_in(slot):
        rows = token_rows(z, slot)
        prompt = resp_prompt[me * z.count + slot]
        return (
            *row_copies((q_hbm, og_hbm, kv_hbm), (q, og, kv), rows, rows, sem_in.at[slot]),
            pltpu.make_async_copy(prompts.at[prompt], prefix.at[slot], sem_prefix.at[slot]),
        )

    def copies_out(slot):
        rows = token_rows(z, slot)
        return (
            *result_copies(out, own, q_out, self_out, slot, rows, sem_out),
            pltpu.make_async_copy(grads.at[slot], prefix_outs.at[slot], sem_out.at[slot, 3]),
        )

    def start(slot, _):
        for copy in copies_in(slot):
            copy.start()
        return 0

    lax.fori_loop(0, z.count, start, 0)

    def add(i, _):
        prompt = resp_prompt[i]
        totals[prompt] = totals[prompt] + rewards[i]
        return 0

    lax.fori_loop(0, z.n_dp * z.count, add, 0)

    def find_factor(slot, _):
        place = me * z.count + slot
        lens[slot] = resp_len[slot]
        factors[slot] = reward_factor(z, rewards[place], totals[resp_prompt[place]], resp_len[slot])
        return 0

    lax.fori_loop(0, z.count, find_factor, 0)

    def unit(slot, _):
        for copy in copies_in(slot):
            copy.wait()

        def sink(_, cols, key_grad, value_grad):
            grads[slot, 0, :, cols] = key_grad.astype(BF16)
            grads[slot, 1, :, cols] = value_grad.astype(BF16)

        attend_pair(
            z, [token_rows(z, slot)], [slot], q, og, kv, prefix.at[slot], [lens[slot]], [factors[slot]], out, own, sink, True
        )
        for copy in copies_out(slot):
            copy.start()
        return 0

    lax.fori_loop(0, z.count, unit, 0)

    def end(slot, _):
        for copy in copies_out(slot):
            copy.wait()
        return 0

    lax.fori_loop(0, z.count, end, 0)


def far_shards(z, prompt_kv, resp_q, resp_kv, out_grad, rewards, resp_prompt, resp_len):
    assert z.slots == 1
    count, n_dp = z.count, z.n_dp
    one = (2, z.prefix_len, z.width)
    smem = pl.BlockSpec(memory_space=pltpu.SMEM)
    q_out, self_out, per_resp = pl.pallas_call(
        functools.partial(far_kernel, z),
        out_shape=[
            jax.ShapeDtypeStruct(resp_q.shape, BF16),
            jax.ShapeDtypeStruct(resp_kv.shape, BF16),
            jax.ShapeDtypeStruct((count,) + one, BF16),
        ],
        in_specs=[smem] * 3 + [ANYWHERE] * 4,
        out_specs=[ANYWHERE] * 3,
        scratch_shapes=[
            pltpu.SMEM((n_dp,), F32),
            pltpu.SMEM((count,), jnp.int32),
            pltpu.SMEM((count,), F32),
            pltpu.VMEM(resp_q.shape, BF16),
            pltpu.VMEM(resp_q.shape, BF16),
            pltpu.VMEM(resp_kv.shape, BF16),
            pltpu.VMEM((count,) + one, BF16),
            pltpu.VMEM((count, z.tokens, z.lanes), BF16),
            pltpu.VMEM((count, 2, z.tokens, z.width), BF16),
            pltpu.VMEM((count,) + one, BF16),
            pltpu.SemaphoreType.DMA((count, 4)),
            pltpu.SemaphoreType.DMA((count,)),
            pltpu.SemaphoreType.DMA((count, 4)),
        ],
        compiler_params=pltpu.CompilerParams(vmem_limit_bytes=VMEM_BYTES),
        name="far_grads",
    )(
        resp_prompt,
        resp_len,
        lax.all_gather(rewards, "dp", axis=0, tiled=True),
        resp_q,
        out_grad,
        resp_kv,
        lax.all_gather(prompt_kv, "dp", axis=0),
    )
    my_prompts = lax.dynamic_slice_in_dim(resp_prompt, lax.axis_index("dp") * count, count)
    route = (jnp.arange(n_dp, dtype=jnp.int32)[:, None] == my_prompts[None, :]).astype(BF16)
    outgoing = jnp.dot(route, per_resp.reshape(count, -1), preferred_element_type=F32).astype(BF16)
    outgoing = outgoing.reshape((n_dp,) + one)
    incoming = lax.all_to_all(outgoing, "dp", split_axis=0, concat_axis=0, tiled=True)
    prefix_out = jnp.sum(incoming, axis=0, dtype=F32).astype(BF16)
    return (q_out, self_out, prefix_out)


def shards(prompt_kv, resp_q, resp_kv, out_grad, rewards, resp_prompt, resp_len):
    n_dp = lax.axis_size("dp")
    count = rewards.shape[0]
    prefix_len, width = prompt_kv.shape[1:]
    slots = (count + n_dp - 1) // n_dp
    z = Sizes(
        n_dp, count, slots, width // HD, resp_q.shape[1] // width, resp_q.shape[0] // count, prefix_len
    )
    part = near_shards if count // slots == n_dp else far_shards
    return part(z, prompt_kv, resp_q, resp_kv, out_grad, rewards, resp_prompt, resp_len)


def solution(mesh):
    in_specs = (
        P(None, ("groups", "dp"), "tensor"),
        P(("groups", "dp"), "tensor"),
        P(None, ("groups", "dp"), "tensor"),
        P(("groups", "dp"), "tensor"),
        P(("groups", "dp")),
        P("groups"),
        P(("groups", "dp")),
    )
    out_specs = (
        P(("groups", "dp"), "tensor"),
        P(None, ("groups", "dp"), "tensor"),
        P(None, ("groups", "dp"), "tensor"),
    )
    return jax.shard_map(shards, mesh=mesh, in_specs=in_specs, out_specs=out_specs, check_vma=False)
```

```python
import functools
import math
from typing import NamedTuple

import jax
import jax.numpy as jnp
from jax import lax
from jax.experimental import pallas as pl
from jax.experimental.pallas import tpu as pltpu
from jax.sharding import PartitionSpec as P

HD = 128
NEG = -1e30
TAIL = 16
F32 = jnp.float32
BF16 = jnp.bfloat16
PAIR = 2
FAR = 3
VMEM_BYTES = 63 * 1024 * 1024
GROUP_BYTES = 53 * 1024 * 1024
FINISH_BYTES = 24 * 1024 * 1024
ANYWHERE = pl.BlockSpec(memory_space=pl.ANY)


class Sizes(NamedTuple):
    n_dp: int
    count: int
    slots: int
    kv_heads: int
    group_size: int
    tokens: int
    prefix_len: int

    @property
    def width(self):
        return self.kv_heads * HD

    @property
    def lanes(self):
        return self.kv_heads * self.group_size * HD


def dot(a, b, dims):
    return lax.dot_general(a, b, (dims, ((), ())), preferred_element_type=F32)


NN = ((1,), (0,))
NT = ((1,), (1,))


class Bag:
    pass


def attend_pair(z, at, places, q, og, kv, prefix, lens, factors, out, own_out, sink, apart):
    tokens, prefix_len, group_size = z.tokens, z.prefix_len, z.group_size
    scale = 1.0 / math.sqrt(HD)
    log_scale = scale * math.log2(math.e)
    whole = group_size - group_size % 2
    single = len(at) == 1
    members = range(len(at))
    sides = (0, 0) if single else (0, 1)
    most = max(whole, 2) * tokens
    assert tokens & (tokens - 1) == 0
    token = lax.broadcasted_iota(jnp.int32, (1, most), 1) & (tokens - 1)
    key = lax.broadcasted_iota(jnp.int32, (tokens, most), 0)
    causal = key <= (lax.broadcasted_iota(jnp.int32, (tokens, most), 1) & (tokens - 1))
    left = lax.broadcasted_iota(jnp.int32, (1, 2 * tokens), 1) < tokens

    def head(k, h):
        start = (k * group_size + h) * HD
        return slice(start, start + HD)

    def rows(ref, k, blocks):
        return jnp.concatenate([ref[at[n], head(k, h)] for n, h in blocks], axis=0)

    def halves(part):
        none = jnp.zeros_like(part)
        return [jnp.where(left, part, none), jnp.where(left, none, part)]

    def own_half(both):
        return jnp.where(left, both[:tokens], both[tokens:])

    def rounded(*parts):
        return jnp.concatenate([part.astype(BF16) for part in parts], axis=0)

    chunks = []
    for k in range(z.kv_heads):
        t = Bag()
        t.cols = slice(k * HD, (k + 1) * HD)
        t.key_p, t.value_p = prefix[0, :, t.cols], prefix[1, :, t.cols]
        t.keys = [kv[0, at[n], t.cols] for n in sides]
        t.values = [kv[1, at[n], t.cols] for n in sides]
        t.key_pair = jnp.concatenate(t.keys, axis=0)
        t.value_pair = jnp.concatenate(t.values, axis=0)
        t.key_t = jnp.concatenate([t.key_p.T, t.key_pair.T], axis=1)
        t.prefix_sums = {n: [] for n in members}
        t.self_sums = {n: [] for n in members}
        mine = []
        for n in members:
            c = Bag()
            c.k, c.t, c.side, c.blocks = k, t, n, [(n, h) for h in range(whole)]
            mine.append(c)
        if group_size % 2:
            c = Bag()
            c.k, c.t, c.side, c.blocks = k, t, None, [(n, group_size - 1) for n in sides]
            mine.append(c)
        t.left_over = len(mine)
        chunks += mine

    def products(c):
        t = c.t
        c.q_rows, c.g_rows = rows(q, c.k, c.blocks), rows(og, c.k, c.blocks)
        if c.side is None:
            key_s, value_s = t.key_pair, t.value_pair
        else:
            key_s, value_s = t.keys[c.side], t.values[c.side]
        c.scores = dot(jnp.concatenate([t.key_p, key_s], axis=0), c.q_rows, NT)
        c.gw = dot(jnp.concatenate([t.value_p, value_s], axis=0), c.g_rows, NT)

    def weigh(c):
        scores_p, scores_s = c.scores[:prefix_len], c.scores[prefix_len:]
        c.gw_p, c.gw_s = c.gw[:prefix_len], c.gw[prefix_len:]
        if c.side is None:
            scores_s, c.gw_s = own_half(scores_s), own_half(c.gw_s)
        scores_s = jnp.where(causal[:, : scores_s.shape[1]], scores_s, NEG)
        top = jnp.maximum(
            jnp.max(scores_p, axis=0, keepdims=True), jnp.max(scores_s, axis=0, keepdims=True)
        )
        c.e_p = jnp.exp2((scores_p - top) * log_scale)
        c.e_s = jnp.exp2((scores_s - top) * log_scale)
        total = jnp.sum(c.e_p, axis=0, keepdims=True) + jnp.sum(c.e_s, axis=0, keepdims=True)
        weighted = jnp.sum(c.e_p * c.gw_p, axis=0, keepdims=True) + jnp.sum(
            c.e_s * c.gw_s, axis=0, keepdims=True
        )
        if c.side is None:
            length = jnp.where(left, lens[0], 0 if single else lens[1])
            gain = jnp.where(left, factors[0], factors[-1])
        else:
            length, gain = lens[c.side], factors[c.side]
        inverse = 1.0 / total
        c.delta = weighted * inverse
        c.gain = inverse * jnp.where(token[:, : total.shape[1]] < length, gain, 0.0)

    def gradients(c):
        w_p, w_s = c.e_p * c.gain, c.e_s * c.gain
        d_p, d_s = w_p * (c.gw_p - c.delta), w_s * (c.gw_s - c.delta)
        if c.side is None:
            d_s, w_s = halves(d_s), halves(w_s)
            c.d_wide = rounded(d_p, *d_s)
            c.d_all = rounded(*halves(d_p), *d_s) if apart else c.d_wide
            c.w_all = rounded(*(halves(w_p) if apart else [w_p]), *w_s)
        else:
            empty = jnp.zeros_like(d_s)
            c.d_wide = rounded(*([d_p, empty, d_s] if c.side else [d_p, d_s, empty]))
            c.d_all = rounded(d_p, d_s)
            c.w_all = rounded(w_p, w_s)

    def outgoing(c):
        t = c.t
        q_grad = (dot(t.key_t, c.d_wide, NN) * scale).astype(BF16).T
        kg = dot(c.d_all, c.q_rows, NN)
        vg = dot(c.w_all, c.g_rows, NN)
        targets = members if c.side is None else [c.side]
        for place, (n, h) in enumerate(c.blocks):
            if c.side is not None or place < len(targets):
                out[places[n], :, head(c.k, h)] = q_grad[place * tokens : (place + 1) * tokens]
        many = 2 if c.side is None and apart else 1
        for place, n in enumerate(targets):
            if place < many:
                rows_p = slice(place * prefix_len, (place + 1) * prefix_len)
                t.prefix_sums[n if apart else 0].append((kg[rows_p], vg[rows_p]))
            start = many * prefix_len + place * tokens
            rows_s = slice(start, start + tokens)
            t.self_sums[n].append((kg[rows_s], vg[rows_s]))
        t.left_over -= 1
        if t.left_over == 0:
            for n in members:
                keys, values = zip(*t.self_sums[n])
                own_out[places[n], 0, :, t.cols] = (sum(keys) * scale).astype(BF16)
                own_out[places[n], 1, :, t.cols] = sum(values).astype(BF16)
                if apart or n == 0:
                    keys, values = zip(*t.prefix_sums[n])
                    sink(n, t.cols, sum(keys) * scale, sum(values))

    stages = (products, weigh, gradients, outgoing)
    for step in range(len(chunks) + len(stages) - 1):
        for late, stage in reversed(list(enumerate(stages))):
            if 0 <= step - late < len(chunks):
                stage(chunks[step - late])


def token_rows(z, i):
    return pl.ds(pl.multiple_of(i * z.tokens, z.tokens), z.tokens)


def find_responses(z, me, turns, resp_prompt, order):
    for t, turn in enumerate(turns):
        prompt = me ^ turn
        found = t * z.slots
        for i in range(z.count):
            order[found] = i
            found = found + (resp_prompt[me * z.count + i] == prompt).astype(jnp.int32)


def prompt_total(z, me, prompt, resp_prompt, tails, far_rewards):
    sums = jnp.zeros((1, z.width), F32)
    for s in range(tails.shape[0]):
        tail = tails[s].astype(F32)
        sums += tail[0:1] + tail[1:2] + tail[2:3]
    lane = lax.broadcasted_iota(jnp.int32, sums.shape, 1)
    total = jnp.sum(jnp.where(lane == prompt, sums, 0.0))
    for i in range(z.count):
        total += jnp.where(resp_prompt[(me ^ FAR) * z.count + i] == prompt, far_rewards[i], 0.0)
    return total


def reward_factor(z, reward, total, length):
    return (reward - total / z.count) * (z.tokens / length.astype(F32))


def pack_kernel(z, prompt_hbm, rewards_hbm, resp_prompt_hbm, payload, rewards, resp_prompt, staged, sems):
    me = lax.axis_index("dp")
    small = [
        pltpu.make_async_copy(rewards_hbm, rewards, sems.at[0]),
        pltpu.make_async_copy(resp_prompt_hbm, resp_prompt, sems.at[1]),
    ]
    large = [
        pltpu.make_async_copy(
            prompt_hbm.at[n], staged.at[pl.ds(n * z.prefix_len, z.prefix_len)], sems.at[2 + n]
        )
        for n in range(2)
    ]
    for copy in small + large:
        copy.start()
    for copy in small:
        copy.wait()
    lane = lax.broadcasted_iota(jnp.int32, (1, z.width), 1)
    sums = jnp.zeros((1, z.width), F32)
    for i in range(z.count):
        sums += jnp.where(lane == resp_prompt[me * z.count + i], rewards[i], 0.0)
    high = sums.astype(BF16).astype(F32)
    middle = (sums - high).astype(BF16).astype(F32)
    low = sums - high - middle
    row = lax.broadcasted_iota(jnp.int32, (TAIL, z.width), 0)
    pieces = jnp.where(row == 0, high, jnp.where(row == 1, middle, jnp.where(row == 2, low, 0.0)))
    staged[2 * z.prefix_len :, :] = pieces.astype(BF16)
    for copy in large:
        copy.wait()
    last = pltpu.make_async_copy(staged, payload, sems.at[0])
    last.start()
    last.wait()


def tail_copies(z, payloads, tails, sems):
    return [
        pltpu.make_async_copy(payload.at[pl.ds(2 * z.prefix_len, TAIL)], tails.at[n], sems.at[n])
        for n, payload in enumerate(payloads)
    ]


def row_copies(here, there, at_here, at_there, sems):
    (q0, og0, kv0), (q1, og1, kv1) = here, there
    return (
        pltpu.make_async_copy(q0.at[at_here], q1.at[at_there], sems.at[0]),
        pltpu.make_async_copy(og0.at[at_here], og1.at[at_there], sems.at[1]),
        pltpu.make_async_copy(kv0.at[:, at_here], kv1.at[:, at_there], sems.at[2]),
    )


def result_copies(out, own, q_out, self_out, place, at, sems, back=False):
    pairs = [
        (out.at[place], q_out.at[at]),
        (own.at[place], self_out.at[:, at]),
    ]
    return [
        pltpu.make_async_copy(*(reversed(pair) if back else pair), sems.at[place, n])
        for n, pair in enumerate(pairs)
    ]


def group_kernel(z, turns, raw, n_tails, aliased, *refs):
    small_hbm, given = refs[:4], refs[4:7]
    tail_hbm, prompts = refs[7 : 7 + n_tails], refs[7 + n_tails : 7 + n_tails + len(turns)]
    refs = refs[7 + n_tails + len(turns) + aliased :]
    (q_out, self_out), grads_out = refs[:2], refs[2 : 2 + len(turns)]
    (resp_prompt, resp_len, rewards, far_rewards, order, lens, factors, q, og, kv, prefix, tails, acc, out, own, grads,
     sem_small, sem_tails, sem_prefix, sem_in, sem_out, sem_grads) = refs[2 + len(turns) :]
    me = lax.axis_index("dp")
    n_slots = len(turns) * z.slots

    small = [
        pltpu.make_async_copy(src, dst, sem_small.at[n])
        for n, (src, dst) in enumerate(zip(small_hbm, (resp_prompt, resp_len, rewards, far_rewards)))
    ]
    prefix_copies = [
        pltpu.make_async_copy(
            prompts[t].at[pl.ds(n * z.prefix_len, z.prefix_len)], prefix.at[t, n], sem_prefix.at[t, n]
        )
        for t in range(len(turns))
        for n in range(2)
    ]
    late = tail_copies(z, tail_hbm, tails, sem_tails)
    for copy in small + prefix_copies + late:
        copy.start()
    small[0].wait()
    find_responses(z, me, turns, resp_prompt, order)

    def copies_in(slot):
        return row_copies(
            given, (q, og, kv), token_rows(z, order[slot]), token_rows(z, slot), sem_in.at[slot]
        )

    def copies_out(slot):
        return result_copies(out, own, q_out, self_out, slot, token_rows(z, order[slot]), sem_out)

    for slot in range(n_slots):
        for copy in copies_in(slot):
            copy.start()
    for copy in small[1:] + late:
        copy.wait()
    for t, turn in enumerate(turns):
        total = None if raw else prompt_total(z, me, me ^ turn, resp_prompt, tails, far_rewards)
        for slot in range(t * z.slots, (t + 1) * z.slots):
            i = order[slot]
            lens[slot] = resp_len[i]
            factors[slot] = 1.0 if raw else reward_factor(z, rewards[i], total, resp_len[i])
    if not raw:
        acc[...] = jnp.zeros(acc.shape, F32)
    for copy in prefix_copies:
        copy.wait()

    def unit(u, _):
        at = [u * PAIR + n for n in range(PAIR)]
        t = u // (z.slots // PAIR)
        for slot in at:
            for copy in copies_in(slot):
                copy.wait()

        def sink(n, cols, key_grad, value_grad):
            if raw:
                grads[at[n], 0, :, cols] = key_grad.astype(BF16)
                grads[at[n], 1, :, cols] = value_grad.astype(BF16)
            else:
                acc[t, 0, :, cols] += key_grad
                acc[t, 1, :, cols] += value_grad

        attend_pair(
            z, [token_rows(z, n) for n in at], at, q, og, kv, prefix.at[t], [lens[n] for n in at],
            [factors[n] for n in at], out, own, sink, raw,
        )
        for slot in at:
            for copy in copies_out(slot):
                copy.start()
        return 0

    lax.fori_loop(0, n_slots // PAIR, unit, 0)
    if raw:
        last = [pltpu.make_async_copy(grads, grads_out[0], sem_grads.at[0])]
    else:
        grads[...] = acc[...].astype(BF16)
        last = [
            pltpu.make_async_copy(grads.at[t], grads_out[t], sem_grads.at[t]) for t in range(len(turns))
        ]
    for copy in last:
        copy.start()
    for slot in range(n_slots):
        for copy in copies_out(slot):
            copy.wait()
    for copy in last:
        copy.wait()


def finish_kernel(z, n_tails, n_come, *refs):
    small_hbm, tail_hbm = refs[:4], refs[4 : 4 + n_tails]
    per_resp_hbm, come_hbm = refs[4 + n_tails], refs[5 + n_tails : 5 + n_tails + n_come]
    q_out, self_out, grads_out = refs[7 + n_tails + n_come : 10 + n_tails + n_come]
    (resp_prompt, resp_len, rewards, far_rewards, order, tails, out, own, per_resp, come, grads,
     sem_small, sem_tails, sem_come, sem_in, sem_out) = refs[10 + n_tails + n_come :]
    me = lax.axis_index("dp")
    small = [
        pltpu.make_async_copy(src, dst, sem_small.at[n])
        for n, (src, dst) in enumerate(zip(small_hbm, (resp_prompt, resp_len, rewards, far_rewards)))
    ]
    late = tail_copies(z, tail_hbm, tails, sem_tails)
    late += [pltpu.make_async_copy(src, come.at[n], sem_come.at[n]) for n, src in enumerate(come_hbm)]
    late += [pltpu.make_async_copy(per_resp_hbm, per_resp, sem_come.at[n_come])]
    for copy in small + late:
        copy.start()
    small[0].wait()
    find_responses(z, me, (0,), resp_prompt, order)

    def moves(slot, back):
        sems = sem_in if back else sem_out
        return result_copies(out, own, q_out, self_out, slot, token_rows(z, order[slot]), sems, back)

    for slot in range(z.slots):
        for copy in moves(slot, True):
            copy.start()
    for copy in small[1:] + late:
        copy.wait()
    total = prompt_total(z, me, me, resp_prompt, tails, far_rewards)
    summed = come[0].astype(F32)
    for n in range(1, n_come):
        summed += come[n].astype(F32)
    factors = [reward_factor(z, rewards[order[n]], total, resp_len[order[n]]) for n in range(z.slots)]
    for slot in range(z.slots):
        summed += per_resp[slot].astype(F32) * factors[slot]
    grads[...] = summed
    last = pltpu.make_async_copy(grads, grads_out, sem_small.at[0])
    last.start()
    for slot in range(z.slots):
        for copy in moves(slot, True):
            copy.wait()
        out[slot] = (out[slot].astype(F32) * factors[slot]).astype(BF16)
        own[slot] = (own[slot].astype(F32) * factors[slot]).astype(BF16)
        for copy in moves(slot, False):
            copy.start()
    for slot in range(z.slots):
        for copy in moves(slot, False):
            copy.wait()
    last.wait()


def near_shards(z, prompt_kv, resp_q, resp_kv, out_grad, rewards, resp_prompt, resp_len):
    n_dp = z.n_dp
    assert z.slots % PAIR == 0
    shape = jax.ShapeDtypeStruct
    one = (2, z.prefix_len, z.width)
    params = pltpu.CompilerParams(vmem_limit_bytes=VMEM_BYTES)
    cost = pl.CostEstimate(flops=0, bytes_accessed=0, transcendentals=0)
    payload = pl.pallas_call(
        functools.partial(pack_kernel, z),
        out_shape=jax.ShapeDtypeStruct((2 * z.prefix_len + TAIL, z.width), BF16),
        in_specs=[ANYWHERE] * 3,
        out_specs=ANYWHERE,
        scratch_shapes=[
            pltpu.SMEM(rewards.shape, F32),
            pltpu.SMEM(resp_prompt.shape, jnp.int32),
            pltpu.VMEM((2 * z.prefix_len + TAIL, z.width), BF16),
            pltpu.SemaphoreType.DMA((4,)),
        ],
        compiler_params=pltpu.CompilerParams(vmem_limit_bytes=VMEM_BYTES),
        name="pack",
    )(prompt_kv, rewards, resp_prompt)

    assert n_dp == FAR + 1

    def swap(x, s):
        return lax.ppermute(x, "dp", [(i, i ^ s) for i in range(n_dp)])

    payloads = {0: payload, 2: swap(payload, 2), 1: swap(payload, 1)}
    tails = [payloads[s] for s in range(FAR)]
    small = (resp_prompt, resp_len, rewards)
    far_rewards = swap(rewards, FAR)
    smem = [pltpu.SMEM(x.shape, x.dtype) for x in (*small, rewards)]
    slots = z.slots

    def grads_of(turns, raw, written):
        n_slots, n_turns = len(turns) * slots, len(turns)
        used_tails = [] if raw else tails
        used_small = (*small, rewards if raw else far_rewards)
        prompts = [payloads[turn] for turn in turns]
        operands = [*used_small, resp_q, out_grad, resp_kv, *used_tails, *prompts, *written]
        grads_shapes = [(slots,) + one] if raw else [one] * n_turns
        return pl.pallas_call(
            functools.partial(group_kernel, z, turns, raw, len(used_tails), len(written)),
            out_shape=[shape(resp_q.shape, BF16), shape(resp_kv.shape, BF16)]
            + [shape(x, BF16) for x in grads_shapes],
            in_specs=[ANYWHERE] * len(operands),
            out_specs=[ANYWHERE] * (2 + len(grads_shapes)),
            input_output_aliases={len(operands) - 2: 0, len(operands) - 1: 1} if written else {},
            scratch_shapes=[
                *smem,
                pltpu.SMEM((n_slots + 1,), jnp.int32),
                pltpu.SMEM((n_slots,), jnp.int32),
                pltpu.SMEM((n_slots,), F32),
                pltpu.VMEM((n_slots * z.tokens, z.lanes), BF16),
                pltpu.VMEM((n_slots * z.tokens, z.lanes), BF16),
                pltpu.VMEM((2, n_slots * z.tokens, z.width), BF16),
                pltpu.VMEM((n_turns,) + one, BF16),
                pltpu.VMEM((FAR, TAIL, z.width), BF16),
                pltpu.VMEM((n_turns,) + one, F32),
                pltpu.VMEM((n_slots, z.tokens, z.lanes), BF16),
                pltpu.VMEM((n_slots, 2, z.tokens, z.width), BF16),
                pltpu.VMEM(grads_shapes[0] if raw else (n_turns,) + one, BF16),
                pltpu.SemaphoreType.DMA((len(smem),)),
                pltpu.SemaphoreType.DMA((FAR,)),
                pltpu.SemaphoreType.DMA((n_turns, 2)),
                pltpu.SemaphoreType.DMA((n_slots, 4)),
                pltpu.SemaphoreType.DMA((n_slots, 3)),
                pltpu.SemaphoreType.DMA((n_turns,)),
            ],
            compiler_params=params if raw else pltpu.CompilerParams(vmem_limit_bytes=GROUP_BYTES),
            cost_estimate=cost,
            name="raw_grads" if raw else "group_grads",
        )(*operands)

    *written, per_resp = grads_of((0,), True, ())
    onward, per_resp, far_rewards = lax.optimization_barrier((payloads[2], per_resp, far_rewards))
    payloads[FAR] = swap(onward, 1)
    *written, for_2, for_1 = grads_of((2, 1), False, written)
    come = [swap(for_2, 2)]
    *written, for_far = grads_of((FAR,), False, written)
    for_far, for_1 = lax.optimization_barrier((for_far, for_1))
    last = [swap(for_far, FAR), swap(for_1, 1)]
    operands = [*small, far_rewards, *tails, per_resp, *come, *written]
    q_out, self_out, own_grads = pl.pallas_call(
        functools.partial(finish_kernel, z, len(tails), len(come)),
        out_shape=[shape(resp_q.shape, BF16), shape(resp_kv.shape, BF16), shape(one, F32)],
        in_specs=[ANYWHERE] * len(operands),
        out_specs=[ANYWHERE] * 3,
        input_output_aliases={len(operands) - 2: 0, len(operands) - 1: 1},
        scratch_shapes=[
            *smem,
            pltpu.SMEM((slots + 1,), jnp.int32),
            pltpu.VMEM((FAR, TAIL, z.width), BF16),
            pltpu.VMEM((slots, z.tokens, z.lanes), BF16),
            pltpu.VMEM((slots, 2, z.tokens, z.width), BF16),
            pltpu.VMEM((slots,) + one, BF16),
            pltpu.VMEM((len(come),) + one, BF16),
            pltpu.VMEM(one, F32),
            pltpu.SemaphoreType.DMA((len(smem),)),
            pltpu.SemaphoreType.DMA((FAR,)),
            pltpu.SemaphoreType.DMA((len(come) + 1,)),
            pltpu.SemaphoreType.DMA((slots, 3)),
            pltpu.SemaphoreType.DMA((slots, 3)),
        ],
        compiler_params=pltpu.CompilerParams(vmem_limit_bytes=FINISH_BYTES),
        cost_estimate=cost,
        name="finish_own",
    )(*operands)
    prefix_out = (own_grads + sum(part.astype(F32) for part in last)).astype(BF16)
    return (q_out, self_out, prefix_out)


def far_kernel(z, *refs):
    (resp_prompt, resp_len, rewards, q_hbm, og_hbm, kv_hbm, prompts, q_out, self_out, prefix_outs,
     totals, lens, factors, q, og, kv, prefix, out, own, grads, sem_in, sem_prefix, sem_out) = refs
    me = lax.axis_index("dp")

    for p in range(z.n_dp):
        totals[p] = 0.0

    def copies_in(slot):
        rows = token_rows(z, slot)
        prompt = resp_prompt[me * z.count + slot]
        return (
            *row_copies((q_hbm, og_hbm, kv_hbm), (q, og, kv), rows, rows, sem_in.at[slot]),
            pltpu.make_async_copy(prompts.at[prompt], prefix.at[slot], sem_prefix.at[slot]),
        )

    def copies_out(slot):
        rows = token_rows(z, slot)
        return (
            *result_copies(out, own, q_out, self_out, slot, rows, sem_out),
            pltpu.make_async_copy(grads.at[slot], prefix_outs.at[slot], sem_out.at[slot, 3]),
        )

    def start(slot, _):
        for copy in copies_in(slot):
            copy.start()
        return 0

    lax.fori_loop(0, z.count, start, 0)

    def add(i, _):
        prompt = resp_prompt[i]
        totals[prompt] = totals[prompt] + rewards[i]
        return 0

    lax.fori_loop(0, z.n_dp * z.count, add, 0)

    def find_factor(slot, _):
        place = me * z.count + slot
        lens[slot] = resp_len[slot]
        factors[slot] = reward_factor(z, rewards[place], totals[resp_prompt[place]], resp_len[slot])
        return 0

    lax.fori_loop(0, z.count, find_factor, 0)

    def unit(slot, _):
        for copy in copies_in(slot):
            copy.wait()

        def sink(_, cols, key_grad, value_grad):
            grads[slot, 0, :, cols] = key_grad.astype(BF16)
            grads[slot, 1, :, cols] = value_grad.astype(BF16)

        attend_pair(
            z, [token_rows(z, slot)], [slot], q, og, kv, prefix.at[slot], [lens[slot]], [factors[slot]], out, own, sink, True
        )
        for copy in copies_out(slot):
            copy.start()
        return 0

    lax.fori_loop(0, z.count, unit, 0)

    def end(slot, _):
        for copy in copies_out(slot):
            copy.wait()
        return 0

    lax.fori_loop(0, z.count, end, 0)


def far_shards(z, prompt_kv, resp_q, resp_kv, out_grad, rewards, resp_prompt, resp_len):
    assert z.slots == 1
    count, n_dp = z.count, z.n_dp
    one = (2, z.prefix_len, z.width)
    smem = pl.BlockSpec(memory_space=pltpu.SMEM)
    q_out, self_out, per_resp = pl.pallas_call(
        functools.partial(far_kernel, z),
        out_shape=[
            jax.ShapeDtypeStruct(resp_q.shape, BF16),
            jax.ShapeDtypeStruct(resp_kv.shape, BF16),
            jax.ShapeDtypeStruct((count,) + one, BF16),
        ],
        in_specs=[smem] * 3 + [ANYWHERE] * 4,
        out_specs=[ANYWHERE] * 3,
        scratch_shapes=[
            pltpu.SMEM((n_dp,), F32),
            pltpu.SMEM((count,), jnp.int32),
            pltpu.SMEM((count,), F32),
            pltpu.VMEM(resp_q.shape, BF16),
            pltpu.VMEM(resp_q.shape, BF16),
            pltpu.VMEM(resp_kv.shape, BF16),
            pltpu.VMEM((count,) + one, BF16),
            pltpu.VMEM((count, z.tokens, z.lanes), BF16),
            pltpu.VMEM((count, 2, z.tokens, z.width), BF16),
            pltpu.VMEM((count,) + one, BF16),
            pltpu.SemaphoreType.DMA((count, 4)),
            pltpu.SemaphoreType.DMA((count,)),
            pltpu.SemaphoreType.DMA((count, 4)),
        ],
        compiler_params=pltpu.CompilerParams(vmem_limit_bytes=VMEM_BYTES),
        name="far_grads",
    )(
        resp_prompt,
        resp_len,
        lax.all_gather(rewards, "dp", axis=0, tiled=True),
        resp_q,
        out_grad,
        resp_kv,
        lax.all_gather(prompt_kv, "dp", axis=0),
    )
    my_prompts = lax.dynamic_slice_in_dim(resp_prompt, lax.axis_index("dp") * count, count)
    route = (jnp.arange(n_dp, dtype=jnp.int32)[:, None] == my_prompts[None, :]).astype(BF16)
    outgoing = jnp.dot(route, per_resp.reshape(count, -1), preferred_element_type=F32).astype(BF16)
    outgoing = outgoing.reshape((n_dp,) + one)
    incoming = lax.all_to_all(outgoing, "dp", split_axis=0, concat_axis=0, tiled=True)
    prefix_out = jnp.sum(incoming, axis=0, dtype=F32).astype(BF16)
    return (q_out, self_out, prefix_out)


def shards(prompt_kv, resp_q, resp_kv, out_grad, rewards, resp_prompt, resp_len):
    n_dp = lax.axis_size("dp")
    count = rewards.shape[0]
    prefix_len, width = prompt_kv.shape[1:]
    slots = (count + n_dp - 1) // n_dp
    z = Sizes(
        n_dp, count, slots, width // HD, resp_q.shape[1] // width, resp_q.shape[0] // count, prefix_len
    )
    part = near_shards if count // slots == n_dp else far_shards
    return part(z, prompt_kv, resp_q, resp_kv, out_grad, rewards, resp_prompt, resp_len)


def solution(mesh):
    in_specs = (
        P(None, ("groups", "dp"), "tensor"),
        P(("groups", "dp"), "tensor"),
        P(None, ("groups", "dp"), "tensor"),
        P(("groups", "dp"), "tensor"),
        P(("groups", "dp")),
        P("groups"),
        P(("groups", "dp")),
    )
    out_specs = (
        P(("groups", "dp"), "tensor"),
        P(None, ("groups", "dp"), "tensor"),
        P(None, ("groups", "dp"), "tensor"),
    )
    return jax.shard_map(shards, mesh=mesh, in_specs=in_specs, out_specs=out_specs, check_vma=False)
```

```python
import functools
import math
from typing import NamedTuple

import jax
import jax.numpy as jnp
from jax import lax
from jax.experimental import pallas as pl
from jax.experimental.pallas import tpu as pltpu
from jax.sharding import PartitionSpec as P

HD = 128
NEG = -1e30
TAIL = 16
F32 = jnp.float32
BF16 = jnp.bfloat16
PAIR = 2
FAR = 3
VMEM_BYTES = 63 * 1024 * 1024
GROUP_BYTES = 53 * 1024 * 1024
FINISH_BYTES = 24 * 1024 * 1024
ANYWHERE = pl.BlockSpec(memory_space=pl.ANY)


class Sizes(NamedTuple):
    n_dp: int
    count: int
    slots: int
    kv_heads: int
    group_size: int
    tokens: int
    prefix_len: int

    @property
    def width(self):
        return self.kv_heads * HD

    @property
    def lanes(self):
        return self.kv_heads * self.group_size * HD


def dot(a, b, dims):
    return lax.dot_general(a, b, (dims, ((), ())), preferred_element_type=F32)


NN = ((1,), (0,))
NT = ((1,), (1,))


class Bag:
    pass


def attend_pair(z, at, places, q, og, kv, prefix, lens, factors, out, own_out, sink, apart):
    tokens, prefix_len, group_size = z.tokens, z.prefix_len, z.group_size
    scale = 1.0 / math.sqrt(HD)
    log_scale = scale * math.log2(math.e)
    whole = group_size - group_size % 2
    single = len(at) == 1
    members = range(len(at))
    sides = (0, 0) if single else (0, 1)
    most = max(whole, 2) * tokens
    assert tokens & (tokens - 1) == 0
    token = lax.broadcasted_iota(jnp.int32, (1, most), 1) & (tokens - 1)
    key = lax.broadcasted_iota(jnp.int32, (tokens, most), 0)
    causal = key <= (lax.broadcasted_iota(jnp.int32, (tokens, most), 1) & (tokens - 1))
    left = lax.broadcasted_iota(jnp.int32, (1, 2 * tokens), 1) < tokens

    def head(k, h):
        start = (k * group_size + h) * HD
        return slice(start, start + HD)

    def rows(ref, k, blocks):
        return jnp.concatenate([ref[at[n], head(k, h)] for n, h in blocks], axis=0)

    def halves(part):
        none = jnp.zeros_like(part)
        return [jnp.where(left, part, none), jnp.where(left, none, part)]

    def over_keys(combine, *parts):
        reduce = jnp.max if combine is jnp.maximum else jnp.sum
        eights = [reduce(part.reshape(-1, 8, part.shape[1]), axis=0) for part in parts]
        return reduce(functools.reduce(combine, eights), axis=0, keepdims=True)

    def own_half(both):
        return jnp.where(left, both[:tokens], both[tokens:])

    def rounded(*parts):
        return jnp.concatenate([part.astype(BF16) for part in parts], axis=0)

    chunks = []
    for k in range(z.kv_heads):
        t = Bag()
        t.cols = slice(k * HD, (k + 1) * HD)
        t.key_p, t.value_p = prefix[0, :, t.cols], prefix[1, :, t.cols]
        t.keys = [kv[0, at[n], t.cols] for n in sides]
        t.values = [kv[1, at[n], t.cols] for n in sides]
        t.key_pair = jnp.concatenate(t.keys, axis=0)
        t.value_pair = jnp.concatenate(t.values, axis=0)
        t.key_t = jnp.concatenate([t.key_p.T, t.key_pair.T], axis=1)
        t.prefix_sums = {n: [] for n in members}
        t.self_sums = {n: [] for n in members}
        mine = []
        for n in members:
            c = Bag()
            c.k, c.t, c.side, c.blocks = k, t, n, [(n, h) for h in range(whole)]
            mine.append(c)
        if group_size % 2:
            c = Bag()
            c.k, c.t, c.side, c.blocks = k, t, None, [(n, group_size - 1) for n in sides]
            mine.append(c)
        t.left_over = len(mine)
        chunks += mine

    def products(c):
        t = c.t
        c.q_rows, c.g_rows = rows(q, c.k, c.blocks), rows(og, c.k, c.blocks)
        if c.side is None:
            key_s, value_s = t.key_pair, t.value_pair
        else:
            key_s, value_s = t.keys[c.side], t.values[c.side]
        c.scores = dot(jnp.concatenate([t.key_p, key_s], axis=0), c.q_rows, NT)
        c.gw = dot(jnp.concatenate([t.value_p, value_s], axis=0), c.g_rows, NT)

    def weigh(c):
        scores_p, scores_s = c.scores[:prefix_len], c.scores[prefix_len:]
        c.gw_p, c.gw_s = c.gw[:prefix_len], c.gw[prefix_len:]
        if c.side is None:
            scores_s, c.gw_s = own_half(scores_s), own_half(c.gw_s)
        scores_s = jnp.where(causal[:, : scores_s.shape[1]], scores_s, NEG)
        top = over_keys(jnp.maximum, scores_p, scores_s)
        c.e_p = jnp.exp2((scores_p - top) * log_scale)
        c.e_s = jnp.exp2((scores_s - top) * log_scale)
        total = over_keys(jnp.add, c.e_p, c.e_s)
        weighted = over_keys(jnp.add, c.e_p * c.gw_p, c.e_s * c.gw_s)
        if c.side is None:
            length = jnp.where(left, lens[0], 0 if single else lens[1])
            gain = jnp.where(left, factors[0], factors[-1])
        else:
            length, gain = lens[c.side], factors[c.side]
        inverse = 1.0 / total
        c.delta = weighted * inverse
        c.gain = inverse * jnp.where(token[:, : total.shape[1]] < length, gain, 0.0)

    def gradients(c):
        w_p, w_s = c.e_p * c.gain, c.e_s * c.gain
        d_p, d_s = w_p * (c.gw_p - c.delta), w_s * (c.gw_s - c.delta)
        if c.side is None:
            d_s, w_s = halves(d_s), halves(w_s)
            c.d_wide = rounded(d_p, *d_s)
            c.d_all = rounded(*halves(d_p), *d_s) if apart else c.d_wide
            c.w_all = rounded(*(halves(w_p) if apart else [w_p]), *w_s)
        else:
            empty = jnp.zeros_like(d_s)
            c.d_wide = rounded(*([d_p, empty, d_s] if c.side else [d_p, d_s, empty]))
            c.d_all = rounded(d_p, d_s)
            c.w_all = rounded(w_p, w_s)

    def outgoing(c):
        t = c.t
        q_grad = (dot(t.key_t, c.d_wide, NN) * scale).astype(BF16).T
        kg = dot(c.d_all, c.q_rows, NN)
        vg = dot(c.w_all, c.g_rows, NN)
        targets = members if c.side is None else [c.side]
        for place, (n, h) in enumerate(c.blocks):
            if c.side is not None or place < len(targets):
                out[places[n], :, head(c.k, h)] = q_grad[place * tokens : (place + 1) * tokens]
        many = 2 if c.side is None and apart else 1
        for place, n in enumerate(targets):
            if place < many:
                rows_p = slice(place * prefix_len, (place + 1) * prefix_len)
                t.prefix_sums[n if apart else 0].append((kg[rows_p], vg[rows_p]))
            start = many * prefix_len + place * tokens
            rows_s = slice(start, start + tokens)
            t.self_sums[n].append((kg[rows_s], vg[rows_s]))
        t.left_over -= 1
        if t.left_over == 0:
            for n in members:
                keys, values = zip(*t.self_sums[n])
                own_out[places[n], 0, :, t.cols] = (sum(keys) * scale).astype(BF16)
                own_out[places[n], 1, :, t.cols] = sum(values).astype(BF16)
                if apart or n == 0:
                    keys, values = zip(*t.prefix_sums[n])
                    sink(n, t.cols, sum(keys) * scale, sum(values))

    stages = (products, weigh, gradients, outgoing)
    for step in range(len(chunks) + len(stages) - 1):
        for late, stage in enumerate(stages):
            if 0 <= step - late < len(chunks):
                stage(chunks[step - late])


def token_rows(z, i):
    return pl.ds(pl.multiple_of(i * z.tokens, z.tokens), z.tokens)


def find_responses(z, me, turns, resp_prompt, order):
    for t, turn in enumerate(turns):
        prompt = me ^ turn
        found = t * z.slots
        for i in range(z.count):
            order[found] = i
            found = found + (resp_prompt[me * z.count + i] == prompt).astype(jnp.int32)


def prompt_total(z, me, prompt, resp_prompt, tails, far_rewards):
    sums = jnp.zeros((1, z.width), F32)
    for s in range(tails.shape[0]):
        tail = tails[s].astype(F32)
        sums += tail[0:1] + tail[1:2] + tail[2:3]
    lane = lax.broadcasted_iota(jnp.int32, sums.shape, 1)
    total = jnp.sum(jnp.where(lane == prompt, sums, 0.0))
    for i in range(z.count):
        total += jnp.where(resp_prompt[(me ^ FAR) * z.count + i] == prompt, far_rewards[i], 0.0)
    return total


def reward_factor(z, reward, total, length):
    return (reward - total / z.count) * (z.tokens / length.astype(F32))


def pack_kernel(z, prompt_hbm, rewards_hbm, resp_prompt_hbm, payload, rewards, resp_prompt, staged, sems):
    me = lax.axis_index("dp")
    small = [
        pltpu.make_async_copy(rewards_hbm, rewards, sems.at[0]),
        pltpu.make_async_copy(resp_prompt_hbm, resp_prompt, sems.at[1]),
    ]
    large = [
        pltpu.make_async_copy(
            prompt_hbm.at[n], staged.at[pl.ds(n * z.prefix_len, z.prefix_len)], sems.at[2 + n]
        )
        for n in range(2)
    ]
    for copy in small + large:
        copy.start()
    for copy in small:
        copy.wait()
    lane = lax.broadcasted_iota(jnp.int32, (1, z.width), 1)
    sums = jnp.zeros((1, z.width), F32)
    for i in range(z.count):
        sums += jnp.where(lane == resp_prompt[me * z.count + i], rewards[i], 0.0)
    high = sums.astype(BF16).astype(F32)
    middle = (sums - high).astype(BF16).astype(F32)
    low = sums - high - middle
    row = lax.broadcasted_iota(jnp.int32, (TAIL, z.width), 0)
    pieces = jnp.where(row == 0, high, jnp.where(row == 1, middle, jnp.where(row == 2, low, 0.0)))
    staged[2 * z.prefix_len :, :] = pieces.astype(BF16)
    for copy in large:
        copy.wait()
    last = pltpu.make_async_copy(staged, payload, sems.at[0])
    last.start()
    last.wait()


def tail_copies(z, payloads, tails, sems):
    return [
        pltpu.make_async_copy(payload.at[pl.ds(2 * z.prefix_len, TAIL)], tails.at[n], sems.at[n])
        for n, payload in enumerate(payloads)
    ]


def row_copies(here, there, at_here, at_there, sems):
    (q0, og0, kv0), (q1, og1, kv1) = here, there
    return (
        pltpu.make_async_copy(q0.at[at_here], q1.at[at_there], sems.at[0]),
        pltpu.make_async_copy(og0.at[at_here], og1.at[at_there], sems.at[1]),
        pltpu.make_async_copy(kv0.at[:, at_here], kv1.at[:, at_there], sems.at[2]),
    )


def result_copies(out, own, q_out, self_out, place, at, sems, back=False):
    pairs = [
        (out.at[place], q_out.at[at]),
        (own.at[place], self_out.at[:, at]),
    ]
    return [
        pltpu.make_async_copy(*(reversed(pair) if back else pair), sems.at[place, n])
        for n, pair in enumerate(pairs)
    ]


def group_kernel(z, turns, raw, n_tails, aliased, *refs):
    small_hbm, given = refs[:4], refs[4:7]
    tail_hbm, prompts = refs[7 : 7 + n_tails], refs[7 + n_tails : 7 + n_tails + len(turns)]
    refs = refs[7 + n_tails + len(turns) + aliased :]
    (q_out, self_out), grads_out = refs[:2], refs[2 : 2 + len(turns)]
    (resp_prompt, resp_len, rewards, far_rewards, order, lens, factors, q, og, kv, prefix, tails, acc, out, own, grads,
     sem_small, sem_tails, sem_prefix, sem_in, sem_out, sem_grads) = refs[2 + len(turns) :]
    me = lax.axis_index("dp")
    n_slots = len(turns) * z.slots

    small = [
        pltpu.make_async_copy(src, dst, sem_small.at[n])
        for n, (src, dst) in enumerate(zip(small_hbm, (resp_prompt, resp_len, rewards, far_rewards)))
    ]
    prefix_copies = [
        pltpu.make_async_copy(
            prompts[t].at[pl.ds(n * z.prefix_len, z.prefix_len)], prefix.at[t, n], sem_prefix.at[t, n]
        )
        for t in range(len(turns))
        for n in range(2)
    ]
    late = tail_copies(z, tail_hbm, tails, sem_tails)
    for copy in small + prefix_copies + late:
        copy.start()
    small[0].wait()
    find_responses(z, me, turns, resp_prompt, order)

    def copies_in(slot):
        return row_copies(
            given, (q, og, kv), token_rows(z, order[slot]), token_rows(z, slot), sem_in.at[slot]
        )

    def copies_out(slot):
        return result_copies(out, own, q_out, self_out, slot, token_rows(z, order[slot]), sem_out)

    for slot in range(n_slots):
        for copy in copies_in(slot):
            copy.start()
    for copy in small[1:] + late:
        copy.wait()
    for t, turn in enumerate(turns):
        total = None if raw else prompt_total(z, me, me ^ turn, resp_prompt, tails, far_rewards)
        for slot in range(t * z.slots, (t + 1) * z.slots):
            i = order[slot]
            lens[slot] = resp_len[i]
            factors[slot] = 1.0 if raw else reward_factor(z, rewards[i], total, resp_len[i])
    if not raw:
        acc[...] = jnp.zeros(acc.shape, F32)
    for copy in prefix_copies:
        copy.wait()

    def unit(u, _):
        at = [u * PAIR + n for n in range(PAIR)]
        t = u // (z.slots // PAIR)
        for slot in at:
            for copy in copies_in(slot):
                copy.wait()

        def sink(n, cols, key_grad, value_grad):
            if raw:
                grads[at[n], 0, :, cols] = key_grad.astype(BF16)
                grads[at[n], 1, :, cols] = value_grad.astype(BF16)
            else:
                acc[t, 0, :, cols] += key_grad
                acc[t, 1, :, cols] += value_grad

        attend_pair(
            z, [token_rows(z, n) for n in at], at, q, og, kv, prefix.at[t], [lens[n] for n in at],
            [factors[n] for n in at], out, own, sink, raw,
        )
        for slot in at:
            for copy in copies_out(slot):
                copy.start()
        return 0

    lax.fori_loop(0, n_slots // PAIR, unit, 0)
    if raw:
        last = [pltpu.make_async_copy(grads, grads_out[0], sem_grads.at[0])]
    else:
        grads[...] = acc[...].astype(BF16)
        last = [
            pltpu.make_async_copy(grads.at[t], grads_out[t], sem_grads.at[t]) for t in range(len(turns))
        ]
    for copy in last:
        copy.start()
    for slot in range(n_slots):
        for copy in copies_out(slot):
            copy.wait()
    for copy in last:
        copy.wait()


def finish_kernel(z, n_tails, n_come, *refs):
    small_hbm, tail_hbm = refs[:4], refs[4 : 4 + n_tails]
    per_resp_hbm, come_hbm = refs[4 + n_tails], refs[5 + n_tails : 5 + n_tails + n_come]
    q_out, self_out, grads_out = refs[7 + n_tails + n_come : 10 + n_tails + n_come]
    (resp_prompt, resp_len, rewards, far_rewards, order, tails, out, own, per_resp, come, grads,
     sem_small, sem_tails, sem_come, sem_in, sem_out) = refs[10 + n_tails + n_come :]
    me = lax.axis_index("dp")
    small = [
        pltpu.make_async_copy(src, dst, sem_small.at[n])
        for n, (src, dst) in enumerate(zip(small_hbm, (resp_prompt, resp_len, rewards, far_rewards)))
    ]
    late = tail_copies(z, tail_hbm, tails, sem_tails)
    late += [pltpu.make_async_copy(src, come.at[n], sem_come.at[n]) for n, src in enumerate(come_hbm)]
    late += [pltpu.make_async_copy(per_resp_hbm, per_resp, sem_come.at[n_come])]
    for copy in small + late:
        copy.start()
    small[0].wait()
    find_responses(z, me, (0,), resp_prompt, order)

    def moves(slot, back):
        sems = sem_in if back else sem_out
        return result_copies(out, own, q_out, self_out, slot, token_rows(z, order[slot]), sems, back)

    for slot in range(z.slots):
        for copy in moves(slot, True):
            copy.start()
    for copy in small[1:] + late:
        copy.wait()
    total = prompt_total(z, me, me, resp_prompt, tails, far_rewards)
    summed = come[0].astype(F32)
    for n in range(1, n_come):
        summed += come[n].astype(F32)
    factors = [reward_factor(z, rewards[order[n]], total, resp_len[order[n]]) for n in range(z.slots)]
    for slot in range(z.slots):
        summed += per_resp[slot].astype(F32) * factors[slot]
    grads[...] = summed
    last = pltpu.make_async_copy(grads, grads_out, sem_small.at[0])
    last.start()
    for slot in range(z.slots):
        for copy in moves(slot, True):
            copy.wait()
        out[slot] = (out[slot].astype(F32) * factors[slot]).astype(BF16)
        own[slot] = (own[slot].astype(F32) * factors[slot]).astype(BF16)
        for copy in moves(slot, False):
            copy.start()
    for slot in range(z.slots):
        for copy in moves(slot, False):
            copy.wait()
    last.wait()


def near_shards(z, prompt_kv, resp_q, resp_kv, out_grad, rewards, resp_prompt, resp_len):
    n_dp = z.n_dp
    assert z.slots % PAIR == 0
    shape = jax.ShapeDtypeStruct
    one = (2, z.prefix_len, z.width)
    params = pltpu.CompilerParams(vmem_limit_bytes=VMEM_BYTES)
    cost = pl.CostEstimate(flops=0, bytes_accessed=0, transcendentals=0)
    payload = pl.pallas_call(
        functools.partial(pack_kernel, z),
        out_shape=jax.ShapeDtypeStruct((2 * z.prefix_len + TAIL, z.width), BF16),
        in_specs=[ANYWHERE] * 3,
        out_specs=ANYWHERE,
        scratch_shapes=[
            pltpu.SMEM(rewards.shape, F32),
            pltpu.SMEM(resp_prompt.shape, jnp.int32),
            pltpu.VMEM((2 * z.prefix_len + TAIL, z.width), BF16),
            pltpu.SemaphoreType.DMA((4,)),
        ],
        compiler_params=pltpu.CompilerParams(vmem_limit_bytes=VMEM_BYTES),
        name="pack",
    )(prompt_kv, rewards, resp_prompt)

    assert n_dp == FAR + 1

    def swap(x, s):
        return lax.ppermute(x, "dp", [(i, i ^ s) for i in range(n_dp)])

    payloads = {0: payload, 2: swap(payload, 2), 1: swap(payload, 1)}
    tails = [payloads[s] for s in range(FAR)]
    small = (resp_prompt, resp_len, rewards)
    far_rewards = swap(rewards, FAR)
    smem = [pltpu.SMEM(x.shape, x.dtype) for x in (*small, rewards)]
    slots = z.slots

    def grads_of(turns, raw, written):
        n_slots, n_turns = len(turns) * slots, len(turns)
        used_tails = [] if raw else tails
        used_small = (*small, rewards if raw else far_rewards)
        prompts = [payloads[turn] for turn in turns]
        operands = [*used_small, resp_q, out_grad, resp_kv, *used_tails, *prompts, *written]
        grads_shapes = [(slots,) + one] if raw else [one] * n_turns
        return pl.pallas_call(
            functools.partial(group_kernel, z, turns, raw, len(used_tails), len(written)),
            out_shape=[shape(resp_q.shape, BF16), shape(resp_kv.shape, BF16)]
            + [shape(x, BF16) for x in grads_shapes],
            in_specs=[ANYWHERE] * len(operands),
            out_specs=[ANYWHERE] * (2 + len(grads_shapes)),
            input_output_aliases={len(operands) - 2: 0, len(operands) - 1: 1} if written else {},
            scratch_shapes=[
                *smem,
                pltpu.SMEM((n_slots + 1,), jnp.int32),
                pltpu.SMEM((n_slots,), jnp.int32),
                pltpu.SMEM((n_slots,), F32),
                pltpu.VMEM((n_slots * z.tokens, z.lanes), BF16),
                pltpu.VMEM((n_slots * z.tokens, z.lanes), BF16),
                pltpu.VMEM((2, n_slots * z.tokens, z.width), BF16),
                pltpu.VMEM((n_turns,) + one, BF16),
                pltpu.VMEM((FAR, TAIL, z.width), BF16),
                pltpu.VMEM((n_turns,) + one, F32),
                pltpu.VMEM((n_slots, z.tokens, z.lanes), BF16),
                pltpu.VMEM((n_slots, 2, z.tokens, z.width), BF16),
                pltpu.VMEM(grads_shapes[0] if raw else (n_turns,) + one, BF16),
                pltpu.SemaphoreType.DMA((len(smem),)),
                pltpu.SemaphoreType.DMA((FAR,)),
                pltpu.SemaphoreType.DMA((n_turns, 2)),
                pltpu.SemaphoreType.DMA((n_slots, 4)),
                pltpu.SemaphoreType.DMA((n_slots, 3)),
                pltpu.SemaphoreType.DMA((n_turns,)),
            ],
            compiler_params=params if raw else pltpu.CompilerParams(vmem_limit_bytes=GROUP_BYTES),
            cost_estimate=cost,
            name="raw_grads" if raw else "group_grads",
        )(*operands)

    *written, per_resp = grads_of((0,), True, ())
    onward, per_resp, far_rewards = lax.optimization_barrier((payloads[2], per_resp, far_rewards))
    payloads[FAR] = swap(onward, 1)
    *written, for_2, for_1 = grads_of((2, 1), False, written)
    come = [swap(for_2, 2)]
    *written, for_far = grads_of((FAR,), False, written)
    for_far, for_1 = lax.optimization_barrier((for_far, for_1))
    last = [swap(for_far, FAR), swap(for_1, 1)]
    operands = [*small, far_rewards, *tails, per_resp, *come, *written]
    q_out, self_out, own_grads = pl.pallas_call(
        functools.partial(finish_kernel, z, len(tails), len(come)),
        out_shape=[shape(resp_q.shape, BF16), shape(resp_kv.shape, BF16), shape(one, F32)],
        in_specs=[ANYWHERE] * len(operands),
        out_specs=[ANYWHERE] * 3,
        input_output_aliases={len(operands) - 2: 0, len(operands) - 1: 1},
        scratch_shapes=[
            *smem,
            pltpu.SMEM((slots + 1,), jnp.int32),
            pltpu.VMEM((FAR, TAIL, z.width), BF16),
            pltpu.VMEM((slots, z.tokens, z.lanes), BF16),
            pltpu.VMEM((slots, 2, z.tokens, z.width), BF16),
            pltpu.VMEM((slots,) + one, BF16),
            pltpu.VMEM((len(come),) + one, BF16),
            pltpu.VMEM(one, F32),
            pltpu.SemaphoreType.DMA((len(smem),)),
            pltpu.SemaphoreType.DMA((FAR,)),
            pltpu.SemaphoreType.DMA((len(come) + 1,)),
            pltpu.SemaphoreType.DMA((slots, 3)),
            pltpu.SemaphoreType.DMA((slots, 3)),
        ],
        compiler_params=pltpu.CompilerParams(vmem_limit_bytes=FINISH_BYTES),
        cost_estimate=cost,
        name="finish_own",
    )(*operands)
    prefix_out = (own_grads + sum(part.astype(F32) for part in last)).astype(BF16)
    return (q_out, self_out, prefix_out)


def far_kernel(z, *refs):
    (resp_prompt, resp_len, rewards, q_hbm, og_hbm, kv_hbm, prompts, q_out, self_out, prefix_outs,
     totals, lens, factors, q, og, kv, prefix, out, own, grads, sem_in, sem_prefix, sem_out) = refs
    me = lax.axis_index("dp")

    for p in range(z.n_dp):
        totals[p] = 0.0

    def copies_in(slot):
        rows = token_rows(z, slot)
        prompt = resp_prompt[me * z.count + slot]
        return (
            *row_copies((q_hbm, og_hbm, kv_hbm), (q, og, kv), rows, rows, sem_in.at[slot]),
            pltpu.make_async_copy(prompts.at[prompt], prefix.at[slot], sem_prefix.at[slot]),
        )

    def copies_out(slot):
        rows = token_rows(z, slot)
        return (
            *result_copies(out, own, q_out, self_out, slot, rows, sem_out),
            pltpu.make_async_copy(grads.at[slot], prefix_outs.at[slot], sem_out.at[slot, 3]),
        )

    def start(slot, _):
        for copy in copies_in(slot):
            copy.start()
        return 0

    lax.fori_loop(0, z.count, start, 0)

    def add(i, _):
        prompt = resp_prompt[i]
        totals[prompt] = totals[prompt] + rewards[i]
        return 0

    lax.fori_loop(0, z.n_dp * z.count, add, 0)

    def find_factor(slot, _):
        place = me * z.count + slot
        lens[slot] = resp_len[slot]
        factors[slot] = reward_factor(z, rewards[place], totals[resp_prompt[place]], resp_len[slot])
        return 0

    lax.fori_loop(0, z.count, find_factor, 0)

    def unit(slot, _):
        for copy in copies_in(slot):
            copy.wait()

        def sink(_, cols, key_grad, value_grad):
            grads[slot, 0, :, cols] = key_grad.astype(BF16)
            grads[slot, 1, :, cols] = value_grad.astype(BF16)

        attend_pair(
            z, [token_rows(z, slot)], [slot], q, og, kv, prefix.at[slot], [lens[slot]], [factors[slot]], out, own, sink, True
        )
        for copy in copies_out(slot):
            copy.start()
        return 0

    lax.fori_loop(0, z.count, unit, 0)

    def end(slot, _):
        for copy in copies_out(slot):
            copy.wait()
        return 0

    lax.fori_loop(0, z.count, end, 0)


def far_shards(z, prompt_kv, resp_q, resp_kv, out_grad, rewards, resp_prompt, resp_len):
    assert z.slots == 1
    count, n_dp = z.count, z.n_dp
    one = (2, z.prefix_len, z.width)
    smem = pl.BlockSpec(memory_space=pltpu.SMEM)
    q_out, self_out, per_resp = pl.pallas_call(
        functools.partial(far_kernel, z),
        out_shape=[
            jax.ShapeDtypeStruct(resp_q.shape, BF16),
            jax.ShapeDtypeStruct(resp_kv.shape, BF16),
            jax.ShapeDtypeStruct((count,) + one, BF16),
        ],
        in_specs=[smem] * 3 + [ANYWHERE] * 4,
        out_specs=[ANYWHERE] * 3,
        scratch_shapes=[
            pltpu.SMEM((n_dp,), F32),
            pltpu.SMEM((count,), jnp.int32),
            pltpu.SMEM((count,), F32),
            pltpu.VMEM(resp_q.shape, BF16),
            pltpu.VMEM(resp_q.shape, BF16),
            pltpu.VMEM(resp_kv.shape, BF16),
            pltpu.VMEM((count,) + one, BF16),
            pltpu.VMEM((count, z.tokens, z.lanes), BF16),
            pltpu.VMEM((count, 2, z.tokens, z.width), BF16),
            pltpu.VMEM((count,) + one, BF16),
            pltpu.SemaphoreType.DMA((count, 4)),
            pltpu.SemaphoreType.DMA((count,)),
            pltpu.SemaphoreType.DMA((count, 4)),
        ],
        compiler_params=pltpu.CompilerParams(vmem_limit_bytes=VMEM_BYTES),
        name="far_grads",
    )(
        resp_prompt,
        resp_len,
        lax.all_gather(rewards, "dp", axis=0, tiled=True),
        resp_q,
        out_grad,
        resp_kv,
        lax.all_gather(prompt_kv, "dp", axis=0),
    )
    my_prompts = lax.dynamic_slice_in_dim(resp_prompt, lax.axis_index("dp") * count, count)
    route = (jnp.arange(n_dp, dtype=jnp.int32)[:, None] == my_prompts[None, :]).astype(BF16)
    outgoing = jnp.dot(route, per_resp.reshape(count, -1), preferred_element_type=F32).astype(BF16)
    outgoing = outgoing.reshape((n_dp,) + one)
    incoming = lax.all_to_all(outgoing, "dp", split_axis=0, concat_axis=0, tiled=True)
    prefix_out = jnp.sum(incoming, axis=0, dtype=F32).astype(BF16)
    return (q_out, self_out, prefix_out)


def shards(prompt_kv, resp_q, resp_kv, out_grad, rewards, resp_prompt, resp_len):
    n_dp = lax.axis_size("dp")
    count = rewards.shape[0]
    prefix_len, width = prompt_kv.shape[1:]
    slots = (count + n_dp - 1) // n_dp
    z = Sizes(
        n_dp, count, slots, width // HD, resp_q.shape[1] // width, resp_q.shape[0] // count, prefix_len
    )
    part = near_shards if count // slots == n_dp else far_shards
    return part(z, prompt_kv, resp_q, resp_kv, out_grad, rewards, resp_prompt, resp_len)


def solution(mesh):
    in_specs = (
        P(None, ("groups", "dp"), "tensor"),
        P(("groups", "dp"), "tensor"),
        P(None, ("groups", "dp"), "tensor"),
        P(("groups", "dp"), "tensor"),
        P(("groups", "dp")),
        P("groups"),
        P(("groups", "dp")),
    )
    out_specs = (
        P(("groups", "dp"), "tensor"),
        P(None, ("groups", "dp"), "tensor"),
        P(None, ("groups", "dp"), "tensor"),
    )
    return jax.shard_map(shards, mesh=mesh, in_specs=in_specs, out_specs=out_specs, check_vma=False)
```

```python
import functools
import math
from typing import NamedTuple

import jax
import jax.numpy as jnp
from jax import lax
from jax.experimental import pallas as pl
from jax.experimental.pallas import tpu as pltpu
from jax.sharding import PartitionSpec as P

HD = 128
NEG = -1e30
TAIL = 16
F32 = jnp.float32
BF16 = jnp.bfloat16
PAIR = 2
FAR = 3
VMEM_BYTES = 63 * 1024 * 1024
GROUP_BYTES = 53 * 1024 * 1024
FINISH_BYTES = 24 * 1024 * 1024
ANYWHERE = pl.BlockSpec(memory_space=pl.ANY)


class Sizes(NamedTuple):
    n_dp: int
    count: int
    slots: int
    kv_heads: int
    group_size: int
    tokens: int
    prefix_len: int

    @property
    def width(self):
        return self.kv_heads * HD

    @property
    def lanes(self):
        return self.kv_heads * self.group_size * HD


def dot(a, b, dims):
    return lax.dot_general(a, b, (dims, ((), ())), preferred_element_type=F32)


NN = ((1,), (0,))
NT = ((1,), (1,))


class Bag:
    pass


class Unit(NamedTuple):
    at: list
    places: list
    k: object
    lens: list
    factors: list


def attend(z, units, q, og, kv, prefix, out, own_out, sink, apart):
    tokens, prefix_len, group_size = z.tokens, z.prefix_len, z.group_size
    scale = 1.0 / math.sqrt(HD)
    log_scale = scale * math.log2(math.e)
    whole = group_size - group_size % 2
    most = max(whole, 2) * tokens
    assert tokens & (tokens - 1) == 0
    token = lax.broadcasted_iota(jnp.int32, (1, most), 1) & (tokens - 1)
    key = lax.broadcasted_iota(jnp.int32, (tokens, most), 0)
    causal = key <= (lax.broadcasted_iota(jnp.int32, (tokens, most), 1) & (tokens - 1))
    left = lax.broadcasted_iota(jnp.int32, (1, 2 * tokens), 1) < tokens

    def columns(index):
        if isinstance(index, int):
            return slice(index * HD, (index + 1) * HD)
        return pl.ds(pl.multiple_of(index * HD, HD), HD)

    def head(k, h):
        return columns(k * group_size + h)

    def rows(ref, c):
        return jnp.concatenate([ref[c.t.at[n], head(c.t.k, h)] for n, h in c.blocks], axis=0)

    def halves(part):
        none = jnp.zeros_like(part)
        return [jnp.where(left, part, none), jnp.where(left, none, part)]

    def over_keys(combine, *parts):
        reduce = jnp.max if combine is jnp.maximum else jnp.sum
        eights = [reduce(part.reshape(-1, 8, part.shape[1]), axis=0) for part in parts]
        return reduce(functools.reduce(combine, eights), axis=0, keepdims=True)

    def own_half(both):
        return jnp.where(left, both[:tokens], both[tokens:])

    def rounded(*parts):
        return jnp.concatenate([part.astype(BF16) for part in parts], axis=0)

    chunks = []
    for unit in units:
        t = Bag()
        t.at, t.places, t.k, t.lens, t.factors = unit
        t.single = len(t.at) == 1
        t.members = range(len(t.at))
        sides = (0, 0) if t.single else (0, 1)
        t.cols = columns(t.k)
        t.key_p, t.value_p = prefix[0, :, t.cols], prefix[1, :, t.cols]
        t.keys = [kv[0, t.at[n], t.cols] for n in sides]
        t.values = [kv[1, t.at[n], t.cols] for n in sides]
        t.key_pair = jnp.concatenate(t.keys, axis=0)
        t.value_pair = jnp.concatenate(t.values, axis=0)
        t.key_t = jnp.concatenate([t.key_p.T, t.key_pair.T], axis=1)
        t.prefix_sums = {n: [] for n in t.members}
        t.self_sums = {n: [] for n in t.members}
        mine = []
        for n in t.members:
            c = Bag()
            c.t, c.side, c.blocks = t, n, [(n, h) for h in range(whole)]
            mine.append(c)
        if group_size % 2:
            c = Bag()
            c.t, c.side, c.blocks = t, None, [(n, group_size - 1) for n in sides]
            mine.append(c)
        t.left_over = len(mine)
        chunks += mine

    def products(c):
        t = c.t
        c.q_rows, c.g_rows = rows(q, c), rows(og, c)
        if c.side is None:
            key_s, value_s = t.key_pair, t.value_pair
        else:
            key_s, value_s = t.keys[c.side], t.values[c.side]
        c.scores = dot(jnp.concatenate([t.key_p, key_s], axis=0), c.q_rows, NT)
        c.gw = dot(jnp.concatenate([t.value_p, value_s], axis=0), c.g_rows, NT)

    def weigh(c):
        scores_p, scores_s = c.scores[:prefix_len], c.scores[prefix_len:]
        c.gw_p, c.gw_s = c.gw[:prefix_len], c.gw[prefix_len:]
        if c.side is None:
            scores_s, c.gw_s = own_half(scores_s), own_half(c.gw_s)
        scores_s = jnp.where(causal[:, : scores_s.shape[1]], scores_s, NEG)
        top = over_keys(jnp.maximum, scores_p, scores_s)
        c.e_p = jnp.exp2((scores_p - top) * log_scale)
        c.e_s = jnp.exp2((scores_s - top) * log_scale)
        total = over_keys(jnp.add, c.e_p, c.e_s)
        weighted = over_keys(jnp.add, c.e_p * c.gw_p, c.e_s * c.gw_s)
        if c.side is None:
            length = jnp.where(left, c.t.lens[0], 0 if c.t.single else c.t.lens[1])
            gain = jnp.where(left, c.t.factors[0], c.t.factors[-1])
        else:
            length, gain = c.t.lens[c.side], c.t.factors[c.side]
        inverse = 1.0 / total
        c.delta = weighted * inverse
        c.gain = inverse * jnp.where(token[:, : total.shape[1]] < length, gain, 0.0)

    def gradients(c):
        w_p, w_s = c.e_p * c.gain, c.e_s * c.gain
        d_p, d_s = w_p * (c.gw_p - c.delta), w_s * (c.gw_s - c.delta)
        if c.side is None:
            d_s, w_s = halves(d_s), halves(w_s)
            c.d_wide = rounded(d_p, *d_s)
            c.d_all = rounded(*halves(d_p), *d_s) if apart else c.d_wide
            c.w_all = rounded(*(halves(w_p) if apart else [w_p]), *w_s)
        else:
            empty = jnp.zeros_like(d_s)
            c.d_wide = rounded(*([d_p, empty, d_s] if c.side else [d_p, d_s, empty]))
            c.d_all = rounded(d_p, d_s)
            c.w_all = rounded(w_p, w_s)

    def outgoing(c):
        t = c.t
        q_grad = (dot(t.key_t, c.d_wide, NN) * scale).astype(BF16).T
        kg = dot(c.d_all, c.q_rows, NN)
        vg = dot(c.w_all, c.g_rows, NN)
        targets = t.members if c.side is None else [c.side]
        for place, (n, h) in enumerate(c.blocks):
            if c.side is not None or place < len(targets):
                out[t.places[n], :, head(t.k, h)] = q_grad[place * tokens : (place + 1) * tokens]
        many = 2 if c.side is None and apart else 1
        for place, n in enumerate(targets):
            if place < many:
                rows_p = slice(place * prefix_len, (place + 1) * prefix_len)
                t.prefix_sums[n if apart else 0].append((kg[rows_p], vg[rows_p]))
            start = many * prefix_len + place * tokens
            rows_s = slice(start, start + tokens)
            t.self_sums[n].append((kg[rows_s], vg[rows_s]))
        t.left_over -= 1
        if t.left_over == 0:
            for n in t.members:
                keys, values = zip(*t.self_sums[n])
                own_out[t.places[n], 0, :, t.cols] = (sum(keys) * scale).astype(BF16)
                own_out[t.places[n], 1, :, t.cols] = sum(values).astype(BF16)
                if apart or n == 0:
                    keys, values = zip(*t.prefix_sums[n])
                    sink(t.places[n], t.cols, sum(keys) * scale, sum(values))

    stages = (products, weigh, gradients, outgoing)
    for step in range(len(chunks) + len(stages) - 1):
        for late, stage in enumerate(stages):
            if 0 <= step - late < len(chunks):
                stage(chunks[step - late])


def token_rows(z, i):
    return pl.ds(pl.multiple_of(i * z.tokens, z.tokens), z.tokens)


def find_responses(z, me, turns, resp_prompt, order):
    for t, turn in enumerate(turns):
        prompt = me ^ turn
        found = t * z.slots
        for i in range(z.count):
            order[found] = i
            found = found + (resp_prompt[me * z.count + i] == prompt).astype(jnp.int32)


def prompt_total(z, me, prompt, resp_prompt, tails, far_rewards):
    sums = jnp.zeros((1, z.width), F32)
    for s in range(tails.shape[0]):
        tail = tails[s].astype(F32)
        sums += tail[0:1] + tail[1:2] + tail[2:3]
    lane = lax.broadcasted_iota(jnp.int32, sums.shape, 1)
    total = jnp.sum(jnp.where(lane == prompt, sums, 0.0))
    for i in range(z.count):
        total += jnp.where(resp_prompt[(me ^ FAR) * z.count + i] == prompt, far_rewards[i], 0.0)
    return total


def reward_factor(z, reward, total, length):
    return (reward - total / z.count) * (z.tokens / length.astype(F32))


def pack_kernel(z, prompt_hbm, rewards_hbm, resp_prompt_hbm, payload, rewards, resp_prompt, staged, sems):
    me = lax.axis_index("dp")
    small = [
        pltpu.make_async_copy(rewards_hbm, rewards, sems.at[0]),
        pltpu.make_async_copy(resp_prompt_hbm, resp_prompt, sems.at[1]),
    ]
    large = [
        pltpu.make_async_copy(
            prompt_hbm.at[n], staged.at[pl.ds(n * z.prefix_len, z.prefix_len)], sems.at[2 + n]
        )
        for n in range(2)
    ]
    for copy in small + large:
        copy.start()
    for copy in small:
        copy.wait()
    lane = lax.broadcasted_iota(jnp.int32, (1, z.width), 1)
    sums = jnp.zeros((1, z.width), F32)
    for i in range(z.count):
        sums += jnp.where(lane == resp_prompt[me * z.count + i], rewards[i], 0.0)
    high = sums.astype(BF16).astype(F32)
    middle = (sums - high).astype(BF16).astype(F32)
    low = sums - high - middle
    row = lax.broadcasted_iota(jnp.int32, (TAIL, z.width), 0)
    pieces = jnp.where(row == 0, high, jnp.where(row == 1, middle, jnp.where(row == 2, low, 0.0)))
    staged[2 * z.prefix_len :, :] = pieces.astype(BF16)
    for copy in large:
        copy.wait()
    last = pltpu.make_async_copy(staged, payload, sems.at[0])
    last.start()
    last.wait()


def tail_copies(z, payloads, tails, sems):
    return [
        pltpu.make_async_copy(payload.at[pl.ds(2 * z.prefix_len, TAIL)], tails.at[n], sems.at[n])
        for n, payload in enumerate(payloads)
    ]


def row_copies(here, there, at_here, at_there, sems):
    (q0, og0, kv0), (q1, og1, kv1) = here, there
    return (
        pltpu.make_async_copy(q0.at[at_here], q1.at[at_there], sems.at[0]),
        pltpu.make_async_copy(og0.at[at_here], og1.at[at_there], sems.at[1]),
        pltpu.make_async_copy(kv0.at[:, at_here], kv1.at[:, at_there], sems.at[2]),
    )


def result_copies(out, own, q_out, self_out, place, at, sems, back=False):
    pairs = [
        (out.at[place], q_out.at[at]),
        (own.at[place], self_out.at[:, at]),
    ]
    return [
        pltpu.make_async_copy(*(reversed(pair) if back else pair), sems.at[place, n])
        for n, pair in enumerate(pairs)
    ]


def group_kernel(z, turns, raw, body, n_tails, aliased, *refs):
    small_hbm, given = refs[:4], refs[4:7]
    tail_hbm, prompts = refs[7 : 7 + n_tails], refs[7 + n_tails : 7 + n_tails + len(turns)]
    refs = refs[7 + n_tails + len(turns) + aliased :]
    (q_out, self_out), grads_out = refs[:2], refs[2 : 2 + len(turns)]
    (resp_prompt, resp_len, rewards, far_rewards, order, lens, factors, q, og, kv, prefix, tails, acc, out, own, grads,
     sem_small, sem_tails, sem_prefix, sem_in, sem_out, sem_grads) = refs[2 + len(turns) :]
    me = lax.axis_index("dp")
    n_slots = len(turns) * z.slots

    small = [
        pltpu.make_async_copy(src, dst, sem_small.at[n])
        for n, (src, dst) in enumerate(zip(small_hbm, (resp_prompt, resp_len, rewards, far_rewards)))
    ]
    prefix_copies = [
        pltpu.make_async_copy(
            prompts[t].at[pl.ds(n * z.prefix_len, z.prefix_len)], prefix.at[t, n], sem_prefix.at[t, n]
        )
        for t in range(len(turns))
        for n in range(2)
    ]
    late = tail_copies(z, tail_hbm, tails, sem_tails)
    for copy in small + prefix_copies + late:
        copy.start()
    small[0].wait()
    find_responses(z, me, turns, resp_prompt, order)

    def copies_in(slot):
        return row_copies(
            given, (q, og, kv), token_rows(z, order[slot]), token_rows(z, slot), sem_in.at[slot]
        )

    def copies_out(slot):
        return result_copies(out, own, q_out, self_out, slot, token_rows(z, order[slot]), sem_out)

    for slot in range(n_slots):
        for copy in copies_in(slot):
            copy.start()
    for copy in small[1:] + late:
        copy.wait()
    for t, turn in enumerate(turns):
        total = None if raw else prompt_total(z, me, me ^ turn, resp_prompt, tails, far_rewards)
        for slot in range(t * z.slots, (t + 1) * z.slots):
            i = order[slot]
            lens[slot] = resp_len[i]
            factors[slot] = 1.0 if raw else reward_factor(z, rewards[i], total, resp_len[i])
    if not raw:
        acc[...] = jnp.zeros(acc.shape, F32)
    for copy in prefix_copies:
        copy.wait()

    pairs_per_turn = z.slots // PAIR
    pairs_in_body, heads_in_body = body
    head_steps = z.kv_heads // heads_in_body
    pair_steps = pairs_per_turn // pairs_in_body

    def step(u, _):
        k_step = lax.rem(u, head_steps) if head_steps > 1 else 0
        pair_step = u // head_steps
        t = pair_step // pair_steps
        first = pair_step * pairs_in_body * PAIR
        mine = range(pairs_in_body * PAIR)

        def moves(starting):
            for n in mine:
                for copy in copies_out(first + n) if starting else copies_in(first + n):
                    copy.start() if starting else copy.wait()

        if head_steps > 1:
            pl.when(k_step == 0)(lambda: moves(False))
        else:
            moves(False)

        def sink(place, cols, key_grad, value_grad):
            if raw:
                grads[place, 0, :, cols] = key_grad.astype(BF16)
                grads[place, 1, :, cols] = value_grad.astype(BF16)
            else:
                acc[t, 0, :, cols] += key_grad
                acc[t, 1, :, cols] += value_grad

        units = []
        for pair in range(pairs_in_body):
            places = [first + pair * PAIR + n for n in range(PAIR)]
            for k in range(heads_in_body):
                units.append(
                    Unit(
                        [token_rows(z, n) for n in places],
                        places,
                        k_step * heads_in_body + k if head_steps > 1 else k,
                        [lens[n] for n in places],
                        [factors[n] for n in places],
                    )
                )
        attend(z, units, q, og, kv, prefix.at[t], out, own, sink, raw)
        if head_steps > 1:
            pl.when(k_step == head_steps - 1)(lambda: moves(True))
        else:
            moves(True)
        return 0

    lax.fori_loop(0, len(turns) * pair_steps * head_steps, step, 0)
    if raw:
        last = [pltpu.make_async_copy(grads, grads_out[0], sem_grads.at[0])]
    else:
        grads[...] = acc[...].astype(BF16)
        last = [
            pltpu.make_async_copy(grads.at[t], grads_out[t], sem_grads.at[t]) for t in range(len(turns))
        ]
    for copy in last:
        copy.start()
    for slot in range(n_slots):
        for copy in copies_out(slot):
            copy.wait()
    for copy in last:
        copy.wait()


def finish_kernel(z, n_tails, n_come, *refs):
    small_hbm, tail_hbm = refs[:4], refs[4 : 4 + n_tails]
    per_resp_hbm, come_hbm = refs[4 + n_tails], refs[5 + n_tails : 5 + n_tails + n_come]
    q_out, self_out, grads_out = refs[7 + n_tails + n_come : 10 + n_tails + n_come]
    (resp_prompt, resp_len, rewards, far_rewards, order, tails, out, own, per_resp, come, grads,
     sem_small, sem_tails, sem_come, sem_in, sem_out) = refs[10 + n_tails + n_come :]
    me = lax.axis_index("dp")
    small = [
        pltpu.make_async_copy(src, dst, sem_small.at[n])
        for n, (src, dst) in enumerate(zip(small_hbm, (resp_prompt, resp_len, rewards, far_rewards)))
    ]
    late = tail_copies(z, tail_hbm, tails, sem_tails)
    late += [pltpu.make_async_copy(src, come.at[n], sem_come.at[n]) for n, src in enumerate(come_hbm)]
    late += [pltpu.make_async_copy(per_resp_hbm, per_resp, sem_come.at[n_come])]
    for copy in small + late:
        copy.start()
    small[0].wait()
    find_responses(z, me, (0,), resp_prompt, order)

    def moves(slot, back):
        sems = sem_in if back else sem_out
        return result_copies(out, own, q_out, self_out, slot, token_rows(z, order[slot]), sems, back)

    for slot in range(z.slots):
        for copy in moves(slot, True):
            copy.start()
    for copy in small[1:] + late:
        copy.wait()
    total = prompt_total(z, me, me, resp_prompt, tails, far_rewards)
    summed = come[0].astype(F32)
    for n in range(1, n_come):
        summed += come[n].astype(F32)
    factors = [reward_factor(z, rewards[order[n]], total, resp_len[order[n]]) for n in range(z.slots)]
    for slot in range(z.slots):
        summed += per_resp[slot].astype(F32) * factors[slot]
    grads[...] = summed
    last = pltpu.make_async_copy(grads, grads_out, sem_small.at[0])
    last.start()
    for slot in range(z.slots):
        for copy in moves(slot, True):
            copy.wait()
        out[slot] = (out[slot].astype(F32) * factors[slot]).astype(BF16)
        own[slot] = (own[slot].astype(F32) * factors[slot]).astype(BF16)
        for copy in moves(slot, False):
            copy.start()
    for slot in range(z.slots):
        for copy in moves(slot, False):
            copy.wait()
    last.wait()


def near_shards(z, prompt_kv, resp_q, resp_kv, out_grad, rewards, resp_prompt, resp_len):
    n_dp = z.n_dp
    assert z.slots % PAIR == 0
    shape = jax.ShapeDtypeStruct
    one = (2, z.prefix_len, z.width)
    params = pltpu.CompilerParams(vmem_limit_bytes=VMEM_BYTES)
    cost = pl.CostEstimate(flops=0, bytes_accessed=0, transcendentals=0)
    payload = pl.pallas_call(
        functools.partial(pack_kernel, z),
        out_shape=jax.ShapeDtypeStruct((2 * z.prefix_len + TAIL, z.width), BF16),
        in_specs=[ANYWHERE] * 3,
        out_specs=ANYWHERE,
        scratch_shapes=[
            pltpu.SMEM(rewards.shape, F32),
            pltpu.SMEM(resp_prompt.shape, jnp.int32),
            pltpu.VMEM((2 * z.prefix_len + TAIL, z.width), BF16),
            pltpu.SemaphoreType.DMA((4,)),
        ],
        compiler_params=pltpu.CompilerParams(vmem_limit_bytes=VMEM_BYTES),
        name="pack",
    )(prompt_kv, rewards, resp_prompt)

    assert n_dp == FAR + 1

    def swap(x, s):
        return lax.ppermute(x, "dp", [(i, i ^ s) for i in range(n_dp)])

    payloads = {0: payload, 2: swap(payload, 2), 1: swap(payload, 1)}
    tails = [payloads[s] for s in range(FAR)]
    small = (resp_prompt, resp_len, rewards)
    far_rewards = swap(rewards, FAR)
    smem = [pltpu.SMEM(x.shape, x.dtype) for x in (*small, rewards)]
    slots = z.slots

    def grads_of(turns, raw, written, body):
        n_slots, n_turns = len(turns) * slots, len(turns)
        used_tails = [] if raw else tails
        used_small = (*small, rewards if raw else far_rewards)
        prompts = [payloads[turn] for turn in turns]
        operands = [*used_small, resp_q, out_grad, resp_kv, *used_tails, *prompts, *written]
        grads_shapes = [(slots,) + one] if raw else [one] * n_turns
        return pl.pallas_call(
            functools.partial(group_kernel, z, turns, raw, body, len(used_tails), len(written)),
            out_shape=[shape(resp_q.shape, BF16), shape(resp_kv.shape, BF16)]
            + [shape(x, BF16) for x in grads_shapes],
            in_specs=[ANYWHERE] * len(operands),
            out_specs=[ANYWHERE] * (2 + len(grads_shapes)),
            input_output_aliases={len(operands) - 2: 0, len(operands) - 1: 1} if written else {},
            scratch_shapes=[
                *smem,
                pltpu.SMEM((n_slots + 1,), jnp.int32),
                pltpu.SMEM((n_slots,), jnp.int32),
                pltpu.SMEM((n_slots,), F32),
                pltpu.VMEM((n_slots * z.tokens, z.lanes), BF16),
                pltpu.VMEM((n_slots * z.tokens, z.lanes), BF16),
                pltpu.VMEM((2, n_slots * z.tokens, z.width), BF16),
                pltpu.VMEM((n_turns,) + one, BF16),
                pltpu.VMEM((FAR, TAIL, z.width), BF16),
                pltpu.VMEM((n_turns,) + one, F32),
                pltpu.VMEM((n_slots, z.tokens, z.lanes), BF16),
                pltpu.VMEM((n_slots, 2, z.tokens, z.width), BF16),
                pltpu.VMEM(grads_shapes[0] if raw else (n_turns,) + one, BF16),
                pltpu.SemaphoreType.DMA((len(smem),)),
                pltpu.SemaphoreType.DMA((FAR,)),
                pltpu.SemaphoreType.DMA((n_turns, 2)),
                pltpu.SemaphoreType.DMA((n_slots, 4)),
                pltpu.SemaphoreType.DMA((n_slots, 3)),
                pltpu.SemaphoreType.DMA((n_turns,)),
            ],
            compiler_params=params if raw else pltpu.CompilerParams(vmem_limit_bytes=GROUP_BYTES),
            cost_estimate=cost,
            name="raw_grads" if raw else "group_grads",
        )(*operands)

    *written, per_resp = grads_of((0,), True, (), (1, z.kv_heads))
    onward, per_resp, far_rewards = lax.optimization_barrier((payloads[2], per_resp, far_rewards))
    payloads[FAR] = swap(onward, 1)
    *written, for_2, for_1 = grads_of((2, 1), False, written, (slots // PAIR, z.kv_heads))
    come = [swap(for_2, 2)]
    *written, for_far = grads_of((FAR,), False, written, (1, 1))
    for_far, for_1 = lax.optimization_barrier((for_far, for_1))
    last = [swap(for_far, FAR), swap(for_1, 1)]
    operands = [*small, far_rewards, *tails, per_resp, *come, *written]
    q_out, self_out, own_grads = pl.pallas_call(
        functools.partial(finish_kernel, z, len(tails), len(come)),
        out_shape=[shape(resp_q.shape, BF16), shape(resp_kv.shape, BF16), shape(one, F32)],
        in_specs=[ANYWHERE] * len(operands),
        out_specs=[ANYWHERE] * 3,
        input_output_aliases={len(operands) - 2: 0, len(operands) - 1: 1},
        scratch_shapes=[
            *smem,
            pltpu.SMEM((slots + 1,), jnp.int32),
            pltpu.VMEM((FAR, TAIL, z.width), BF16),
            pltpu.VMEM((slots, z.tokens, z.lanes), BF16),
            pltpu.VMEM((slots, 2, z.tokens, z.width), BF16),
            pltpu.VMEM((slots,) + one, BF16),
            pltpu.VMEM((len(come),) + one, BF16),
            pltpu.VMEM(one, F32),
            pltpu.SemaphoreType.DMA((len(smem),)),
            pltpu.SemaphoreType.DMA((FAR,)),
            pltpu.SemaphoreType.DMA((len(come) + 1,)),
            pltpu.SemaphoreType.DMA((slots, 3)),
            pltpu.SemaphoreType.DMA((slots, 3)),
        ],
        compiler_params=pltpu.CompilerParams(vmem_limit_bytes=FINISH_BYTES),
        cost_estimate=cost,
        name="finish_own",
    )(*operands)
    prefix_out = (own_grads + sum(part.astype(F32) for part in last)).astype(BF16)
    return (q_out, self_out, prefix_out)


def far_kernel(z, *refs):
    (resp_prompt, resp_len, rewards, q_hbm, og_hbm, kv_hbm, prompts, q_out, self_out, prefix_outs,
     totals, lens, factors, q, og, kv, prefix, out, own, grads, sem_in, sem_prefix, sem_out) = refs
    me = lax.axis_index("dp")

    for p in range(z.n_dp):
        totals[p] = 0.0

    def copies_in(slot):
        rows = token_rows(z, slot)
        prompt = resp_prompt[me * z.count + slot]
        return (
            *row_copies((q_hbm, og_hbm, kv_hbm), (q, og, kv), rows, rows, sem_in.at[slot]),
            pltpu.make_async_copy(prompts.at[prompt], prefix.at[slot], sem_prefix.at[slot]),
        )

    def copies_out(slot):
        rows = token_rows(z, slot)
        return (
            *result_copies(out, own, q_out, self_out, slot, rows, sem_out),
            pltpu.make_async_copy(grads.at[slot], prefix_outs.at[slot], sem_out.at[slot, 3]),
        )

    def start(slot, _):
        for copy in copies_in(slot):
            copy.start()
        return 0

    lax.fori_loop(0, z.count, start, 0)

    def add(i, _):
        prompt = resp_prompt[i]
        totals[prompt] = totals[prompt] + rewards[i]
        return 0

    lax.fori_loop(0, z.n_dp * z.count, add, 0)

    def find_factor(slot, _):
        place = me * z.count + slot
        lens[slot] = resp_len[slot]
        factors[slot] = reward_factor(z, rewards[place], totals[resp_prompt[place]], resp_len[slot])
        return 0

    lax.fori_loop(0, z.count, find_factor, 0)

    def unit(slot, _):
        for copy in copies_in(slot):
            copy.wait()

        def sink(_, cols, key_grad, value_grad):
            grads[slot, 0, :, cols] = key_grad.astype(BF16)
            grads[slot, 1, :, cols] = value_grad.astype(BF16)

        units = [
            Unit([token_rows(z, slot)], [slot], k, [lens[slot]], [factors[slot]]) for k in range(z.kv_heads)
        ]
        attend(z, units, q, og, kv, prefix.at[slot], out, own, sink, True)
        for copy in copies_out(slot):
            copy.start()
        return 0

    lax.fori_loop(0, z.count, unit, 0)

    def end(slot, _):
        for copy in copies_out(slot):
            copy.wait()
        return 0

    lax.fori_loop(0, z.count, end, 0)


def far_shards(z, prompt_kv, resp_q, resp_kv, out_grad, rewards, resp_prompt, resp_len):
    assert z.slots == 1
    count, n_dp = z.count, z.n_dp
    one = (2, z.prefix_len, z.width)
    smem = pl.BlockSpec(memory_space=pltpu.SMEM)
    q_out, self_out, per_resp = pl.pallas_call(
        functools.partial(far_kernel, z),
        out_shape=[
            jax.ShapeDtypeStruct(resp_q.shape, BF16),
            jax.ShapeDtypeStruct(resp_kv.shape, BF16),
            jax.ShapeDtypeStruct((count,) + one, BF16),
        ],
        in_specs=[smem] * 3 + [ANYWHERE] * 4,
        out_specs=[ANYWHERE] * 3,
        scratch_shapes=[
            pltpu.SMEM((n_dp,), F32),
            pltpu.SMEM((count,), jnp.int32),
            pltpu.SMEM((count,), F32),
            pltpu.VMEM(resp_q.shape, BF16),
            pltpu.VMEM(resp_q.shape, BF16),
            pltpu.VMEM(resp_kv.shape, BF16),
            pltpu.VMEM((count,) + one, BF16),
            pltpu.VMEM((count, z.tokens, z.lanes), BF16),
            pltpu.VMEM((count, 2, z.tokens, z.width), BF16),
            pltpu.VMEM((count,) + one, BF16),
            pltpu.SemaphoreType.DMA((count, 4)),
            pltpu.SemaphoreType.DMA((count,)),
            pltpu.SemaphoreType.DMA((count, 4)),
        ],
        compiler_params=pltpu.CompilerParams(vmem_limit_bytes=VMEM_BYTES),
        name="far_grads",
    )(
        resp_prompt,
        resp_len,
        lax.all_gather(rewards, "dp", axis=0, tiled=True),
        resp_q,
        out_grad,
        resp_kv,
        lax.all_gather(prompt_kv, "dp", axis=0),
    )
    my_prompts = lax.dynamic_slice_in_dim(resp_prompt, lax.axis_index("dp") * count, count)
    route = (jnp.arange(n_dp, dtype=jnp.int32)[:, None] == my_prompts[None, :]).astype(BF16)
    outgoing = jnp.dot(route, per_resp.reshape(count, -1), preferred_element_type=F32).astype(BF16)
    outgoing = outgoing.reshape((n_dp,) + one)
    incoming = lax.all_to_all(outgoing, "dp", split_axis=0, concat_axis=0, tiled=True)
    prefix_out = jnp.sum(incoming, axis=0, dtype=F32).astype(BF16)
    return (q_out, self_out, prefix_out)


def shards(prompt_kv, resp_q, resp_kv, out_grad, rewards, resp_prompt, resp_len):
    n_dp = lax.axis_size("dp")
    count = rewards.shape[0]
    prefix_len, width = prompt_kv.shape[1:]
    slots = (count + n_dp - 1) // n_dp
    z = Sizes(
        n_dp, count, slots, width // HD, resp_q.shape[1] // width, resp_q.shape[0] // count, prefix_len
    )
    part = near_shards if count // slots == n_dp else far_shards
    return part(z, prompt_kv, resp_q, resp_kv, out_grad, rewards, resp_prompt, resp_len)


def solution(mesh):
    in_specs = (
        P(None, ("groups", "dp"), "tensor"),
        P(("groups", "dp"), "tensor"),
        P(None, ("groups", "dp"), "tensor"),
        P(("groups", "dp"), "tensor"),
        P(("groups", "dp")),
        P("groups"),
        P(("groups", "dp")),
    )
    out_specs = (
        P(("groups", "dp"), "tensor"),
        P(None, ("groups", "dp"), "tensor"),
        P(None, ("groups", "dp"), "tensor"),
    )
    return jax.shard_map(shards, mesh=mesh, in_specs=in_specs, out_specs=out_specs, check_vma=False)
```

```python
import functools
import math
from typing import NamedTuple

import jax
import jax.numpy as jnp
from jax import lax
from jax.experimental import pallas as pl
from jax.experimental.pallas import tpu as pltpu
from jax.sharding import PartitionSpec as P

HD = 128
NEG = -1e30
TAIL = 16
F32 = jnp.float32
BF16 = jnp.bfloat16
PAIR = 2
FAR = 3
VMEM_BYTES = 63 * 1024 * 1024
GROUP_BYTES = 53 * 1024 * 1024
FINISH_BYTES = 24 * 1024 * 1024
ANYWHERE = pl.BlockSpec(memory_space=pl.ANY)


class Sizes(NamedTuple):
    n_dp: int
    count: int
    slots: int
    kv_heads: int
    group_size: int
    tokens: int
    prefix_len: int

    @property
    def width(self):
        return self.kv_heads * HD

    @property
    def lanes(self):
        return self.kv_heads * self.group_size * HD


def dot(a, b, dims):
    return lax.dot_general(a, b, (dims, ((), ())), preferred_element_type=F32)


NN = ((1,), (0,))
NT = ((1,), (1,))


class Bag:
    pass


class Unit(NamedTuple):
    at: list
    places: list
    k: object
    lens: list
    factors: list


def attend(z, units, q, og, kv, prefix, out, own_out, sink, apart):
    tokens, prefix_len, group_size = z.tokens, z.prefix_len, z.group_size
    scale = 1.0 / math.sqrt(HD)
    log_scale = scale * math.log2(math.e)
    whole = group_size - group_size % 2
    most = max(whole, 2) * tokens
    assert tokens & (tokens - 1) == 0
    token = lax.broadcasted_iota(jnp.int32, (1, most), 1) & (tokens - 1)
    key = lax.broadcasted_iota(jnp.int32, (tokens, most), 0)
    causal = key <= (lax.broadcasted_iota(jnp.int32, (tokens, most), 1) & (tokens - 1))
    left = lax.broadcasted_iota(jnp.int32, (1, 2 * tokens), 1) < tokens

    def columns(index):
        if isinstance(index, int):
            return slice(index * HD, (index + 1) * HD)
        return pl.ds(pl.multiple_of(index * HD, HD), HD)

    def head(k, h):
        return columns(k * group_size + h)

    def rows(ref, c):
        return jnp.concatenate([ref[c.t.at[n], head(c.t.k, h)] for n, h in c.blocks], axis=0)

    def halves(part):
        none = jnp.zeros_like(part)
        return [jnp.where(left, part, none), jnp.where(left, none, part)]

    def over_keys(combine, *parts):
        reduce = jnp.max if combine is jnp.maximum else jnp.sum
        eights = [reduce(part.reshape(-1, 8, part.shape[1]), axis=0) for part in parts]
        return reduce(functools.reduce(combine, eights), axis=0, keepdims=True)

    def own_half(both):
        return jnp.where(left, both[:tokens], both[tokens:])

    def rounded(*parts):
        return jnp.concatenate([part.astype(BF16) for part in parts], axis=0)

    chunks = []
    for unit in units:
        t = Bag()
        t.at, t.places, t.k, t.lens, t.factors = unit
        t.single = len(t.at) == 1
        t.members = range(len(t.at))
        sides = (0, 0) if t.single else (0, 1)
        t.cols = columns(t.k)
        t.key_p, t.value_p = prefix[0, :, t.cols], prefix[1, :, t.cols]
        t.keys = [kv[0, t.at[n], t.cols] for n in sides]
        t.values = [kv[1, t.at[n], t.cols] for n in sides]
        t.key_pair = jnp.concatenate(t.keys, axis=0)
        t.value_pair = jnp.concatenate(t.values, axis=0)
        t.key_t = jnp.concatenate([t.key_p.T, t.key_pair.T], axis=1)
        t.prefix_sums = {n: [] for n in t.members}
        t.self_sums = {n: [] for n in t.members}
        mine = []
        for n in t.members:
            c = Bag()
            c.t, c.side, c.blocks = t, n, [(n, h) for h in range(whole)]
            mine.append(c)
        if group_size % 2:
            c = Bag()
            c.t, c.side, c.blocks = t, None, [(n, group_size - 1) for n in sides]
            mine.append(c)
        t.left_over = len(mine)
        chunks += mine

    def products(c):
        t = c.t
        c.q_rows, c.g_rows = rows(q, c), rows(og, c)
        if c.side is None:
            key_s, value_s = t.key_pair, t.value_pair
        else:
            key_s, value_s = t.keys[c.side], t.values[c.side]
        c.scores = dot(jnp.concatenate([t.key_p, key_s], axis=0), c.q_rows, NT)
        c.gw = dot(jnp.concatenate([t.value_p, value_s], axis=0), c.g_rows, NT)

    def weigh(c):
        scores_p, scores_s = c.scores[:prefix_len], c.scores[prefix_len:]
        c.gw_p, c.gw_s = c.gw[:prefix_len], c.gw[prefix_len:]
        if c.side is None:
            scores_s, c.gw_s = own_half(scores_s), own_half(c.gw_s)
        scores_s = jnp.where(causal[:, : scores_s.shape[1]], scores_s, NEG)
        top = over_keys(jnp.maximum, scores_p, scores_s)
        c.e_p = jnp.exp2((scores_p - top) * log_scale)
        c.e_s = jnp.exp2((scores_s - top) * log_scale)
        total = over_keys(jnp.add, c.e_p, c.e_s)
        weighted = over_keys(jnp.add, c.e_p * c.gw_p, c.e_s * c.gw_s)
        if c.side is None:
            length = jnp.where(left, c.t.lens[0], 0 if c.t.single else c.t.lens[1])
            gain = jnp.where(left, c.t.factors[0], c.t.factors[-1])
        else:
            length, gain = c.t.lens[c.side], c.t.factors[c.side]
        inverse = 1.0 / total
        c.delta = weighted * inverse
        c.gain = inverse * jnp.where(token[:, : total.shape[1]] < length, gain, 0.0)

    def gradients(c):
        w_p, w_s = c.e_p * c.gain, c.e_s * c.gain
        d_p, d_s = w_p * (c.gw_p - c.delta), w_s * (c.gw_s - c.delta)
        if c.side is None:
            d_s, w_s = halves(d_s), halves(w_s)
            c.d_wide = rounded(d_p, *d_s)
            c.d_all = rounded(*halves(d_p), *d_s) if apart else c.d_wide
            c.w_all = rounded(*(halves(w_p) if apart else [w_p]), *w_s)
        else:
            empty = jnp.zeros_like(d_s)
            c.d_wide = rounded(*([d_p, empty, d_s] if c.side else [d_p, d_s, empty]))
            c.d_all = rounded(d_p, d_s)
            c.w_all = rounded(w_p, w_s)

    def outgoing(c):
        t = c.t
        q_grad = (dot(t.key_t, c.d_wide, NN) * scale).astype(BF16).T
        kg = dot(c.d_all, c.q_rows, NN)
        vg = dot(c.w_all, c.g_rows, NN)
        targets = t.members if c.side is None else [c.side]
        for place, (n, h) in enumerate(c.blocks):
            if c.side is not None or place < len(targets):
                out[t.places[n], :, head(t.k, h)] = q_grad[place * tokens : (place + 1) * tokens]
        many = 2 if c.side is None and apart else 1
        for place, n in enumerate(targets):
            if place < many:
                rows_p = slice(place * prefix_len, (place + 1) * prefix_len)
                t.prefix_sums[n if apart else 0].append((kg[rows_p], vg[rows_p]))
            start = many * prefix_len + place * tokens
            rows_s = slice(start, start + tokens)
            t.self_sums[n].append((kg[rows_s], vg[rows_s]))
        t.left_over -= 1
        if t.left_over == 0:
            for n in t.members:
                keys, values = zip(*t.self_sums[n])
                own_out[t.places[n], 0, :, t.cols] = (sum(keys) * scale).astype(BF16)
                own_out[t.places[n], 1, :, t.cols] = sum(values).astype(BF16)
                if apart or n == 0:
                    keys, values = zip(*t.prefix_sums[n])
                    sink(t.places[n], t.cols, sum(keys) * scale, sum(values))

    stages = (products, weigh, gradients, outgoing)
    for step in range(len(chunks) + len(stages) - 1):
        for late, stage in enumerate(stages):
            if 0 <= step - late < len(chunks):
                stage(chunks[step - late])


def token_rows(z, i):
    return pl.ds(pl.multiple_of(i * z.tokens, z.tokens), z.tokens)


def find_responses(z, me, turns, resp_prompt, order):
    for t, turn in enumerate(turns):
        prompt = me ^ turn
        found = t * z.slots
        for i in range(z.count):
            order[found] = i
            found = found + (resp_prompt[me * z.count + i] == prompt).astype(jnp.int32)


def prompt_total(z, me, prompt, resp_prompt, tails, far_rewards):
    sums = jnp.zeros((1, z.width), F32)
    for s in range(tails.shape[0]):
        tail = tails[s].astype(F32)
        sums += tail[0:1] + tail[1:2] + tail[2:3]
    lane = lax.broadcasted_iota(jnp.int32, sums.shape, 1)
    total = jnp.sum(jnp.where(lane == prompt, sums, 0.0))
    for i in range(z.count):
        total += jnp.where(resp_prompt[(me ^ FAR) * z.count + i] == prompt, far_rewards[i], 0.0)
    return total


def reward_factor(z, reward, total, length):
    return (reward - total / z.count) * (z.tokens / length.astype(F32))


def pack_kernel(z, prompt_hbm, rewards_hbm, resp_prompt_hbm, payload, rewards, resp_prompt, staged, sems):
    me = lax.axis_index("dp")
    small = [
        pltpu.make_async_copy(rewards_hbm, rewards, sems.at[0]),
        pltpu.make_async_copy(resp_prompt_hbm, resp_prompt, sems.at[1]),
    ]
    large = [
        pltpu.make_async_copy(
            prompt_hbm.at[n], staged.at[pl.ds(n * z.prefix_len, z.prefix_len)], sems.at[2 + n]
        )
        for n in range(2)
    ]
    for copy in small + large:
        copy.start()
    for copy in small:
        copy.wait()
    lane = lax.broadcasted_iota(jnp.int32, (1, z.width), 1)
    sums = jnp.zeros((1, z.width), F32)
    for i in range(z.count):
        sums += jnp.where(lane == resp_prompt[me * z.count + i], rewards[i], 0.0)
    high = sums.astype(BF16).astype(F32)
    middle = (sums - high).astype(BF16).astype(F32)
    low = sums - high - middle
    row = lax.broadcasted_iota(jnp.int32, (TAIL, z.width), 0)
    pieces = jnp.where(row == 0, high, jnp.where(row == 1, middle, jnp.where(row == 2, low, 0.0)))
    staged[2 * z.prefix_len :, :] = pieces.astype(BF16)
    for copy in large:
        copy.wait()
    last = pltpu.make_async_copy(staged, payload, sems.at[0])
    last.start()
    last.wait()


def tail_copies(z, payloads, tails, sems):
    return [
        pltpu.make_async_copy(payload.at[pl.ds(2 * z.prefix_len, TAIL)], tails.at[n], sems.at[n])
        for n, payload in enumerate(payloads)
    ]


def row_copies(here, there, at_here, at_there, sems):
    (q0, og0, kv0), (q1, og1, kv1) = here, there
    return (
        pltpu.make_async_copy(q0.at[at_here], q1.at[at_there], sems.at[0]),
        pltpu.make_async_copy(og0.at[at_here], og1.at[at_there], sems.at[1]),
        pltpu.make_async_copy(kv0.at[:, at_here], kv1.at[:, at_there], sems.at[2]),
    )


def result_copies(out, own, q_out, self_out, place, at, sems, back=False):
    pairs = [
        (out.at[place], q_out.at[at]),
        (own.at[place], self_out.at[:, at]),
    ]
    return [
        pltpu.make_async_copy(*(reversed(pair) if back else pair), sems.at[place, n])
        for n, pair in enumerate(pairs)
    ]


def group_kernel(z, turns, raw, body, ahead, n_tails, aliased, *refs):
    small_hbm, given = refs[:4], refs[4:7]
    tail_hbm, prompts = refs[7 : 7 + n_tails], refs[7 + n_tails : 7 + n_tails + len(turns)]
    refs = refs[7 + n_tails + len(turns) :]
    if raw:
        (q_out, self_out), grads_out, in_order, refs = refs[:2], refs[2:3], refs[3:5], refs[5:]
    else:
        in_order, refs = refs[:2], refs[2 + aliased :]
        (q_out, self_out), grads_out, refs = refs[:2], refs[2 : 2 + len(turns)], refs[2 + len(turns) :]
    in_order = (in_order[0].at[0], in_order[0].at[1], in_order[1])
    (resp_prompt, resp_len, rewards, far_rewards, order, lens, factors, q, og, kv, prefix, tails, acc, out, own, grads,
     sem_small, sem_tails, sem_prefix, sem_in, sem_out, sem_grads, sem_order) = refs
    me = lax.axis_index("dp")
    n_slots = len(turns) * z.slots
    span = z.slots * z.tokens

    small = [
        pltpu.make_async_copy(src, dst, sem_small.at[n])
        for n, (src, dst) in enumerate(zip(small_hbm, (resp_prompt, resp_len, rewards, far_rewards)))
    ]
    prefix_copies = [
        pltpu.make_async_copy(
            prompts[t].at[pl.ds(n * z.prefix_len, z.prefix_len)], prefix.at[t, n], sem_prefix.at[t, n]
        )
        for t in range(len(turns))
        for n in range(2)
    ]
    late = tail_copies(z, tail_hbm, tails, sem_tails)
    first_rows = []
    if not raw:
        first_rows = row_copies(in_order, (q, og, kv), pl.ds(ahead * span, span), pl.ds(0, span), sem_order.at[0])
    for copy in [*small, *first_rows, *prefix_copies, *late]:
        copy.start()
    small[0].wait()
    ordered = [*turns, *ahead] if raw else turns
    find_responses(z, me, ordered, resp_prompt, order)

    def copies_in(slot):
        return row_copies(
            given, (q, og, kv), token_rows(z, order[slot]), token_rows(z, slot), sem_in.at[slot]
        )

    def copies_out(slot):
        return result_copies(out, own, q_out, self_out, slot, token_rows(z, order[slot]), sem_out)

    def copies_ordered(slot):
        rows = token_rows(z, slot - n_slots)
        return row_copies((q, og, kv), in_order, token_rows(z, slot), rows, sem_order.at[slot - n_slots])

    for slot in range(0 if raw else z.slots, len(ordered) * z.slots):
        for copy in copies_in(slot):
            copy.start()
    for copy in small[1:] + late:
        copy.wait()
    for t, turn in enumerate(turns):
        total = None if raw else prompt_total(z, me, me ^ turn, resp_prompt, tails, far_rewards)
        for slot in range(t * z.slots, (t + 1) * z.slots):
            i = order[slot]
            lens[slot] = resp_len[i]
            factors[slot] = 1.0 if raw else reward_factor(z, rewards[i], total, resp_len[i])
    if not raw:
        acc[...] = jnp.zeros(acc.shape, F32)
    for copy in prefix_copies:
        copy.wait()

    pairs_in_body = body
    steps_per_turn = z.slots // PAIR // pairs_in_body

    def step(u, _):
        t = u // steps_per_turn
        first = u * pairs_in_body * PAIR
        mine = range(pairs_in_body * PAIR)

        def wait_for_slots():
            for n in mine:
                for copy in copies_in(first + n):
                    copy.wait()

        if raw:
            wait_for_slots()
        else:

            @pl.when(u == 0)
            def _():
                for copy in first_rows:
                    copy.wait()

            if len(turns) > 1:
                pl.when(u >= steps_per_turn)(wait_for_slots)

        def sink(place, cols, key_grad, value_grad):
            if raw:
                grads[place, 0, :, cols] = key_grad.astype(BF16)
                grads[place, 1, :, cols] = value_grad.astype(BF16)
            else:
                acc[t, 0, :, cols] += key_grad
                acc[t, 1, :, cols] += value_grad

        units = []
        for pair in range(pairs_in_body):
            places = [first + pair * PAIR + n for n in range(PAIR)]
            at = [token_rows(z, n) for n in places]
            for k in range(z.kv_heads):
                units.append(Unit(at, places, k, [lens[n] for n in places], [factors[n] for n in places]))
        attend(z, units, q, og, kv, prefix.at[t], out, own, sink, raw)
        for n in mine:
            for copy in copies_out(first + n):
                copy.start()
        if raw:

            @pl.when(u == 0)
            def _():
                def pass_on(slot, _):
                    for copy in copies_in(slot):
                        copy.wait()
                    for copy in copies_ordered(slot):
                        copy.start()
                    return 0

                lax.fori_loop(n_slots, len(ordered) * z.slots, pass_on, 0)

        return 0

    lax.fori_loop(0, len(turns) * steps_per_turn, step, 0)
    if raw:
        last = [pltpu.make_async_copy(grads, grads_out[0], sem_grads.at[0])]
    else:
        grads[...] = acc[...].astype(BF16)
        last = [
            pltpu.make_async_copy(grads.at[t], grads_out[t], sem_grads.at[t]) for t in range(len(turns))
        ]
    for copy in last:
        copy.start()
    for slot in range(n_slots):
        for copy in copies_out(slot):
            copy.wait()
    if raw:
        for slot in range(n_slots, len(ordered) * z.slots):
            for copy in copies_ordered(slot):
                copy.wait()
    for copy in last:
        copy.wait()


def finish_kernel(z, n_tails, n_come, *refs):
    small_hbm, tail_hbm = refs[:4], refs[4 : 4 + n_tails]
    per_resp_hbm, come_hbm = refs[4 + n_tails], refs[5 + n_tails : 5 + n_tails + n_come]
    q_out, self_out, grads_out = refs[7 + n_tails + n_come : 10 + n_tails + n_come]
    (resp_prompt, resp_len, rewards, far_rewards, order, tails, out, own, per_resp, come, grads,
     sem_small, sem_tails, sem_come, sem_in, sem_out) = refs[10 + n_tails + n_come :]
    me = lax.axis_index("dp")
    small = [
        pltpu.make_async_copy(src, dst, sem_small.at[n])
        for n, (src, dst) in enumerate(zip(small_hbm, (resp_prompt, resp_len, rewards, far_rewards)))
    ]
    late = tail_copies(z, tail_hbm, tails, sem_tails)
    late += [pltpu.make_async_copy(src, come.at[n], sem_come.at[n]) for n, src in enumerate(come_hbm)]
    late += [pltpu.make_async_copy(per_resp_hbm, per_resp, sem_come.at[n_come])]
    for copy in small + late:
        copy.start()
    small[0].wait()
    find_responses(z, me, (0,), resp_prompt, order)

    def moves(slot, back):
        sems = sem_in if back else sem_out
        return result_copies(out, own, q_out, self_out, slot, token_rows(z, order[slot]), sems, back)

    for slot in range(z.slots):
        for copy in moves(slot, True):
            copy.start()
    for copy in small[1:] + late:
        copy.wait()
    total = prompt_total(z, me, me, resp_prompt, tails, far_rewards)
    summed = come[0].astype(F32)
    for n in range(1, n_come):
        summed += come[n].astype(F32)
    factors = [reward_factor(z, rewards[order[n]], total, resp_len[order[n]]) for n in range(z.slots)]
    for slot in range(z.slots):
        summed += per_resp[slot].astype(F32) * factors[slot]
    grads[...] = summed
    last = pltpu.make_async_copy(grads, grads_out, sem_small.at[0])
    last.start()
    for slot in range(z.slots):
        for copy in moves(slot, True):
            copy.wait()
        out[slot] = (out[slot].astype(F32) * factors[slot]).astype(BF16)
        own[slot] = (own[slot].astype(F32) * factors[slot]).astype(BF16)
        for copy in moves(slot, False):
            copy.start()
    for slot in range(z.slots):
        for copy in moves(slot, False):
            copy.wait()
    last.wait()


def near_shards(z, prompt_kv, resp_q, resp_kv, out_grad, rewards, resp_prompt, resp_len):
    n_dp = z.n_dp
    assert z.slots % PAIR == 0
    shape = jax.ShapeDtypeStruct
    one = (2, z.prefix_len, z.width)
    params = pltpu.CompilerParams(vmem_limit_bytes=VMEM_BYTES)
    cost = pl.CostEstimate(flops=0, bytes_accessed=0, transcendentals=0)
    payload = pl.pallas_call(
        functools.partial(pack_kernel, z),
        out_shape=jax.ShapeDtypeStruct((2 * z.prefix_len + TAIL, z.width), BF16),
        in_specs=[ANYWHERE] * 3,
        out_specs=ANYWHERE,
        scratch_shapes=[
            pltpu.SMEM(rewards.shape, F32),
            pltpu.SMEM(resp_prompt.shape, jnp.int32),
            pltpu.VMEM((2 * z.prefix_len + TAIL, z.width), BF16),
            pltpu.SemaphoreType.DMA((4,)),
        ],
        compiler_params=pltpu.CompilerParams(vmem_limit_bytes=VMEM_BYTES),
        name="pack",
    )(prompt_kv, rewards, resp_prompt)

    assert n_dp == FAR + 1

    def swap(x, s):
        return lax.ppermute(x, "dp", [(i, i ^ s) for i in range(n_dp)])

    payloads = {0: payload, 2: swap(payload, 2), 1: swap(payload, 1)}
    tails = [payloads[s] for s in range(FAR)]
    small = (resp_prompt, resp_len, rewards)
    far_rewards = swap(rewards, FAR)
    smem = [pltpu.SMEM(x.shape, x.dtype) for x in (*small, rewards)]
    slots = z.slots

    def grads_of(turns, raw, body, ahead, in_order=(), written=()):
        n_slots, n_turns = len(turns) * slots, len(turns)
        n_ahead = len(ahead) * slots if raw else 0
        n_held = n_slots + n_ahead
        used_tails = [] if raw else tails
        used_small = (*small, rewards if raw else far_rewards)
        prompts = [payloads[turn] for turn in turns]
        operands = [*used_small, resp_q, out_grad, resp_kv, *used_tails, *prompts, *in_order, *written]
        grads_shapes = [(slots,) + one] if raw else [one] * n_turns
        ordered_shapes = [(2, n_ahead * z.tokens, z.lanes), (2, n_ahead * z.tokens, z.width)] if raw else []
        return pl.pallas_call(
            functools.partial(group_kernel, z, turns, raw, body, ahead, len(used_tails), len(written)),
            out_shape=[shape(resp_q.shape, BF16), shape(resp_kv.shape, BF16)]
            + [shape(x, BF16) for x in grads_shapes + ordered_shapes],
            in_specs=[ANYWHERE] * len(operands),
            out_specs=[ANYWHERE] * (2 + len(grads_shapes) + len(ordered_shapes)),
            input_output_aliases={len(operands) - 2: 0, len(operands) - 1: 1} if written else {},
            scratch_shapes=[
                *smem,
                pltpu.SMEM((n_held + 1,), jnp.int32),
                pltpu.SMEM((n_slots,), jnp.int32),
                pltpu.SMEM((n_slots,), F32),
                pltpu.VMEM((n_held * z.tokens, z.lanes), BF16),
                pltpu.VMEM((n_held * z.tokens, z.lanes), BF16),
                pltpu.VMEM((2, n_held * z.tokens, z.width), BF16),
                pltpu.VMEM((n_turns,) + one, BF16),
                pltpu.VMEM((FAR, TAIL, z.width), BF16),
                pltpu.VMEM((n_turns,) + one, F32),
                pltpu.VMEM((n_slots, z.tokens, z.lanes), BF16),
                pltpu.VMEM((n_slots, 2, z.tokens, z.width), BF16),
                pltpu.VMEM(grads_shapes[0] if raw else (n_turns,) + one, BF16),
                pltpu.SemaphoreType.DMA((len(smem),)),
                pltpu.SemaphoreType.DMA((FAR,)),
                pltpu.SemaphoreType.DMA((n_turns, 2)),
                pltpu.SemaphoreType.DMA((n_held, 3)),
                pltpu.SemaphoreType.DMA((n_slots, 2)),
                pltpu.SemaphoreType.DMA((n_turns,)),
                pltpu.SemaphoreType.DMA((max(n_ahead, 1), 3)),
            ],
            compiler_params=params if raw else pltpu.CompilerParams(vmem_limit_bytes=GROUP_BYTES),
            cost_estimate=cost,
            name="raw_grads" if raw else "group_grads",
        )(*operands)

    *written, per_resp, rows_ahead, kv_ahead = grads_of((0,), True, 1, (2, FAR))
    in_order = (rows_ahead, kv_ahead)
    onward, per_resp, far_rewards = lax.optimization_barrier((payloads[2], per_resp, far_rewards))
    payloads[FAR] = swap(onward, 1)
    *written, for_2, for_1 = grads_of((2, 1), False, slots // PAIR, 0, in_order, written)
    come = [swap(for_2, 2)]
    *written, for_far = grads_of((FAR,), False, slots // PAIR, 1, in_order, written)
    for_far, for_1 = lax.optimization_barrier((for_far, for_1))
    last = [swap(for_far, FAR), swap(for_1, 1)]
    operands = [*small, far_rewards, *tails, per_resp, *come, *written]
    q_out, self_out, own_grads = pl.pallas_call(
        functools.partial(finish_kernel, z, len(tails), len(come)),
        out_shape=[shape(resp_q.shape, BF16), shape(resp_kv.shape, BF16), shape(one, F32)],
        in_specs=[ANYWHERE] * len(operands),
        out_specs=[ANYWHERE] * 3,
        input_output_aliases={len(operands) - 2: 0, len(operands) - 1: 1},
        scratch_shapes=[
            *smem,
            pltpu.SMEM((slots + 1,), jnp.int32),
            pltpu.VMEM((FAR, TAIL, z.width), BF16),
            pltpu.VMEM((slots, z.tokens, z.lanes), BF16),
            pltpu.VMEM((slots, 2, z.tokens, z.width), BF16),
            pltpu.VMEM((slots,) + one, BF16),
            pltpu.VMEM((len(come),) + one, BF16),
            pltpu.VMEM(one, F32),
            pltpu.SemaphoreType.DMA((len(smem),)),
            pltpu.SemaphoreType.DMA((FAR,)),
            pltpu.SemaphoreType.DMA((len(come) + 1,)),
            pltpu.SemaphoreType.DMA((slots, 3)),
            pltpu.SemaphoreType.DMA((slots, 3)),
        ],
        compiler_params=pltpu.CompilerParams(vmem_limit_bytes=FINISH_BYTES),
        cost_estimate=cost,
        name="finish_own",
    )(*operands)
    prefix_out = (own_grads + sum(part.astype(F32) for part in last)).astype(BF16)
    return (q_out, self_out, prefix_out)


def far_kernel(z, *refs):
    (resp_prompt, resp_len, rewards, q_hbm, og_hbm, kv_hbm, prompts, q_out, self_out, prefix_outs,
     totals, lens, factors, q, og, kv, prefix, out, own, grads, sem_in, sem_prefix, sem_out) = refs
    me = lax.axis_index("dp")

    for p in range(z.n_dp):
        totals[p] = 0.0

    def copies_in(slot):
        rows = token_rows(z, slot)
        prompt = resp_prompt[me * z.count + slot]
        return (
            *row_copies((q_hbm, og_hbm, kv_hbm), (q, og, kv), rows, rows, sem_in.at[slot]),
            pltpu.make_async_copy(prompts.at[prompt], prefix.at[slot], sem_prefix.at[slot]),
        )

    def copies_out(slot):
        rows = token_rows(z, slot)
        return (
            *result_copies(out, own, q_out, self_out, slot, rows, sem_out),
            pltpu.make_async_copy(grads.at[slot], prefix_outs.at[slot], sem_out.at[slot, 3]),
        )

    def start(slot, _):
        for copy in copies_in(slot):
            copy.start()
        return 0

    lax.fori_loop(0, z.count, start, 0)

    def add(i, _):
        prompt = resp_prompt[i]
        totals[prompt] = totals[prompt] + rewards[i]
        return 0

    lax.fori_loop(0, z.n_dp * z.count, add, 0)

    def find_factor(slot, _):
        place = me * z.count + slot
        lens[slot] = resp_len[slot]
        factors[slot] = reward_factor(z, rewards[place], totals[resp_prompt[place]], resp_len[slot])
        return 0

    lax.fori_loop(0, z.count, find_factor, 0)

    def unit(slot, _):
        for copy in copies_in(slot):
            copy.wait()

        def sink(_, cols, key_grad, value_grad):
            grads[slot, 0, :, cols] = key_grad.astype(BF16)
            grads[slot, 1, :, cols] = value_grad.astype(BF16)

        units = [
            Unit([token_rows(z, slot)], [slot], k, [lens[slot]], [factors[slot]]) for k in range(z.kv_heads)
        ]
        attend(z, units, q, og, kv, prefix.at[slot], out, own, sink, True)
        for copy in copies_out(slot):
            copy.start()
        return 0

    lax.fori_loop(0, z.count, unit, 0)

    def end(slot, _):
        for copy in copies_out(slot):
            copy.wait()
        return 0

    lax.fori_loop(0, z.count, end, 0)


def far_shards(z, prompt_kv, resp_q, resp_kv, out_grad, rewards, resp_prompt, resp_len):
    assert z.slots == 1
    count, n_dp = z.count, z.n_dp
    one = (2, z.prefix_len, z.width)
    smem = pl.BlockSpec(memory_space=pltpu.SMEM)
    q_out, self_out, per_resp = pl.pallas_call(
        functools.partial(far_kernel, z),
        out_shape=[
            jax.ShapeDtypeStruct(resp_q.shape, BF16),
            jax.ShapeDtypeStruct(resp_kv.shape, BF16),
            jax.ShapeDtypeStruct((count,) + one, BF16),
        ],
        in_specs=[smem] * 3 + [ANYWHERE] * 4,
        out_specs=[ANYWHERE] * 3,
        scratch_shapes=[
            pltpu.SMEM((n_dp,), F32),
            pltpu.SMEM((count,), jnp.int32),
            pltpu.SMEM((count,), F32),
            pltpu.VMEM(resp_q.shape, BF16),
            pltpu.VMEM(resp_q.shape, BF16),
            pltpu.VMEM(resp_kv.shape, BF16),
            pltpu.VMEM((count,) + one, BF16),
            pltpu.VMEM((count, z.tokens, z.lanes), BF16),
            pltpu.VMEM((count, 2, z.tokens, z.width), BF16),
            pltpu.VMEM((count,) + one, BF16),
            pltpu.SemaphoreType.DMA((count, 4)),
            pltpu.SemaphoreType.DMA((count,)),
            pltpu.SemaphoreType.DMA((count, 4)),
        ],
        compiler_params=pltpu.CompilerParams(vmem_limit_bytes=VMEM_BYTES),
        name="far_grads",
    )(
        resp_prompt,
        resp_len,
        lax.all_gather(rewards, "dp", axis=0, tiled=True),
        resp_q,
        out_grad,
        resp_kv,
        lax.all_gather(prompt_kv, "dp", axis=0),
    )
    my_prompts = lax.dynamic_slice_in_dim(resp_prompt, lax.axis_index("dp") * count, count)
    route = (jnp.arange(n_dp, dtype=jnp.int32)[:, None] == my_prompts[None, :]).astype(BF16)
    outgoing = jnp.dot(route, per_resp.reshape(count, -1), preferred_element_type=F32).astype(BF16)
    outgoing = outgoing.reshape((n_dp,) + one)
    incoming = lax.all_to_all(outgoing, "dp", split_axis=0, concat_axis=0, tiled=True)
    prefix_out = jnp.sum(incoming, axis=0, dtype=F32).astype(BF16)
    return (q_out, self_out, prefix_out)


def shards(prompt_kv, resp_q, resp_kv, out_grad, rewards, resp_prompt, resp_len):
    n_dp = lax.axis_size("dp")
    count = rewards.shape[0]
    prefix_len, width = prompt_kv.shape[1:]
    slots = (count + n_dp - 1) // n_dp
    z = Sizes(
        n_dp, count, slots, width // HD, resp_q.shape[1] // width, resp_q.shape[0] // count, prefix_len
    )
    part = near_shards if count // slots == n_dp else far_shards
    return part(z, prompt_kv, resp_q, resp_kv, out_grad, rewards, resp_prompt, resp_len)


def solution(mesh):
    in_specs = (
        P(None, ("groups", "dp"), "tensor"),
        P(("groups", "dp"), "tensor"),
        P(None, ("groups", "dp"), "tensor"),
        P(("groups", "dp"), "tensor"),
        P(("groups", "dp")),
        P("groups"),
        P(("groups", "dp")),
    )
    out_specs = (
        P(("groups", "dp"), "tensor"),
        P(None, ("groups", "dp"), "tensor"),
        P(None, ("groups", "dp"), "tensor"),
    )
    return jax.shard_map(shards, mesh=mesh, in_specs=in_specs, out_specs=out_specs, check_vma=False)
```

```python
import functools
import math
from typing import NamedTuple

import jax
import jax.numpy as jnp
from jax import lax
from jax.experimental import pallas as pl
from jax.experimental.pallas import tpu as pltpu
from jax.sharding import PartitionSpec as P

HD = 128
NEG = -1e30
TAIL = 16
F32 = jnp.float32
BF16 = jnp.bfloat16
PAIR = 2
FAR = 3
VMEM_BYTES = 63 * 1024 * 1024
GROUP_BYTES = 53 * 1024 * 1024
FINISH_BYTES = 24 * 1024 * 1024
ANYWHERE = pl.BlockSpec(memory_space=pl.ANY)


class Sizes(NamedTuple):
    n_dp: int
    count: int
    slots: int
    kv_heads: int
    group_size: int
    tokens: int
    prefix_len: int

    @property
    def width(self):
        return self.kv_heads * HD

    @property
    def lanes(self):
        return self.kv_heads * self.group_size * HD


def dot(a, b, dims):
    return lax.dot_general(a, b, (dims, ((), ())), preferred_element_type=F32)


NN = ((1,), (0,))
NT = ((1,), (1,))


class Bag:
    pass


class Unit(NamedTuple):
    at: list
    places: list
    k: object
    lens: list
    factors: list


def attend(z, units, q, og, kv, prefix, out, own_out, sink, apart):
    tokens, prefix_len, group_size = z.tokens, z.prefix_len, z.group_size
    scale = 1.0 / math.sqrt(HD)
    log_scale = scale * math.log2(math.e)
    whole = group_size - group_size % 2
    most = max(whole, 2) * tokens
    assert tokens & (tokens - 1) == 0
    token = lax.broadcasted_iota(jnp.int32, (1, most), 1) & (tokens - 1)
    key = lax.broadcasted_iota(jnp.int32, (tokens, most), 0)
    causal = key <= (lax.broadcasted_iota(jnp.int32, (tokens, most), 1) & (tokens - 1))
    left = lax.broadcasted_iota(jnp.int32, (1, 2 * tokens), 1) < tokens

    def columns(index):
        if isinstance(index, int):
            return slice(index * HD, (index + 1) * HD)
        return pl.ds(pl.multiple_of(index * HD, HD), HD)

    def head(k, h):
        return columns(k * group_size + h)

    def rows(ref, c):
        return jnp.concatenate([ref[c.t.at[n], head(c.t.k, h)] for n, h in c.blocks], axis=0)

    def halves(part):
        none = jnp.zeros_like(part)
        return [jnp.where(left, part, none), jnp.where(left, none, part)]

    def over_keys(combine, *parts):
        reduce = jnp.max if combine is jnp.maximum else jnp.sum
        eights = [reduce(part.reshape(-1, 8, part.shape[1]), axis=0) for part in parts]
        return reduce(functools.reduce(combine, eights), axis=0, keepdims=True)

    def own_half(both):
        return jnp.where(left, both[:tokens], both[tokens:])

    def rounded(*parts):
        return jnp.concatenate([part.astype(BF16) for part in parts], axis=0)

    chunks = []
    for unit in units:
        t = Bag()
        t.at, t.places, t.k, t.lens, t.factors = unit
        t.single = len(t.at) == 1
        t.members = range(len(t.at))
        sides = (0, 0) if t.single else (0, 1)
        t.cols = columns(t.k)
        t.key_p, t.value_p = prefix[0, :, t.cols], prefix[1, :, t.cols]
        t.keys = [kv[0, t.at[n], t.cols] for n in sides]
        t.values = [kv[1, t.at[n], t.cols] for n in sides]
        t.key_pair = jnp.concatenate(t.keys, axis=0)
        t.value_pair = jnp.concatenate(t.values, axis=0)
        t.key_t = jnp.concatenate([t.key_p.T, t.key_pair.T], axis=1)
        t.prefix_sums = {n: [] for n in t.members}
        t.self_sums = {n: [] for n in t.members}
        mine = []
        for n in t.members:
            c = Bag()
            c.t, c.side, c.blocks = t, n, [(n, h) for h in range(whole)]
            mine.append(c)
        if group_size % 2:
            c = Bag()
            c.t, c.side, c.blocks = t, None, [(n, group_size - 1) for n in sides]
            mine.append(c)
        t.left_over = len(mine)
        chunks += mine

    def products(c):
        t = c.t
        c.q_rows, c.g_rows = rows(q, c), rows(og, c)
        if c.side is None:
            key_s, value_s = t.key_pair, t.value_pair
        else:
            key_s, value_s = t.keys[c.side], t.values[c.side]
        c.scores = dot(jnp.concatenate([t.key_p, key_s], axis=0), c.q_rows, NT)
        c.gw = dot(jnp.concatenate([t.value_p, value_s], axis=0), c.g_rows, NT)

    def weigh(c):
        scores_p, scores_s = c.scores[:prefix_len], c.scores[prefix_len:]
        c.gw_p, c.gw_s = c.gw[:prefix_len], c.gw[prefix_len:]
        if c.side is None:
            scores_s, c.gw_s = own_half(scores_s), own_half(c.gw_s)
        scores_s = jnp.where(causal[:, : scores_s.shape[1]], scores_s, NEG)
        top = over_keys(jnp.maximum, scores_p, scores_s)
        c.e_p = jnp.exp2((scores_p - top) * log_scale)
        c.e_s = jnp.exp2((scores_s - top) * log_scale)
        total = over_keys(jnp.add, c.e_p, c.e_s)
        weighted = over_keys(jnp.add, c.e_p * c.gw_p, c.e_s * c.gw_s)
        if c.side is None:
            length = jnp.where(left, c.t.lens[0], 0 if c.t.single else c.t.lens[1])
            gain = jnp.where(left, c.t.factors[0], c.t.factors[-1])
        else:
            length, gain = c.t.lens[c.side], c.t.factors[c.side]
        inverse = 1.0 / total
        c.delta = weighted * inverse
        c.gain = inverse * jnp.where(token[:, : total.shape[1]] < length, gain, 0.0)

    def gradients(c):
        w_p, w_s = c.e_p * c.gain, c.e_s * c.gain
        d_p, d_s = w_p * (c.gw_p - c.delta), w_s * (c.gw_s - c.delta)
        if c.side is None:
            d_s, w_s = halves(d_s), halves(w_s)
            c.d_wide = rounded(d_p, *d_s)
            c.d_all = rounded(*halves(d_p), *d_s) if apart else c.d_wide
            c.w_all = rounded(*(halves(w_p) if apart else [w_p]), *w_s)
        else:
            empty = jnp.zeros_like(d_s)
            c.d_wide = rounded(*([d_p, empty, d_s] if c.side else [d_p, d_s, empty]))
            c.d_all = rounded(d_p, d_s)
            c.w_all = rounded(w_p, w_s)

    def outgoing(c):
        t = c.t
        q_grad = (dot(t.key_t, c.d_wide, NN) * scale).astype(BF16).T
        kg = dot(c.d_all, c.q_rows, NN)
        vg = dot(c.w_all, c.g_rows, NN)
        targets = t.members if c.side is None else [c.side]
        for place, (n, h) in enumerate(c.blocks):
            if c.side is not None or place < len(targets):
                out[t.places[n], :, head(t.k, h)] = q_grad[place * tokens : (place + 1) * tokens]
        many = 2 if c.side is None and apart else 1
        for place, n in enumerate(targets):
            if place < many:
                rows_p = slice(place * prefix_len, (place + 1) * prefix_len)
                t.prefix_sums[n if apart else 0].append((kg[rows_p], vg[rows_p]))
            start = many * prefix_len + place * tokens
            rows_s = slice(start, start + tokens)
            t.self_sums[n].append((kg[rows_s], vg[rows_s]))
        t.left_over -= 1
        if t.left_over == 0:
            for n in t.members:
                keys, values = zip(*t.self_sums[n])
                own_out[t.places[n], 0, :, t.cols] = (sum(keys) * scale).astype(BF16)
                own_out[t.places[n], 1, :, t.cols] = sum(values).astype(BF16)
                if apart or n == 0:
                    keys, values = zip(*t.prefix_sums[n])
                    sink(t.places[n], t.cols, sum(keys) * scale, sum(values))

    stages = (products, weigh, gradients, outgoing)
    for step in range(len(chunks) + len(stages) - 1):
        for late, stage in enumerate(stages):
            if 0 <= step - late < len(chunks):
                stage(chunks[step - late])


def token_rows(z, i):
    return pl.ds(pl.multiple_of(i * z.tokens, z.tokens), z.tokens)


def find_responses(z, me, turns, resp_prompt, order):
    for t, turn in enumerate(turns):
        prompt = me ^ turn
        found = t * z.slots
        for i in range(z.count):
            order[found] = i
            found = found + (resp_prompt[me * z.count + i] == prompt).astype(jnp.int32)


def prompt_total(z, me, prompt, resp_prompt, tails, far_rewards):
    sums = jnp.zeros((1, z.width), F32)
    for s in range(tails.shape[0]):
        tail = tails[s].astype(F32)
        sums += tail[0:1] + tail[1:2] + tail[2:3]
    lane = lax.broadcasted_iota(jnp.int32, sums.shape, 1)
    total = jnp.sum(jnp.where(lane == prompt, sums, 0.0))
    for i in range(z.count):
        total += jnp.where(resp_prompt[(me ^ FAR) * z.count + i] == prompt, far_rewards[i], 0.0)
    return total


def reward_factor(z, reward, total, length):
    return (reward - total / z.count) * (z.tokens / length.astype(F32))


def pack_kernel(z, prompt_hbm, rewards_hbm, resp_prompt_hbm, payload, rewards, resp_prompt, staged, sems):
    me = lax.axis_index("dp")
    small = [
        pltpu.make_async_copy(rewards_hbm, rewards, sems.at[0]),
        pltpu.make_async_copy(resp_prompt_hbm, resp_prompt, sems.at[1]),
    ]
    large = [
        pltpu.make_async_copy(
            prompt_hbm.at[n], staged.at[pl.ds(n * z.prefix_len, z.prefix_len)], sems.at[2 + n]
        )
        for n in range(2)
    ]
    for copy in small + large:
        copy.start()
    for copy in small:
        copy.wait()
    lane = lax.broadcasted_iota(jnp.int32, (1, z.width), 1)
    sums = jnp.zeros((1, z.width), F32)
    for i in range(z.count):
        sums += jnp.where(lane == resp_prompt[me * z.count + i], rewards[i], 0.0)
    high = sums.astype(BF16).astype(F32)
    middle = (sums - high).astype(BF16).astype(F32)
    low = sums - high - middle
    row = lax.broadcasted_iota(jnp.int32, (TAIL, z.width), 0)
    pieces = jnp.where(row == 0, high, jnp.where(row == 1, middle, jnp.where(row == 2, low, 0.0)))
    staged[2 * z.prefix_len :, :] = pieces.astype(BF16)
    for copy in large:
        copy.wait()
    last = pltpu.make_async_copy(staged, payload, sems.at[0])
    last.start()
    last.wait()


def tail_copies(z, payloads, tails, sems):
    return [
        pltpu.make_async_copy(payload.at[pl.ds(2 * z.prefix_len, TAIL)], tails.at[n], sems.at[n])
        for n, payload in enumerate(payloads)
    ]


def row_copies(here, there, at_here, at_there, sems):
    (q0, og0, kv0), (q1, og1, kv1) = here, there
    return (
        pltpu.make_async_copy(q0.at[at_here], q1.at[at_there], sems.at[0]),
        pltpu.make_async_copy(og0.at[at_here], og1.at[at_there], sems.at[1]),
        pltpu.make_async_copy(kv0.at[:, at_here], kv1.at[:, at_there], sems.at[2]),
    )


def result_copies(out, own, q_out, self_out, place, at, sems, back=False):
    pairs = [
        (out.at[place], q_out.at[at]),
        (own.at[place], self_out.at[:, at]),
    ]
    return [
        pltpu.make_async_copy(*(reversed(pair) if back else pair), sems.at[place, n])
        for n, pair in enumerate(pairs)
    ]


def group_kernel(z, turns, raw, body, ahead, n_tails, aliased, *refs):
    small_hbm, given = refs[:4], refs[4:7]
    tail_hbm, prompts = refs[7 : 7 + n_tails], refs[7 + n_tails : 7 + n_tails + len(turns)]
    refs = refs[7 + n_tails + len(turns) :]
    if raw:
        (q_out, self_out), grads_out, in_order, refs = refs[:2], refs[2:3], refs[3:5], refs[5:]
    else:
        in_order, refs = refs[:2], refs[2 + aliased :]
        (q_out, self_out), grads_out, refs = refs[:2], refs[2 : 2 + len(turns)], refs[2 + len(turns) :]
    in_order = (in_order[0].at[0], in_order[0].at[1], in_order[1])
    (resp_prompt, resp_len, rewards, far_rewards, order, lens, factors, q, og, kv, prefix, tails, acc, out, own, grads,
     sem_small, sem_tails, sem_prefix, sem_in, sem_out, sem_grads, sem_order) = refs
    me = lax.axis_index("dp")
    n_slots = len(turns) * z.slots
    span = z.slots * z.tokens

    small = [
        pltpu.make_async_copy(src, dst, sem_small.at[n])
        for n, (src, dst) in enumerate(zip(small_hbm, (resp_prompt, resp_len, rewards, far_rewards)))
    ]
    prefix_copies = [
        pltpu.make_async_copy(
            prompts[t].at[pl.ds(n * z.prefix_len, z.prefix_len)], prefix.at[t, n], sem_prefix.at[t, n]
        )
        for t in range(len(turns))
        for n in range(2)
    ]
    late = tail_copies(z, tail_hbm, tails, sem_tails)
    first_rows = []
    if not raw:
        first_rows = row_copies(in_order, (q, og, kv), pl.ds(ahead * span, span), pl.ds(0, span), sem_order.at[0])
    for copy in [*small, *first_rows, *prefix_copies, *late]:
        copy.start()
    small[0].wait()
    ordered = [*turns, *ahead] if raw else turns
    find_responses(z, me, ordered, resp_prompt, order)

    def copies_in(slot):
        return row_copies(
            given, (q, og, kv), token_rows(z, order[slot]), token_rows(z, slot), sem_in.at[slot]
        )

    def copies_out(slot):
        return result_copies(out, own, q_out, self_out, slot, token_rows(z, order[slot]), sem_out)

    def copies_ordered(slot):
        rows = token_rows(z, slot - n_slots)
        return row_copies((q, og, kv), in_order, token_rows(z, slot), rows, sem_order.at[slot - n_slots])

    for slot in range(0 if raw else z.slots, len(ordered) * z.slots):
        for copy in copies_in(slot):
            copy.start()
    for copy in small[1:] + late:
        copy.wait()
    for t, turn in enumerate(turns):
        total = None if raw else prompt_total(z, me, me ^ turn, resp_prompt, tails, far_rewards)
        for slot in range(t * z.slots, (t + 1) * z.slots):
            i = order[slot]
            lens[slot] = resp_len[i]
            factors[slot] = 1.0 if raw else reward_factor(z, rewards[i], total, resp_len[i])
    if not raw:
        acc[...] = jnp.zeros(acc.shape, F32)
    for copy in prefix_copies:
        copy.wait()

    pairs_in_body = body
    steps_per_turn = z.slots // PAIR // pairs_in_body

    def step(u, _):
        t = u // steps_per_turn
        first = u * pairs_in_body * PAIR
        mine = range(pairs_in_body * PAIR)

        def wait_for_slots():
            for n in mine:
                for copy in copies_in(first + n):
                    copy.wait()

        if raw:
            wait_for_slots()
        else:

            @pl.when(u == 0)
            def _():
                for copy in first_rows:
                    copy.wait()

            if len(turns) > 1:
                pl.when(u >= steps_per_turn)(wait_for_slots)

        def sink(place, cols, key_grad, value_grad):
            if raw:
                grads[place, 0, :, cols] = key_grad.astype(BF16)
                grads[place, 1, :, cols] = value_grad.astype(BF16)
            else:
                acc[t, 0, :, cols] += key_grad
                acc[t, 1, :, cols] += value_grad

        units = []
        for pair in range(pairs_in_body):
            places = [first + pair * PAIR + n for n in range(PAIR)]
            at = [token_rows(z, n) for n in places]
            for k in range(z.kv_heads):
                units.append(Unit(at, places, k, [lens[n] for n in places], [factors[n] for n in places]))
        attend(z, units, q, og, kv, prefix.at[t], out, own, sink, raw)
        for n in mine:
            for copy in copies_out(first + n):
                copy.start()
        if raw:

            @pl.when(u == 0)
            def _():
                def pass_on(slot, _):
                    for copy in copies_in(slot):
                        copy.wait()
                    for copy in copies_ordered(slot):
                        copy.start()
                    return 0

                lax.fori_loop(n_slots, len(ordered) * z.slots, pass_on, 0)

        return 0

    lax.fori_loop(0, len(turns) * steps_per_turn, step, 0)
    if raw:
        last = [pltpu.make_async_copy(grads, grads_out[0], sem_grads.at[0])]
    else:
        grads[...] = acc[...].astype(BF16)
        last = [
            pltpu.make_async_copy(grads.at[t], grads_out[t], sem_grads.at[t]) for t in range(len(turns))
        ]
    for copy in last:
        copy.start()
    for slot in range(n_slots):
        for copy in copies_out(slot):
            copy.wait()
    if raw:
        for slot in range(n_slots, len(ordered) * z.slots):
            for copy in copies_ordered(slot):
                copy.wait()
    for copy in last:
        copy.wait()


def finish_kernel(z, n_tails, n_come, *refs):
    small_hbm, tail_hbm = refs[:4], refs[4 : 4 + n_tails]
    per_resp_hbm, come_hbm = refs[4 + n_tails], refs[5 + n_tails : 5 + n_tails + n_come]
    q_out, self_out, grads_out = refs[7 + n_tails + n_come : 10 + n_tails + n_come]
    (resp_prompt, resp_len, rewards, far_rewards, order, tails, out, own, per_resp, come, grads,
     sem_small, sem_tails, sem_come, sem_in, sem_out) = refs[10 + n_tails + n_come :]
    me = lax.axis_index("dp")
    small = [
        pltpu.make_async_copy(src, dst, sem_small.at[n])
        for n, (src, dst) in enumerate(zip(small_hbm, (resp_prompt, resp_len, rewards, far_rewards)))
    ]
    late = tail_copies(z, tail_hbm, tails, sem_tails)
    late += [pltpu.make_async_copy(src, come.at[n], sem_come.at[n]) for n, src in enumerate(come_hbm)]
    late += [pltpu.make_async_copy(per_resp_hbm, per_resp, sem_come.at[n_come])]
    for copy in small + late:
        copy.start()
    small[0].wait()
    find_responses(z, me, (0,), resp_prompt, order)

    def moves(slot, back):
        sems = sem_in if back else sem_out
        return result_copies(out, own, q_out, self_out, slot, token_rows(z, order[slot]), sems, back)

    for slot in range(z.slots):
        for copy in moves(slot, True):
            copy.start()
    for copy in small[1:] + late:
        copy.wait()
    total = prompt_total(z, me, me, resp_prompt, tails, far_rewards)
    summed = come[0].astype(F32)
    for n in range(1, n_come):
        summed += come[n].astype(F32)
    factors = [reward_factor(z, rewards[order[n]], total, resp_len[order[n]]) for n in range(z.slots)]
    for slot in range(z.slots):
        summed += per_resp[slot].astype(F32) * factors[slot]
    grads[...] = summed
    last = pltpu.make_async_copy(grads, grads_out, sem_small.at[0])
    last.start()
    for slot in range(z.slots):
        for copy in moves(slot, True):
            copy.wait()
        out[slot] = (out[slot].astype(F32) * factors[slot]).astype(BF16)
        own[slot] = (own[slot].astype(F32) * factors[slot]).astype(BF16)
        for copy in moves(slot, False):
            copy.start()
    for slot in range(z.slots):
        for copy in moves(slot, False):
            copy.wait()
    last.wait()


def near_shards(z, prompt_kv, resp_q, resp_kv, out_grad, rewards, resp_prompt, resp_len):
    n_dp = z.n_dp
    assert z.slots % PAIR == 0
    shape = jax.ShapeDtypeStruct
    one = (2, z.prefix_len, z.width)
    params = pltpu.CompilerParams(vmem_limit_bytes=VMEM_BYTES)
    cost = pl.CostEstimate(flops=0, bytes_accessed=0, transcendentals=0)
    payload = pl.pallas_call(
        functools.partial(pack_kernel, z),
        out_shape=jax.ShapeDtypeStruct((2 * z.prefix_len + TAIL, z.width), BF16),
        in_specs=[ANYWHERE] * 3,
        out_specs=ANYWHERE,
        scratch_shapes=[
            pltpu.SMEM(rewards.shape, F32),
            pltpu.SMEM(resp_prompt.shape, jnp.int32),
            pltpu.VMEM((2 * z.prefix_len + TAIL, z.width), BF16),
            pltpu.SemaphoreType.DMA((4,)),
        ],
        compiler_params=pltpu.CompilerParams(vmem_limit_bytes=VMEM_BYTES),
        name="pack",
    )(prompt_kv, rewards, resp_prompt)

    assert n_dp == FAR + 1

    def swap(x, s):
        return lax.ppermute(x, "dp", [(i, i ^ s) for i in range(n_dp)])

    payloads = {0: payload, 2: swap(payload, 2), 1: swap(payload, 1)}
    tails = [payloads[s] for s in range(FAR)]
    small = (resp_prompt, resp_len, rewards)
    far_rewards = swap(rewards, FAR)
    smem = [pltpu.SMEM(x.shape, x.dtype) for x in (*small, rewards)]
    slots = z.slots

    def grads_of(turns, raw, body, ahead, in_order=(), written=()):
        n_slots, n_turns = len(turns) * slots, len(turns)
        n_ahead = len(ahead) * slots if raw else 0
        n_held = n_slots + n_ahead
        used_tails = [] if raw else tails
        used_small = (*small, rewards if raw else far_rewards)
        prompts = [payloads[turn] for turn in turns]
        operands = [*used_small, resp_q, out_grad, resp_kv, *used_tails, *prompts, *in_order, *written]
        grads_shapes = [(slots,) + one] if raw else [one] * n_turns
        ordered_shapes = [(2, n_ahead * z.tokens, z.lanes), (2, n_ahead * z.tokens, z.width)] if raw else []
        return pl.pallas_call(
            functools.partial(group_kernel, z, turns, raw, body, ahead, len(used_tails), len(written)),
            out_shape=[shape(resp_q.shape, BF16), shape(resp_kv.shape, BF16)]
            + [shape(x, BF16) for x in grads_shapes + ordered_shapes],
            in_specs=[ANYWHERE] * len(operands),
            out_specs=[ANYWHERE] * (2 + len(grads_shapes) + len(ordered_shapes)),
            input_output_aliases={len(operands) - 2: 0, len(operands) - 1: 1} if written else {},
            scratch_shapes=[
                *smem,
                pltpu.SMEM((n_held + 1,), jnp.int32),
                pltpu.SMEM((n_slots,), jnp.int32),
                pltpu.SMEM((n_slots,), F32),
                pltpu.VMEM((n_held * z.tokens, z.lanes), BF16),
                pltpu.VMEM((n_held * z.tokens, z.lanes), BF16),
                pltpu.VMEM((2, n_held * z.tokens, z.width), BF16),
                pltpu.VMEM((n_turns,) + one, BF16),
                pltpu.VMEM((FAR, TAIL, z.width), BF16),
                pltpu.VMEM((n_turns,) + one, F32),
                pltpu.VMEM((n_slots, z.tokens, z.lanes), BF16),
                pltpu.VMEM((n_slots, 2, z.tokens, z.width), BF16),
                pltpu.VMEM(grads_shapes[0] if raw else (n_turns,) + one, BF16),
                pltpu.SemaphoreType.DMA((len(smem),)),
                pltpu.SemaphoreType.DMA((FAR,)),
                pltpu.SemaphoreType.DMA((n_turns, 2)),
                pltpu.SemaphoreType.DMA((n_held, 3)),
                pltpu.SemaphoreType.DMA((n_slots, 2)),
                pltpu.SemaphoreType.DMA((n_turns,)),
                pltpu.SemaphoreType.DMA((max(n_ahead, 1), 3)),
            ],
            compiler_params=params if raw else pltpu.CompilerParams(vmem_limit_bytes=GROUP_BYTES),
            cost_estimate=cost,
            name="raw_grads" if raw else "group_grads",
        )(*operands)

    *written, per_resp, rows_ahead, kv_ahead = grads_of((0,), True, 1, (2, FAR))
    in_order = (rows_ahead, kv_ahead)
    onward, per_resp, far_rewards = lax.optimization_barrier((payloads[2], per_resp, far_rewards))
    payloads[FAR] = swap(onward, 1)
    *written, for_2 = grads_of((2,), False, slots // PAIR, 0, in_order, written)
    come = [swap(for_2, 2)]
    *written, for_far, for_1 = grads_of((FAR, 1), False, slots // PAIR, 1, in_order, written)
    last = [swap(for_far, FAR), swap(for_1, 1)]
    operands = [*small, far_rewards, *tails, per_resp, *come, *written]
    q_out, self_out, own_grads = pl.pallas_call(
        functools.partial(finish_kernel, z, len(tails), len(come)),
        out_shape=[shape(resp_q.shape, BF16), shape(resp_kv.shape, BF16), shape(one, F32)],
        in_specs=[ANYWHERE] * len(operands),
        out_specs=[ANYWHERE] * 3,
        input_output_aliases={len(operands) - 2: 0, len(operands) - 1: 1},
        scratch_shapes=[
            *smem,
            pltpu.SMEM((slots + 1,), jnp.int32),
            pltpu.VMEM((FAR, TAIL, z.width), BF16),
            pltpu.VMEM((slots, z.tokens, z.lanes), BF16),
            pltpu.VMEM((slots, 2, z.tokens, z.width), BF16),
            pltpu.VMEM((slots,) + one, BF16),
            pltpu.VMEM((len(come),) + one, BF16),
            pltpu.VMEM(one, F32),
            pltpu.SemaphoreType.DMA((len(smem),)),
            pltpu.SemaphoreType.DMA((FAR,)),
            pltpu.SemaphoreType.DMA((len(come) + 1,)),
            pltpu.SemaphoreType.DMA((slots, 3)),
            pltpu.SemaphoreType.DMA((slots, 3)),
        ],
        compiler_params=pltpu.CompilerParams(vmem_limit_bytes=FINISH_BYTES),
        cost_estimate=cost,
        name="finish_own",
    )(*operands)
    prefix_out = (own_grads + sum(part.astype(F32) for part in last)).astype(BF16)
    return (q_out, self_out, prefix_out)


def far_kernel(z, *refs):
    (resp_prompt, resp_len, rewards, q_hbm, og_hbm, kv_hbm, prompts, q_out, self_out, prefix_outs,
     totals, lens, factors, q, og, kv, prefix, out, own, grads, sem_in, sem_prefix, sem_out) = refs
    me = lax.axis_index("dp")

    for p in range(z.n_dp):
        totals[p] = 0.0

    def copies_in(slot):
        rows = token_rows(z, slot)
        prompt = resp_prompt[me * z.count + slot]
        return (
            *row_copies((q_hbm, og_hbm, kv_hbm), (q, og, kv), rows, rows, sem_in.at[slot]),
            pltpu.make_async_copy(prompts.at[prompt], prefix.at[slot], sem_prefix.at[slot]),
        )

    def copies_out(slot):
        rows = token_rows(z, slot)
        return (
            *result_copies(out, own, q_out, self_out, slot, rows, sem_out),
            pltpu.make_async_copy(grads.at[slot], prefix_outs.at[slot], sem_out.at[slot, 3]),
        )

    def start(slot, _):
        for copy in copies_in(slot):
            copy.start()
        return 0

    lax.fori_loop(0, z.count, start, 0)

    def add(i, _):
        prompt = resp_prompt[i]
        totals[prompt] = totals[prompt] + rewards[i]
        return 0

    lax.fori_loop(0, z.n_dp * z.count, add, 0)

    def find_factor(slot, _):
        place = me * z.count + slot
        lens[slot] = resp_len[slot]
        factors[slot] = reward_factor(z, rewards[place], totals[resp_prompt[place]], resp_len[slot])
        return 0

    lax.fori_loop(0, z.count, find_factor, 0)

    def unit(slot, _):
        for copy in copies_in(slot):
            copy.wait()

        def sink(_, cols, key_grad, value_grad):
            grads[slot, 0, :, cols] = key_grad.astype(BF16)
            grads[slot, 1, :, cols] = value_grad.astype(BF16)

        units = [
            Unit([token_rows(z, slot)], [slot], k, [lens[slot]], [factors[slot]]) for k in range(z.kv_heads)
        ]
        attend(z, units, q, og, kv, prefix.at[slot], out, own, sink, True)
        for copy in copies_out(slot):
            copy.start()
        return 0

    lax.fori_loop(0, z.count, unit, 0)

    def end(slot, _):
        for copy in copies_out(slot):
            copy.wait()
        return 0

    lax.fori_loop(0, z.count, end, 0)


def far_shards(z, prompt_kv, resp_q, resp_kv, out_grad, rewards, resp_prompt, resp_len):
    assert z.slots == 1
    count, n_dp = z.count, z.n_dp
    one = (2, z.prefix_len, z.width)
    smem = pl.BlockSpec(memory_space=pltpu.SMEM)
    q_out, self_out, per_resp = pl.pallas_call(
        functools.partial(far_kernel, z),
        out_shape=[
            jax.ShapeDtypeStruct(resp_q.shape, BF16),
            jax.ShapeDtypeStruct(resp_kv.shape, BF16),
            jax.ShapeDtypeStruct((count,) + one, BF16),
        ],
        in_specs=[smem] * 3 + [ANYWHERE] * 4,
        out_specs=[ANYWHERE] * 3,
        scratch_shapes=[
            pltpu.SMEM((n_dp,), F32),
            pltpu.SMEM((count,), jnp.int32),
            pltpu.SMEM((count,), F32),
            pltpu.VMEM(resp_q.shape, BF16),
            pltpu.VMEM(resp_q.shape, BF16),
            pltpu.VMEM(resp_kv.shape, BF16),
            pltpu.VMEM((count,) + one, BF16),
            pltpu.VMEM((count, z.tokens, z.lanes), BF16),
            pltpu.VMEM((count, 2, z.tokens, z.width), BF16),
            pltpu.VMEM((count,) + one, BF16),
            pltpu.SemaphoreType.DMA((count, 4)),
            pltpu.SemaphoreType.DMA((count,)),
            pltpu.SemaphoreType.DMA((count, 4)),
        ],
        compiler_params=pltpu.CompilerParams(vmem_limit_bytes=VMEM_BYTES),
        name="far_grads",
    )(
        resp_prompt,
        resp_len,
        lax.all_gather(rewards, "dp", axis=0, tiled=True),
        resp_q,
        out_grad,
        resp_kv,
        lax.all_gather(prompt_kv, "dp", axis=0),
    )
    my_prompts = lax.dynamic_slice_in_dim(resp_prompt, lax.axis_index("dp") * count, count)
    route = (jnp.arange(n_dp, dtype=jnp.int32)[:, None] == my_prompts[None, :]).astype(BF16)
    outgoing = jnp.dot(route, per_resp.reshape(count, -1), preferred_element_type=F32).astype(BF16)
    outgoing = outgoing.reshape((n_dp,) + one)
    incoming = lax.all_to_all(outgoing, "dp", split_axis=0, concat_axis=0, tiled=True)
    prefix_out = jnp.sum(incoming, axis=0, dtype=F32).astype(BF16)
    return (q_out, self_out, prefix_out)


def shards(prompt_kv, resp_q, resp_kv, out_grad, rewards, resp_prompt, resp_len):
    n_dp = lax.axis_size("dp")
    count = rewards.shape[0]
    prefix_len, width = prompt_kv.shape[1:]
    slots = (count + n_dp - 1) // n_dp
    z = Sizes(
        n_dp, count, slots, width // HD, resp_q.shape[1] // width, resp_q.shape[0] // count, prefix_len
    )
    part = near_shards if count // slots == n_dp else far_shards
    return part(z, prompt_kv, resp_q, resp_kv, out_grad, rewards, resp_prompt, resp_len)


def solution(mesh):
    in_specs = (
        P(None, ("groups", "dp"), "tensor"),
        P(("groups", "dp"), "tensor"),
        P(None, ("groups", "dp"), "tensor"),
        P(("groups", "dp"), "tensor"),
        P(("groups", "dp")),
        P("groups"),
        P(("groups", "dp")),
    )
    out_specs = (
        P(("groups", "dp"), "tensor"),
        P(None, ("groups", "dp"), "tensor"),
        P(None, ("groups", "dp"), "tensor"),
    )
    return jax.shard_map(shards, mesh=mesh, in_specs=in_specs, out_specs=out_specs, check_vma=False)
```

```python
import functools
import math
from typing import NamedTuple

import jax
import jax.numpy as jnp
from jax import lax
from jax.experimental import pallas as pl
from jax.experimental.pallas import tpu as pltpu
from jax.sharding import PartitionSpec as P

HD = 128
NEG = -1e30
TAIL = 16
F32 = jnp.float32
BF16 = jnp.bfloat16
PAIR = 2
FAR = 3
VMEM_BYTES = 63 * 1024 * 1024
GROUP_BYTES = 53 * 1024 * 1024
ANYWHERE = pl.BlockSpec(memory_space=pl.ANY)


class Sizes(NamedTuple):
    n_dp: int
    count: int
    slots: int
    kv_heads: int
    group_size: int
    tokens: int
    prefix_len: int

    @property
    def width(self):
        return self.kv_heads * HD

    @property
    def lanes(self):
        return self.kv_heads * self.group_size * HD


def dot(a, b, dims):
    return lax.dot_general(a, b, (dims, ((), ())), preferred_element_type=F32)


NN = ((1,), (0,))
NT = ((1,), (1,))


class Bag:
    pass


class Unit(NamedTuple):
    at: list
    places: list
    k: object
    lens: list
    factors: list


def attend(z, units, q, og, kv, prefix, out, own_out, sink, apart):
    tokens, prefix_len, group_size = z.tokens, z.prefix_len, z.group_size
    scale = 1.0 / math.sqrt(HD)
    log_scale = scale * math.log2(math.e)
    whole = group_size - group_size % 2
    most = max(whole, 2) * tokens
    assert tokens & (tokens - 1) == 0
    token = lax.broadcasted_iota(jnp.int32, (1, most), 1) & (tokens - 1)
    key = lax.broadcasted_iota(jnp.int32, (tokens, most), 0)
    causal = key <= (lax.broadcasted_iota(jnp.int32, (tokens, most), 1) & (tokens - 1))
    left = lax.broadcasted_iota(jnp.int32, (1, 2 * tokens), 1) < tokens

    def columns(index):
        if isinstance(index, int):
            return slice(index * HD, (index + 1) * HD)
        return pl.ds(pl.multiple_of(index * HD, HD), HD)

    def head(k, h):
        return columns(k * group_size + h)

    def rows(ref, c):
        return jnp.concatenate([ref[c.t.at[n], head(c.t.k, h)] for n, h in c.blocks], axis=0)

    def halves(part):
        none = jnp.zeros_like(part)
        return [jnp.where(left, part, none), jnp.where(left, none, part)]

    def over_keys(combine, *parts):
        reduce = jnp.max if combine is jnp.maximum else jnp.sum
        eights = [reduce(part.reshape(-1, 8, part.shape[1]), axis=0) for part in parts]
        return reduce(functools.reduce(combine, eights), axis=0, keepdims=True)

    def own_half(both):
        return jnp.where(left, both[:tokens], both[tokens:])

    def rounded(*parts):
        return jnp.concatenate([part.astype(BF16) for part in parts], axis=0)

    chunks = []
    for unit in units:
        t = Bag()
        t.at, t.places, t.k, t.lens, t.factors = unit
        t.single = len(t.at) == 1
        t.members = range(len(t.at))
        sides = (0, 0) if t.single else (0, 1)
        t.cols = columns(t.k)
        t.key_p, t.value_p = prefix[0, :, t.cols], prefix[1, :, t.cols]
        t.keys = [kv[0, t.at[n], t.cols] for n in sides]
        t.values = [kv[1, t.at[n], t.cols] for n in sides]
        t.key_pair = jnp.concatenate(t.keys, axis=0)
        t.value_pair = jnp.concatenate(t.values, axis=0)
        t.key_t = jnp.concatenate([t.key_p.T, t.key_pair.T], axis=1)
        t.prefix_sums = {n: [] for n in t.members}
        t.self_sums = {n: [] for n in t.members}
        mine = []
        for n in t.members:
            c = Bag()
            c.t, c.side, c.blocks = t, n, [(n, h) for h in range(whole)]
            mine.append(c)
        if group_size % 2:
            c = Bag()
            c.t, c.side, c.blocks = t, None, [(n, group_size - 1) for n in sides]
            mine.append(c)
        t.left_over = len(mine)
        chunks += mine

    def products(c):
        t = c.t
        c.q_rows, c.g_rows = rows(q, c), rows(og, c)
        if c.side is None:
            key_s, value_s = t.key_pair, t.value_pair
        else:
            key_s, value_s = t.keys[c.side], t.values[c.side]
        c.scores = dot(jnp.concatenate([t.key_p, key_s], axis=0), c.q_rows, NT)
        c.gw = dot(jnp.concatenate([t.value_p, value_s], axis=0), c.g_rows, NT)

    def weigh(c):
        scores_p, scores_s = c.scores[:prefix_len], c.scores[prefix_len:]
        c.gw_p, c.gw_s = c.gw[:prefix_len], c.gw[prefix_len:]
        if c.side is None:
            scores_s, c.gw_s = own_half(scores_s), own_half(c.gw_s)
        scores_s = jnp.where(causal[:, : scores_s.shape[1]], scores_s, NEG)
        top = over_keys(jnp.maximum, scores_p, scores_s)
        c.e_p = jnp.exp2((scores_p - top) * log_scale)
        c.e_s = jnp.exp2((scores_s - top) * log_scale)
        total = over_keys(jnp.add, c.e_p, c.e_s)
        weighted = over_keys(jnp.add, c.e_p * c.gw_p, c.e_s * c.gw_s)
        if c.side is None:
            length = jnp.where(left, c.t.lens[0], 0 if c.t.single else c.t.lens[1])
            gain = jnp.where(left, c.t.factors[0], c.t.factors[-1])
        else:
            length, gain = c.t.lens[c.side], c.t.factors[c.side]
        inverse = 1.0 / total
        c.delta = weighted * inverse
        c.gain = inverse * jnp.where(token[:, : total.shape[1]] < length, gain, 0.0)

    def gradients(c):
        w_p, w_s = c.e_p * c.gain, c.e_s * c.gain
        d_p, d_s = w_p * (c.gw_p - c.delta), w_s * (c.gw_s - c.delta)
        if c.side is None:
            d_s, w_s = halves(d_s), halves(w_s)
            c.d_wide = rounded(d_p, *d_s)
            c.d_all = rounded(*halves(d_p), *d_s) if apart else c.d_wide
            c.w_all = rounded(*(halves(w_p) if apart else [w_p]), *w_s)
        else:
            empty = jnp.zeros_like(d_s)
            c.d_wide = rounded(*([d_p, empty, d_s] if c.side else [d_p, d_s, empty]))
            c.d_all = rounded(d_p, d_s)
            c.w_all = rounded(w_p, w_s)

    def outgoing(c):
        t = c.t
        q_grad = (dot(t.key_t, c.d_wide, NN) * scale).astype(BF16).T
        kg = dot(c.d_all, c.q_rows, NN)
        vg = dot(c.w_all, c.g_rows, NN)
        targets = t.members if c.side is None else [c.side]
        for place, (n, h) in enumerate(c.blocks):
            if c.side is not None or place < len(targets):
                out[t.places[n], :, head(t.k, h)] = q_grad[place * tokens : (place + 1) * tokens]
        many = 2 if c.side is None and apart else 1
        for place, n in enumerate(targets):
            if place < many:
                rows_p = slice(place * prefix_len, (place + 1) * prefix_len)
                t.prefix_sums[n if apart else 0].append((kg[rows_p], vg[rows_p]))
            start = many * prefix_len + place * tokens
            rows_s = slice(start, start + tokens)
            t.self_sums[n].append((kg[rows_s], vg[rows_s]))
        t.left_over -= 1
        if t.left_over == 0:
            for n in t.members:
                keys, values = zip(*t.self_sums[n])
                own_out[t.places[n], 0, :, t.cols] = (sum(keys) * scale).astype(BF16)
                own_out[t.places[n], 1, :, t.cols] = sum(values).astype(BF16)
                if apart or n == 0:
                    keys, values = zip(*t.prefix_sums[n])
                    sink(t.places[n], t.cols, sum(keys) * scale, sum(values))

    stages = (products, weigh, gradients, outgoing)
    for step in range(len(chunks) + len(stages) - 1):
        for late, stage in enumerate(stages):
            if 0 <= step - late < len(chunks):
                stage(chunks[step - late])


def token_rows(z, i):
    return pl.ds(pl.multiple_of(i * z.tokens, z.tokens), z.tokens)


def find_responses(z, me, turns, resp_prompt, order):
    for t, turn in enumerate(turns):
        prompt = me ^ turn
        found = t * z.slots
        for i in range(z.count):
            order[found] = i
            found = found + (resp_prompt[me * z.count + i] == prompt).astype(jnp.int32)


def prompt_total(z, me, prompt, resp_prompt, tails, far_rewards):
    sums = jnp.zeros((1, z.width), F32)
    for s in range(tails.shape[0]):
        tail = tails[s].astype(F32)
        sums += tail[0:1] + tail[1:2] + tail[2:3]
    lane = lax.broadcasted_iota(jnp.int32, sums.shape, 1)
    total = jnp.sum(jnp.where(lane == prompt, sums, 0.0))
    for i in range(z.count):
        total += jnp.where(resp_prompt[(me ^ FAR) * z.count + i] == prompt, far_rewards[i], 0.0)
    return total


def reward_factor(z, reward, total, length):
    return (reward - total / z.count) * (z.tokens / length.astype(F32))


def pack_kernel(z, prompt_hbm, rewards_hbm, resp_prompt_hbm, payload, rewards, resp_prompt, staged, sems):
    me = lax.axis_index("dp")
    small = [
        pltpu.make_async_copy(rewards_hbm, rewards, sems.at[0]),
        pltpu.make_async_copy(resp_prompt_hbm, resp_prompt, sems.at[1]),
    ]
    large = [
        pltpu.make_async_copy(
            prompt_hbm.at[n], staged.at[pl.ds(n * z.prefix_len, z.prefix_len)], sems.at[2 + n]
        )
        for n in range(2)
    ]
    for copy in small + large:
        copy.start()
    for copy in small:
        copy.wait()
    lane = lax.broadcasted_iota(jnp.int32, (1, z.width), 1)
    sums = jnp.zeros((1, z.width), F32)
    for i in range(z.count):
        sums += jnp.where(lane == resp_prompt[me * z.count + i], rewards[i], 0.0)
    high = sums.astype(BF16).astype(F32)
    middle = (sums - high).astype(BF16).astype(F32)
    low = sums - high - middle
    row = lax.broadcasted_iota(jnp.int32, (TAIL, z.width), 0)
    pieces = jnp.where(row == 0, high, jnp.where(row == 1, middle, jnp.where(row == 2, low, 0.0)))
    staged[2 * z.prefix_len :, :] = pieces.astype(BF16)
    for copy in large:
        copy.wait()
    last = pltpu.make_async_copy(staged, payload, sems.at[0])
    last.start()
    last.wait()


def tail_copies(z, payloads, tails, sems):
    return [
        pltpu.make_async_copy(payload.at[pl.ds(2 * z.prefix_len, TAIL)], tails.at[n], sems.at[n])
        for n, payload in enumerate(payloads)
    ]


def row_copies(here, there, at_here, at_there, sems):
    (q0, og0, kv0), (q1, og1, kv1) = here, there
    return (
        pltpu.make_async_copy(q0.at[at_here], q1.at[at_there], sems.at[0]),
        pltpu.make_async_copy(og0.at[at_here], og1.at[at_there], sems.at[1]),
        pltpu.make_async_copy(kv0.at[:, at_here], kv1.at[:, at_there], sems.at[2]),
    )


def result_copies(out, own, q_out, self_out, place, at, sems, back=False):
    pairs = [
        (out.at[place], q_out.at[at]),
        (own.at[place], self_out.at[:, at]),
    ]
    return [
        pltpu.make_async_copy(*(reversed(pair) if back else pair), sems.at[place, n])
        for n, pair in enumerate(pairs)
    ]


def sort_kernel(z, ahead, resp_prompt_hbm, q_hbm, og_hbm, kv_hbm, both_out, kv_out, *scratch):
    resp_prompt, order, q, og, kv, sem_small, sem_in, sem_out = scratch
    me = lax.axis_index("dp")
    small = pltpu.make_async_copy(resp_prompt_hbm, resp_prompt, sem_small)
    small.start()
    small.wait()
    find_responses(z, me, ahead, resp_prompt, order)
    held, in_order = (q, og, kv), (both_out.at[0], both_out.at[1], kv_out)
    slots = range(len(ahead) * z.slots)

    def copies_in(slot):
        return row_copies(
            (q_hbm, og_hbm, kv_hbm), held, token_rows(z, order[slot]), token_rows(z, slot), sem_in.at[slot]
        )

    def copies_out(slot):
        rows = token_rows(z, slot)
        return row_copies(held, in_order, rows, rows, sem_out.at[slot])

    for slot in slots:
        for copy in copies_in(slot):
            copy.start()
    for slot in slots:
        for copy in copies_in(slot):
            copy.wait()
        for copy in copies_out(slot):
            copy.start()
    for slot in slots:
        for copy in copies_out(slot):
            copy.wait()


def group_kernel(z, turns, ahead, n_come, aliased, *refs):
    small_hbm, given, tail_hbm = refs[:4], refs[4:7], refs[7 : 7 + FAR]
    refs = refs[7 + FAR :]
    prompts, refs = refs[: len(turns)], refs[len(turns) :]
    come_hbm, refs = refs[:n_come], refs[n_come:]
    if ahead is not None:
        (both, kv_ordered), refs = refs[:2], refs[2:]
    (q_out, self_out), refs = refs[aliased : aliased + 2], refs[aliased + 2 :]
    grads_out, refs = refs[: len(turns)], refs[len(turns) :]
    (resp_prompt, resp_len, rewards, far_rewards, order, lens, factors, q, og, kv, prefix, tails, come, acc, out, own,
     grads, sem_small, sem_tails, sem_prefix, sem_in, sem_out, sem_grads, sem_first) = refs
    me = lax.axis_index("dp")
    n_slots = len(turns) * z.slots
    span = z.slots * z.tokens

    small = [
        pltpu.make_async_copy(src, dst, sem_small.at[n])
        for n, (src, dst) in enumerate(zip(small_hbm, (resp_prompt, resp_len, rewards, far_rewards)))
    ]
    first_rows = ()
    if ahead is not None:
        first_rows = row_copies(
            (both.at[0], both.at[1], kv_ordered), (q, og, kv), pl.ds(ahead * span, span), pl.ds(0, span), sem_first
        )
    prefix_copies = [
        pltpu.make_async_copy(
            prompts[t].at[pl.ds(n * z.prefix_len, z.prefix_len)], prefix.at[t, n], sem_prefix.at[t, n]
        )
        for t in range(len(turns))
        for n in range(2)
    ]
    late = tail_copies(z, tail_hbm, tails, sem_tails)
    late += [pltpu.make_async_copy(src, come, sem_grads.at[0]) for src in come_hbm]
    for copy in [*small, *first_rows, *prefix_copies, *late]:
        copy.start()
    small[0].wait()
    find_responses(z, me, turns, resp_prompt, order)

    def copies_in(slot):
        return row_copies(
            given, (q, og, kv), token_rows(z, order[slot]), token_rows(z, slot), sem_in.at[slot]
        )

    def copies_out(slot):
        return result_copies(out, own, q_out, self_out, slot, token_rows(z, order[slot]), sem_out)

    for slot in range(0 if ahead is None else z.slots, n_slots):
        for copy in copies_in(slot):
            copy.start()
    for copy in small[1:] + late:
        copy.wait()
    for t, turn in enumerate(turns):
        total = prompt_total(z, me, me ^ turn, resp_prompt, tails, far_rewards)
        for slot in range(t * z.slots, (t + 1) * z.slots):
            i = order[slot]
            lens[slot] = resp_len[i]
            factors[slot] = reward_factor(z, rewards[i], total, resp_len[i])
    if n_come:
        acc[0] = come[...].astype(F32)
    else:
        acc[...] = jnp.zeros(acc.shape, F32)
    for copy in prefix_copies:
        copy.wait()

    def step(t, _):
        slots = [t * z.slots + n for n in range(z.slots)]

        def wait_for_slots():
            for slot in slots:
                for copy in copies_in(slot):
                    copy.wait()

        if ahead is None:
            wait_for_slots()
        else:

            @pl.when(t == 0)
            def _():
                for copy in first_rows:
                    copy.wait()

            if len(turns) > 1:
                pl.when(t > 0)(wait_for_slots)

        def sink(_, cols, key_grad, value_grad):
            acc[t, 0, :, cols] += key_grad
            acc[t, 1, :, cols] += value_grad

        units = []
        for pair in range(0, z.slots, PAIR):
            places = slots[pair : pair + PAIR]
            at = [token_rows(z, n) for n in places]
            for k in range(z.kv_heads):
                units.append(Unit(at, places, k, [lens[n] for n in places], [factors[n] for n in places]))
        attend(z, units, q, og, kv, prefix.at[t], out, own, sink, False)
        for slot in slots:
            for copy in copies_out(slot):
                copy.start()
        return 0

    lax.fori_loop(0, len(turns), step, 0)
    grads[...] = acc[...].astype(grads.dtype)
    last = [pltpu.make_async_copy(grads.at[t], grads_out[t], sem_grads.at[t]) for t in range(len(turns))]
    for copy in last:
        copy.start()
    for slot in range(n_slots):
        for copy in copies_out(slot):
            copy.wait()
    for copy in last:
        copy.wait()


def near_shards(z, prompt_kv, resp_q, resp_kv, out_grad, rewards, resp_prompt, resp_len):
    n_dp = z.n_dp
    assert z.slots % PAIR == 0
    shape = jax.ShapeDtypeStruct
    one = (2, z.prefix_len, z.width)
    params = pltpu.CompilerParams(vmem_limit_bytes=VMEM_BYTES)
    cost = pl.CostEstimate(flops=0, bytes_accessed=0, transcendentals=0)
    payload = pl.pallas_call(
        functools.partial(pack_kernel, z),
        out_shape=jax.ShapeDtypeStruct((2 * z.prefix_len + TAIL, z.width), BF16),
        in_specs=[ANYWHERE] * 3,
        out_specs=ANYWHERE,
        scratch_shapes=[
            pltpu.SMEM(rewards.shape, F32),
            pltpu.SMEM(resp_prompt.shape, jnp.int32),
            pltpu.VMEM((2 * z.prefix_len + TAIL, z.width), BF16),
            pltpu.SemaphoreType.DMA((4,)),
        ],
        compiler_params=pltpu.CompilerParams(vmem_limit_bytes=VMEM_BYTES),
        name="pack",
    )(prompt_kv, rewards, resp_prompt)

    assert n_dp == FAR + 1

    def swap(x, s):
        return lax.ppermute(x, "dp", [(i, i ^ s) for i in range(n_dp)])

    payloads = {0: payload, 2: swap(payload, 2), 1: swap(payload, 1)}
    tails = [payloads[s] for s in range(FAR)]
    small = (resp_prompt, resp_len, rewards)
    far_rewards = swap(rewards, FAR)
    smem = [pltpu.SMEM(x.shape, x.dtype) for x in (*small, rewards)]
    slots = z.slots

    given = (resp_q, out_grad, resp_kv)
    n_ahead = 2 * slots * z.tokens
    in_order = pl.pallas_call(
        functools.partial(sort_kernel, z, (2, FAR)),
        out_shape=[shape((2, n_ahead, z.lanes), BF16), shape((2, n_ahead, z.width), BF16)],
        in_specs=[ANYWHERE] * 4,
        out_specs=[ANYWHERE] * 2,
        scratch_shapes=[
            smem[0],
            pltpu.SMEM((2 * slots + 1,), jnp.int32),
            pltpu.VMEM((n_ahead, z.lanes), BF16),
            pltpu.VMEM((n_ahead, z.lanes), BF16),
            pltpu.VMEM((2, n_ahead, z.width), BF16),
            pltpu.SemaphoreType.DMA,
            pltpu.SemaphoreType.DMA((2 * slots, 3)),
            pltpu.SemaphoreType.DMA((2 * slots, 3)),
        ],
        compiler_params=params,
        cost_estimate=cost,
        name="sort_rows",
    )(resp_prompt, *given)
    onward, far_rewards, *in_order = lax.optimization_barrier((payloads[2], far_rewards, *in_order))
    payloads[FAR] = swap(onward, 1)

    def grads_of(turns, ahead, written, come=(), kind=BF16):
        n_slots, n_turns = len(turns) * slots, len(turns)
        rows = () if ahead is None else in_order
        prompts = [payloads[turn] for turn in turns]
        operands = [*small, far_rewards, *given, *tails, *prompts, *come, *rows, *written]
        return pl.pallas_call(
            functools.partial(group_kernel, z, turns, ahead, len(come), len(written)),
            out_shape=[shape(resp_q.shape, BF16), shape(resp_kv.shape, BF16)] + [shape(one, kind)] * n_turns,
            in_specs=[ANYWHERE] * len(operands),
            out_specs=[ANYWHERE] * (2 + n_turns),
            input_output_aliases={len(operands) - 2: 0, len(operands) - 1: 1} if written else {},
            scratch_shapes=[
                *smem,
                pltpu.SMEM((n_slots + 1,), jnp.int32),
                pltpu.SMEM((n_slots,), jnp.int32),
                pltpu.SMEM((n_slots,), F32),
                pltpu.VMEM((n_slots * z.tokens, z.lanes), BF16),
                pltpu.VMEM((n_slots * z.tokens, z.lanes), BF16),
                pltpu.VMEM((2, n_slots * z.tokens, z.width), BF16),
                pltpu.VMEM((n_turns,) + one, BF16),
                pltpu.VMEM((FAR, TAIL, z.width), BF16),
                pltpu.VMEM(one, BF16),
                pltpu.VMEM((n_turns,) + one, F32),
                pltpu.VMEM((n_slots, z.tokens, z.lanes), BF16),
                pltpu.VMEM((n_slots, 2, z.tokens, z.width), BF16),
                pltpu.VMEM((n_turns,) + one, kind),
                pltpu.SemaphoreType.DMA((len(smem),)),
                pltpu.SemaphoreType.DMA((FAR,)),
                pltpu.SemaphoreType.DMA((n_turns, 2)),
                pltpu.SemaphoreType.DMA((n_slots, 3)),
                pltpu.SemaphoreType.DMA((n_slots, 2)),
                pltpu.SemaphoreType.DMA((n_turns,)),
                pltpu.SemaphoreType.DMA((3,)),
            ],
            compiler_params=pltpu.CompilerParams(vmem_limit_bytes=GROUP_BYTES),
            cost_estimate=cost,
            name="group_grads" if turns[0] else "own_grads",
        )(*operands)

    *written, for_2 = grads_of((2,), 0, ())
    come = [swap(for_2, 2)]
    *written, for_far, for_1 = grads_of((FAR, 1), 1, written)
    last = [swap(for_far, FAR), swap(for_1, 1)]
    q_out, self_out, summed = grads_of((0,), None, written, come, F32)
    prefix_out = (summed + sum(part.astype(F32) for part in last)).astype(BF16)
    return (q_out, self_out, prefix_out)


def far_kernel(z, *refs):
    (resp_prompt, resp_len, rewards, q_hbm, og_hbm, kv_hbm, prompts, q_out, self_out, prefix_outs,
     totals, lens, factors, q, og, kv, prefix, out, own, grads, sem_in, sem_prefix, sem_out) = refs
    me = lax.axis_index("dp")

    for p in range(z.n_dp):
        totals[p] = 0.0

    def copies_in(slot):
        rows = token_rows(z, slot)
        prompt = resp_prompt[me * z.count + slot]
        return (
            *row_copies((q_hbm, og_hbm, kv_hbm), (q, og, kv), rows, rows, sem_in.at[slot]),
            pltpu.make_async_copy(prompts.at[prompt], prefix.at[slot], sem_prefix.at[slot]),
        )

    def copies_out(slot):
        rows = token_rows(z, slot)
        return (
            *result_copies(out, own, q_out, self_out, slot, rows, sem_out),
            pltpu.make_async_copy(grads.at[slot], prefix_outs.at[slot], sem_out.at[slot, 3]),
        )

    def start(slot, _):
        for copy in copies_in(slot):
            copy.start()
        return 0

    lax.fori_loop(0, z.count, start, 0)

    def add(i, _):
        prompt = resp_prompt[i]
        totals[prompt] = totals[prompt] + rewards[i]
        return 0

    lax.fori_loop(0, z.n_dp * z.count, add, 0)

    def find_factor(slot, _):
        place = me * z.count + slot
        lens[slot] = resp_len[slot]
        factors[slot] = reward_factor(z, rewards[place], totals[resp_prompt[place]], resp_len[slot])
        return 0

    lax.fori_loop(0, z.count, find_factor, 0)

    def unit(slot, _):
        for copy in copies_in(slot):
            copy.wait()

        def sink(_, cols, key_grad, value_grad):
            grads[slot, 0, :, cols] = key_grad.astype(BF16)
            grads[slot, 1, :, cols] = value_grad.astype(BF16)

        units = [
            Unit([token_rows(z, slot)], [slot], k, [lens[slot]], [factors[slot]]) for k in range(z.kv_heads)
        ]
        attend(z, units, q, og, kv, prefix.at[slot], out, own, sink, True)
        for copy in copies_out(slot):
            copy.start()
        return 0

    lax.fori_loop(0, z.count, unit, 0)

    def end(slot, _):
        for copy in copies_out(slot):
            copy.wait()
        return 0

    lax.fori_loop(0, z.count, end, 0)


def far_shards(z, prompt_kv, resp_q, resp_kv, out_grad, rewards, resp_prompt, resp_len):
    assert z.slots == 1
    count, n_dp = z.count, z.n_dp
    one = (2, z.prefix_len, z.width)
    smem = pl.BlockSpec(memory_space=pltpu.SMEM)
    q_out, self_out, per_resp = pl.pallas_call(
        functools.partial(far_kernel, z),
        out_shape=[
            jax.ShapeDtypeStruct(resp_q.shape, BF16),
            jax.ShapeDtypeStruct(resp_kv.shape, BF16),
            jax.ShapeDtypeStruct((count,) + one, BF16),
        ],
        in_specs=[smem] * 3 + [ANYWHERE] * 4,
        out_specs=[ANYWHERE] * 3,
        scratch_shapes=[
            pltpu.SMEM((n_dp,), F32),
            pltpu.SMEM((count,), jnp.int32),
            pltpu.SMEM((count,), F32),
            pltpu.VMEM(resp_q.shape, BF16),
            pltpu.VMEM(resp_q.shape, BF16),
            pltpu.VMEM(resp_kv.shape, BF16),
            pltpu.VMEM((count,) + one, BF16),
            pltpu.VMEM((count, z.tokens, z.lanes), BF16),
            pltpu.VMEM((count, 2, z.tokens, z.width), BF16),
            pltpu.VMEM((count,) + one, BF16),
            pltpu.SemaphoreType.DMA((count, 4)),
            pltpu.SemaphoreType.DMA((count,)),
            pltpu.SemaphoreType.DMA((count, 4)),
        ],
        compiler_params=pltpu.CompilerParams(vmem_limit_bytes=VMEM_BYTES),
        name="far_grads",
    )(
        resp_prompt,
        resp_len,
        lax.all_gather(rewards, "dp", axis=0, tiled=True),
        resp_q,
        out_grad,
        resp_kv,
        lax.all_gather(prompt_kv, "dp", axis=0),
    )
    my_prompts = lax.dynamic_slice_in_dim(resp_prompt, lax.axis_index("dp") * count, count)
    route = (jnp.arange(n_dp, dtype=jnp.int32)[:, None] == my_prompts[None, :]).astype(BF16)
    outgoing = jnp.dot(route, per_resp.reshape(count, -1), preferred_element_type=F32).astype(BF16)
    outgoing = outgoing.reshape((n_dp,) + one)
    incoming = lax.all_to_all(outgoing, "dp", split_axis=0, concat_axis=0, tiled=True)
    prefix_out = jnp.sum(incoming, axis=0, dtype=F32).astype(BF16)
    return (q_out, self_out, prefix_out)


def shards(prompt_kv, resp_q, resp_kv, out_grad, rewards, resp_prompt, resp_len):
    n_dp = lax.axis_size("dp")
    count = rewards.shape[0]
    prefix_len, width = prompt_kv.shape[1:]
    slots = (count + n_dp - 1) // n_dp
    z = Sizes(
        n_dp, count, slots, width // HD, resp_q.shape[1] // width, resp_q.shape[0] // count, prefix_len
    )
    part = near_shards if count // slots == n_dp else far_shards
    return part(z, prompt_kv, resp_q, resp_kv, out_grad, rewards, resp_prompt, resp_len)


def solution(mesh):
    in_specs = (
        P(None, ("groups", "dp"), "tensor"),
        P(("groups", "dp"), "tensor"),
        P(None, ("groups", "dp"), "tensor"),
        P(("groups", "dp"), "tensor"),
        P(("groups", "dp")),
        P("groups"),
        P(("groups", "dp")),
    )
    out_specs = (
        P(("groups", "dp"), "tensor"),
        P(None, ("groups", "dp"), "tensor"),
        P(None, ("groups", "dp"), "tensor"),
    )
    return jax.shard_map(shards, mesh=mesh, in_specs=in_specs, out_specs=out_specs, check_vma=False)
```

```python
import functools
import math
from typing import NamedTuple

import jax
import jax.numpy as jnp
from jax import lax
from jax.experimental import pallas as pl
from jax.experimental.pallas import tpu as pltpu
from jax.sharding import PartitionSpec as P

HD = 128
NEG = -1e30
TAIL = 16
F32 = jnp.float32
BF16 = jnp.bfloat16
PAIR = 2
VMEM_BYTES = 63 * 1024 * 1024
GROUP_BYTES = 55 * 1024 * 1024
OWN_BYTES = 53 * 1024 * 1024
ANYWHERE = pl.BlockSpec(memory_space=pl.ANY)


class Sizes(NamedTuple):
    n_dp: int
    count: int
    slots: int
    kv_heads: int
    group_size: int
    tokens: int
    prefix_len: int

    @property
    def width(self):
        return self.kv_heads * HD

    @property
    def lanes(self):
        return self.kv_heads * self.group_size * HD


def dot(a, b, dims):
    return lax.dot_general(a, b, (dims, ((), ())), preferred_element_type=F32)


NN = ((1,), (0,))
NT = ((1,), (1,))


class Bag:
    pass


class Unit(NamedTuple):
    at: list
    places: list
    k: object
    lens: list
    factors: list


def attend(z, units, q, og, kv, prefix, out, own_out, sink, apart):
    tokens, prefix_len, group_size = z.tokens, z.prefix_len, z.group_size
    scale = 1.0 / math.sqrt(HD)
    log_scale = scale * math.log2(math.e)
    whole = group_size - group_size % 2
    most = max(whole, 2) * tokens
    assert tokens & (tokens - 1) == 0
    token = lax.broadcasted_iota(jnp.int32, (1, most), 1) & (tokens - 1)
    key = lax.broadcasted_iota(jnp.int32, (tokens, most), 0)
    causal = key <= (lax.broadcasted_iota(jnp.int32, (tokens, most), 1) & (tokens - 1))
    left = lax.broadcasted_iota(jnp.int32, (1, 2 * tokens), 1) < tokens

    def columns(index):
        if isinstance(index, int):
            return slice(index * HD, (index + 1) * HD)
        return pl.ds(pl.multiple_of(index * HD, HD), HD)

    def head(k, h):
        return columns(k * group_size + h)

    def rows(ref, c):
        return jnp.concatenate([ref[c.t.at[n], head(c.t.k, h)] for n, h in c.blocks], axis=0)

    def halves(part):
        none = jnp.zeros_like(part)
        return [jnp.where(left, part, none), jnp.where(left, none, part)]

    def over_keys(combine, *parts):
        reduce = jnp.max if combine is jnp.maximum else jnp.sum
        eights = [reduce(part.reshape(-1, 8, part.shape[1]), axis=0) for part in parts]
        return reduce(functools.reduce(combine, eights), axis=0, keepdims=True)

    def own_half(both):
        return jnp.where(left, both[:tokens], both[tokens:])

    def rounded(*parts):
        return jnp.concatenate([part.astype(BF16) for part in parts], axis=0)

    chunks = []
    for unit in units:
        t = Bag()
        t.at, t.places, t.k, t.lens, t.factors = unit
        t.single = len(t.at) == 1
        t.members = range(len(t.at))
        sides = (0, 0) if t.single else (0, 1)
        t.cols = columns(t.k)
        t.key_p, t.value_p = prefix[0, :, t.cols], prefix[1, :, t.cols]
        t.keys = [kv[0, t.at[n], t.cols] for n in sides]
        t.values = [kv[1, t.at[n], t.cols] for n in sides]
        t.key_pair = jnp.concatenate(t.keys, axis=0)
        t.value_pair = jnp.concatenate(t.values, axis=0)
        t.key_t = jnp.concatenate([t.key_p.T, t.key_pair.T], axis=1)
        t.prefix_sums = {n: [] for n in t.members}
        t.self_sums = {n: [] for n in t.members}
        mine = []
        for n in t.members:
            c = Bag()
            c.t, c.side, c.blocks = t, n, [(n, h) for h in range(whole)]
            mine.append(c)
        if group_size % 2:
            c = Bag()
            c.t, c.side, c.blocks = t, None, [(n, group_size - 1) for n in sides]
            mine.append(c)
        t.left_over = len(mine)
        chunks += mine

    def products(c):
        t = c.t
        c.q_rows, c.g_rows = rows(q, c), rows(og, c)
        if c.side is None:
            key_s, value_s = t.key_pair, t.value_pair
        else:
            key_s, value_s = t.keys[c.side], t.values[c.side]
        c.scores = dot(jnp.concatenate([t.key_p, key_s], axis=0), c.q_rows, NT)
        c.gw = dot(jnp.concatenate([t.value_p, value_s], axis=0), c.g_rows, NT)

    def weigh(c):
        scores_p, scores_s = c.scores[:prefix_len], c.scores[prefix_len:]
        c.gw_p, c.gw_s = c.gw[:prefix_len], c.gw[prefix_len:]
        if c.side is None:
            scores_s, c.gw_s = own_half(scores_s), own_half(c.gw_s)
        scores_s = jnp.where(causal[:, : scores_s.shape[1]], scores_s, NEG)
        top = over_keys(jnp.maximum, scores_p, scores_s)
        c.e_p = jnp.exp2((scores_p - top) * log_scale)
        c.e_s = jnp.exp2((scores_s - top) * log_scale)
        total = over_keys(jnp.add, c.e_p, c.e_s)
        weighted = over_keys(jnp.add, c.e_p * c.gw_p, c.e_s * c.gw_s)
        if c.side is None:
            length = jnp.where(left, c.t.lens[0], 0 if c.t.single else c.t.lens[1])
            gain = jnp.where(left, c.t.factors[0], c.t.factors[-1])
        else:
            length, gain = c.t.lens[c.side], c.t.factors[c.side]
        inverse = 1.0 / total
        c.delta = weighted * inverse
        c.gain = inverse * jnp.where(token[:, : total.shape[1]] < length, gain, 0.0)

    def gradients(c):
        w_p, w_s = c.e_p * c.gain, c.e_s * c.gain
        d_p, d_s = w_p * (c.gw_p - c.delta), w_s * (c.gw_s - c.delta)
        if c.side is None:
            d_s, w_s = halves(d_s), halves(w_s)
            c.d_wide = rounded(d_p, *d_s)
            c.d_all = rounded(*halves(d_p), *d_s) if apart else c.d_wide
            c.w_all = rounded(*(halves(w_p) if apart else [w_p]), *w_s)
        else:
            empty = jnp.zeros_like(d_s)
            c.d_wide = rounded(*([d_p, empty, d_s] if c.side else [d_p, d_s, empty]))
            c.d_all = rounded(d_p, d_s)
            c.w_all = rounded(w_p, w_s)

    def outgoing(c):
        t = c.t
        q_grad = (dot(t.key_t, c.d_wide, NN) * scale).astype(BF16).T
        kg = dot(c.d_all, c.q_rows, NN)
        vg = dot(c.w_all, c.g_rows, NN)
        targets = t.members if c.side is None else [c.side]
        for place, (n, h) in enumerate(c.blocks):
            if c.side is not None or place < len(targets):
                out[t.places[n], :, head(t.k, h)] = q_grad[place * tokens : (place + 1) * tokens]
        many = 2 if c.side is None and apart else 1
        for place, n in enumerate(targets):
            if place < many:
                rows_p = slice(place * prefix_len, (place + 1) * prefix_len)
                t.prefix_sums[n if apart else 0].append((kg[rows_p], vg[rows_p]))
            start = many * prefix_len + place * tokens
            rows_s = slice(start, start + tokens)
            t.self_sums[n].append((kg[rows_s], vg[rows_s]))
        t.left_over -= 1
        if t.left_over == 0:
            for n in t.members:
                keys, values = zip(*t.self_sums[n])
                own_out[t.places[n], 0, :, t.cols] = (sum(keys) * scale).astype(BF16)
                own_out[t.places[n], 1, :, t.cols] = sum(values).astype(BF16)
                if apart or n == 0:
                    keys, values = zip(*t.prefix_sums[n])
                    sink(t.places[n], t.cols, sum(keys) * scale, sum(values))

    stages = (products, weigh, gradients, outgoing)
    for step in range(len(chunks) + len(stages) - 1):
        for late, stage in enumerate(stages):
            if 0 <= step - late < len(chunks):
                stage(chunks[step - late])


def token_rows(z, i):
    return pl.ds(pl.multiple_of(i * z.tokens, z.tokens), z.tokens)


def find_responses(z, me, turns, resp_prompt, order):
    for t, turn in enumerate(turns):
        prompt = me ^ turn
        found = t * z.slots
        for i in range(z.count):
            order[found] = i
            found = found + (resp_prompt[me * z.count + i] == prompt).astype(jnp.int32)


def prompt_total(z, prompt, tails):
    sums = jnp.zeros((1, z.width), F32)
    for s in range(z.n_dp):
        tail = tails[s].astype(F32)
        sums += tail[0:1] + tail[1:2] + tail[2:3]
    lane = lax.broadcasted_iota(jnp.int32, sums.shape, 1)
    return jnp.sum(jnp.where(lane == prompt, sums, 0.0))


def reward_factor(z, reward, total, length):
    return (reward - total / z.count) * (z.tokens / length.astype(F32))


def pack_kernel(z, prompt_hbm, rewards_hbm, resp_prompt_hbm, payload, rewards, resp_prompt, staged, sems):
    me = lax.axis_index("dp")
    small = [
        pltpu.make_async_copy(rewards_hbm, rewards, sems.at[0]),
        pltpu.make_async_copy(resp_prompt_hbm, resp_prompt, sems.at[1]),
    ]
    large = [
        pltpu.make_async_copy(
            prompt_hbm.at[n], staged.at[pl.ds(n * z.prefix_len, z.prefix_len)], sems.at[2 + n]
        )
        for n in range(2)
    ]
    for copy in small + large:
        copy.start()
    for copy in small:
        copy.wait()
    lane = lax.broadcasted_iota(jnp.int32, (1, z.width), 1)
    sums = jnp.zeros((1, z.width), F32)
    for i in range(z.count):
        sums += jnp.where(lane == resp_prompt[me * z.count + i], rewards[i], 0.0)
    high = sums.astype(BF16).astype(F32)
    middle = (sums - high).astype(BF16).astype(F32)
    low = sums - high - middle
    row = lax.broadcasted_iota(jnp.int32, (TAIL, z.width), 0)
    pieces = jnp.where(row == 0, high, jnp.where(row == 1, middle, jnp.where(row == 2, low, 0.0)))
    staged[2 * z.prefix_len :, :] = pieces.astype(BF16)
    for copy in large:
        copy.wait()
    last = pltpu.make_async_copy(staged, payload, sems.at[0])
    last.start()
    last.wait()


def row_copies(here, there, at_here, at_there, sems):
    (q0, og0, kv0), (q1, og1, kv1) = here, there
    return (
        pltpu.make_async_copy(q0.at[at_here], q1.at[at_there], sems.at[0]),
        pltpu.make_async_copy(og0.at[at_here], og1.at[at_there], sems.at[1]),
        pltpu.make_async_copy(kv0.at[:, at_here], kv1.at[:, at_there], sems.at[2]),
    )


def result_copies(out, own, q_out, self_out, place, at, sems, back=False):
    pairs = [
        (out.at[place], q_out.at[at]),
        (own.at[place], self_out.at[:, at]),
    ]
    return [
        pltpu.make_async_copy(*(reversed(pair) if back else pair), sems.at[place, n])
        for n, pair in enumerate(pairs)
    ]


def sort_kernel(z, resp_prompt_hbm, q_hbm, og_hbm, kv_hbm, both_out, kv_out, *scratch):
    resp_prompt, order, q, og, kv, sem_small, sem_in, sem_out = scratch
    me = lax.axis_index("dp")
    small = pltpu.make_async_copy(resp_prompt_hbm, resp_prompt, sem_small)
    small.start()
    small.wait()
    find_responses(z, me, range(z.n_dp), resp_prompt, order)
    held, in_order = (q, og, kv), (both_out.at[0], both_out.at[1], kv_out)

    def copies_in(slot):
        return row_copies(
            (q_hbm, og_hbm, kv_hbm), held, token_rows(z, order[slot]), token_rows(z, slot), sem_in.at[slot]
        )

    def copies_out(slot):
        rows = token_rows(z, slot)
        return row_copies(held, in_order, rows, rows, sem_out.at[slot])

    for slot in range(z.count):
        for copy in copies_in(slot):
            copy.start()
    for slot in range(z.count):
        for copy in copies_in(slot):
            copy.wait()
        for copy in copies_out(slot):
            copy.start()
    for slot in range(z.count):
        for copy in copies_out(slot):
            copy.wait()


def group_kernel(z, turns, n_come, aliased, *refs):
    small_hbm, (both, kv_hbm, everyone), refs = refs[:3], refs[3:6], refs[6:]
    come_hbm, refs = refs[:n_come], refs[n_come + aliased :]
    (q_out, self_out), grads_out, refs = refs[:2], refs[2 : 2 + len(turns)], refs[2 + len(turns) :]
    (resp_prompt, resp_len, rewards, order, lens, factors, q, og, kv, prefix, tails, come, acc, out, own,
     grads, sem_small, sem_late, sem_prefix, sem_in, sem_out, sem_grads) = refs
    me = lax.axis_index("dp")
    n_slots = len(turns) * z.slots
    span = z.slots * z.tokens

    small = [
        pltpu.make_async_copy(src, dst, sem_small.at[n])
        for n, (src, dst) in enumerate(zip(small_hbm, (resp_prompt, resp_len, rewards)))
    ]
    late = [pltpu.make_async_copy(everyone.at[:, pl.ds(2 * z.prefix_len, TAIL)], tails, sem_late.at[0])]
    late += [pltpu.make_async_copy(src, come, sem_late.at[1]) for src in come_hbm]
    groups_in = []
    for t, turn in enumerate(turns):
        copies = list(
            row_copies(
                (both.at[0], both.at[1], kv_hbm),
                (q, og, kv),
                pl.ds(turn * span, span),
                pl.ds(t * span, span),
                sem_in.at[t],
            )
        )
        copies += [
            pltpu.make_async_copy(
                everyone.at[me ^ turn, pl.ds(n * z.prefix_len, z.prefix_len)], prefix.at[t, n], sem_prefix.at[t, n]
            )
            for n in range(2)
        ]
        groups_in.append(copies)
    for copy in [*small, *late, *sum(groups_in, [])]:
        copy.start()
    for copy in small + late:
        copy.wait()
    find_responses(z, me, turns, resp_prompt, order)
    for t, turn in enumerate(turns):
        total = prompt_total(z, me ^ turn, tails)
        for slot in range(t * z.slots, (t + 1) * z.slots):
            i = order[slot]
            lens[slot] = resp_len[i]
            factors[slot] = reward_factor(z, rewards[i], total, resp_len[i])
    if n_come:
        acc[0] = come[...].astype(F32)
    else:
        acc[...] = jnp.zeros(acc.shape, F32)

    def copies_out(slot):
        return result_copies(out, own, q_out, self_out, slot, token_rows(z, order[slot]), sem_out)

    def step(t, _):
        slots = [t * z.slots + n for n in range(z.slots)]
        for n, copies in enumerate(groups_in):

            @pl.when(t == n)
            def _():
                for copy in copies:
                    copy.wait()

        def sink(_, cols, key_grad, value_grad):
            acc[t, 0, :, cols] += key_grad
            acc[t, 1, :, cols] += value_grad

        units = []
        for pair in range(0, z.slots, PAIR):
            places = slots[pair : pair + PAIR]
            at = [token_rows(z, n) for n in places]
            for k in range(z.kv_heads):
                units.append(Unit(at, places, k, [lens[n] for n in places], [factors[n] for n in places]))
        attend(z, units, q, og, kv, prefix.at[t], out, own, sink, False)
        for slot in slots:
            for copy in copies_out(slot):
                copy.start()
        return 0

    lax.fori_loop(0, len(turns), step, 0)
    grads[...] = acc[...].astype(grads.dtype)
    last = [pltpu.make_async_copy(grads.at[t], grads_out[t], sem_grads.at[t]) for t in range(len(turns))]
    for copy in last:
        copy.start()
    for slot in range(n_slots):
        for copy in copies_out(slot):
            copy.wait()
    for copy in last:
        copy.wait()


def near_shards(z, prompt_kv, resp_q, resp_kv, out_grad, rewards, resp_prompt, resp_len):
    n_dp = z.n_dp
    assert z.slots % PAIR == 0
    shape = jax.ShapeDtypeStruct
    one = (2, z.prefix_len, z.width)
    params = pltpu.CompilerParams(vmem_limit_bytes=VMEM_BYTES)
    cost = pl.CostEstimate(flops=0, bytes_accessed=0, transcendentals=0)
    payload = pl.pallas_call(
        functools.partial(pack_kernel, z),
        out_shape=jax.ShapeDtypeStruct((2 * z.prefix_len + TAIL, z.width), BF16),
        in_specs=[ANYWHERE] * 3,
        out_specs=ANYWHERE,
        scratch_shapes=[
            pltpu.SMEM(rewards.shape, F32),
            pltpu.SMEM(resp_prompt.shape, jnp.int32),
            pltpu.VMEM((2 * z.prefix_len + TAIL, z.width), BF16),
            pltpu.SemaphoreType.DMA((4,)),
        ],
        compiler_params=pltpu.CompilerParams(vmem_limit_bytes=VMEM_BYTES),
        name="pack",
    )(prompt_kv, rewards, resp_prompt)

    assert n_dp & (n_dp - 1) == 0

    def swap(x, s):
        return lax.ppermute(x, "dp", [(i, i ^ s) for i in range(n_dp)])

    small = (resp_prompt, resp_len, rewards)
    smem = [pltpu.SMEM(x.shape, x.dtype) for x in small]
    slots = z.slots
    everyone = lax.all_gather(payload, "dp")
    in_order = pl.pallas_call(
        functools.partial(sort_kernel, z),
        out_shape=[shape((2,) + resp_q.shape, BF16), shape(resp_kv.shape, BF16)],
        in_specs=[ANYWHERE] * 4,
        out_specs=[ANYWHERE] * 2,
        scratch_shapes=[
            smem[0],
            pltpu.SMEM((z.count + 1,), jnp.int32),
            pltpu.VMEM(resp_q.shape, BF16),
            pltpu.VMEM(resp_q.shape, BF16),
            pltpu.VMEM(resp_kv.shape, BF16),
            pltpu.SemaphoreType.DMA,
            pltpu.SemaphoreType.DMA((z.count, 3)),
            pltpu.SemaphoreType.DMA((z.count, 3)),
        ],
        compiler_params=params,
        cost_estimate=cost,
        name="sort_rows",
    )(resp_prompt, resp_q, out_grad, resp_kv)

    def grads_of(turns, written, come=(), kind=BF16):
        n_slots, n_turns = len(turns) * slots, len(turns)
        operands = [*small, *in_order, everyone, *come, *written]
        return pl.pallas_call(
            functools.partial(group_kernel, z, turns, len(come), len(written)),
            out_shape=[shape(resp_q.shape, BF16), shape(resp_kv.shape, BF16)] + [shape(one, kind)] * n_turns,
            in_specs=[ANYWHERE] * len(operands),
            out_specs=[ANYWHERE] * (2 + n_turns),
            input_output_aliases={len(operands) - 2: 0, len(operands) - 1: 1} if written else {},
            scratch_shapes=[
                *smem,
                pltpu.SMEM((n_slots + 1,), jnp.int32),
                pltpu.SMEM((n_slots,), jnp.int32),
                pltpu.SMEM((n_slots,), F32),
                pltpu.VMEM((n_slots * z.tokens, z.lanes), BF16),
                pltpu.VMEM((n_slots * z.tokens, z.lanes), BF16),
                pltpu.VMEM((2, n_slots * z.tokens, z.width), BF16),
                pltpu.VMEM((n_turns,) + one, BF16),
                pltpu.VMEM((n_dp, TAIL, z.width), BF16),
                pltpu.VMEM(one, BF16),
                pltpu.VMEM((n_turns,) + one, F32),
                pltpu.VMEM((n_slots, z.tokens, z.lanes), BF16),
                pltpu.VMEM((n_slots, 2, z.tokens, z.width), BF16),
                pltpu.VMEM((n_turns,) + one, kind),
                pltpu.SemaphoreType.DMA((len(smem),)),
                pltpu.SemaphoreType.DMA((2,)),
                pltpu.SemaphoreType.DMA((n_turns, 2)),
                pltpu.SemaphoreType.DMA((n_turns, 3)),
                pltpu.SemaphoreType.DMA((n_slots, 2)),
                pltpu.SemaphoreType.DMA((n_turns,)),
            ],
            compiler_params=pltpu.CompilerParams(vmem_limit_bytes=GROUP_BYTES if turns[0] else OWN_BYTES),
            cost_estimate=cost,
            name="group_grads" if turns[0] else "own_grads",
        )(*operands)

    *written, for_2 = grads_of((2,), ())
    come = [swap(for_2, 2)]
    *written, for_far, for_1 = grads_of((3, 1), written)
    last = [swap(for_far, 3), swap(for_1, 1)]
    q_out, self_out, summed = grads_of((0,), written, come, F32)
    prefix_out = (summed + sum(part.astype(F32) for part in last)).astype(BF16)
    return (q_out, self_out, prefix_out)


def far_kernel(z, *refs):
    (resp_prompt, resp_len, rewards, q_hbm, og_hbm, kv_hbm, prompts, q_out, self_out, prefix_outs,
     totals, lens, factors, q, og, kv, prefix, out, own, grads, sem_in, sem_prefix, sem_out) = refs
    me = lax.axis_index("dp")

    for p in range(z.n_dp):
        totals[p] = 0.0

    def copies_in(slot):
        rows = token_rows(z, slot)
        prompt = resp_prompt[me * z.count + slot]
        return (
            *row_copies((q_hbm, og_hbm, kv_hbm), (q, og, kv), rows, rows, sem_in.at[slot]),
            pltpu.make_async_copy(prompts.at[prompt], prefix.at[slot], sem_prefix.at[slot]),
        )

    def copies_out(slot):
        rows = token_rows(z, slot)
        return (
            *result_copies(out, own, q_out, self_out, slot, rows, sem_out),
            pltpu.make_async_copy(grads.at[slot], prefix_outs.at[slot], sem_out.at[slot, 3]),
        )

    def start(slot, _):
        for copy in copies_in(slot):
            copy.start()
        return 0

    lax.fori_loop(0, z.count, start, 0)

    def add(i, _):
        prompt = resp_prompt[i]
        totals[prompt] = totals[prompt] + rewards[i]
        return 0

    lax.fori_loop(0, z.n_dp * z.count, add, 0)

    def find_factor(slot, _):
        place = me * z.count + slot
        lens[slot] = resp_len[slot]
        factors[slot] = reward_factor(z, rewards[place], totals[resp_prompt[place]], resp_len[slot])
        return 0

    lax.fori_loop(0, z.count, find_factor, 0)

    def unit(slot, _):
        for copy in copies_in(slot):
            copy.wait()

        def sink(_, cols, key_grad, value_grad):
            grads[slot, 0, :, cols] = key_grad.astype(BF16)
            grads[slot, 1, :, cols] = value_grad.astype(BF16)

        units = [
            Unit([token_rows(z, slot)], [slot], k, [lens[slot]], [factors[slot]]) for k in range(z.kv_heads)
        ]
        attend(z, units, q, og, kv, prefix.at[slot], out, own, sink, True)
        for copy in copies_out(slot):
            copy.start()
        return 0

    lax.fori_loop(0, z.count, unit, 0)

    def end(slot, _):
        for copy in copies_out(slot):
            copy.wait()
        return 0

    lax.fori_loop(0, z.count, end, 0)


def far_shards(z, prompt_kv, resp_q, resp_kv, out_grad, rewards, resp_prompt, resp_len):
    assert z.slots == 1
    count, n_dp = z.count, z.n_dp
    one = (2, z.prefix_len, z.width)
    smem = pl.BlockSpec(memory_space=pltpu.SMEM)
    q_out, self_out, per_resp = pl.pallas_call(
        functools.partial(far_kernel, z),
        out_shape=[
            jax.ShapeDtypeStruct(resp_q.shape, BF16),
            jax.ShapeDtypeStruct(resp_kv.shape, BF16),
            jax.ShapeDtypeStruct((count,) + one, BF16),
        ],
        in_specs=[smem] * 3 + [ANYWHERE] * 4,
        out_specs=[ANYWHERE] * 3,
        scratch_shapes=[
            pltpu.SMEM((n_dp,), F32),
            pltpu.SMEM((count,), jnp.int32),
            pltpu.SMEM((count,), F32),
            pltpu.VMEM(resp_q.shape, BF16),
            pltpu.VMEM(resp_q.shape, BF16),
            pltpu.VMEM(resp_kv.shape, BF16),
            pltpu.VMEM((count,) + one, BF16),
            pltpu.VMEM((count, z.tokens, z.lanes), BF16),
            pltpu.VMEM((count, 2, z.tokens, z.width), BF16),
            pltpu.VMEM((count,) + one, BF16),
            pltpu.SemaphoreType.DMA((count, 4)),
            pltpu.SemaphoreType.DMA((count,)),
            pltpu.SemaphoreType.DMA((count, 4)),
        ],
        compiler_params=pltpu.CompilerParams(vmem_limit_bytes=VMEM_BYTES),
        name="far_grads",
    )(
        resp_prompt,
        resp_len,
        lax.all_gather(rewards, "dp", axis=0, tiled=True),
        resp_q,
        out_grad,
        resp_kv,
        lax.all_gather(prompt_kv, "dp", axis=0),
    )
    my_prompts = lax.dynamic_slice_in_dim(resp_prompt, lax.axis_index("dp") * count, count)
    route = (jnp.arange(n_dp, dtype=jnp.int32)[:, None] == my_prompts[None, :]).astype(BF16)
    outgoing = jnp.dot(route, per_resp.reshape(count, -1), preferred_element_type=F32).astype(BF16)
    outgoing = outgoing.reshape((n_dp,) + one)
    incoming = lax.all_to_all(outgoing, "dp", split_axis=0, concat_axis=0, tiled=True)
    prefix_out = jnp.sum(incoming, axis=0, dtype=F32).astype(BF16)
    return (q_out, self_out, prefix_out)


def shards(prompt_kv, resp_q, resp_kv, out_grad, rewards, resp_prompt, resp_len):
    n_dp = lax.axis_size("dp")
    count = rewards.shape[0]
    prefix_len, width = prompt_kv.shape[1:]
    slots = (count + n_dp - 1) // n_dp
    z = Sizes(
        n_dp, count, slots, width // HD, resp_q.shape[1] // width, resp_q.shape[0] // count, prefix_len
    )
    part = near_shards if count // slots == n_dp else far_shards
    return part(z, prompt_kv, resp_q, resp_kv, out_grad, rewards, resp_prompt, resp_len)


def solution(mesh):
    in_specs = (
        P(None, ("groups", "dp"), "tensor"),
        P(("groups", "dp"), "tensor"),
        P(None, ("groups", "dp"), "tensor"),
        P(("groups", "dp"), "tensor"),
        P(("groups", "dp")),
        P("groups"),
        P(("groups", "dp")),
    )
    out_specs = (
        P(("groups", "dp"), "tensor"),
        P(None, ("groups", "dp"), "tensor"),
        P(None, ("groups", "dp"), "tensor"),
    )
    return jax.shard_map(shards, mesh=mesh, in_specs=in_specs, out_specs=out_specs, check_vma=False)
```

```python
import functools
import math
from typing import NamedTuple

import jax
import jax.numpy as jnp
from jax import lax
from jax.experimental import pallas as pl
from jax.experimental.pallas import tpu as pltpu
from jax.sharding import PartitionSpec as P

HD = 128
NEG = -1e30
TAIL = 16
F32 = jnp.float32
BF16 = jnp.bfloat16
PAIR = 2
FAR = 3
VMEM_BYTES = 63 * 1024 * 1024
GROUP_BYTES = 53 * 1024 * 1024
FINISH_BYTES = 24 * 1024 * 1024
ANYWHERE = pl.BlockSpec(memory_space=pl.ANY)


class Sizes(NamedTuple):
    n_dp: int
    count: int
    slots: int
    kv_heads: int
    group_size: int
    tokens: int
    prefix_len: int

    @property
    def width(self):
        return self.kv_heads * HD

    @property
    def lanes(self):
        return self.kv_heads * self.group_size * HD


def dot(a, b, dims):
    return lax.dot_general(a, b, (dims, ((), ())), preferred_element_type=F32)


NN = ((1,), (0,))
NT = ((1,), (1,))


class Bag:
    pass


class Unit(NamedTuple):
    at: list
    places: list
    k: object
    lens: list
    factors: list


def attend(z, units, q, og, kv, prefix, out, own_out, sink, apart):
    tokens, prefix_len, group_size = z.tokens, z.prefix_len, z.group_size
    scale = 1.0 / math.sqrt(HD)
    log_scale = scale * math.log2(math.e)
    whole = group_size - group_size % 2
    most = max(whole, 2) * tokens
    assert tokens & (tokens - 1) == 0
    token = lax.broadcasted_iota(jnp.int32, (1, most), 1) & (tokens - 1)
    key = lax.broadcasted_iota(jnp.int32, (tokens, most), 0)
    causal = key <= (lax.broadcasted_iota(jnp.int32, (tokens, most), 1) & (tokens - 1))
    left = lax.broadcasted_iota(jnp.int32, (1, 2 * tokens), 1) < tokens

    def columns(index):
        if isinstance(index, int):
            return slice(index * HD, (index + 1) * HD)
        return pl.ds(pl.multiple_of(index * HD, HD), HD)

    def head(k, h):
        return columns(k * group_size + h)

    def rows(ref, c):
        return jnp.concatenate([ref[c.t.at[n], head(c.t.k, h)] for n, h in c.blocks], axis=0)

    def halves(part):
        none = jnp.zeros_like(part)
        return [jnp.where(left, part, none), jnp.where(left, none, part)]

    def over_keys(combine, *parts):
        reduce = jnp.max if combine is jnp.maximum else jnp.sum
        eights = [reduce(part.reshape(-1, 8, part.shape[1]), axis=0) for part in parts]
        return reduce(functools.reduce(combine, eights), axis=0, keepdims=True)

    def own_half(both):
        return jnp.where(left, both[:tokens], both[tokens:])

    def rounded(*parts):
        return jnp.concatenate([part.astype(BF16) for part in parts], axis=0)

    chunks = []
    for unit in units:
        t = Bag()
        t.at, t.places, t.k, t.lens, t.factors = unit
        t.single = len(t.at) == 1
        t.members = range(len(t.at))
        sides = (0, 0) if t.single else (0, 1)
        t.cols = columns(t.k)
        t.key_p, t.value_p = prefix[0, :, t.cols], prefix[1, :, t.cols]
        t.keys = [kv[0, t.at[n], t.cols] for n in sides]
        t.values = [kv[1, t.at[n], t.cols] for n in sides]
        t.key_pair = jnp.concatenate(t.keys, axis=0)
        t.value_pair = jnp.concatenate(t.values, axis=0)
        t.key_t = jnp.concatenate([t.key_p.T, t.key_pair.T], axis=1)
        t.prefix_sums = {n: [] for n in t.members}
        t.self_sums = {n: [] for n in t.members}
        mine = []
        for n in t.members:
            c = Bag()
            c.t, c.side, c.blocks = t, n, [(n, h) for h in range(whole)]
            mine.append(c)
        if group_size % 2:
            c = Bag()
            c.t, c.side, c.blocks = t, None, [(n, group_size - 1) for n in sides]
            mine.append(c)
        t.left_over = len(mine)
        chunks += mine

    def products(c):
        t = c.t
        c.q_rows, c.g_rows = rows(q, c), rows(og, c)
        if c.side is None:
            key_s, value_s = t.key_pair, t.value_pair
        else:
            key_s, value_s = t.keys[c.side], t.values[c.side]
        c.scores = dot(jnp.concatenate([t.key_p, key_s], axis=0), c.q_rows, NT)
        c.gw = dot(jnp.concatenate([t.value_p, value_s], axis=0), c.g_rows, NT)

    def weigh(c):
        scores_p, scores_s = c.scores[:prefix_len], c.scores[prefix_len:]
        c.gw_p, c.gw_s = c.gw[:prefix_len], c.gw[prefix_len:]
        if c.side is None:
            scores_s, c.gw_s = own_half(scores_s), own_half(c.gw_s)
        scores_s = jnp.where(causal[:, : scores_s.shape[1]], scores_s, NEG)
        top = over_keys(jnp.maximum, scores_p, scores_s)
        c.e_p = jnp.exp2((scores_p - top) * log_scale)
        c.e_s = jnp.exp2((scores_s - top) * log_scale)
        total = over_keys(jnp.add, c.e_p, c.e_s)
        weighted = over_keys(jnp.add, c.e_p * c.gw_p, c.e_s * c.gw_s)
        if c.side is None:
            length = jnp.where(left, c.t.lens[0], 0 if c.t.single else c.t.lens[1])
            gain = jnp.where(left, c.t.factors[0], c.t.factors[-1])
        else:
            length, gain = c.t.lens[c.side], c.t.factors[c.side]
        inverse = 1.0 / total
        c.delta = weighted * inverse
        c.gain = inverse * jnp.where(token[:, : total.shape[1]] < length, gain, 0.0)

    def gradients(c):
        w_p, w_s = c.e_p * c.gain, c.e_s * c.gain
        d_p, d_s = w_p * (c.gw_p - c.delta), w_s * (c.gw_s - c.delta)
        if c.side is None:
            d_s, w_s = halves(d_s), halves(w_s)
            c.d_wide = rounded(d_p, *d_s)
            c.d_all = rounded(*halves(d_p), *d_s) if apart else c.d_wide
            c.w_all = rounded(*(halves(w_p) if apart else [w_p]), *w_s)
        else:
            empty = jnp.zeros_like(d_s)
            c.d_wide = rounded(*([d_p, empty, d_s] if c.side else [d_p, d_s, empty]))
            c.d_all = rounded(d_p, d_s)
            c.w_all = rounded(w_p, w_s)

    def outgoing(c):
        t = c.t
        q_grad = (dot(t.key_t, c.d_wide, NN) * scale).astype(BF16).T
        kg = dot(c.d_all, c.q_rows, NN)
        vg = dot(c.w_all, c.g_rows, NN)
        targets = t.members if c.side is None else [c.side]
        for place, (n, h) in enumerate(c.blocks):
            if c.side is not None or place < len(targets):
                out[t.places[n], :, head(t.k, h)] = q_grad[place * tokens : (place + 1) * tokens]
        many = 2 if c.side is None and apart else 1
        for place, n in enumerate(targets):
            if place < many:
                rows_p = slice(place * prefix_len, (place + 1) * prefix_len)
                t.prefix_sums[n if apart else 0].append((kg[rows_p], vg[rows_p]))
            start = many * prefix_len + place * tokens
            rows_s = slice(start, start + tokens)
            t.self_sums[n].append((kg[rows_s], vg[rows_s]))
        t.left_over -= 1
        if t.left_over == 0:
            for n in t.members:
                keys, values = zip(*t.self_sums[n])
                own_out[t.places[n], 0, :, t.cols] = (sum(keys) * scale).astype(BF16)
                own_out[t.places[n], 1, :, t.cols] = sum(values).astype(BF16)
                if apart or n == 0:
                    keys, values = zip(*t.prefix_sums[n])
                    sink(t.places[n], t.cols, sum(keys) * scale, sum(values))

    stages = (products, weigh, gradients, outgoing)
    for step in range(len(chunks) + len(stages) - 1):
        for late, stage in enumerate(stages):
            if 0 <= step - late < len(chunks):
                stage(chunks[step - late])


def token_rows(z, i):
    return pl.ds(pl.multiple_of(i * z.tokens, z.tokens), z.tokens)


def find_responses(z, me, turns, resp_prompt, order):
    for t, turn in enumerate(turns):
        prompt = me ^ turn
        found = t * z.slots
        for i in range(z.count):
            order[found] = i
            found = found + (resp_prompt[me * z.count + i] == prompt).astype(jnp.int32)


def prompt_total(z, me, prompt, resp_prompt, tails, far_rewards):
    sums = jnp.zeros((1, z.width), F32)
    for s in range(tails.shape[0]):
        tail = tails[s].astype(F32)
        sums += tail[0:1] + tail[1:2] + tail[2:3]
    lane = lax.broadcasted_iota(jnp.int32, sums.shape, 1)
    total = jnp.sum(jnp.where(lane == prompt, sums, 0.0))
    for i in range(z.count):
        total += jnp.where(resp_prompt[(me ^ FAR) * z.count + i] == prompt, far_rewards[i], 0.0)
    return total


def reward_factor(z, reward, total, length):
    return (reward - total / z.count) * (z.tokens / length.astype(F32))


def pack_kernel(z, prompt_hbm, rewards_hbm, resp_prompt_hbm, payload, rewards, resp_prompt, staged, sems):
    me = lax.axis_index("dp")
    small = [
        pltpu.make_async_copy(rewards_hbm, rewards, sems.at[0]),
        pltpu.make_async_copy(resp_prompt_hbm, resp_prompt, sems.at[1]),
    ]
    large = [
        pltpu.make_async_copy(
            prompt_hbm.at[n], staged.at[pl.ds(n * z.prefix_len, z.prefix_len)], sems.at[2 + n]
        )
        for n in range(2)
    ]
    for copy in small + large:
        copy.start()
    for copy in small:
        copy.wait()
    lane = lax.broadcasted_iota(jnp.int32, (1, z.width), 1)
    sums = jnp.zeros((1, z.width), F32)
    for i in range(z.count):
        sums += jnp.where(lane == resp_prompt[me * z.count + i], rewards[i], 0.0)
    high = sums.astype(BF16).astype(F32)
    middle = (sums - high).astype(BF16).astype(F32)
    low = sums - high - middle
    row = lax.broadcasted_iota(jnp.int32, (TAIL, z.width), 0)
    pieces = jnp.where(row == 0, high, jnp.where(row == 1, middle, jnp.where(row == 2, low, 0.0)))
    staged[2 * z.prefix_len :, :] = pieces.astype(BF16)
    for copy in large:
        copy.wait()
    last = pltpu.make_async_copy(staged, payload, sems.at[0])
    last.start()
    last.wait()


def tail_copies(z, payloads, tails, sems):
    return [
        pltpu.make_async_copy(payload.at[pl.ds(2 * z.prefix_len, TAIL)], tails.at[n], sems.at[n])
        for n, payload in enumerate(payloads)
    ]


def row_copies(here, there, at_here, at_there, sems):
    (q0, og0, kv0), (q1, og1, kv1) = here, there
    return (
        pltpu.make_async_copy(q0.at[at_here], q1.at[at_there], sems.at[0]),
        pltpu.make_async_copy(og0.at[at_here], og1.at[at_there], sems.at[1]),
        pltpu.make_async_copy(kv0.at[:, at_here], kv1.at[:, at_there], sems.at[2]),
    )


def result_copies(out, own, q_out, self_out, place, at, sems, back=False):
    pairs = [
        (out.at[place], q_out.at[at]),
        (own.at[place], self_out.at[:, at]),
    ]
    return [
        pltpu.make_async_copy(*(reversed(pair) if back else pair), sems.at[place, n])
        for n, pair in enumerate(pairs)
    ]


def group_kernel(z, turns, raw, body, ahead, n_tails, aliased, *refs):
    small_hbm, given = refs[:4], refs[4:7]
    tail_hbm, prompts = refs[7 : 7 + n_tails], refs[7 + n_tails : 7 + n_tails + len(turns)]
    refs = refs[7 + n_tails + len(turns) :]
    if raw:
        (q_out, self_out), grads_out, in_order, refs = refs[:2], refs[2:3], refs[3:5], refs[5:]
    else:
        in_order, refs = refs[:2], refs[2 + aliased :]
        (q_out, self_out), grads_out, refs = refs[:2], refs[2 : 2 + len(turns)], refs[2 + len(turns) :]
    in_order = (in_order[0].at[0], in_order[0].at[1], in_order[1])
    (resp_prompt, resp_len, rewards, far_rewards, order, lens, factors, q, og, kv, prefix, tails, acc, out, own, grads,
     sem_small, sem_tails, sem_prefix, sem_in, sem_out, sem_grads, sem_order) = refs
    me = lax.axis_index("dp")
    n_slots = len(turns) * z.slots
    span = z.slots * z.tokens

    small = [
        pltpu.make_async_copy(src, dst, sem_small.at[n])
        for n, (src, dst) in enumerate(zip(small_hbm, (resp_prompt, resp_len, rewards, far_rewards)))
    ]
    prefix_copies = [
        pltpu.make_async_copy(
            prompts[t].at[pl.ds(n * z.prefix_len, z.prefix_len)], prefix.at[t, n], sem_prefix.at[t, n]
        )
        for t in range(len(turns))
        for n in range(2)
    ]
    late = tail_copies(z, tail_hbm, tails, sem_tails)
    first_rows = []
    if not raw:
        first_rows = row_copies(in_order, (q, og, kv), pl.ds(ahead * span, span), pl.ds(0, span), sem_order.at[0])
    for copy in [*small, *first_rows, *prefix_copies, *late]:
        copy.start()
    small[0].wait()
    ordered = [*turns, *ahead] if raw else turns
    find_responses(z, me, ordered, resp_prompt, order)

    def copies_in(slot):
        return row_copies(
            given, (q, og, kv), token_rows(z, order[slot]), token_rows(z, slot), sem_in.at[slot]
        )

    def copies_out(slot):
        return result_copies(out, own, q_out, self_out, slot, token_rows(z, order[slot]), sem_out)

    def copies_ordered(slot):
        rows = token_rows(z, slot - n_slots)
        return row_copies((q, og, kv), in_order, token_rows(z, slot), rows, sem_order.at[slot - n_slots])

    for slot in range(0 if raw else z.slots, len(ordered) * z.slots):
        for copy in copies_in(slot):
            copy.start()
    for copy in small[1:] + late:
        copy.wait()
    for t, turn in enumerate(turns):
        total = None if raw else prompt_total(z, me, me ^ turn, resp_prompt, tails, far_rewards)
        for slot in range(t * z.slots, (t + 1) * z.slots):
            i = order[slot]
            lens[slot] = resp_len[i]
            factors[slot] = 1.0 if raw else reward_factor(z, rewards[i], total, resp_len[i])
    if not raw:
        acc[...] = jnp.zeros(acc.shape, F32)
    for copy in prefix_copies:
        copy.wait()

    pairs_in_body = body
    steps_per_turn = z.slots // PAIR // pairs_in_body

    def step(u, _):
        t = u // steps_per_turn
        first = u * pairs_in_body * PAIR
        mine = range(pairs_in_body * PAIR)

        def wait_for_slots():
            for n in mine:
                for copy in copies_in(first + n):
                    copy.wait()

        if raw:
            wait_for_slots()
        else:

            @pl.when(u == 0)
            def _():
                for copy in first_rows:
                    copy.wait()

            if len(turns) > 1:
                pl.when(u >= steps_per_turn)(wait_for_slots)

        def sink(place, cols, key_grad, value_grad):
            if raw:
                grads[place, 0, :, cols] = key_grad.astype(BF16)
                grads[place, 1, :, cols] = value_grad.astype(BF16)
            else:
                acc[t, 0, :, cols] += key_grad
                acc[t, 1, :, cols] += value_grad

        units = []
        for pair in range(pairs_in_body):
            places = [first + pair * PAIR + n for n in range(PAIR)]
            at = [token_rows(z, n) for n in places]
            for k in range(z.kv_heads):
                units.append(Unit(at, places, k, [lens[n] for n in places], [factors[n] for n in places]))
        attend(z, units, q, og, kv, prefix.at[t], out, own, sink, raw)
        for n in mine:
            for copy in copies_out(first + n):
                copy.start()
        if raw:

            @pl.when(u == 0)
            def _():
                def pass_on(slot, _):
                    for copy in copies_in(slot):
                        copy.wait()
                    for copy in copies_ordered(slot):
                        copy.start()
                    return 0

                lax.fori_loop(n_slots, len(ordered) * z.slots, pass_on, 0)

        return 0

    lax.fori_loop(0, len(turns) * steps_per_turn, step, 0)
    if raw:
        last = [pltpu.make_async_copy(grads, grads_out[0], sem_grads.at[0])]
    else:
        grads[...] = acc[...].astype(BF16)
        last = [
            pltpu.make_async_copy(grads.at[t], grads_out[t], sem_grads.at[t]) for t in range(len(turns))
        ]
    for copy in last:
        copy.start()
    for slot in range(n_slots):
        for copy in copies_out(slot):
            copy.wait()
    if raw:
        for slot in range(n_slots, len(ordered) * z.slots):
            for copy in copies_ordered(slot):
                copy.wait()
    for copy in last:
        copy.wait()


def finish_kernel(z, n_tails, n_come, *refs):
    small_hbm, tail_hbm = refs[:4], refs[4 : 4 + n_tails]
    per_resp_hbm, come_hbm = refs[4 + n_tails], refs[5 + n_tails : 5 + n_tails + n_come]
    q_out, self_out, grads_out = refs[7 + n_tails + n_come : 10 + n_tails + n_come]
    (resp_prompt, resp_len, rewards, far_rewards, order, tails, out, own, per_resp, come, grads,
     sem_small, sem_tails, sem_come, sem_in, sem_out) = refs[10 + n_tails + n_come :]
    me = lax.axis_index("dp")
    small = [
        pltpu.make_async_copy(src, dst, sem_small.at[n])
        for n, (src, dst) in enumerate(zip(small_hbm, (resp_prompt, resp_len, rewards, far_rewards)))
    ]
    late = tail_copies(z, tail_hbm, tails, sem_tails)
    late += [pltpu.make_async_copy(src, come.at[n], sem_come.at[n]) for n, src in enumerate(come_hbm)]
    late += [pltpu.make_async_copy(per_resp_hbm, per_resp, sem_come.at[n_come])]
    for copy in small + late:
        copy.start()
    small[0].wait()
    find_responses(z, me, (0,), resp_prompt, order)

    def moves(slot, back):
        sems = sem_in if back else sem_out
        return result_copies(out, own, q_out, self_out, slot, token_rows(z, order[slot]), sems, back)

    for slot in range(z.slots):
        for copy in moves(slot, True):
            copy.start()
    for copy in small[1:] + late:
        copy.wait()
    total = prompt_total(z, me, me, resp_prompt, tails, far_rewards)
    summed = come[0].astype(F32)
    for n in range(1, n_come):
        summed += come[n].astype(F32)
    factors = [reward_factor(z, rewards[order[n]], total, resp_len[order[n]]) for n in range(z.slots)]
    for slot in range(z.slots):
        summed += per_resp[slot].astype(F32) * factors[slot]
    grads[...] = summed
    last = pltpu.make_async_copy(grads, grads_out, sem_small.at[0])
    last.start()
    for slot in range(z.slots):
        for copy in moves(slot, True):
            copy.wait()
        out[slot] = (out[slot].astype(F32) * factors[slot]).astype(BF16)
        own[slot] = (own[slot].astype(F32) * factors[slot]).astype(BF16)
        for copy in moves(slot, False):
            copy.start()
    for slot in range(z.slots):
        for copy in moves(slot, False):
            copy.wait()
    last.wait()


def near_shards(z, prompt_kv, resp_q, resp_kv, out_grad, rewards, resp_prompt, resp_len):
    n_dp = z.n_dp
    assert z.slots % PAIR == 0
    shape = jax.ShapeDtypeStruct
    one = (2, z.prefix_len, z.width)
    params = pltpu.CompilerParams(vmem_limit_bytes=VMEM_BYTES)
    cost = pl.CostEstimate(flops=0, bytes_accessed=0, transcendentals=0)
    payload = pl.pallas_call(
        functools.partial(pack_kernel, z),
        out_shape=jax.ShapeDtypeStruct((2 * z.prefix_len + TAIL, z.width), BF16),
        in_specs=[ANYWHERE] * 3,
        out_specs=ANYWHERE,
        scratch_shapes=[
            pltpu.SMEM(rewards.shape, F32),
            pltpu.SMEM(resp_prompt.shape, jnp.int32),
            pltpu.VMEM((2 * z.prefix_len + TAIL, z.width), BF16),
            pltpu.SemaphoreType.DMA((4,)),
        ],
        compiler_params=pltpu.CompilerParams(vmem_limit_bytes=VMEM_BYTES),
        name="pack",
    )(prompt_kv, rewards, resp_prompt)

    assert n_dp == FAR + 1

    def swap(x, s):
        return lax.ppermute(x, "dp", [(i, i ^ s) for i in range(n_dp)])

    payloads = {0: payload, 2: swap(payload, 2), 1: swap(payload, 1)}
    tails = [payloads[s] for s in range(FAR)]
    small = (resp_prompt, resp_len, rewards)
    far_rewards = swap(rewards, FAR)
    smem = [pltpu.SMEM(x.shape, x.dtype) for x in (*small, rewards)]
    slots = z.slots

    def grads_of(turns, raw, body, ahead, in_order=(), written=()):
        n_slots, n_turns = len(turns) * slots, len(turns)
        n_ahead = len(ahead) * slots if raw else 0
        n_held = n_slots + n_ahead
        used_tails = [] if raw else tails
        used_small = (*small, rewards if raw else far_rewards)
        prompts = [payloads[turn] for turn in turns]
        operands = [*used_small, resp_q, out_grad, resp_kv, *used_tails, *prompts, *in_order, *written]
        grads_shapes = [(slots,) + one] if raw else [one] * n_turns
        ordered_shapes = [(2, n_ahead * z.tokens, z.lanes), (2, n_ahead * z.tokens, z.width)] if raw else []
        return pl.pallas_call(
            functools.partial(group_kernel, z, turns, raw, body, ahead, len(used_tails), len(written)),
            out_shape=[shape(resp_q.shape, BF16), shape(resp_kv.shape, BF16)]
            + [shape(x, BF16) for x in grads_shapes + ordered_shapes],
            in_specs=[ANYWHERE] * len(operands),
            out_specs=[ANYWHERE] * (2 + len(grads_shapes) + len(ordered_shapes)),
            input_output_aliases={len(operands) - 2: 0, len(operands) - 1: 1} if written else {},
            scratch_shapes=[
                *smem,
                pltpu.SMEM((n_held + 1,), jnp.int32),
                pltpu.SMEM((n_slots,), jnp.int32),
                pltpu.SMEM((n_slots,), F32),
                pltpu.VMEM((n_held * z.tokens, z.lanes), BF16),
                pltpu.VMEM((n_held * z.tokens, z.lanes), BF16),
                pltpu.VMEM((2, n_held * z.tokens, z.width), BF16),
                pltpu.VMEM((n_turns,) + one, BF16),
                pltpu.VMEM((FAR, TAIL, z.width), BF16),
                pltpu.VMEM((n_turns,) + one, F32),
                pltpu.VMEM((n_slots, z.tokens, z.lanes), BF16),
                pltpu.VMEM((n_slots, 2, z.tokens, z.width), BF16),
                pltpu.VMEM(grads_shapes[0] if raw else (n_turns,) + one, BF16),
                pltpu.SemaphoreType.DMA((len(smem),)),
                pltpu.SemaphoreType.DMA((FAR,)),
                pltpu.SemaphoreType.DMA((n_turns, 2)),
                pltpu.SemaphoreType.DMA((n_held, 3)),
                pltpu.SemaphoreType.DMA((n_slots, 2)),
                pltpu.SemaphoreType.DMA((n_turns,)),
                pltpu.SemaphoreType.DMA((max(n_ahead, 1), 3)),
            ],
            compiler_params=params if raw else pltpu.CompilerParams(vmem_limit_bytes=GROUP_BYTES),
            cost_estimate=cost,
            name="raw_grads" if raw else "group_grads",
        )(*operands)

    *written, per_resp, rows_ahead, kv_ahead = grads_of((0,), True, 1, (2, FAR))
    in_order = (rows_ahead, kv_ahead)
    onward, per_resp, far_rewards = lax.optimization_barrier((payloads[2], per_resp, far_rewards))
    payloads[FAR] = swap(onward, 1)
    *written, for_2, for_1 = grads_of((2, 1), False, slots // PAIR, 0, in_order, written)
    come = [swap(for_2, 2), swap(for_1, 1)]
    *written, for_far = grads_of((FAR,), False, slots // PAIR, 1, in_order, written)
    last = swap(for_far, FAR)
    operands = [*small, far_rewards, *tails, per_resp, *come, *written]
    q_out, self_out, own_grads = pl.pallas_call(
        functools.partial(finish_kernel, z, len(tails), len(come)),
        out_shape=[shape(resp_q.shape, BF16), shape(resp_kv.shape, BF16), shape(one, F32)],
        in_specs=[ANYWHERE] * len(operands),
        out_specs=[ANYWHERE] * 3,
        input_output_aliases={len(operands) - 2: 0, len(operands) - 1: 1},
        scratch_shapes=[
            *smem,
            pltpu.SMEM((slots + 1,), jnp.int32),
            pltpu.VMEM((FAR, TAIL, z.width), BF16),
            pltpu.VMEM((slots, z.tokens, z.lanes), BF16),
            pltpu.VMEM((slots, 2, z.tokens, z.width), BF16),
            pltpu.VMEM((slots,) + one, BF16),
            pltpu.VMEM((len(come),) + one, BF16),
            pltpu.VMEM(one, F32),
            pltpu.SemaphoreType.DMA((len(smem),)),
            pltpu.SemaphoreType.DMA((FAR,)),
            pltpu.SemaphoreType.DMA((len(come) + 1,)),
            pltpu.SemaphoreType.DMA((slots, 3)),
            pltpu.SemaphoreType.DMA((slots, 3)),
        ],
        compiler_params=pltpu.CompilerParams(vmem_limit_bytes=FINISH_BYTES),
        cost_estimate=cost,
        name="finish_own",
    )(*operands)
    prefix_out = (own_grads + last.astype(F32)).astype(BF16)
    return (q_out, self_out, prefix_out)


def far_kernel(z, *refs):
    (resp_prompt, resp_len, rewards, q_hbm, og_hbm, kv_hbm, prompts, q_out, self_out, prefix_outs,
     totals, lens, factors, q, og, kv, prefix, out, own, grads, sem_in, sem_prefix, sem_out) = refs
    me = lax.axis_index("dp")

    for p in range(z.n_dp):
        totals[p] = 0.0

    def copies_in(slot):
        rows = token_rows(z, slot)
        prompt = resp_prompt[me * z.count + slot]
        return (
            *row_copies((q_hbm, og_hbm, kv_hbm), (q, og, kv), rows, rows, sem_in.at[slot]),
            pltpu.make_async_copy(prompts.at[prompt], prefix.at[slot], sem_prefix.at[slot]),
        )

    def copies_out(slot):
        rows = token_rows(z, slot)
        return (
            *result_copies(out, own, q_out, self_out, slot, rows, sem_out),
            pltpu.make_async_copy(grads.at[slot], prefix_outs.at[slot], sem_out.at[slot, 3]),
        )

    def start(slot, _):
        for copy in copies_in(slot):
            copy.start()
        return 0

    lax.fori_loop(0, z.count, start, 0)

    def add(i, _):
        prompt = resp_prompt[i]
        totals[prompt] = totals[prompt] + rewards[i]
        return 0

    lax.fori_loop(0, z.n_dp * z.count, add, 0)

    def find_factor(slot, _):
        place = me * z.count + slot
        lens[slot] = resp_len[slot]
        factors[slot] = reward_factor(z, rewards[place], totals[resp_prompt[place]], resp_len[slot])
        return 0

    lax.fori_loop(0, z.count, find_factor, 0)

    def unit(slot, _):
        for copy in copies_in(slot):
            copy.wait()

        def sink(_, cols, key_grad, value_grad):
            grads[slot, 0, :, cols] = key_grad.astype(BF16)
            grads[slot, 1, :, cols] = value_grad.astype(BF16)

        units = [
            Unit([token_rows(z, slot)], [slot], k, [lens[slot]], [factors[slot]]) for k in range(z.kv_heads)
        ]
        attend(z, units, q, og, kv, prefix.at[slot], out, own, sink, True)
        for copy in copies_out(slot):
            copy.start()
        return 0

    lax.fori_loop(0, z.count, unit, 0)

    def end(slot, _):
        for copy in copies_out(slot):
            copy.wait()
        return 0

    lax.fori_loop(0, z.count, end, 0)


def far_shards(z, prompt_kv, resp_q, resp_kv, out_grad, rewards, resp_prompt, resp_len):
    assert z.slots == 1
    count, n_dp = z.count, z.n_dp
    one = (2, z.prefix_len, z.width)
    smem = pl.BlockSpec(memory_space=pltpu.SMEM)
    q_out, self_out, per_resp = pl.pallas_call(
        functools.partial(far_kernel, z),
        out_shape=[
            jax.ShapeDtypeStruct(resp_q.shape, BF16),
            jax.ShapeDtypeStruct(resp_kv.shape, BF16),
            jax.ShapeDtypeStruct((count,) + one, BF16),
        ],
        in_specs=[smem] * 3 + [ANYWHERE] * 4,
        out_specs=[ANYWHERE] * 3,
        scratch_shapes=[
            pltpu.SMEM((n_dp,), F32),
            pltpu.SMEM((count,), jnp.int32),
            pltpu.SMEM((count,), F32),
            pltpu.VMEM(resp_q.shape, BF16),
            pltpu.VMEM(resp_q.shape, BF16),
            pltpu.VMEM(resp_kv.shape, BF16),
            pltpu.VMEM((count,) + one, BF16),
            pltpu.VMEM((count, z.tokens, z.lanes), BF16),
            pltpu.VMEM((count, 2, z.tokens, z.width), BF16),
            pltpu.VMEM((count,) + one, BF16),
            pltpu.SemaphoreType.DMA((count, 4)),
            pltpu.SemaphoreType.DMA((count,)),
            pltpu.SemaphoreType.DMA((count, 4)),
        ],
        compiler_params=pltpu.CompilerParams(vmem_limit_bytes=VMEM_BYTES),
        name="far_grads",
    )(
        resp_prompt,
        resp_len,
        lax.all_gather(rewards, "dp", axis=0, tiled=True),
        resp_q,
        out_grad,
        resp_kv,
        lax.all_gather(prompt_kv, "dp", axis=0),
    )
    my_prompts = lax.dynamic_slice_in_dim(resp_prompt, lax.axis_index("dp") * count, count)
    route = (jnp.arange(n_dp, dtype=jnp.int32)[:, None] == my_prompts[None, :]).astype(BF16)
    outgoing = jnp.dot(route, per_resp.reshape(count, -1), preferred_element_type=F32).astype(BF16)
    outgoing = outgoing.reshape((n_dp,) + one)
    incoming = lax.all_to_all(outgoing, "dp", split_axis=0, concat_axis=0, tiled=True)
    prefix_out = jnp.sum(incoming, axis=0, dtype=F32).astype(BF16)
    return (q_out, self_out, prefix_out)


def shards(prompt_kv, resp_q, resp_kv, out_grad, rewards, resp_prompt, resp_len):
    n_dp = lax.axis_size("dp")
    count = rewards.shape[0]
    prefix_len, width = prompt_kv.shape[1:]
    slots = (count + n_dp - 1) // n_dp
    z = Sizes(
        n_dp, count, slots, width // HD, resp_q.shape[1] // width, resp_q.shape[0] // count, prefix_len
    )
    part = near_shards if count // slots == n_dp else far_shards
    return part(z, prompt_kv, resp_q, resp_kv, out_grad, rewards, resp_prompt, resp_len)


def solution(mesh):
    in_specs = (
        P(None, ("groups", "dp"), "tensor"),
        P(("groups", "dp"), "tensor"),
        P(None, ("groups", "dp"), "tensor"),
        P(("groups", "dp"), "tensor"),
        P(("groups", "dp")),
        P("groups"),
        P(("groups", "dp")),
    )
    out_specs = (
        P(("groups", "dp"), "tensor"),
        P(None, ("groups", "dp"), "tensor"),
        P(None, ("groups", "dp"), "tensor"),
    )
    return jax.shard_map(shards, mesh=mesh, in_specs=in_specs, out_specs=out_specs, check_vma=False)
```

```python
import functools
import math
from typing import NamedTuple

import jax
import jax.numpy as jnp
from jax import lax
from jax.experimental import pallas as pl
from jax.experimental.pallas import tpu as pltpu
from jax.sharding import PartitionSpec as P

HD = 128
NEG = -1e30
TAIL = 16
F32 = jnp.float32
BF16 = jnp.bfloat16
PAIR = 2
FAR = 3
VMEM_BYTES = 63 * 1024 * 1024
GROUP_BYTES = 53 * 1024 * 1024
FINISH_BYTES = 24 * 1024 * 1024
ANYWHERE = pl.BlockSpec(memory_space=pl.ANY)


class Sizes(NamedTuple):
    n_dp: int
    count: int
    slots: int
    kv_heads: int
    group_size: int
    tokens: int
    prefix_len: int

    @property
    def width(self):
        return self.kv_heads * HD

    @property
    def lanes(self):
        return self.kv_heads * self.group_size * HD


def dot(a, b, dims):
    return lax.dot_general(a, b, (dims, ((), ())), preferred_element_type=F32)


NN = ((1,), (0,))
NT = ((1,), (1,))


class Bag:
    pass


class Unit(NamedTuple):
    at: list
    places: list
    k: object
    lens: list
    factors: list


def attend(z, units, q, og, kv, prefix, out, own_out, sink, apart):
    tokens, prefix_len, group_size = z.tokens, z.prefix_len, z.group_size
    scale = 1.0 / math.sqrt(HD)
    log_scale = scale * math.log2(math.e)
    whole = group_size - group_size % 2
    most = max([whole, 2, *(len(unit.at) for unit in units)]) * tokens
    assert tokens & (tokens - 1) == 0
    lane = lax.broadcasted_iota(jnp.int32, (1, most), 1)
    token = lane & (tokens - 1)
    key = lax.broadcasted_iota(jnp.int32, (tokens, most), 0)
    causal = key <= (lax.broadcasted_iota(jnp.int32, (tokens, most), 1) & (tokens - 1))

    def columns(index):
        if isinstance(index, int):
            return slice(index * HD, (index + 1) * HD)
        return pl.ds(pl.multiple_of(index * HD, HD), HD)

    def head(k, h):
        return columns(k * group_size + h)

    def rows(ref, c):
        return jnp.concatenate([ref[c.t.at[n], head(c.t.k, h)] for n, h in c.blocks], axis=0)

    def side_lanes(n, lanes):
        return (lane[:, :lanes] >= n * tokens) & (lane[:, :lanes] < (n + 1) * tokens)

    def by_side(parts):
        lanes = len(parts) * tokens
        chosen = parts[0]
        for n, part in enumerate(parts[1:], 1):
            chosen = jnp.where(lane[:, :lanes] >= n * tokens, part, chosen)
        return chosen

    def apart_by_side(part):
        none = jnp.zeros_like(part)
        lanes = part.shape[1]
        return [jnp.where(side_lanes(n, lanes), part, none) for n in range(lanes // tokens)]

    def over_keys(combine, *parts):
        reduce = jnp.max if combine is jnp.maximum else jnp.sum
        eights = [reduce(part.reshape(-1, 8, part.shape[1]), axis=0) for part in parts]
        return reduce(functools.reduce(combine, eights), axis=0, keepdims=True)

    def own_rows(every):
        return by_side([every[n * tokens : (n + 1) * tokens] for n in range(every.shape[0] // tokens)])

    def rounded(*parts):
        return jnp.concatenate([part.astype(BF16) for part in parts], axis=0)

    chunks = []
    for unit in units:
        t = Bag()
        t.at, t.places, t.k, t.lens, t.factors = unit
        t.members = range(len(t.at))
        sides = (0, 0) if len(t.at) == 1 else t.members
        t.cols = columns(t.k)
        t.key_p, t.value_p = prefix[0, :, t.cols], prefix[1, :, t.cols]
        t.keys = [kv[0, t.at[n], t.cols] for n in sides]
        t.values = [kv[1, t.at[n], t.cols] for n in sides]
        t.key_pt = t.key_p.T
        t.key_st = [jnp.concatenate(t.keys[n : n + 2], axis=0).T for n in range(0, len(sides), 2)]
        t.prefix_sums = {n: [] for n in t.members}
        t.self_sums = {n: [] for n in t.members}
        mine = []
        for n in t.members:
            c = Bag()
            c.t, c.side, c.blocks = t, n, [(n, h) for h in range(whole)]
            mine.append(c)
        if group_size % 2:
            c = Bag()
            c.t, c.side, c.blocks = t, None, [(n, group_size - 1) for n in sides]
            mine.append(c)
        t.left_over = len(mine)
        chunks += mine

    def products(c):
        t = c.t
        c.q_rows, c.g_rows = rows(q, c), rows(og, c)
        if c.side is None:
            keys, values = t.keys, t.values
        else:
            keys, values = t.keys[c.side : c.side + 1], t.values[c.side : c.side + 1]
        c.scores = dot(jnp.concatenate([t.key_p, *keys], axis=0), c.q_rows, NT)
        c.gw = dot(jnp.concatenate([t.value_p, *values], axis=0), c.g_rows, NT)

    def weigh(c):
        scores_p, scores_s = c.scores[:prefix_len], c.scores[prefix_len:]
        c.gw_p, c.gw_s = c.gw[:prefix_len], c.gw[prefix_len:]
        if c.side is None:
            scores_s, c.gw_s = own_rows(scores_s), own_rows(c.gw_s)
        scores_s = jnp.where(causal[:, : scores_s.shape[1]], scores_s, NEG)
        top = over_keys(jnp.maximum, scores_p, scores_s)
        c.e_p = jnp.exp2((scores_p - top) * log_scale)
        c.e_s = jnp.exp2((scores_s - top) * log_scale)
        total = over_keys(jnp.add, c.e_p, c.e_s)
        weighted = over_keys(jnp.add, c.e_p * c.gw_p, c.e_s * c.gw_s)
        if c.side is None:
            single = len(c.t.at) == 1
            length = by_side([c.t.lens[0], 0] if single else c.t.lens)
            gain = by_side([c.t.factors[0]] * 2 if single else c.t.factors)
        else:
            length, gain = c.t.lens[c.side], c.t.factors[c.side]
        inverse = 1.0 / total
        c.delta = weighted * inverse
        c.gain = inverse * jnp.where(token[:, : total.shape[1]] < length, gain, 0.0)

    def gradients(c):
        w_p, w_s = c.e_p * c.gain, c.e_s * c.gain
        d_p, d_s = w_p * (c.gw_p - c.delta), w_s * (c.gw_s - c.delta)
        if c.side is None:
            d_s, w_s = apart_by_side(d_s), apart_by_side(w_s)
            c.d_wide = rounded(d_p, *d_s)
            c.d_all = rounded(*apart_by_side(d_p), *d_s) if apart else c.d_wide
            c.w_all = rounded(*(apart_by_side(w_p) if apart else [w_p]), *w_s)
        else:
            empty = jnp.zeros_like(d_s)
            c.d_wide = rounded(*([d_p, empty, d_s] if c.side % 2 else [d_p, d_s, empty]))
            c.d_all = rounded(d_p, d_s)
            c.w_all = rounded(w_p, w_s)

    def outgoing(c):
        t = c.t
        key_st = t.key_st if c.side is None else [t.key_st[c.side // 2]]
        key_t = jnp.concatenate([t.key_pt, *key_st], axis=1)
        q_grad = (dot(key_t, c.d_wide, NN) * scale).astype(BF16).T
        kg = dot(c.d_all, c.q_rows, NN)
        vg = dot(c.w_all, c.g_rows, NN)
        targets = t.members if c.side is None else [c.side]
        for place, (n, h) in enumerate(c.blocks):
            if c.side is not None or place < len(targets):
                out[t.places[n], :, head(t.k, h)] = q_grad[place * tokens : (place + 1) * tokens]
        many = len(c.blocks) if c.side is None and apart else 1
        for place, n in enumerate(targets):
            if place < many:
                rows_p = slice(place * prefix_len, (place + 1) * prefix_len)
                t.prefix_sums[n if apart else 0].append((kg[rows_p], vg[rows_p]))
            start = many * prefix_len + place * tokens
            rows_s = slice(start, start + tokens)
            t.self_sums[n].append((kg[rows_s], vg[rows_s]))
        t.left_over -= 1
        if t.left_over == 0:
            for n in t.members:
                keys, values = zip(*t.self_sums[n])
                own_out[t.places[n], 0, :, t.cols] = (sum(keys) * scale).astype(BF16)
                own_out[t.places[n], 1, :, t.cols] = sum(values).astype(BF16)
                if apart or n == 0:
                    keys, values = zip(*t.prefix_sums[n])
                    sink(t.places[n], t.cols, sum(keys) * scale, sum(values))

    stages = (products, weigh, gradients, outgoing)
    for step in range(len(chunks) + len(stages) - 1):
        for late, stage in enumerate(stages):
            if 0 <= step - late < len(chunks):
                stage(chunks[step - late])


def token_rows(z, i):
    return pl.ds(pl.multiple_of(i * z.tokens, z.tokens), z.tokens)


def find_responses(z, me, turns, resp_prompt, order):
    for t, turn in enumerate(turns):
        prompt = me ^ turn
        found = t * z.slots
        for i in range(z.count):
            order[found] = i
            found = found + (resp_prompt[me * z.count + i] == prompt).astype(jnp.int32)


def prompt_total(z, me, prompt, resp_prompt, tails, far_rewards):
    sums = jnp.zeros((1, z.width), F32)
    for s in range(tails.shape[0]):
        tail = tails[s].astype(F32)
        sums += tail[0:1] + tail[1:2] + tail[2:3]
    lane = lax.broadcasted_iota(jnp.int32, sums.shape, 1)
    total = jnp.sum(jnp.where(lane == prompt, sums, 0.0))
    for i in range(z.count):
        total += jnp.where(resp_prompt[(me ^ FAR) * z.count + i] == prompt, far_rewards[i], 0.0)
    return total


def reward_factor(z, reward, total, length):
    return (reward - total / z.count) * (z.tokens / length.astype(F32))


def pack_kernel(z, prompt_hbm, rewards_hbm, resp_prompt_hbm, payload, rewards, resp_prompt, staged, sems):
    me = lax.axis_index("dp")
    small = [
        pltpu.make_async_copy(rewards_hbm, rewards, sems.at[0]),
        pltpu.make_async_copy(resp_prompt_hbm, resp_prompt, sems.at[1]),
    ]
    large = [
        pltpu.make_async_copy(
            prompt_hbm.at[n], staged.at[pl.ds(n * z.prefix_len, z.prefix_len)], sems.at[2 + n]
        )
        for n in range(2)
    ]
    for copy in small + large:
        copy.start()
    for copy in small:
        copy.wait()
    lane = lax.broadcasted_iota(jnp.int32, (1, z.width), 1)
    sums = jnp.zeros((1, z.width), F32)
    for i in range(z.count):
        sums += jnp.where(lane == resp_prompt[me * z.count + i], rewards[i], 0.0)
    high = sums.astype(BF16).astype(F32)
    middle = (sums - high).astype(BF16).astype(F32)
    low = sums - high - middle
    row = lax.broadcasted_iota(jnp.int32, (TAIL, z.width), 0)
    pieces = jnp.where(row == 0, high, jnp.where(row == 1, middle, jnp.where(row == 2, low, 0.0)))
    staged[2 * z.prefix_len :, :] = pieces.astype(BF16)
    for copy in large:
        copy.wait()
    last = pltpu.make_async_copy(staged, payload, sems.at[0])
    last.start()
    last.wait()


def tail_copies(z, payloads, tails, sems):
    return [
        pltpu.make_async_copy(payload.at[pl.ds(2 * z.prefix_len, TAIL)], tails.at[n], sems.at[n])
        for n, payload in enumerate(payloads)
    ]


def row_copies(here, there, at_here, at_there, sems):
    (q0, og0, kv0), (q1, og1, kv1) = here, there
    return (
        pltpu.make_async_copy(q0.at[at_here], q1.at[at_there], sems.at[0]),
        pltpu.make_async_copy(og0.at[at_here], og1.at[at_there], sems.at[1]),
        pltpu.make_async_copy(kv0.at[:, at_here], kv1.at[:, at_there], sems.at[2]),
    )


def result_copies(out, own, q_out, self_out, place, at, sems, back=False):
    pairs = [
        (out.at[place], q_out.at[at]),
        (own.at[place], self_out.at[:, at]),
    ]
    return [
        pltpu.make_async_copy(*(reversed(pair) if back else pair), sems.at[place, n])
        for n, pair in enumerate(pairs)
    ]


def group_kernel(z, turns, raw, body, ahead, n_tails, aliased, *refs):
    small_hbm, given = refs[:4], refs[4:7]
    tail_hbm, prompts = refs[7 : 7 + n_tails], refs[7 + n_tails : 7 + n_tails + len(turns)]
    refs = refs[7 + n_tails + len(turns) :]
    if raw:
        (q_out, self_out), grads_out, in_order, refs = refs[:2], refs[2:3], refs[3:5], refs[5:]
    else:
        in_order, refs = refs[:2], refs[2 + aliased :]
        (q_out, self_out), grads_out, refs = refs[:2], refs[2 : 2 + len(turns)], refs[2 + len(turns) :]
    in_order = (in_order[0].at[0], in_order[0].at[1], in_order[1])
    (resp_prompt, resp_len, rewards, far_rewards, order, lens, factors, q, og, kv, prefix, tails, acc, out, own, grads,
     sem_small, sem_tails, sem_prefix, sem_in, sem_out, sem_grads, sem_order) = refs
    me = lax.axis_index("dp")
    n_slots = len(turns) * z.slots
    span = z.slots * z.tokens

    small = [
        pltpu.make_async_copy(src, dst, sem_small.at[n])
        for n, (src, dst) in enumerate(zip(small_hbm, (resp_prompt, resp_len, rewards, far_rewards)))
    ]
    prefix_copies = [
        pltpu.make_async_copy(
            prompts[t].at[pl.ds(n * z.prefix_len, z.prefix_len)], prefix.at[t, n], sem_prefix.at[t, n]
        )
        for t in range(len(turns))
        for n in range(2)
    ]
    late = tail_copies(z, tail_hbm, tails, sem_tails)
    first_rows = []
    if not raw:
        first_rows = row_copies(in_order, (q, og, kv), pl.ds(ahead * span, span), pl.ds(0, span), sem_order.at[0])
    for copy in [*small, *first_rows, *prefix_copies, *late]:
        copy.start()
    small[0].wait()
    ordered = [*turns, *ahead] if raw else turns
    find_responses(z, me, ordered, resp_prompt, order)

    def copies_in(slot):
        return row_copies(
            given, (q, og, kv), token_rows(z, order[slot]), token_rows(z, slot), sem_in.at[slot]
        )

    def copies_out(slot):
        return result_copies(out, own, q_out, self_out, slot, token_rows(z, order[slot]), sem_out)

    def copies_ordered(slot):
        rows = token_rows(z, slot - n_slots)
        return row_copies((q, og, kv), in_order, token_rows(z, slot), rows, sem_order.at[slot - n_slots])

    for slot in range(0 if raw else z.slots, len(ordered) * z.slots):
        for copy in copies_in(slot):
            copy.start()
    for copy in small[1:] + late:
        copy.wait()
    for t, turn in enumerate(turns):
        total = None if raw else prompt_total(z, me, me ^ turn, resp_prompt, tails, far_rewards)
        for slot in range(t * z.slots, (t + 1) * z.slots):
            i = order[slot]
            lens[slot] = resp_len[i]
            factors[slot] = 1.0 if raw else reward_factor(z, rewards[i], total, resp_len[i])
    if not raw:
        acc[...] = jnp.zeros(acc.shape, F32)
    for copy in prefix_copies:
        copy.wait()

    pairs_in_body = body
    steps_per_turn = z.slots // PAIR // pairs_in_body

    def step(u, _):
        t = u // steps_per_turn
        first = u * pairs_in_body * PAIR
        mine = range(pairs_in_body * PAIR)

        def wait_for_slots():
            for n in mine:
                for copy in copies_in(first + n):
                    copy.wait()

        if raw:
            wait_for_slots()
        else:

            @pl.when(u == 0)
            def _():
                for copy in first_rows:
                    copy.wait()

            if len(turns) > 1:
                pl.when(u >= steps_per_turn)(wait_for_slots)

        def sink(place, cols, key_grad, value_grad):
            if raw:
                grads[place, 0, :, cols] = key_grad.astype(BF16)
                grads[place, 1, :, cols] = value_grad.astype(BF16)
            else:
                acc[t, 0, :, cols] += key_grad
                acc[t, 1, :, cols] += value_grad

        places = [first + n for n in mine]
        at = [token_rows(z, n) for n in places]
        units = [
            Unit(at, places, k, [lens[n] for n in places], [factors[n] for n in places]) for k in range(z.kv_heads)
        ]
        attend(z, units, q, og, kv, prefix.at[t], out, own, sink, raw)
        for n in mine:
            for copy in copies_out(first + n):
                copy.start()
        if raw:

            @pl.when(u == 0)
            def _():
                def pass_on(slot, _):
                    for copy in copies_in(slot):
                        copy.wait()
                    for copy in copies_ordered(slot):
                        copy.start()
                    return 0

                lax.fori_loop(n_slots, len(ordered) * z.slots, pass_on, 0)

        return 0

    lax.fori_loop(0, len(turns) * steps_per_turn, step, 0)
    if raw:
        last = [pltpu.make_async_copy(grads, grads_out[0], sem_grads.at[0])]
    else:
        grads[...] = acc[...].astype(BF16)
        last = [
            pltpu.make_async_copy(grads.at[t], grads_out[t], sem_grads.at[t]) for t in range(len(turns))
        ]
    for copy in last:
        copy.start()
    for slot in range(n_slots):
        for copy in copies_out(slot):
            copy.wait()
    if raw:
        for slot in range(n_slots, len(ordered) * z.slots):
            for copy in copies_ordered(slot):
                copy.wait()
    for copy in last:
        copy.wait()


def finish_kernel(z, n_tails, n_come, *refs):
    small_hbm, tail_hbm = refs[:4], refs[4 : 4 + n_tails]
    per_resp_hbm, come_hbm = refs[4 + n_tails], refs[5 + n_tails : 5 + n_tails + n_come]
    q_out, self_out, grads_out = refs[7 + n_tails + n_come : 10 + n_tails + n_come]
    (resp_prompt, resp_len, rewards, far_rewards, order, tails, out, own, per_resp, come, grads,
     sem_small, sem_tails, sem_come, sem_in, sem_out) = refs[10 + n_tails + n_come :]
    me = lax.axis_index("dp")
    small = [
        pltpu.make_async_copy(src, dst, sem_small.at[n])
        for n, (src, dst) in enumerate(zip(small_hbm, (resp_prompt, resp_len, rewards, far_rewards)))
    ]
    late = tail_copies(z, tail_hbm, tails, sem_tails)
    late += [pltpu.make_async_copy(src, come.at[n], sem_come.at[n]) for n, src in enumerate(come_hbm)]
    late += [pltpu.make_async_copy(per_resp_hbm, per_resp, sem_come.at[n_come])]
    for copy in small + late:
        copy.start()
    small[0].wait()
    find_responses(z, me, (0,), resp_prompt, order)

    def moves(slot, back):
        sems = sem_in if back else sem_out
        return result_copies(out, own, q_out, self_out, slot, token_rows(z, order[slot]), sems, back)

    for slot in range(z.slots):
        for copy in moves(slot, True):
            copy.start()
    for copy in small[1:] + late:
        copy.wait()
    total = prompt_total(z, me, me, resp_prompt, tails, far_rewards)
    summed = come[0].astype(F32)
    for n in range(1, n_come):
        summed += come[n].astype(F32)
    factors = [reward_factor(z, rewards[order[n]], total, resp_len[order[n]]) for n in range(z.slots)]
    for slot in range(z.slots):
        summed += per_resp[slot].astype(F32) * factors[slot]
    grads[...] = summed
    last = pltpu.make_async_copy(grads, grads_out, sem_small.at[0])
    last.start()
    for slot in range(z.slots):
        for copy in moves(slot, True):
            copy.wait()
        out[slot] = (out[slot].astype(F32) * factors[slot]).astype(BF16)
        own[slot] = (own[slot].astype(F32) * factors[slot]).astype(BF16)
        for copy in moves(slot, False):
            copy.start()
    for slot in range(z.slots):
        for copy in moves(slot, False):
            copy.wait()
    last.wait()


def near_shards(z, prompt_kv, resp_q, resp_kv, out_grad, rewards, resp_prompt, resp_len):
    n_dp = z.n_dp
    assert z.slots % PAIR == 0
    shape = jax.ShapeDtypeStruct
    one = (2, z.prefix_len, z.width)
    params = pltpu.CompilerParams(vmem_limit_bytes=VMEM_BYTES)
    cost = pl.CostEstimate(flops=0, bytes_accessed=0, transcendentals=0)
    payload = pl.pallas_call(
        functools.partial(pack_kernel, z),
        out_shape=jax.ShapeDtypeStruct((2 * z.prefix_len + TAIL, z.width), BF16),
        in_specs=[ANYWHERE] * 3,
        out_specs=ANYWHERE,
        scratch_shapes=[
            pltpu.SMEM(rewards.shape, F32),
            pltpu.SMEM(resp_prompt.shape, jnp.int32),
            pltpu.VMEM((2 * z.prefix_len + TAIL, z.width), BF16),
            pltpu.SemaphoreType.DMA((4,)),
        ],
        compiler_params=pltpu.CompilerParams(vmem_limit_bytes=VMEM_BYTES),
        name="pack",
    )(prompt_kv, rewards, resp_prompt)

    assert n_dp == FAR + 1

    def swap(x, s):
        return lax.ppermute(x, "dp", [(i, i ^ s) for i in range(n_dp)])

    payloads = {0: payload, 2: swap(payload, 2), 1: swap(payload, 1)}
    tails = [payloads[s] for s in range(FAR)]
    small = (resp_prompt, resp_len, rewards)
    far_rewards = swap(rewards, FAR)
    smem = [pltpu.SMEM(x.shape, x.dtype) for x in (*small, rewards)]
    slots = z.slots

    def grads_of(turns, raw, body, ahead, in_order=(), written=()):
        n_slots, n_turns = len(turns) * slots, len(turns)
        n_ahead = len(ahead) * slots if raw else 0
        n_held = n_slots + n_ahead
        used_tails = [] if raw else tails
        used_small = (*small, rewards if raw else far_rewards)
        prompts = [payloads[turn] for turn in turns]
        operands = [*used_small, resp_q, out_grad, resp_kv, *used_tails, *prompts, *in_order, *written]
        grads_shapes = [(slots,) + one] if raw else [one] * n_turns
        ordered_shapes = [(2, n_ahead * z.tokens, z.lanes), (2, n_ahead * z.tokens, z.width)] if raw else []
        return pl.pallas_call(
            functools.partial(group_kernel, z, turns, raw, body, ahead, len(used_tails), len(written)),
            out_shape=[shape(resp_q.shape, BF16), shape(resp_kv.shape, BF16)]
            + [shape(x, BF16) for x in grads_shapes + ordered_shapes],
            in_specs=[ANYWHERE] * len(operands),
            out_specs=[ANYWHERE] * (2 + len(grads_shapes) + len(ordered_shapes)),
            input_output_aliases={len(operands) - 2: 0, len(operands) - 1: 1} if written else {},
            scratch_shapes=[
                *smem,
                pltpu.SMEM((n_held + 1,), jnp.int32),
                pltpu.SMEM((n_slots,), jnp.int32),
                pltpu.SMEM((n_slots,), F32),
                pltpu.VMEM((n_held * z.tokens, z.lanes), BF16),
                pltpu.VMEM((n_held * z.tokens, z.lanes), BF16),
                pltpu.VMEM((2, n_held * z.tokens, z.width), BF16),
                pltpu.VMEM((n_turns,) + one, BF16),
                pltpu.VMEM((FAR, TAIL, z.width), BF16),
                pltpu.VMEM((n_turns,) + one, F32),
                pltpu.VMEM((n_slots, z.tokens, z.lanes), BF16),
                pltpu.VMEM((n_slots, 2, z.tokens, z.width), BF16),
                pltpu.VMEM(grads_shapes[0] if raw else (n_turns,) + one, BF16),
                pltpu.SemaphoreType.DMA((len(smem),)),
                pltpu.SemaphoreType.DMA((FAR,)),
                pltpu.SemaphoreType.DMA((n_turns, 2)),
                pltpu.SemaphoreType.DMA((n_held, 3)),
                pltpu.SemaphoreType.DMA((n_slots, 2)),
                pltpu.SemaphoreType.DMA((n_turns,)),
                pltpu.SemaphoreType.DMA((max(n_ahead, 1), 3)),
            ],
            compiler_params=params if raw else pltpu.CompilerParams(vmem_limit_bytes=GROUP_BYTES),
            cost_estimate=cost,
            name="raw_grads" if raw else "group_grads",
        )(*operands)

    *written, per_resp, rows_ahead, kv_ahead = grads_of((0,), True, 1, (2, FAR))
    in_order = (rows_ahead, kv_ahead)
    onward, per_resp, far_rewards = lax.optimization_barrier((payloads[2], per_resp, far_rewards))
    payloads[FAR] = swap(onward, 1)
    *written, for_2 = grads_of((2,), False, slots // PAIR, 0, in_order, written)
    come = [swap(for_2, 2)]
    *written, for_far, for_1 = grads_of((FAR, 1), False, slots // PAIR, 1, in_order, written)
    come.append(swap(for_1, 1))
    last = swap(for_far, FAR)
    operands = [*small, far_rewards, *tails, per_resp, *come, *written]
    q_out, self_out, own_grads = pl.pallas_call(
        functools.partial(finish_kernel, z, len(tails), len(come)),
        out_shape=[shape(resp_q.shape, BF16), shape(resp_kv.shape, BF16), shape(one, F32)],
        in_specs=[ANYWHERE] * len(operands),
        out_specs=[ANYWHERE] * 3,
        input_output_aliases={len(operands) - 2: 0, len(operands) - 1: 1},
        scratch_shapes=[
            *smem,
            pltpu.SMEM((slots + 1,), jnp.int32),
            pltpu.VMEM((FAR, TAIL, z.width), BF16),
            pltpu.VMEM((slots, z.tokens, z.lanes), BF16),
            pltpu.VMEM((slots, 2, z.tokens, z.width), BF16),
            pltpu.VMEM((slots,) + one, BF16),
            pltpu.VMEM((len(come),) + one, BF16),
            pltpu.VMEM(one, F32),
            pltpu.SemaphoreType.DMA((len(smem),)),
            pltpu.SemaphoreType.DMA((FAR,)),
            pltpu.SemaphoreType.DMA((len(come) + 1,)),
            pltpu.SemaphoreType.DMA((slots, 3)),
            pltpu.SemaphoreType.DMA((slots, 3)),
        ],
        compiler_params=pltpu.CompilerParams(vmem_limit_bytes=FINISH_BYTES),
        cost_estimate=cost,
        name="finish_own",
    )(*operands)
    prefix_out = (own_grads + last.astype(F32)).astype(BF16)
    return (q_out, self_out, prefix_out)


def far_kernel(z, *refs):
    (resp_prompt, resp_len, rewards, q_hbm, og_hbm, kv_hbm, prompts, q_out, self_out, prefix_outs,
     totals, lens, factors, q, og, kv, prefix, out, own, grads, sem_in, sem_prefix, sem_out) = refs
    me = lax.axis_index("dp")

    for p in range(z.n_dp):
        totals[p] = 0.0

    def copies_in(slot):
        rows = token_rows(z, slot)
        prompt = resp_prompt[me * z.count + slot]
        return (
            *row_copies((q_hbm, og_hbm, kv_hbm), (q, og, kv), rows, rows, sem_in.at[slot]),
            pltpu.make_async_copy(prompts.at[prompt], prefix.at[slot], sem_prefix.at[slot]),
        )

    def copies_out(slot):
        rows = token_rows(z, slot)
        return (
            *result_copies(out, own, q_out, self_out, slot, rows, sem_out),
            pltpu.make_async_copy(grads.at[slot], prefix_outs.at[slot], sem_out.at[slot, 3]),
        )

    def start(slot, _):
        for copy in copies_in(slot):
            copy.start()
        return 0

    lax.fori_loop(0, z.count, start, 0)

    def add(i, _):
        prompt = resp_prompt[i]
        totals[prompt] = totals[prompt] + rewards[i]
        return 0

    lax.fori_loop(0, z.n_dp * z.count, add, 0)

    def find_factor(slot, _):
        place = me * z.count + slot
        lens[slot] = resp_len[slot]
        factors[slot] = reward_factor(z, rewards[place], totals[resp_prompt[place]], resp_len[slot])
        return 0

    lax.fori_loop(0, z.count, find_factor, 0)

    def unit(slot, _):
        for copy in copies_in(slot):
            copy.wait()

        def sink(_, cols, key_grad, value_grad):
            grads[slot, 0, :, cols] = key_grad.astype(BF16)
            grads[slot, 1, :, cols] = value_grad.astype(BF16)

        units = [
            Unit([token_rows(z, slot)], [slot], k, [lens[slot]], [factors[slot]]) for k in range(z.kv_heads)
        ]
        attend(z, units, q, og, kv, prefix.at[slot], out, own, sink, True)
        for copy in copies_out(slot):
            copy.start()
        return 0

    lax.fori_loop(0, z.count, unit, 0)

    def end(slot, _):
        for copy in copies_out(slot):
            copy.wait()
        return 0

    lax.fori_loop(0, z.count, end, 0)


def far_shards(z, prompt_kv, resp_q, resp_kv, out_grad, rewards, resp_prompt, resp_len):
    assert z.slots == 1
    count, n_dp = z.count, z.n_dp
    one = (2, z.prefix_len, z.width)
    smem = pl.BlockSpec(memory_space=pltpu.SMEM)
    q_out, self_out, per_resp = pl.pallas_call(
        functools.partial(far_kernel, z),
        out_shape=[
            jax.ShapeDtypeStruct(resp_q.shape, BF16),
            jax.ShapeDtypeStruct(resp_kv.shape, BF16),
            jax.ShapeDtypeStruct((count,) + one, BF16),
        ],
        in_specs=[smem] * 3 + [ANYWHERE] * 4,
        out_specs=[ANYWHERE] * 3,
        scratch_shapes=[
            pltpu.SMEM((n_dp,), F32),
            pltpu.SMEM((count,), jnp.int32),
            pltpu.SMEM((count,), F32),
            pltpu.VMEM(resp_q.shape, BF16),
            pltpu.VMEM(resp_q.shape, BF16),
            pltpu.VMEM(resp_kv.shape, BF16),
            pltpu.VMEM((count,) + one, BF16),
            pltpu.VMEM((count, z.tokens, z.lanes), BF16),
            pltpu.VMEM((count, 2, z.tokens, z.width), BF16),
            pltpu.VMEM((count,) + one, BF16),
            pltpu.SemaphoreType.DMA((count, 4)),
            pltpu.SemaphoreType.DMA((count,)),
            pltpu.SemaphoreType.DMA((count, 4)),
        ],
        compiler_params=pltpu.CompilerParams(vmem_limit_bytes=VMEM_BYTES),
        name="far_grads",
    )(
        resp_prompt,
        resp_len,
        lax.all_gather(rewards, "dp", axis=0, tiled=True),
        resp_q,
        out_grad,
        resp_kv,
        lax.all_gather(prompt_kv, "dp", axis=0),
    )
    my_prompts = lax.dynamic_slice_in_dim(resp_prompt, lax.axis_index("dp") * count, count)
    route = (jnp.arange(n_dp, dtype=jnp.int32)[:, None] == my_prompts[None, :]).astype(BF16)
    outgoing = jnp.dot(route, per_resp.reshape(count, -1), preferred_element_type=F32).astype(BF16)
    outgoing = outgoing.reshape((n_dp,) + one)
    incoming = lax.all_to_all(outgoing, "dp", split_axis=0, concat_axis=0, tiled=True)
    prefix_out = jnp.sum(incoming, axis=0, dtype=F32).astype(BF16)
    return (q_out, self_out, prefix_out)


def shards(prompt_kv, resp_q, resp_kv, out_grad, rewards, resp_prompt, resp_len):
    n_dp = lax.axis_size("dp")
    count = rewards.shape[0]
    prefix_len, width = prompt_kv.shape[1:]
    slots = (count + n_dp - 1) // n_dp
    z = Sizes(
        n_dp, count, slots, width // HD, resp_q.shape[1] // width, resp_q.shape[0] // count, prefix_len
    )
    part = near_shards if count // slots == n_dp else far_shards
    return part(z, prompt_kv, resp_q, resp_kv, out_grad, rewards, resp_prompt, resp_len)


def solution(mesh):
    in_specs = (
        P(None, ("groups", "dp"), "tensor"),
        P(("groups", "dp"), "tensor"),
        P(None, ("groups", "dp"), "tensor"),
        P(("groups", "dp"), "tensor"),
        P(("groups", "dp")),
        P("groups"),
        P(("groups", "dp")),
    )
    out_specs = (
        P(("groups", "dp"), "tensor"),
        P(None, ("groups", "dp"), "tensor"),
        P(None, ("groups", "dp"), "tensor"),
    )
    return jax.shard_map(shards, mesh=mesh, in_specs=in_specs, out_specs=out_specs, check_vma=False)
```

```python
import functools
import math
from typing import NamedTuple

import jax
import jax.numpy as jnp
from jax import lax
from jax.experimental import pallas as pl
from jax.experimental.pallas import tpu as pltpu
from jax.sharding import PartitionSpec as P

HD = 128
NEG = -1e30
TAIL = 16
F32 = jnp.float32
BF16 = jnp.bfloat16
PAIR = 2
FAR = 3
VMEM_BYTES = 63 * 1024 * 1024
GROUP_BYTES = 53 * 1024 * 1024
FINISH_BYTES = 24 * 1024 * 1024
ANYWHERE = pl.BlockSpec(memory_space=pl.ANY)


class Sizes(NamedTuple):
    n_dp: int
    count: int
    slots: int
    kv_heads: int
    group_size: int
    tokens: int
    prefix_len: int

    @property
    def width(self):
        return self.kv_heads * HD

    @property
    def lanes(self):
        return self.kv_heads * self.group_size * HD


def dot(a, b, dims):
    return lax.dot_general(a, b, (dims, ((), ())), preferred_element_type=F32)


NN = ((1,), (0,))
NT = ((1,), (1,))


class Bag:
    pass


class Unit(NamedTuple):
    at: list
    places: list
    k: object
    lens: list
    factors: list


def attend(z, units, q, og, kv, prefix, out, own_out, sink, apart):
    tokens, prefix_len, group_size = z.tokens, z.prefix_len, z.group_size
    scale = 1.0 / math.sqrt(HD)
    log_scale = scale * math.log2(math.e)
    whole = group_size - group_size % 2
    most = max(whole, 2) * tokens
    assert tokens & (tokens - 1) == 0
    token = lax.broadcasted_iota(jnp.int32, (1, most), 1) & (tokens - 1)
    key = lax.broadcasted_iota(jnp.int32, (tokens, most), 0)
    causal = key <= (lax.broadcasted_iota(jnp.int32, (tokens, most), 1) & (tokens - 1))
    left = lax.broadcasted_iota(jnp.int32, (1, 2 * tokens), 1) < tokens

    def columns(index):
        if isinstance(index, int):
            return slice(index * HD, (index + 1) * HD)
        return pl.ds(pl.multiple_of(index * HD, HD), HD)

    def head(k, h):
        return columns(k * group_size + h)

    def rows(ref, c):
        return jnp.concatenate([ref[c.t.at[n], head(c.t.k, h)] for n, h in c.blocks], axis=0)

    def halves(part):
        none = jnp.zeros_like(part)
        return [jnp.where(left, part, none), jnp.where(left, none, part)]

    def over_keys(combine, *parts):
        reduce = jnp.max if combine is jnp.maximum else jnp.sum
        eights = [reduce(part.reshape(-1, 8, part.shape[1]), axis=0) for part in parts]
        return reduce(functools.reduce(combine, eights), axis=0, keepdims=True)

    def own_half(both):
        return jnp.where(left, both[:tokens], both[tokens:])

    def rounded(*parts):
        return jnp.concatenate([part.astype(BF16) for part in parts], axis=0)

    chunks = []
    for unit in units:
        t = Bag()
        t.at, t.places, t.k, t.lens, t.factors = unit
        t.single = len(t.at) == 1
        t.members = range(len(t.at))
        sides = (0, 0) if t.single else (0, 1)
        t.cols = columns(t.k)
        t.key_p, t.value_p = prefix[0, :, t.cols], prefix[1, :, t.cols]
        t.keys = [kv[0, t.at[n], t.cols] for n in sides]
        t.values = [kv[1, t.at[n], t.cols] for n in sides]
        t.key_pair = jnp.concatenate(t.keys, axis=0)
        t.value_pair = jnp.concatenate(t.values, axis=0)
        t.key_t = jnp.concatenate([t.key_p.T, t.key_pair.T], axis=1)
        t.prefix_sums = {n: [] for n in t.members}
        t.self_sums = {n: [] for n in t.members}
        mine = []
        for n in t.members:
            c = Bag()
            c.t, c.side, c.blocks = t, n, [(n, h) for h in range(whole)]
            mine.append(c)
        if group_size % 2:
            c = Bag()
            c.t, c.side, c.blocks = t, None, [(n, group_size - 1) for n in sides]
            mine.append(c)
        t.left_over = len(mine)
        chunks += mine

    def products(c):
        t = c.t
        c.q_rows, c.g_rows = rows(q, c), rows(og, c)
        if c.side is None:
            key_s, value_s = t.key_pair, t.value_pair
        else:
            key_s, value_s = t.keys[c.side], t.values[c.side]
        c.scores = dot(jnp.concatenate([t.key_p, key_s], axis=0), c.q_rows, NT)
        c.gw = dot(jnp.concatenate([t.value_p, value_s], axis=0), c.g_rows, NT)

    def weigh(c):
        scores_p, scores_s = c.scores[:prefix_len], c.scores[prefix_len:]
        c.gw_p, c.gw_s = c.gw[:prefix_len], c.gw[prefix_len:]
        if c.side is None:
            scores_s, c.gw_s = own_half(scores_s), own_half(c.gw_s)
        scores_s = jnp.where(causal[:, : scores_s.shape[1]], scores_s, NEG)
        top = over_keys(jnp.maximum, scores_p, scores_s)
        c.e_p = jnp.exp2((scores_p - top) * log_scale)
        c.e_s = jnp.exp2((scores_s - top) * log_scale)
        total = over_keys(jnp.add, c.e_p, c.e_s)
        weighted = over_keys(jnp.add, c.e_p * c.gw_p, c.e_s * c.gw_s)
        if c.side is None:
            length = jnp.where(left, c.t.lens[0], 0 if c.t.single else c.t.lens[1])
            gain = jnp.where(left, c.t.factors[0], c.t.factors[-1])
        else:
            length, gain = c.t.lens[c.side], c.t.factors[c.side]
        inverse = 1.0 / total
        c.delta = weighted * inverse
        c.gain = inverse * jnp.where(token[:, : total.shape[1]] < length, gain, 0.0)

    def gradients(c):
        w_p, w_s = c.e_p * c.gain, c.e_s * c.gain
        d_p, d_s = w_p * (c.gw_p - c.delta), w_s * (c.gw_s - c.delta)
        if c.side is None:
            d_s, w_s = halves(d_s), halves(w_s)
            c.d_wide = rounded(d_p, *d_s)
            c.d_all = rounded(*halves(d_p), *d_s) if apart else c.d_wide
            c.w_all = rounded(*(halves(w_p) if apart else [w_p]), *w_s)
        else:
            empty = jnp.zeros_like(d_s)
            c.d_wide = rounded(*([d_p, empty, d_s] if c.side else [d_p, d_s, empty]))
            c.d_all = rounded(d_p, d_s)
            c.w_all = rounded(w_p, w_s)

    def outgoing(c):
        t = c.t
        q_grad = (dot(t.key_t, c.d_wide, NN) * scale).astype(BF16).T
        kg = dot(c.d_all, c.q_rows, NN)
        vg = dot(c.w_all, c.g_rows, NN)
        targets = t.members if c.side is None else [c.side]
        for place, (n, h) in enumerate(c.blocks):
            if c.side is not None or place < len(targets):
                out[t.places[n], :, head(t.k, h)] = q_grad[place * tokens : (place + 1) * tokens]
        many = 2 if c.side is None and apart else 1
        for place, n in enumerate(targets):
            if place < many:
                rows_p = slice(place * prefix_len, (place + 1) * prefix_len)
                t.prefix_sums[n if apart else 0].append((kg[rows_p], vg[rows_p]))
            start = many * prefix_len + place * tokens
            rows_s = slice(start, start + tokens)
            t.self_sums[n].append((kg[rows_s], vg[rows_s]))
        t.left_over -= 1
        if t.left_over == 0:
            for n in t.members:
                keys, values = zip(*t.self_sums[n])
                own_out[t.places[n], 0, :, t.cols] = (sum(keys) * scale).astype(BF16)
                own_out[t.places[n], 1, :, t.cols] = sum(values).astype(BF16)
                if apart or n == 0:
                    keys, values = zip(*t.prefix_sums[n])
                    sink(t.places[n], t.cols, sum(keys) * scale, sum(values))

    stages = (products, weigh, gradients, outgoing)
    for step in range(len(chunks) + len(stages) - 1):
        for late, stage in enumerate(stages):
            if 0 <= step - late < len(chunks):
                stage(chunks[step - late])


def token_rows(z, i):
    return pl.ds(pl.multiple_of(i * z.tokens, z.tokens), z.tokens)


def find_responses(z, me, turns, resp_prompt, order):
    for t, turn in enumerate(turns):
        prompt = me ^ turn
        found = t * z.slots
        for i in range(z.count):
            order[found] = i
            found = found + (resp_prompt[me * z.count + i] == prompt).astype(jnp.int32)


def prompt_total(z, me, prompt, resp_prompt, tails, far_rewards):
    sums = jnp.zeros((1, z.width), F32)
    for s in range(tails.shape[0]):
        tail = tails[s].astype(F32)
        sums += tail[0:1] + tail[1:2] + tail[2:3]
    lane = lax.broadcasted_iota(jnp.int32, sums.shape, 1)
    total = jnp.sum(jnp.where(lane == prompt, sums, 0.0))
    for i in range(z.count):
        total += jnp.where(resp_prompt[(me ^ FAR) * z.count + i] == prompt, far_rewards[i], 0.0)
    return total


def reward_factor(z, reward, total, length):
    return (reward - total / z.count) * (z.tokens / length.astype(F32))


def pack_kernel(z, prompt_hbm, rewards_hbm, resp_prompt_hbm, payload, rewards, resp_prompt, staged, sems):
    me = lax.axis_index("dp")
    small = [
        pltpu.make_async_copy(rewards_hbm, rewards, sems.at[0]),
        pltpu.make_async_copy(resp_prompt_hbm, resp_prompt, sems.at[1]),
    ]
    large = [
        pltpu.make_async_copy(
            prompt_hbm.at[n], staged.at[pl.ds(n * z.prefix_len, z.prefix_len)], sems.at[2 + n]
        )
        for n in range(2)
    ]
    for copy in small + large:
        copy.start()
    for copy in small:
        copy.wait()
    lane = lax.broadcasted_iota(jnp.int32, (1, z.width), 1)
    sums = jnp.zeros((1, z.width), F32)
    for i in range(z.count):
        sums += jnp.where(lane == resp_prompt[me * z.count + i], rewards[i], 0.0)
    high = sums.astype(BF16).astype(F32)
    middle = (sums - high).astype(BF16).astype(F32)
    low = sums - high - middle
    row = lax.broadcasted_iota(jnp.int32, (TAIL, z.width), 0)
    pieces = jnp.where(row == 0, high, jnp.where(row == 1, middle, jnp.where(row == 2, low, 0.0)))
    staged[2 * z.prefix_len :, :] = pieces.astype(BF16)
    for copy in large:
        copy.wait()
    last = pltpu.make_async_copy(staged, payload, sems.at[0])
    last.start()
    last.wait()


def tail_copies(z, payloads, tails, sems):
    return [
        pltpu.make_async_copy(payload.at[pl.ds(2 * z.prefix_len, TAIL)], tails.at[n], sems.at[n])
        for n, payload in enumerate(payloads)
    ]


def row_copies(here, there, at_here, at_there, sems):
    (q0, og0, kv0), (q1, og1, kv1) = here, there
    return (
        pltpu.make_async_copy(q0.at[at_here], q1.at[at_there], sems.at[0]),
        pltpu.make_async_copy(og0.at[at_here], og1.at[at_there], sems.at[1]),
        pltpu.make_async_copy(kv0.at[:, at_here], kv1.at[:, at_there], sems.at[2]),
    )


def result_copies(out, own, q_out, self_out, place, at, sems, back=False):
    pairs = [
        (out.at[place], q_out.at[at]),
        (own.at[place], self_out.at[:, at]),
    ]
    return [
        pltpu.make_async_copy(*(reversed(pair) if back else pair), sems.at[place, n])
        for n, pair in enumerate(pairs)
    ]


def group_kernel(z, turns, raw, body, ahead, n_tails, aliased, *refs):
    small_hbm, given = refs[:4], refs[4:7]
    tail_hbm, prompts = refs[7 : 7 + n_tails], refs[7 + n_tails : 7 + n_tails + len(turns)]
    refs = refs[7 + n_tails + len(turns) :]
    if raw:
        (q_out, self_out), grads_out, in_order, refs = refs[:2], refs[2:3], refs[3:5], refs[5:]
    else:
        in_order, refs = refs[:2], refs[2 + aliased :]
        (q_out, self_out), grads_out, refs = refs[:2], refs[2 : 2 + len(turns)], refs[2 + len(turns) :]
    in_order = (in_order[0].at[0], in_order[0].at[1], in_order[1])
    (resp_prompt, resp_len, rewards, far_rewards, order, q, og, kv, prefix, tails, acc, out, own, grads,
     sem_small, sem_tails, sem_prefix, sem_in, sem_out, sem_grads, sem_order) = refs
    me = lax.axis_index("dp")
    n_slots = len(turns) * z.slots
    span = z.slots * z.tokens

    small = [
        pltpu.make_async_copy(src, dst, sem_small.at[n])
        for n, (src, dst) in enumerate(zip(small_hbm, (resp_prompt, resp_len, rewards, far_rewards)))
    ]
    prefix_copies = [
        pltpu.make_async_copy(
            prompts[t].at[pl.ds(n * z.prefix_len, z.prefix_len)], prefix.at[t, n], sem_prefix.at[t, n]
        )
        for t in range(len(turns))
        for n in range(2)
    ]
    late = tail_copies(z, tail_hbm, tails, sem_tails)
    first_rows = []
    if not raw:
        first_rows = row_copies(in_order, (q, og, kv), pl.ds(ahead * span, span), pl.ds(0, span), sem_order.at[0])
    for copy in [*small, *first_rows, *prefix_copies, *late]:
        copy.start()
    small[0].wait()
    ordered = [*turns, *ahead] if raw else turns
    find_responses(z, me, ordered, resp_prompt, order)

    def copies_in(slot):
        return row_copies(
            given, (q, og, kv), token_rows(z, order[slot]), token_rows(z, slot), sem_in.at[slot]
        )

    def copies_out(slot):
        return result_copies(out, own, q_out, self_out, slot, token_rows(z, order[slot]), sem_out)

    def copies_ordered(slot):
        rows = token_rows(z, slot - n_slots)
        return row_copies((q, og, kv), in_order, token_rows(z, slot), rows, sem_order.at[slot - n_slots])

    for slot in range(0 if raw else z.slots, len(ordered) * z.slots):
        for copy in copies_in(slot):
            copy.start()
    for copy in small[1:] + late:
        copy.wait()
    if not raw:
        acc[...] = jnp.zeros(acc.shape, F32)
    for copy in prefix_copies:
        copy.wait()

    pairs_in_body = body
    steps_per_turn = z.slots // PAIR // pairs_in_body

    def step(u, _):
        t = u // steps_per_turn
        first = u * pairs_in_body * PAIR
        mine = range(pairs_in_body * PAIR)

        def wait_for_slots():
            for n in mine:
                for copy in copies_in(first + n):
                    copy.wait()

        if raw:
            wait_for_slots()
        else:

            @pl.when(u == 0)
            def _():
                for copy in first_rows:
                    copy.wait()

            if len(turns) > 1:
                pl.when(u >= steps_per_turn)(wait_for_slots)

        def sink(place, cols, key_grad, value_grad):
            if raw:
                grads[place, 0, :, cols] = key_grad.astype(BF16)
                grads[place, 1, :, cols] = value_grad.astype(BF16)
            else:
                acc[t, 0, :, cols] += key_grad
                acc[t, 1, :, cols] += value_grad

        turn = turns[0]
        for n, other in enumerate(turns[1:], 1):
            turn = jnp.where(t == n, other, turn)
        total = None if raw else prompt_total(z, me, me ^ turn, resp_prompt, tails, far_rewards)
        lens, factors = {}, {}
        for n in mine:
            i = order[first + n]
            lens[n] = resp_len[i]
            factors[n] = 1.0 if raw else reward_factor(z, rewards[i], total, resp_len[i])
        units = []
        for pair in range(pairs_in_body):
            places = [first + pair * PAIR + n for n in range(PAIR)]
            own_places = range(pair * PAIR, (pair + 1) * PAIR)
            at = [token_rows(z, n) for n in places]
            for k in range(z.kv_heads):
                units.append(Unit(at, places, k, [lens[n] for n in own_places], [factors[n] for n in own_places]))
        attend(z, units, q, og, kv, prefix.at[t], out, own, sink, raw)
        for n in mine:
            for copy in copies_out(first + n):
                copy.start()
        if raw:

            @pl.when(u == 0)
            def _():
                def pass_on(slot, _):
                    for copy in copies_in(slot):
                        copy.wait()
                    for copy in copies_ordered(slot):
                        copy.start()
                    return 0

                lax.fori_loop(n_slots, len(ordered) * z.slots, pass_on, 0)

        return 0

    lax.fori_loop(0, len(turns) * steps_per_turn, step, 0)
    if raw:
        last = [pltpu.make_async_copy(grads, grads_out[0], sem_grads.at[0])]
    else:
        grads[...] = acc[...].astype(BF16)
        last = [
            pltpu.make_async_copy(grads.at[t], grads_out[t], sem_grads.at[t]) for t in range(len(turns))
        ]
    for copy in last:
        copy.start()
    for slot in range(n_slots):
        for copy in copies_out(slot):
            copy.wait()
    if raw:
        for slot in range(n_slots, len(ordered) * z.slots):
            for copy in copies_ordered(slot):
                copy.wait()
    for copy in last:
        copy.wait()


def finish_kernel(z, n_tails, n_come, *refs):
    small_hbm, tail_hbm = refs[:4], refs[4 : 4 + n_tails]
    per_resp_hbm, come_hbm = refs[4 + n_tails], refs[5 + n_tails : 5 + n_tails + n_come]
    q_out, self_out, grads_out = refs[7 + n_tails + n_come : 10 + n_tails + n_come]
    (resp_prompt, resp_len, rewards, far_rewards, order, tails, out, own, per_resp, come, grads,
     sem_small, sem_tails, sem_come, sem_in, sem_out) = refs[10 + n_tails + n_come :]
    me = lax.axis_index("dp")
    small = [
        pltpu.make_async_copy(src, dst, sem_small.at[n])
        for n, (src, dst) in enumerate(zip(small_hbm, (resp_prompt, resp_len, rewards, far_rewards)))
    ]
    late = tail_copies(z, tail_hbm, tails, sem_tails)
    late += [pltpu.make_async_copy(src, come.at[n], sem_come.at[n]) for n, src in enumerate(come_hbm)]
    late += [pltpu.make_async_copy(per_resp_hbm, per_resp, sem_come.at[n_come])]
    for copy in small + late:
        copy.start()
    small[0].wait()
    find_responses(z, me, (0,), resp_prompt, order)

    def moves(slot, back):
        sems = sem_in if back else sem_out
        return result_copies(out, own, q_out, self_out, slot, token_rows(z, order[slot]), sems, back)

    for slot in range(z.slots):
        for copy in moves(slot, True):
            copy.start()
    for copy in small[1:] + late:
        copy.wait()
    total = prompt_total(z, me, me, resp_prompt, tails, far_rewards)
    summed = come[0].astype(F32)
    for n in range(1, n_come):
        summed += come[n].astype(F32)
    factors = [reward_factor(z, rewards[order[n]], total, resp_len[order[n]]) for n in range(z.slots)]
    for slot in range(z.slots):
        summed += per_resp[slot].astype(F32) * factors[slot]
    grads[...] = summed
    last = pltpu.make_async_copy(grads, grads_out, sem_small.at[0])
    last.start()
    for slot in range(z.slots):
        for copy in moves(slot, True):
            copy.wait()
        out[slot] = (out[slot].astype(F32) * factors[slot]).astype(BF16)
        own[slot] = (own[slot].astype(F32) * factors[slot]).astype(BF16)
        for copy in moves(slot, False):
            copy.start()
    for slot in range(z.slots):
        for copy in moves(slot, False):
            copy.wait()
    last.wait()


def near_shards(z, prompt_kv, resp_q, resp_kv, out_grad, rewards, resp_prompt, resp_len):
    n_dp = z.n_dp
    assert z.slots % PAIR == 0
    shape = jax.ShapeDtypeStruct
    one = (2, z.prefix_len, z.width)
    params = pltpu.CompilerParams(vmem_limit_bytes=VMEM_BYTES)
    cost = pl.CostEstimate(flops=0, bytes_accessed=0, transcendentals=0)
    payload = pl.pallas_call(
        functools.partial(pack_kernel, z),
        out_shape=jax.ShapeDtypeStruct((2 * z.prefix_len + TAIL, z.width), BF16),
        in_specs=[ANYWHERE] * 3,
        out_specs=ANYWHERE,
        scratch_shapes=[
            pltpu.SMEM(rewards.shape, F32),
            pltpu.SMEM(resp_prompt.shape, jnp.int32),
            pltpu.VMEM((2 * z.prefix_len + TAIL, z.width), BF16),
            pltpu.SemaphoreType.DMA((4,)),
        ],
        compiler_params=pltpu.CompilerParams(vmem_limit_bytes=VMEM_BYTES),
        name="pack",
    )(prompt_kv, rewards, resp_prompt)

    assert n_dp == FAR + 1

    def swap(x, s):
        return lax.ppermute(x, "dp", [(i, i ^ s) for i in range(n_dp)])

    payloads = {0: payload, 2: swap(payload, 2), 1: swap(payload, 1)}
    tails = [payloads[s] for s in range(FAR)]
    small = (resp_prompt, resp_len, rewards)
    far_rewards = swap(rewards, FAR)
    smem = [pltpu.SMEM(x.shape, x.dtype) for x in (*small, rewards)]
    slots = z.slots

    def grads_of(turns, raw, body, ahead, in_order=(), written=()):
        n_slots, n_turns = len(turns) * slots, len(turns)
        n_ahead = len(ahead) * slots if raw else 0
        n_held = n_slots + n_ahead
        used_tails = [] if raw else tails
        used_small = (*small, rewards if raw else far_rewards)
        prompts = [payloads[turn] for turn in turns]
        operands = [*used_small, resp_q, out_grad, resp_kv, *used_tails, *prompts, *in_order, *written]
        grads_shapes = [(slots,) + one] if raw else [one] * n_turns
        ordered_shapes = [(2, n_ahead * z.tokens, z.lanes), (2, n_ahead * z.tokens, z.width)] if raw else []
        return pl.pallas_call(
            functools.partial(group_kernel, z, turns, raw, body, ahead, len(used_tails), len(written)),
            out_shape=[shape(resp_q.shape, BF16), shape(resp_kv.shape, BF16)]
            + [shape(x, BF16) for x in grads_shapes + ordered_shapes],
            in_specs=[ANYWHERE] * len(operands),
            out_specs=[ANYWHERE] * (2 + len(grads_shapes) + len(ordered_shapes)),
            input_output_aliases={len(operands) - 2: 0, len(operands) - 1: 1} if written else {},
            scratch_shapes=[
                *smem,
                pltpu.SMEM((n_held + 1,), jnp.int32),
                pltpu.VMEM((n_held * z.tokens, z.lanes), BF16),
                pltpu.VMEM((n_held * z.tokens, z.lanes), BF16),
                pltpu.VMEM((2, n_held * z.tokens, z.width), BF16),
                pltpu.VMEM((n_turns,) + one, BF16),
                pltpu.VMEM((FAR, TAIL, z.width), BF16),
                pltpu.VMEM((n_turns,) + one, F32),
                pltpu.VMEM((n_slots, z.tokens, z.lanes), BF16),
                pltpu.VMEM((n_slots, 2, z.tokens, z.width), BF16),
                pltpu.VMEM(grads_shapes[0] if raw else (n_turns,) + one, BF16),
                pltpu.SemaphoreType.DMA((len(smem),)),
                pltpu.SemaphoreType.DMA((FAR,)),
                pltpu.SemaphoreType.DMA((n_turns, 2)),
                pltpu.SemaphoreType.DMA((n_held, 3)),
                pltpu.SemaphoreType.DMA((n_slots, 2)),
                pltpu.SemaphoreType.DMA((n_turns,)),
                pltpu.SemaphoreType.DMA((max(n_ahead, 1), 3)),
            ],
            compiler_params=params if raw else pltpu.CompilerParams(vmem_limit_bytes=GROUP_BYTES),
            cost_estimate=cost,
            name="raw_grads" if raw else "group_grads",
        )(*operands)

    *written, per_resp, rows_ahead, kv_ahead = grads_of((0,), True, 1, (2, FAR))
    in_order = (rows_ahead, kv_ahead)
    onward, per_resp, far_rewards = lax.optimization_barrier((payloads[2], per_resp, far_rewards))
    payloads[FAR] = swap(onward, 1)
    *written, for_2 = grads_of((2,), False, slots // PAIR, 0, in_order, written)
    come = [swap(for_2, 2)]
    *written, for_far, for_1 = grads_of((FAR, 1), False, slots // PAIR, 1, in_order, written)
    last = [swap(for_far, FAR), swap(for_1, 1)]
    operands = [*small, far_rewards, *tails, per_resp, *come, *written]
    q_out, self_out, own_grads = pl.pallas_call(
        functools.partial(finish_kernel, z, len(tails), len(come)),
        out_shape=[shape(resp_q.shape, BF16), shape(resp_kv.shape, BF16), shape(one, F32)],
        in_specs=[ANYWHERE] * len(operands),
        out_specs=[ANYWHERE] * 3,
        input_output_aliases={len(operands) - 2: 0, len(operands) - 1: 1},
        scratch_shapes=[
            *smem,
            pltpu.SMEM((slots + 1,), jnp.int32),
            pltpu.VMEM((FAR, TAIL, z.width), BF16),
            pltpu.VMEM((slots, z.tokens, z.lanes), BF16),
            pltpu.VMEM((slots, 2, z.tokens, z.width), BF16),
            pltpu.VMEM((slots,) + one, BF16),
            pltpu.VMEM((len(come),) + one, BF16),
            pltpu.VMEM(one, F32),
            pltpu.SemaphoreType.DMA((len(smem),)),
            pltpu.SemaphoreType.DMA((FAR,)),
            pltpu.SemaphoreType.DMA((len(come) + 1,)),
            pltpu.SemaphoreType.DMA((slots, 3)),
            pltpu.SemaphoreType.DMA((slots, 3)),
        ],
        compiler_params=pltpu.CompilerParams(vmem_limit_bytes=FINISH_BYTES),
        cost_estimate=cost,
        name="finish_own",
    )(*operands)
    prefix_out = (own_grads + sum(part.astype(F32) for part in last)).astype(BF16)
    return (q_out, self_out, prefix_out)


def far_kernel(z, *refs):
    (resp_prompt, resp_len, rewards, q_hbm, og_hbm, kv_hbm, prompts, q_out, self_out, prefix_outs,
     totals, lens, factors, q, og, kv, prefix, out, own, grads, sem_in, sem_prefix, sem_out) = refs
    me = lax.axis_index("dp")

    for p in range(z.n_dp):
        totals[p] = 0.0

    def copies_in(slot):
        rows = token_rows(z, slot)
        prompt = resp_prompt[me * z.count + slot]
        return (
            *row_copies((q_hbm, og_hbm, kv_hbm), (q, og, kv), rows, rows, sem_in.at[slot]),
            pltpu.make_async_copy(prompts.at[prompt], prefix.at[slot], sem_prefix.at[slot]),
        )

    def copies_out(slot):
        rows = token_rows(z, slot)
        return (
            *result_copies(out, own, q_out, self_out, slot, rows, sem_out),
            pltpu.make_async_copy(grads.at[slot], prefix_outs.at[slot], sem_out.at[slot, 3]),
        )

    def start(slot, _):
        for copy in copies_in(slot):
            copy.start()
        return 0

    lax.fori_loop(0, z.count, start, 0)

    def add(i, _):
        prompt = resp_prompt[i]
        totals[prompt] = totals[prompt] + rewards[i]
        return 0

    lax.fori_loop(0, z.n_dp * z.count, add, 0)

    def find_factor(slot, _):
        place = me * z.count + slot
        lens[slot] = resp_len[slot]
        factors[slot] = reward_factor(z, rewards[place], totals[resp_prompt[place]], resp_len[slot])
        return 0

    lax.fori_loop(0, z.count, find_factor, 0)

    def unit(slot, _):
        for copy in copies_in(slot):
            copy.wait()

        def sink(_, cols, key_grad, value_grad):
            grads[slot, 0, :, cols] = key_grad.astype(BF16)
            grads[slot, 1, :, cols] = value_grad.astype(BF16)

        units = [
            Unit([token_rows(z, slot)], [slot], k, [lens[slot]], [factors[slot]]) for k in range(z.kv_heads)
        ]
        attend(z, units, q, og, kv, prefix.at[slot], out, own, sink, True)
        for copy in copies_out(slot):
            copy.start()
        return 0

    lax.fori_loop(0, z.count, unit, 0)

    def end(slot, _):
        for copy in copies_out(slot):
            copy.wait()
        return 0

    lax.fori_loop(0, z.count, end, 0)


def far_shards(z, prompt_kv, resp_q, resp_kv, out_grad, rewards, resp_prompt, resp_len):
    assert z.slots == 1
    count, n_dp = z.count, z.n_dp
    one = (2, z.prefix_len, z.width)
    smem = pl.BlockSpec(memory_space=pltpu.SMEM)
    q_out, self_out, per_resp = pl.pallas_call(
        functools.partial(far_kernel, z),
        out_shape=[
            jax.ShapeDtypeStruct(resp_q.shape, BF16),
            jax.ShapeDtypeStruct(resp_kv.shape, BF16),
            jax.ShapeDtypeStruct((count,) + one, BF16),
        ],
        in_specs=[smem] * 3 + [ANYWHERE] * 4,
        out_specs=[ANYWHERE] * 3,
        scratch_shapes=[
            pltpu.SMEM((n_dp,), F32),
            pltpu.SMEM((count,), jnp.int32),
            pltpu.SMEM((count,), F32),
            pltpu.VMEM(resp_q.shape, BF16),
            pltpu.VMEM(resp_q.shape, BF16),
            pltpu.VMEM(resp_kv.shape, BF16),
            pltpu.VMEM((count,) + one, BF16),
            pltpu.VMEM((count, z.tokens, z.lanes), BF16),
            pltpu.VMEM((count, 2, z.tokens, z.width), BF16),
            pltpu.VMEM((count,) + one, BF16),
            pltpu.SemaphoreType.DMA((count, 4)),
            pltpu.SemaphoreType.DMA((count,)),
            pltpu.SemaphoreType.DMA((count, 4)),
        ],
        compiler_params=pltpu.CompilerParams(vmem_limit_bytes=VMEM_BYTES),
        name="far_grads",
    )(
        resp_prompt,
        resp_len,
        lax.all_gather(rewards, "dp", axis=0, tiled=True),
        resp_q,
        out_grad,
        resp_kv,
        lax.all_gather(prompt_kv, "dp", axis=0),
    )
    my_prompts = lax.dynamic_slice_in_dim(resp_prompt, lax.axis_index("dp") * count, count)
    route = (jnp.arange(n_dp, dtype=jnp.int32)[:, None] == my_prompts[None, :]).astype(BF16)
    outgoing = jnp.dot(route, per_resp.reshape(count, -1), preferred_element_type=F32).astype(BF16)
    outgoing = outgoing.reshape((n_dp,) + one)
    incoming = lax.all_to_all(outgoing, "dp", split_axis=0, concat_axis=0, tiled=True)
    prefix_out = jnp.sum(incoming, axis=0, dtype=F32).astype(BF16)
    return (q_out, self_out, prefix_out)


def shards(prompt_kv, resp_q, resp_kv, out_grad, rewards, resp_prompt, resp_len):
    n_dp = lax.axis_size("dp")
    count = rewards.shape[0]
    prefix_len, width = prompt_kv.shape[1:]
    slots = (count + n_dp - 1) // n_dp
    z = Sizes(
        n_dp, count, slots, width // HD, resp_q.shape[1] // width, resp_q.shape[0] // count, prefix_len
    )
    part = near_shards if count // slots == n_dp else far_shards
    return part(z, prompt_kv, resp_q, resp_kv, out_grad, rewards, resp_prompt, resp_len)


def solution(mesh):
    in_specs = (
        P(None, ("groups", "dp"), "tensor"),
        P(("groups", "dp"), "tensor"),
        P(None, ("groups", "dp"), "tensor"),
        P(("groups", "dp"), "tensor"),
        P(("groups", "dp")),
        P("groups"),
        P(("groups", "dp")),
    )
    out_specs = (
        P(("groups", "dp"), "tensor"),
        P(None, ("groups", "dp"), "tensor"),
        P(None, ("groups", "dp"), "tensor"),
    )
    return jax.shard_map(shards, mesh=mesh, in_specs=in_specs, out_specs=out_specs, check_vma=False)
```

```python
import functools
import math
from typing import NamedTuple

import jax
import jax.numpy as jnp
from jax import lax
from jax.experimental import pallas as pl
from jax.experimental.pallas import tpu as pltpu
from jax.sharding import PartitionSpec as P

HD = 128
NEG = -1e30
TAIL = 16
F32 = jnp.float32
BF16 = jnp.bfloat16
PAIR = 2
FAR = 3
VMEM_BYTES = 63 * 1024 * 1024
GROUP_BYTES = 53 * 1024 * 1024
FINISH_BYTES = 24 * 1024 * 1024
ANYWHERE = pl.BlockSpec(memory_space=pl.ANY)


class Sizes(NamedTuple):
    n_dp: int
    count: int
    slots: int
    kv_heads: int
    group_size: int
    tokens: int
    prefix_len: int

    @property
    def width(self):
        return self.kv_heads * HD

    @property
    def lanes(self):
        return self.kv_heads * self.group_size * HD


def dot(a, b, dims):
    return lax.dot_general(a, b, (dims, ((), ())), preferred_element_type=F32)


NN = ((1,), (0,))
NT = ((1,), (1,))


class Bag:
    pass


class Unit(NamedTuple):
    at: list
    places: list
    k: object
    lens: list
    factors: list
    ready: object = None
    done: object = None


def attend(z, units, q, og, kv, prefix, out, own_out, sink, apart):
    tokens, prefix_len, group_size = z.tokens, z.prefix_len, z.group_size
    scale = 1.0 / math.sqrt(HD)
    log_scale = scale * math.log2(math.e)
    whole = group_size - group_size % 2
    most = max(whole, 2) * tokens
    assert tokens & (tokens - 1) == 0
    token = lax.broadcasted_iota(jnp.int32, (1, most), 1) & (tokens - 1)
    key = lax.broadcasted_iota(jnp.int32, (tokens, most), 0)
    causal = key <= (lax.broadcasted_iota(jnp.int32, (tokens, most), 1) & (tokens - 1))
    left = lax.broadcasted_iota(jnp.int32, (1, 2 * tokens), 1) < tokens

    def columns(index):
        if isinstance(index, int):
            return slice(index * HD, (index + 1) * HD)
        return pl.ds(pl.multiple_of(index * HD, HD), HD)

    def head(k, h):
        return columns(k * group_size + h)

    def rows(ref, c):
        return jnp.concatenate([ref[c.t.at[n], head(c.t.k, h)] for n, h in c.blocks], axis=0)

    def halves(part):
        none = jnp.zeros_like(part)
        return [jnp.where(left, part, none), jnp.where(left, none, part)]

    def over_keys(combine, *parts):
        reduce = jnp.max if combine is jnp.maximum else jnp.sum
        eights = [reduce(part.reshape(-1, 8, part.shape[1]), axis=0) for part in parts]
        return reduce(functools.reduce(combine, eights), axis=0, keepdims=True)

    def own_half(both):
        return jnp.where(left, both[:tokens], both[tokens:])

    def rounded(*parts):
        return jnp.concatenate([part.astype(BF16) for part in parts], axis=0)

    chunks = []
    for unit in units:
        t = Bag()
        t.unit = unit
        t.at, t.places, t.k, t.lens, t.factors = unit[:5]
        t.single = len(t.at) == 1
        t.members = range(len(t.at))
        sides = (0, 0) if t.single else (0, 1)
        t.cols = columns(t.k)
        t.keys = None
        t.prefix_sums = {n: [] for n in t.members}
        t.self_sums = {n: [] for n in t.members}
        mine = []
        for n in t.members:
            c = Bag()
            c.t, c.side, c.blocks = t, n, [(n, h) for h in range(whole)]
            mine.append(c)
        if group_size % 2:
            c = Bag()
            c.t, c.side, c.blocks = t, None, [(n, group_size - 1) for n in sides]
            mine.append(c)
        t.left_over = len(mine)
        chunks += mine

    def prepare(t):
        if t.unit.ready is not None:
            t.unit.ready()
        sides = (0, 0) if t.single else (0, 1)
        t.key_p, t.value_p = prefix[0, :, t.cols], prefix[1, :, t.cols]
        t.keys = [kv[0, t.at[n], t.cols] for n in sides]
        t.values = [kv[1, t.at[n], t.cols] for n in sides]
        t.key_pair = jnp.concatenate(t.keys, axis=0)
        t.value_pair = jnp.concatenate(t.values, axis=0)
        t.key_t = jnp.concatenate([t.key_p.T, t.key_pair.T], axis=1)

    def products(c):
        t = c.t
        if t.keys is None:
            prepare(t)
        c.q_rows, c.g_rows = rows(q, c), rows(og, c)
        if c.side is None:
            key_s, value_s = t.key_pair, t.value_pair
        else:
            key_s, value_s = t.keys[c.side], t.values[c.side]
        c.scores = dot(jnp.concatenate([t.key_p, key_s], axis=0), c.q_rows, NT)
        c.gw = dot(jnp.concatenate([t.value_p, value_s], axis=0), c.g_rows, NT)

    def weigh(c):
        scores_p, scores_s = c.scores[:prefix_len], c.scores[prefix_len:]
        c.gw_p, c.gw_s = c.gw[:prefix_len], c.gw[prefix_len:]
        if c.side is None:
            scores_s, c.gw_s = own_half(scores_s), own_half(c.gw_s)
        scores_s = jnp.where(causal[:, : scores_s.shape[1]], scores_s, NEG)
        top = over_keys(jnp.maximum, scores_p, scores_s)
        c.e_p = jnp.exp2((scores_p - top) * log_scale)
        c.e_s = jnp.exp2((scores_s - top) * log_scale)
        total = over_keys(jnp.add, c.e_p, c.e_s)
        weighted = over_keys(jnp.add, c.e_p * c.gw_p, c.e_s * c.gw_s)
        if c.side is None:
            length = jnp.where(left, c.t.lens[0], 0 if c.t.single else c.t.lens[1])
            gain = jnp.where(left, c.t.factors[0], c.t.factors[-1])
        else:
            length, gain = c.t.lens[c.side], c.t.factors[c.side]
        inverse = 1.0 / total
        c.delta = weighted * inverse
        c.gain = inverse * jnp.where(token[:, : total.shape[1]] < length, gain, 0.0)

    def gradients(c):
        w_p, w_s = c.e_p * c.gain, c.e_s * c.gain
        d_p, d_s = w_p * (c.gw_p - c.delta), w_s * (c.gw_s - c.delta)
        if c.side is None:
            d_s, w_s = halves(d_s), halves(w_s)
            c.d_wide = rounded(d_p, *d_s)
            c.d_all = rounded(*halves(d_p), *d_s) if apart else c.d_wide
            c.w_all = rounded(*(halves(w_p) if apart else [w_p]), *w_s)
        else:
            empty = jnp.zeros_like(d_s)
            c.d_wide = rounded(*([d_p, empty, d_s] if c.side else [d_p, d_s, empty]))
            c.d_all = rounded(d_p, d_s)
            c.w_all = rounded(w_p, w_s)

    def outgoing(c):
        t = c.t
        q_grad = (dot(t.key_t, c.d_wide, NN) * scale).astype(BF16).T
        kg = dot(c.d_all, c.q_rows, NN)
        vg = dot(c.w_all, c.g_rows, NN)
        targets = t.members if c.side is None else [c.side]
        for place, (n, h) in enumerate(c.blocks):
            if c.side is not None or place < len(targets):
                out[t.places[n], :, head(t.k, h)] = q_grad[place * tokens : (place + 1) * tokens]
        many = 2 if c.side is None and apart else 1
        for place, n in enumerate(targets):
            if place < many:
                rows_p = slice(place * prefix_len, (place + 1) * prefix_len)
                t.prefix_sums[n if apart else 0].append((kg[rows_p], vg[rows_p]))
            start = many * prefix_len + place * tokens
            rows_s = slice(start, start + tokens)
            t.self_sums[n].append((kg[rows_s], vg[rows_s]))
        t.left_over -= 1
        if t.left_over == 0:
            for n in t.members:
                keys, values = zip(*t.self_sums[n])
                own_out[t.places[n], 0, :, t.cols] = (sum(keys) * scale).astype(BF16)
                own_out[t.places[n], 1, :, t.cols] = sum(values).astype(BF16)
                if apart or n == 0:
                    keys, values = zip(*t.prefix_sums[n])
                    sink(t.places[n], t.cols, sum(keys) * scale, sum(values))
            if t.unit.done is not None:
                t.unit.done()

    stages = (products, weigh, gradients, outgoing)
    for step in range(len(chunks) + len(stages) - 1):
        for late, stage in enumerate(stages):
            if 0 <= step - late < len(chunks):
                stage(chunks[step - late])


def token_rows(z, i):
    return pl.ds(pl.multiple_of(i * z.tokens, z.tokens), z.tokens)


def find_responses(z, me, turns, resp_prompt, order):
    for t, turn in enumerate(turns):
        prompt = me ^ turn
        found = t * z.slots
        for i in range(z.count):
            order[found] = i
            found = found + (resp_prompt[me * z.count + i] == prompt).astype(jnp.int32)


def prompt_total(z, me, prompt, resp_prompt, tails, far_rewards):
    sums = jnp.zeros((1, z.width), F32)
    for s in range(tails.shape[0]):
        tail = tails[s].astype(F32)
        sums += tail[0:1] + tail[1:2] + tail[2:3]
    lane = lax.broadcasted_iota(jnp.int32, sums.shape, 1)
    total = jnp.sum(jnp.where(lane == prompt, sums, 0.0))
    for i in range(z.count):
        total += jnp.where(resp_prompt[(me ^ FAR) * z.count + i] == prompt, far_rewards[i], 0.0)
    return total


def reward_factor(z, reward, total, length):
    return (reward - total / z.count) * (z.tokens / length.astype(F32))


def pack_kernel(z, prompt_hbm, rewards_hbm, resp_prompt_hbm, payload, rewards, resp_prompt, staged, sems):
    me = lax.axis_index("dp")
    small = [
        pltpu.make_async_copy(rewards_hbm, rewards, sems.at[0]),
        pltpu.make_async_copy(resp_prompt_hbm, resp_prompt, sems.at[1]),
    ]
    large = [
        pltpu.make_async_copy(
            prompt_hbm.at[n], staged.at[pl.ds(n * z.prefix_len, z.prefix_len)], sems.at[2 + n]
        )
        for n in range(2)
    ]
    for copy in small + large:
        copy.start()
    for copy in small:
        copy.wait()
    lane = lax.broadcasted_iota(jnp.int32, (1, z.width), 1)
    sums = jnp.zeros((1, z.width), F32)
    for i in range(z.count):
        sums += jnp.where(lane == resp_prompt[me * z.count + i], rewards[i], 0.0)
    high = sums.astype(BF16).astype(F32)
    middle = (sums - high).astype(BF16).astype(F32)
    low = sums - high - middle
    row = lax.broadcasted_iota(jnp.int32, (TAIL, z.width), 0)
    pieces = jnp.where(row == 0, high, jnp.where(row == 1, middle, jnp.where(row == 2, low, 0.0)))
    staged[2 * z.prefix_len :, :] = pieces.astype(BF16)
    for copy in large:
        copy.wait()
    last = pltpu.make_async_copy(staged, payload, sems.at[0])
    last.start()
    last.wait()


def tail_copies(z, payloads, tails, sems):
    return [
        pltpu.make_async_copy(payload.at[pl.ds(2 * z.prefix_len, TAIL)], tails.at[n], sems.at[n])
        for n, payload in enumerate(payloads)
    ]


def row_copies(here, there, at_here, at_there, sems):
    (q0, og0, kv0), (q1, og1, kv1) = here, there
    return (
        pltpu.make_async_copy(q0.at[at_here], q1.at[at_there], sems.at[0]),
        pltpu.make_async_copy(og0.at[at_here], og1.at[at_there], sems.at[1]),
        pltpu.make_async_copy(kv0.at[:, at_here], kv1.at[:, at_there], sems.at[2]),
    )


def result_copies(out, own, q_out, self_out, place, at, sems, back=False):
    pairs = [
        (out.at[place], q_out.at[at]),
        (own.at[place], self_out.at[:, at]),
    ]
    return [
        pltpu.make_async_copy(*(reversed(pair) if back else pair), sems.at[place, n])
        for n, pair in enumerate(pairs)
    ]


def group_kernel(z, turns, raw, body, ahead, n_tails, aliased, *refs):
    small_hbm, given = refs[:4], refs[4:7]
    tail_hbm, prompts = refs[7 : 7 + n_tails], refs[7 + n_tails : 7 + n_tails + len(turns)]
    refs = refs[7 + n_tails + len(turns) :]
    if raw:
        (q_out, self_out), grads_out, in_order, refs = refs[:2], refs[2:3], refs[3:5], refs[5:]
    else:
        in_order, refs = refs[:2], refs[2 + aliased :]
        (q_out, self_out), grads_out, refs = refs[:2], refs[2 : 2 + len(turns)], refs[2 + len(turns) :]
    in_order = (in_order[0].at[0], in_order[0].at[1], in_order[1])
    (resp_prompt, resp_len, rewards, far_rewards, order, q, og, kv, prefix, tails, acc, out, own, grads,
     sem_small, sem_tails, sem_prefix, sem_in, sem_out, sem_grads, sem_order) = refs
    me = lax.axis_index("dp")
    n_slots = len(turns) * z.slots
    span = z.slots * z.tokens

    small = [
        pltpu.make_async_copy(src, dst, sem_small.at[n])
        for n, (src, dst) in enumerate(zip(small_hbm, (resp_prompt, resp_len, rewards, far_rewards)))
    ]
    prefix_copies = [
        pltpu.make_async_copy(
            prompts[t].at[pl.ds(n * z.prefix_len, z.prefix_len)], prefix.at[t, n], sem_prefix.at[t, n]
        )
        for t in range(len(turns))
        for n in range(2)
    ]
    late = tail_copies(z, tail_hbm, tails, sem_tails)
    first_rows = []
    if not raw:
        for slot in range(z.slots):
            first_rows += row_copies(
                in_order,
                (q, og, kv),
                pl.ds((ahead * z.slots + slot) * z.tokens, z.tokens),
                token_rows(z, slot),
                sem_in.at[slot],
            )
    for copy in [*small, *first_rows, *prefix_copies, *late]:
        copy.start()
    small[0].wait()
    ordered = [*turns, *ahead] if raw else turns
    find_responses(z, me, ordered, resp_prompt, order)

    def copies_in(slot):
        return row_copies(
            given, (q, og, kv), token_rows(z, order[slot]), token_rows(z, slot), sem_in.at[slot]
        )

    def copies_out(slot):
        return result_copies(out, own, q_out, self_out, slot, token_rows(z, order[slot]), sem_out)

    def copies_ordered(slot):
        rows = token_rows(z, slot - n_slots)
        return row_copies((q, og, kv), in_order, token_rows(z, slot), rows, sem_order.at[slot - n_slots])

    for slot in range(0 if raw else z.slots, len(ordered) * z.slots):
        for copy in copies_in(slot):
            copy.start()
    for copy in small[1:] + late:
        copy.wait()
    if not raw:
        acc[...] = jnp.zeros(acc.shape, F32)
    for copy in prefix_copies:
        copy.wait()

    pairs_in_body = body
    steps_per_turn = z.slots // PAIR // pairs_in_body

    def step(u, _):
        t = u // steps_per_turn
        first = u * pairs_in_body * PAIR
        mine = range(pairs_in_body * PAIR)

        def ready(pair):
            for n in range(pair * PAIR, (pair + 1) * PAIR):
                for copy in copies_in(first + n):
                    copy.wait()

        def done(pair):
            for n in range(pair * PAIR, (pair + 1) * PAIR):
                for copy in copies_out(first + n):
                    copy.start()

        def sink(place, cols, key_grad, value_grad):
            if raw:
                grads[place, 0, :, cols] = key_grad.astype(BF16)
                grads[place, 1, :, cols] = value_grad.astype(BF16)
            else:
                acc[t, 0, :, cols] += key_grad
                acc[t, 1, :, cols] += value_grad

        turn = turns[0]
        for n, other in enumerate(turns[1:], 1):
            turn = jnp.where(t == n, other, turn)
        total = None if raw else prompt_total(z, me, me ^ turn, resp_prompt, tails, far_rewards)
        lens, factors = {}, {}
        for n in mine:
            i = order[first + n]
            lens[n] = resp_len[i]
            factors[n] = 1.0 if raw else reward_factor(z, rewards[i], total, resp_len[i])
        units = []
        for pair in range(pairs_in_body):
            places = [first + pair * PAIR + n for n in range(PAIR)]
            own_places = range(pair * PAIR, (pair + 1) * PAIR)
            at = [token_rows(z, n) for n in places]
            for k in range(z.kv_heads):
                units.append(
                    Unit(
                        at,
                        places,
                        k,
                        [lens[n] for n in own_places],
                        [factors[n] for n in own_places],
                        functools.partial(ready, pair) if k == 0 else None,
                        functools.partial(done, pair) if k == z.kv_heads - 1 else None,
                    )
                )
        attend(z, units, q, og, kv, prefix.at[t], out, own, sink, raw)
        if raw:

            @pl.when(u == 0)
            def _():
                def pass_on(slot, _):
                    for copy in copies_in(slot):
                        copy.wait()
                    for copy in copies_ordered(slot):
                        copy.start()
                    return 0

                lax.fori_loop(n_slots, len(ordered) * z.slots, pass_on, 0)

        return 0

    lax.fori_loop(0, len(turns) * steps_per_turn, step, 0)
    if raw:
        last = [pltpu.make_async_copy(grads, grads_out[0], sem_grads.at[0])]
    else:
        grads[...] = acc[...].astype(BF16)
        last = [
            pltpu.make_async_copy(grads.at[t], grads_out[t], sem_grads.at[t]) for t in range(len(turns))
        ]
    for copy in last:
        copy.start()
    for slot in range(n_slots):
        for copy in copies_out(slot):
            copy.wait()
    if raw:
        for slot in range(n_slots, len(ordered) * z.slots):
            for copy in copies_ordered(slot):
                copy.wait()
    for copy in last:
        copy.wait()


def finish_kernel(z, n_tails, n_come, *refs):
    small_hbm, tail_hbm = refs[:4], refs[4 : 4 + n_tails]
    per_resp_hbm, come_hbm = refs[4 + n_tails], refs[5 + n_tails : 5 + n_tails + n_come]
    q_out, self_out, grads_out = refs[7 + n_tails + n_come : 10 + n_tails + n_come]
    (resp_prompt, resp_len, rewards, far_rewards, order, tails, out, own, per_resp, come, grads,
     sem_small, sem_tails, sem_come, sem_in, sem_out) = refs[10 + n_tails + n_come :]
    me = lax.axis_index("dp")
    small = [
        pltpu.make_async_copy(src, dst, sem_small.at[n])
        for n, (src, dst) in enumerate(zip(small_hbm, (resp_prompt, resp_len, rewards, far_rewards)))
    ]
    late = tail_copies(z, tail_hbm, tails, sem_tails)
    late += [pltpu.make_async_copy(src, come.at[n], sem_come.at[n]) for n, src in enumerate(come_hbm)]
    late += [pltpu.make_async_copy(per_resp_hbm, per_resp, sem_come.at[n_come])]
    for copy in small + late:
        copy.start()
    small[0].wait()
    find_responses(z, me, (0,), resp_prompt, order)

    def moves(slot, back):
        sems = sem_in if back else sem_out
        return result_copies(out, own, q_out, self_out, slot, token_rows(z, order[slot]), sems, back)

    for slot in range(z.slots):
        for copy in moves(slot, True):
            copy.start()
    for copy in small[1:] + late:
        copy.wait()
    total = prompt_total(z, me, me, resp_prompt, tails, far_rewards)
    summed = come[0].astype(F32)
    for n in range(1, n_come):
        summed += come[n].astype(F32)
    factors = [reward_factor(z, rewards[order[n]], total, resp_len[order[n]]) for n in range(z.slots)]
    for slot in range(z.slots):
        summed += per_resp[slot].astype(F32) * factors[slot]
    grads[...] = summed
    last = pltpu.make_async_copy(grads, grads_out, sem_small.at[0])
    last.start()
    for slot in range(z.slots):
        for copy in moves(slot, True):
            copy.wait()
        out[slot] = (out[slot].astype(F32) * factors[slot]).astype(BF16)
        own[slot] = (own[slot].astype(F32) * factors[slot]).astype(BF16)
        for copy in moves(slot, False):
            copy.start()
    for slot in range(z.slots):
        for copy in moves(slot, False):
            copy.wait()
    last.wait()


def near_shards(z, prompt_kv, resp_q, resp_kv, out_grad, rewards, resp_prompt, resp_len):
    n_dp = z.n_dp
    assert z.slots % PAIR == 0
    shape = jax.ShapeDtypeStruct
    one = (2, z.prefix_len, z.width)
    params = pltpu.CompilerParams(vmem_limit_bytes=VMEM_BYTES)
    cost = pl.CostEstimate(flops=0, bytes_accessed=0, transcendentals=0)
    payload = pl.pallas_call(
        functools.partial(pack_kernel, z),
        out_shape=jax.ShapeDtypeStruct((2 * z.prefix_len + TAIL, z.width), BF16),
        in_specs=[ANYWHERE] * 3,
        out_specs=ANYWHERE,
        scratch_shapes=[
            pltpu.SMEM(rewards.shape, F32),
            pltpu.SMEM(resp_prompt.shape, jnp.int32),
            pltpu.VMEM((2 * z.prefix_len + TAIL, z.width), BF16),
            pltpu.SemaphoreType.DMA((4,)),
        ],
        compiler_params=pltpu.CompilerParams(vmem_limit_bytes=VMEM_BYTES),
        name="pack",
    )(prompt_kv, rewards, resp_prompt)

    assert n_dp == FAR + 1

    def swap(x, s):
        return lax.ppermute(x, "dp", [(i, i ^ s) for i in range(n_dp)])

    payloads = {0: payload, 2: swap(payload, 2), 1: swap(payload, 1)}
    tails = [payloads[s] for s in range(FAR)]
    small = (resp_prompt, resp_len, rewards)
    far_rewards = swap(rewards, FAR)
    smem = [pltpu.SMEM(x.shape, x.dtype) for x in (*small, rewards)]
    slots = z.slots

    def grads_of(turns, raw, body, ahead, in_order=(), written=()):
        n_slots, n_turns = len(turns) * slots, len(turns)
        n_ahead = len(ahead) * slots if raw else 0
        n_held = n_slots + n_ahead
        used_tails = [] if raw else tails
        used_small = (*small, rewards if raw else far_rewards)
        prompts = [payloads[turn] for turn in turns]
        operands = [*used_small, resp_q, out_grad, resp_kv, *used_tails, *prompts, *in_order, *written]
        grads_shapes = [(slots,) + one] if raw else [one] * n_turns
        ordered_shapes = [(2, n_ahead * z.tokens, z.lanes), (2, n_ahead * z.tokens, z.width)] if raw else []
        return pl.pallas_call(
            functools.partial(group_kernel, z, turns, raw, body, ahead, len(used_tails), len(written)),
            out_shape=[shape(resp_q.shape, BF16), shape(resp_kv.shape, BF16)]
            + [shape(x, BF16) for x in grads_shapes + ordered_shapes],
            in_specs=[ANYWHERE] * len(operands),
            out_specs=[ANYWHERE] * (2 + len(grads_shapes) + len(ordered_shapes)),
            input_output_aliases={len(operands) - 2: 0, len(operands) - 1: 1} if written else {},
            scratch_shapes=[
                *smem,
                pltpu.SMEM((n_held + 1,), jnp.int32),
                pltpu.VMEM((n_held * z.tokens, z.lanes), BF16),
                pltpu.VMEM((n_held * z.tokens, z.lanes), BF16),
                pltpu.VMEM((2, n_held * z.tokens, z.width), BF16),
                pltpu.VMEM((n_turns,) + one, BF16),
                pltpu.VMEM((FAR, TAIL, z.width), BF16),
                pltpu.VMEM((n_turns,) + one, F32),
                pltpu.VMEM((n_slots, z.tokens, z.lanes), BF16),
                pltpu.VMEM((n_slots, 2, z.tokens, z.width), BF16),
                pltpu.VMEM(grads_shapes[0] if raw else (n_turns,) + one, BF16),
                pltpu.SemaphoreType.DMA((len(smem),)),
                pltpu.SemaphoreType.DMA((FAR,)),
                pltpu.SemaphoreType.DMA((n_turns, 2)),
                pltpu.SemaphoreType.DMA((n_held, 3)),
                pltpu.SemaphoreType.DMA((n_slots, 2)),
                pltpu.SemaphoreType.DMA((n_turns,)),
                pltpu.SemaphoreType.DMA((max(n_ahead, 1), 3)),
            ],
            compiler_params=params if raw else pltpu.CompilerParams(vmem_limit_bytes=GROUP_BYTES),
            cost_estimate=cost,
            name="raw_grads" if raw else "group_grads",
        )(*operands)

    *written, per_resp, rows_ahead, kv_ahead = grads_of((0,), True, 1, (2, FAR))
    in_order = (rows_ahead, kv_ahead)
    onward, per_resp, far_rewards = lax.optimization_barrier((payloads[2], per_resp, far_rewards))
    payloads[FAR] = swap(onward, 1)
    *written, for_2 = grads_of((2,), False, slots // PAIR, 0, in_order, written)
    come = [swap(for_2, 2)]
    *written, for_far, for_1 = grads_of((FAR, 1), False, slots // PAIR, 1, in_order, written)
    last = [swap(for_1, 1), swap(for_far, FAR)]
    operands = [*small, far_rewards, *tails, per_resp, *come, *written]
    q_out, self_out, own_grads = pl.pallas_call(
        functools.partial(finish_kernel, z, len(tails), len(come)),
        out_shape=[shape(resp_q.shape, BF16), shape(resp_kv.shape, BF16), shape(one, F32)],
        in_specs=[ANYWHERE] * len(operands),
        out_specs=[ANYWHERE] * 3,
        input_output_aliases={len(operands) - 2: 0, len(operands) - 1: 1},
        scratch_shapes=[
            *smem,
            pltpu.SMEM((slots + 1,), jnp.int32),
            pltpu.VMEM((FAR, TAIL, z.width), BF16),
            pltpu.VMEM((slots, z.tokens, z.lanes), BF16),
            pltpu.VMEM((slots, 2, z.tokens, z.width), BF16),
            pltpu.VMEM((slots,) + one, BF16),
            pltpu.VMEM((len(come),) + one, BF16),
            pltpu.VMEM(one, F32),
            pltpu.SemaphoreType.DMA((len(smem),)),
            pltpu.SemaphoreType.DMA((FAR,)),
            pltpu.SemaphoreType.DMA((len(come) + 1,)),
            pltpu.SemaphoreType.DMA((slots, 3)),
            pltpu.SemaphoreType.DMA((slots, 3)),
        ],
        compiler_params=pltpu.CompilerParams(vmem_limit_bytes=FINISH_BYTES),
        cost_estimate=cost,
        name="finish_own",
    )(*operands)
    prefix_out = (own_grads + sum(part.astype(F32) for part in last)).astype(BF16)
    return (q_out, self_out, prefix_out)


def far_kernel(z, *refs):
    (resp_prompt, resp_len, rewards, q_hbm, og_hbm, kv_hbm, prompts, q_out, self_out, prefix_outs,
     totals, lens, factors, q, og, kv, prefix, out, own, grads, sem_in, sem_prefix, sem_out) = refs
    me = lax.axis_index("dp")

    for p in range(z.n_dp):
        totals[p] = 0.0

    def copies_in(slot):
        rows = token_rows(z, slot)
        prompt = resp_prompt[me * z.count + slot]
        return (
            *row_copies((q_hbm, og_hbm, kv_hbm), (q, og, kv), rows, rows, sem_in.at[slot]),
            pltpu.make_async_copy(prompts.at[prompt], prefix.at[slot], sem_prefix.at[slot]),
        )

    def copies_out(slot):
        rows = token_rows(z, slot)
        return (
            *result_copies(out, own, q_out, self_out, slot, rows, sem_out),
            pltpu.make_async_copy(grads.at[slot], prefix_outs.at[slot], sem_out.at[slot, 3]),
        )

    def start(slot, _):
        for copy in copies_in(slot):
            copy.start()
        return 0

    lax.fori_loop(0, z.count, start, 0)

    def add(i, _):
        prompt = resp_prompt[i]
        totals[prompt] = totals[prompt] + rewards[i]
        return 0

    lax.fori_loop(0, z.n_dp * z.count, add, 0)

    def find_factor(slot, _):
        place = me * z.count + slot
        lens[slot] = resp_len[slot]
        factors[slot] = reward_factor(z, rewards[place], totals[resp_prompt[place]], resp_len[slot])
        return 0

    lax.fori_loop(0, z.count, find_factor, 0)

    def unit(slot, _):
        for copy in copies_in(slot):
            copy.wait()

        def sink(_, cols, key_grad, value_grad):
            grads[slot, 0, :, cols] = key_grad.astype(BF16)
            grads[slot, 1, :, cols] = value_grad.astype(BF16)

        units = [
            Unit([token_rows(z, slot)], [slot], k, [lens[slot]], [factors[slot]]) for k in range(z.kv_heads)
        ]
        attend(z, units, q, og, kv, prefix.at[slot], out, own, sink, True)
        for copy in copies_out(slot):
            copy.start()
        return 0

    lax.fori_loop(0, z.count, unit, 0)

    def end(slot, _):
        for copy in copies_out(slot):
            copy.wait()
        return 0

    lax.fori_loop(0, z.count, end, 0)


def far_shards(z, prompt_kv, resp_q, resp_kv, out_grad, rewards, resp_prompt, resp_len):
    assert z.slots == 1
    count, n_dp = z.count, z.n_dp
    one = (2, z.prefix_len, z.width)
    smem = pl.BlockSpec(memory_space=pltpu.SMEM)
    q_out, self_out, per_resp = pl.pallas_call(
        functools.partial(far_kernel, z),
        out_shape=[
            jax.ShapeDtypeStruct(resp_q.shape, BF16),
            jax.ShapeDtypeStruct(resp_kv.shape, BF16),
            jax.ShapeDtypeStruct((count,) + one, BF16),
        ],
        in_specs=[smem] * 3 + [ANYWHERE] * 4,
        out_specs=[ANYWHERE] * 3,
        scratch_shapes=[
            pltpu.SMEM((n_dp,), F32),
            pltpu.SMEM((count,), jnp.int32),
            pltpu.SMEM((count,), F32),
            pltpu.VMEM(resp_q.shape, BF16),
            pltpu.VMEM(resp_q.shape, BF16),
            pltpu.VMEM(resp_kv.shape, BF16),
            pltpu.VMEM((count,) + one, BF16),
            pltpu.VMEM((count, z.tokens, z.lanes), BF16),
            pltpu.VMEM((count, 2, z.tokens, z.width), BF16),
            pltpu.VMEM((count,) + one, BF16),
            pltpu.SemaphoreType.DMA((count, 4)),
            pltpu.SemaphoreType.DMA((count,)),
            pltpu.SemaphoreType.DMA((count, 4)),
        ],
        compiler_params=pltpu.CompilerParams(vmem_limit_bytes=VMEM_BYTES),
        name="far_grads",
    )(
        resp_prompt,
        resp_len,
        lax.all_gather(rewards, "dp", axis=0, tiled=True),
        resp_q,
        out_grad,
        resp_kv,
        lax.all_gather(prompt_kv, "dp", axis=0),
    )
    my_prompts = lax.dynamic_slice_in_dim(resp_prompt, lax.axis_index("dp") * count, count)
    route = (jnp.arange(n_dp, dtype=jnp.int32)[:, None] == my_prompts[None, :]).astype(BF16)
    outgoing = jnp.dot(route, per_resp.reshape(count, -1), preferred_element_type=F32).astype(BF16)
    outgoing = outgoing.reshape((n_dp,) + one)
    incoming = lax.all_to_all(outgoing, "dp", split_axis=0, concat_axis=0, tiled=True)
    prefix_out = jnp.sum(incoming, axis=0, dtype=F32).astype(BF16)
    return (q_out, self_out, prefix_out)


def shards(prompt_kv, resp_q, resp_kv, out_grad, rewards, resp_prompt, resp_len):
    n_dp = lax.axis_size("dp")
    count = rewards.shape[0]
    prefix_len, width = prompt_kv.shape[1:]
    slots = (count + n_dp - 1) // n_dp
    z = Sizes(
        n_dp, count, slots, width // HD, resp_q.shape[1] // width, resp_q.shape[0] // count, prefix_len
    )
    part = near_shards if count // slots == n_dp else far_shards
    return part(z, prompt_kv, resp_q, resp_kv, out_grad, rewards, resp_prompt, resp_len)


def solution(mesh):
    in_specs = (
        P(None, ("groups", "dp"), "tensor"),
        P(("groups", "dp"), "tensor"),
        P(None, ("groups", "dp"), "tensor"),
        P(("groups", "dp"), "tensor"),
        P(("groups", "dp")),
        P("groups"),
        P(("groups", "dp")),
    )
    out_specs = (
        P(("groups", "dp"), "tensor"),
        P(None, ("groups", "dp"), "tensor"),
        P(None, ("groups", "dp"), "tensor"),
    )
    return jax.shard_map(shards, mesh=mesh, in_specs=in_specs, out_specs=out_specs, check_vma=False)
```

```python
import functools
import math
from typing import NamedTuple

import jax
import jax.numpy as jnp
from jax import lax
from jax.experimental import pallas as pl
from jax.experimental.pallas import tpu as pltpu
from jax.sharding import PartitionSpec as P

HD = 128
NEG = -1e30
F32 = jnp.float32
BF16 = jnp.bfloat16
PAIR = 2
FAR = 3
VMEM_BYTES = 63 * 1024 * 1024
GROUP_BYTES = 54528 * 1024
FINISH_BYTES = 24 * 1024 * 1024
ANYWHERE = pl.BlockSpec(memory_space=pl.ANY)


class Sizes(NamedTuple):
    n_dp: int
    count: int
    slots: int
    kv_heads: int
    group_size: int
    tokens: int
    prefix_len: int

    @property
    def width(self):
        return self.kv_heads * HD

    @property
    def lanes(self):
        return self.kv_heads * self.group_size * HD


def dot(a, b, dims):
    return lax.dot_general(a, b, (dims, ((), ())), preferred_element_type=F32)


NN = ((1,), (0,))
NT = ((1,), (1,))


class Bag:
    pass


class Unit(NamedTuple):
    at: list
    places: list
    k: object
    lens: list
    factors: list


def attend(z, units, q, og, kv, prefix, out, own_out, sink, apart):
    tokens, prefix_len, group_size = z.tokens, z.prefix_len, z.group_size
    scale = 1.0 / math.sqrt(HD)
    log_scale = scale * math.log2(math.e)
    whole = group_size - group_size % 2
    most = max(whole, 2) * tokens
    assert tokens & (tokens - 1) == 0
    token = lax.broadcasted_iota(jnp.int32, (1, most), 1) & (tokens - 1)
    key = lax.broadcasted_iota(jnp.int32, (tokens, most), 0)
    causal = key <= (lax.broadcasted_iota(jnp.int32, (tokens, most), 1) & (tokens - 1))
    left = lax.broadcasted_iota(jnp.int32, (1, 2 * tokens), 1) < tokens

    def columns(index):
        if isinstance(index, int):
            return slice(index * HD, (index + 1) * HD)
        return pl.ds(pl.multiple_of(index * HD, HD), HD)

    def head(k, h):
        return columns(k * group_size + h)

    def rows(ref, c):
        return jnp.concatenate([ref[c.t.at[n], head(c.t.k, h)] for n, h in c.blocks], axis=0)

    def halves(part):
        none = jnp.zeros_like(part)
        return [jnp.where(left, part, none), jnp.where(left, none, part)]

    def over_keys(combine, *parts):
        reduce = jnp.max if combine is jnp.maximum else jnp.sum
        eights = [reduce(part.reshape(-1, 8, part.shape[1]), axis=0) for part in parts]
        return reduce(functools.reduce(combine, eights), axis=0, keepdims=True)

    def own_half(both):
        return jnp.where(left, both[:tokens], both[tokens:])

    def rounded(*parts):
        return jnp.concatenate([part.astype(BF16) for part in parts], axis=0)

    chunks = []
    for unit in units:
        t = Bag()
        t.at, t.places, t.k, t.lens, t.factors = unit
        t.single = len(t.at) == 1
        t.members = range(len(t.at))
        sides = (0, 0) if t.single else (0, 1)
        t.cols = columns(t.k)
        t.key_p, t.value_p = prefix[0, :, t.cols], prefix[1, :, t.cols]
        t.keys = [kv[0, t.at[n], t.cols] for n in sides]
        t.values = [kv[1, t.at[n], t.cols] for n in sides]
        t.key_pair = jnp.concatenate(t.keys, axis=0)
        t.value_pair = jnp.concatenate(t.values, axis=0)
        t.key_t = jnp.concatenate([t.key_p.T, t.key_pair.T], axis=1)
        t.prefix_sums = {n: [] for n in t.members}
        t.self_sums = {n: [] for n in t.members}
        mine = []
        for n in t.members:
            c = Bag()
            c.t, c.side, c.blocks = t, n, [(n, h) for h in range(whole)]
            mine.append(c)
        if group_size % 2:
            c = Bag()
            c.t, c.side, c.blocks = t, None, [(n, group_size - 1) for n in sides]
            mine.append(c)
        t.left_over = len(mine)
        chunks += mine

    def products(c):
        t = c.t
        c.q_rows, c.g_rows = rows(q, c), rows(og, c)
        if c.side is None:
            key_s, value_s = t.key_pair, t.value_pair
        else:
            key_s, value_s = t.keys[c.side], t.values[c.side]
        c.scores = dot(jnp.concatenate([t.key_p, key_s], axis=0), c.q_rows, NT)
        c.gw = dot(jnp.concatenate([t.value_p, value_s], axis=0), c.g_rows, NT)

    def weigh(c):
        scores_p, scores_s = c.scores[:prefix_len], c.scores[prefix_len:]
        c.gw_p, c.gw_s = c.gw[:prefix_len], c.gw[prefix_len:]
        if c.side is None:
            scores_s, c.gw_s = own_half(scores_s), own_half(c.gw_s)
        scores_s = jnp.where(causal[:, : scores_s.shape[1]], scores_s, NEG)
        top = over_keys(jnp.maximum, scores_p, scores_s)
        c.e_p = jnp.exp2((scores_p - top) * log_scale)
        c.e_s = jnp.exp2((scores_s - top) * log_scale)
        total = over_keys(jnp.add, c.e_p, c.e_s)
        weighted = over_keys(jnp.add, c.e_p * c.gw_p, c.e_s * c.gw_s)
        if c.side is None:
            length = jnp.where(left, c.t.lens[0], 0 if c.t.single else c.t.lens[1])
            gain = jnp.where(left, c.t.factors[0], c.t.factors[-1])
        else:
            length, gain = c.t.lens[c.side], c.t.factors[c.side]
        inverse = 1.0 / total
        c.delta = weighted * inverse
        c.gain = inverse * jnp.where(token[:, : total.shape[1]] < length, gain, 0.0)

    def gradients(c):
        w_p, w_s = c.e_p * c.gain, c.e_s * c.gain
        d_p, d_s = w_p * (c.gw_p - c.delta), w_s * (c.gw_s - c.delta)
        if c.side is None:
            d_s, w_s = halves(d_s), halves(w_s)
            c.d_wide = rounded(d_p, *d_s)
            c.d_all = rounded(*halves(d_p), *d_s) if apart else c.d_wide
            c.w_all = rounded(*(halves(w_p) if apart else [w_p]), *w_s)
        else:
            empty = jnp.zeros_like(d_s)
            c.d_wide = rounded(*([d_p, empty, d_s] if c.side else [d_p, d_s, empty]))
            c.d_all = rounded(d_p, d_s)
            c.w_all = rounded(w_p, w_s)

    def outgoing(c):
        t = c.t
        q_grad = (dot(t.key_t, c.d_wide, NN) * scale).astype(BF16).T
        kg = dot(c.d_all, c.q_rows, NN)
        vg = dot(c.w_all, c.g_rows, NN)
        targets = t.members if c.side is None else [c.side]
        for place, (n, h) in enumerate(c.blocks):
            if c.side is not None or place < len(targets):
                out[t.places[n], :, head(t.k, h)] = q_grad[place * tokens : (place + 1) * tokens]
        many = 2 if c.side is None and apart else 1
        for place, n in enumerate(targets):
            if place < many:
                rows_p = slice(place * prefix_len, (place + 1) * prefix_len)
                t.prefix_sums[n if apart else 0].append((kg[rows_p], vg[rows_p]))
            start = many * prefix_len + place * tokens
            rows_s = slice(start, start + tokens)
            t.self_sums[n].append((kg[rows_s], vg[rows_s]))
        t.left_over -= 1
        if t.left_over == 0:
            for n in t.members:
                keys, values = zip(*t.self_sums[n])
                own_out[t.places[n], 0, :, t.cols] = (sum(keys) * scale).astype(BF16)
                own_out[t.places[n], 1, :, t.cols] = sum(values).astype(BF16)
                if apart or n == 0:
                    keys, values = zip(*t.prefix_sums[n])
                    sink(t.places[n], t.cols, sum(keys) * scale, sum(values))

    stages = (products, weigh, gradients, outgoing)
    for step in range(len(chunks) + len(stages) - 1):
        for late, stage in enumerate(stages):
            if 0 <= step - late < len(chunks):
                stage(chunks[step - late])


def token_rows(z, i):
    return pl.ds(pl.multiple_of(i * z.tokens, z.tokens), z.tokens)


def find_responses(z, me, turns, resp_prompt, order):
    for t, turn in enumerate(turns):
        prompt = me ^ turn
        found = t * z.slots
        for i in range(z.count):
            order[found] = i
            found = found + (resp_prompt[me * z.count + i] == prompt).astype(jnp.int32)


def prompt_total(z, me, prompt, resp_prompt, rewards):
    total = jnp.float32(0.0)
    for s in range(z.n_dp):
        for i in range(z.count):
            total += jnp.where(resp_prompt[(me ^ s) * z.count + i] == prompt, rewards[s][i], 0.0)
    return total


def reward_factor(z, reward, total, length):
    return (reward - total / z.count) * (z.tokens / length.astype(F32))


def row_copies(here, there, at_here, at_there, sems):
    (q0, og0, kv0), (q1, og1, kv1) = here, there
    return (
        pltpu.make_async_copy(q0.at[at_here], q1.at[at_there], sems.at[0]),
        pltpu.make_async_copy(og0.at[at_here], og1.at[at_there], sems.at[1]),
        pltpu.make_async_copy(kv0.at[:, at_here], kv1.at[:, at_there], sems.at[2]),
    )


def result_copies(out, own, q_out, self_out, place, at, sems, back=False):
    pairs = [
        (out.at[place], q_out.at[at]),
        (own.at[place], self_out.at[:, at]),
    ]
    return [
        pltpu.make_async_copy(*(reversed(pair) if back else pair), sems.at[place, n])
        for n, pair in enumerate(pairs)
    ]


def group_kernel(z, turns, raw, body, ahead, n_rewards, aliased, *refs):
    n_small = 2 + n_rewards
    small_hbm, given, refs = refs[:n_small], refs[n_small : n_small + 3], refs[n_small + 3 :]
    prompts, refs = refs[: len(turns)], refs[len(turns) :]
    if raw:
        (q_out, self_out), grads_out, in_order, refs = refs[:2], refs[2:3], refs[3:5], refs[5:]
    else:
        in_order, refs = refs[:2], refs[2 + aliased :]
        (q_out, self_out), grads_out, refs = refs[:2], refs[2 : 2 + len(turns)], refs[2 + len(turns) :]
    in_order = (in_order[0].at[0], in_order[0].at[1], in_order[1])
    resp_prompt, resp_len, *rewards = refs[:n_small]
    (order, q, og, kv, prefix, acc, out, own, grads,
     sem_small, sem_prefix, sem_in, sem_out, sem_grads, sem_order) = refs[n_small:]
    me = lax.axis_index("dp")
    n_slots = len(turns) * z.slots
    span = z.slots * z.tokens

    small = [
        pltpu.make_async_copy(src, dst, sem_small.at[n])
        for n, (src, dst) in enumerate(zip(small_hbm, (resp_prompt, resp_len, *rewards)))
    ]
    prefix_copies = [
        pltpu.make_async_copy(prompts[t], prefix.at[t], sem_prefix.at[t]) for t in range(len(turns))
    ]
    first_rows = []
    if not raw:
        first_rows = row_copies(in_order, (q, og, kv), pl.ds(ahead * span, span), pl.ds(0, span), sem_order.at[0])
    for copy in [*small, *first_rows, *prefix_copies]:
        copy.start()
    small[0].wait()
    ordered = [*turns, *ahead] if raw else turns
    find_responses(z, me, ordered, resp_prompt, order)

    def copies_in(slot):
        return row_copies(
            given, (q, og, kv), token_rows(z, order[slot]), token_rows(z, slot), sem_in.at[slot]
        )

    def copies_out(slot):
        return result_copies(out, own, q_out, self_out, slot, token_rows(z, order[slot]), sem_out)

    def copies_ordered(slot):
        rows = token_rows(z, slot - n_slots)
        return row_copies((q, og, kv), in_order, token_rows(z, slot), rows, sem_order.at[slot - n_slots])

    for slot in range(0 if raw else z.slots, len(ordered) * z.slots):
        for copy in copies_in(slot):
            copy.start()
    for copy in small[1:]:
        copy.wait()
    if not raw:
        acc[...] = jnp.zeros(acc.shape, F32)
    for copy in prefix_copies:
        copy.wait()

    pairs_in_body = body
    steps_per_turn = z.slots // PAIR // pairs_in_body

    def step(u, _):
        t = u // steps_per_turn
        first = u * pairs_in_body * PAIR
        mine = range(pairs_in_body * PAIR)

        def wait_for_slots():
            for n in mine:
                for copy in copies_in(first + n):
                    copy.wait()

        if raw:
            wait_for_slots()
        else:

            @pl.when(u == 0)
            def _():
                for copy in first_rows:
                    copy.wait()

            if len(turns) > 1:
                pl.when(u >= steps_per_turn)(wait_for_slots)

        def sink(place, cols, key_grad, value_grad):
            if raw:
                grads[place, 0, :, cols] = key_grad.astype(BF16)
                grads[place, 1, :, cols] = value_grad.astype(BF16)
            else:
                acc[t, 0, :, cols] += key_grad
                acc[t, 1, :, cols] += value_grad

        turn = turns[0]
        for n, other in enumerate(turns[1:], 1):
            turn = jnp.where(t == n, other, turn)
        total = None if raw else prompt_total(z, me, me ^ turn, resp_prompt, rewards)
        lens, factors = {}, {}
        for n in mine:
            i = order[first + n]
            lens[n] = resp_len[i]
            factors[n] = 1.0 if raw else reward_factor(z, rewards[0][i], total, resp_len[i])
        units = []
        for pair in range(pairs_in_body):
            places = [first + pair * PAIR + n for n in range(PAIR)]
            own_places = range(pair * PAIR, (pair + 1) * PAIR)
            at = [token_rows(z, n) for n in places]
            for k in range(z.kv_heads):
                units.append(Unit(at, places, k, [lens[n] for n in own_places], [factors[n] for n in own_places]))
        attend(z, units, q, og, kv, prefix.at[t], out, own, sink, raw)
        for n in mine:
            for copy in copies_out(first + n):
                copy.start()
        if raw:

            @pl.when(u == 0)
            def _():
                def pass_on(slot, _):
                    for copy in copies_in(slot):
                        copy.wait()
                    for copy in copies_ordered(slot):
                        copy.start()
                    return 0

                lax.fori_loop(n_slots, len(ordered) * z.slots, pass_on, 0)

        return 0

    lax.fori_loop(0, len(turns) * steps_per_turn, step, 0)
    if raw:
        last = [pltpu.make_async_copy(grads, grads_out[0], sem_grads.at[0])]
    else:
        grads[...] = acc[...].astype(BF16)
        last = [
            pltpu.make_async_copy(grads.at[t], grads_out[t], sem_grads.at[t]) for t in range(len(turns))
        ]
    for copy in last:
        copy.start()
    for slot in range(n_slots):
        for copy in copies_out(slot):
            copy.wait()
    if raw:
        for slot in range(n_slots, len(ordered) * z.slots):
            for copy in copies_ordered(slot):
                copy.wait()
    for copy in last:
        copy.wait()


def finish_kernel(z, n_come, *refs):
    n_small = 2 + z.n_dp
    small_hbm, per_resp_hbm, refs = refs[:n_small], refs[n_small], refs[n_small + 1 :]
    come_hbm, (q_out, self_out, grads_out), refs = refs[:n_come], refs[n_come + 2 : n_come + 5], refs[n_come + 5 :]
    resp_prompt, resp_len, *rewards = refs[:n_small]
    order, out, own, per_resp, come, grads, sem_small, sem_come, sem_in, sem_out = refs[n_small:]
    me = lax.axis_index("dp")
    small = [
        pltpu.make_async_copy(src, dst, sem_small.at[n])
        for n, (src, dst) in enumerate(zip(small_hbm, (resp_prompt, resp_len, *rewards)))
    ]
    late = [pltpu.make_async_copy(src, come.at[n], sem_come.at[n]) for n, src in enumerate(come_hbm)]
    late += [pltpu.make_async_copy(per_resp_hbm, per_resp, sem_come.at[n_come])]
    for copy in small + late:
        copy.start()
    small[0].wait()
    find_responses(z, me, (0,), resp_prompt, order)

    def moves(slot, back):
        sems = sem_in if back else sem_out
        return result_copies(out, own, q_out, self_out, slot, token_rows(z, order[slot]), sems, back)

    for slot in range(z.slots):
        for copy in moves(slot, True):
            copy.start()
    for copy in small[1:] + late:
        copy.wait()
    total = prompt_total(z, me, me, resp_prompt, rewards)
    summed = come[0].astype(F32)
    for n in range(1, n_come):
        summed += come[n].astype(F32)
    factors = [reward_factor(z, rewards[0][order[n]], total, resp_len[order[n]]) for n in range(z.slots)]
    for slot in range(z.slots):
        summed += per_resp[slot].astype(F32) * factors[slot]
    grads[...] = summed
    last = pltpu.make_async_copy(grads, grads_out, sem_small.at[0])
    last.start()
    for slot in range(z.slots):
        for copy in moves(slot, True):
            copy.wait()
        out[slot] = (out[slot].astype(F32) * factors[slot]).astype(BF16)
        own[slot] = (own[slot].astype(F32) * factors[slot]).astype(BF16)
        for copy in moves(slot, False):
            copy.start()
    for slot in range(z.slots):
        for copy in moves(slot, False):
            copy.wait()
    last.wait()


def near_shards(z, prompt_kv, resp_q, resp_kv, out_grad, rewards, resp_prompt, resp_len):
    n_dp = z.n_dp
    assert z.slots % PAIR == 0
    shape = jax.ShapeDtypeStruct
    one = (2, z.prefix_len, z.width)
    params = pltpu.CompilerParams(vmem_limit_bytes=VMEM_BYTES)
    cost = pl.CostEstimate(flops=0, bytes_accessed=0, transcendentals=0)
    assert n_dp == FAR + 1

    def swap(x, s):
        return lax.ppermute(x, "dp", [(i, i ^ s) for i in range(n_dp)])

    prompts = {0: prompt_kv, 2: swap(prompt_kv, 2), 1: swap(prompt_kv, 1)}
    others = [swap(rewards, s) for s in range(1, n_dp)]
    small = (resp_prompt, resp_len)
    slots = z.slots

    def smem_like(arrays):
        return [pltpu.SMEM(x.shape, x.dtype) for x in arrays]

    def grads_of(turns, raw, body, ahead, in_order=(), written=()):
        n_slots, n_turns = len(turns) * slots, len(turns)
        n_ahead = len(ahead) * slots if raw else 0
        n_held = n_slots + n_ahead
        used_rewards = [] if raw else [rewards, *others]
        used_small = [*small, *used_rewards]
        used_prompts = [prompts[turn] for turn in turns]
        operands = [*used_small, resp_q, out_grad, resp_kv, *used_prompts, *in_order, *written]
        grads_shapes = [(slots,) + one] if raw else [one] * n_turns
        ordered_shapes = [(2, n_ahead * z.tokens, z.lanes), (2, n_ahead * z.tokens, z.width)] if raw else []
        return pl.pallas_call(
            functools.partial(group_kernel, z, turns, raw, body, ahead, len(used_rewards), len(written)),
            out_shape=[shape(resp_q.shape, BF16), shape(resp_kv.shape, BF16)]
            + [shape(x, BF16) for x in grads_shapes + ordered_shapes],
            in_specs=[ANYWHERE] * len(operands),
            out_specs=[ANYWHERE] * (2 + len(grads_shapes) + len(ordered_shapes)),
            input_output_aliases={len(operands) - 2: 0, len(operands) - 1: 1} if written else {},
            scratch_shapes=[
                *smem_like(used_small),
                pltpu.SMEM((n_held + 1,), jnp.int32),
                pltpu.VMEM((n_held * z.tokens, z.lanes), BF16),
                pltpu.VMEM((n_held * z.tokens, z.lanes), BF16),
                pltpu.VMEM((2, n_held * z.tokens, z.width), BF16),
                pltpu.VMEM((n_turns,) + one, BF16),
                pltpu.VMEM((n_turns,) + one, F32),
                pltpu.VMEM((n_slots, z.tokens, z.lanes), BF16),
                pltpu.VMEM((n_slots, 2, z.tokens, z.width), BF16),
                pltpu.VMEM(grads_shapes[0] if raw else (n_turns,) + one, BF16),
                pltpu.SemaphoreType.DMA((len(used_small),)),
                pltpu.SemaphoreType.DMA((n_turns,)),
                pltpu.SemaphoreType.DMA((n_held, 3)),
                pltpu.SemaphoreType.DMA((n_slots, 2)),
                pltpu.SemaphoreType.DMA((n_turns,)),
                pltpu.SemaphoreType.DMA((max(n_ahead, 1), 3)),
            ],
            compiler_params=params if raw else pltpu.CompilerParams(vmem_limit_bytes=GROUP_BYTES),
            cost_estimate=cost,
            name="raw_grads" if raw else "group_grads",
        )(*operands)

    *written, per_resp, rows_ahead, kv_ahead = grads_of((0,), True, 1, (2, FAR))
    in_order = (rows_ahead, kv_ahead)
    onward, per_resp, *others = lax.optimization_barrier((prompts[2], per_resp, *others))
    prompts[FAR] = swap(onward, 1)
    *written, for_2 = grads_of((2,), False, slots // PAIR, 0, in_order, written)
    come = [swap(for_2, 2)]
    *written, for_far, for_1 = grads_of((FAR, 1), False, slots // PAIR, 1, in_order, written)
    last = [swap(for_far, FAR), swap(for_1, 1)]
    all_small = [*small, rewards, *others]
    operands = [*all_small, per_resp, *come, *written]
    q_out, self_out, own_grads = pl.pallas_call(
        functools.partial(finish_kernel, z, len(come)),
        out_shape=[shape(resp_q.shape, BF16), shape(resp_kv.shape, BF16), shape(one, F32)],
        in_specs=[ANYWHERE] * len(operands),
        out_specs=[ANYWHERE] * 3,
        input_output_aliases={len(operands) - 2: 0, len(operands) - 1: 1},
        scratch_shapes=[
            *smem_like(all_small),
            pltpu.SMEM((slots + 1,), jnp.int32),
            pltpu.VMEM((slots, z.tokens, z.lanes), BF16),
            pltpu.VMEM((slots, 2, z.tokens, z.width), BF16),
            pltpu.VMEM((slots,) + one, BF16),
            pltpu.VMEM((len(come),) + one, BF16),
            pltpu.VMEM(one, F32),
            pltpu.SemaphoreType.DMA((len(all_small),)),
            pltpu.SemaphoreType.DMA((len(come) + 1,)),
            pltpu.SemaphoreType.DMA((slots, 3)),
            pltpu.SemaphoreType.DMA((slots, 3)),
        ],
        compiler_params=pltpu.CompilerParams(vmem_limit_bytes=FINISH_BYTES),
        cost_estimate=cost,
        name="finish_own",
    )(*operands)
    prefix_out = (own_grads + sum(part.astype(F32) for part in last)).astype(BF16)
    return (q_out, self_out, prefix_out)


def far_kernel(z, *refs):
    (resp_prompt, resp_len, rewards, q_hbm, og_hbm, kv_hbm, prompts, q_out, self_out, prefix_outs,
     totals, lens, factors, q, og, kv, prefix, out, own, grads, sem_in, sem_prefix, sem_out) = refs
    me = lax.axis_index("dp")

    for p in range(z.n_dp):
        totals[p] = 0.0

    def copies_in(slot):
        rows = token_rows(z, slot)
        prompt = resp_prompt[me * z.count + slot]
        return (
            *row_copies((q_hbm, og_hbm, kv_hbm), (q, og, kv), rows, rows, sem_in.at[slot]),
            pltpu.make_async_copy(prompts.at[prompt], prefix.at[slot], sem_prefix.at[slot]),
        )

    def copies_out(slot):
        rows = token_rows(z, slot)
        return (
            *result_copies(out, own, q_out, self_out, slot, rows, sem_out),
            pltpu.make_async_copy(grads.at[slot], prefix_outs.at[slot], sem_out.at[slot, 3]),
        )

    def start(slot, _):
        for copy in copies_in(slot):
            copy.start()
        return 0

    lax.fori_loop(0, z.count, start, 0)

    def add(i, _):
        prompt = resp_prompt[i]
        totals[prompt] = totals[prompt] + rewards[i]
        return 0

    lax.fori_loop(0, z.n_dp * z.count, add, 0)

    def find_factor(slot, _):
        place = me * z.count + slot
        lens[slot] = resp_len[slot]
        factors[slot] = reward_factor(z, rewards[place], totals[resp_prompt[place]], resp_len[slot])
        return 0

    lax.fori_loop(0, z.count, find_factor, 0)

    def unit(slot, _):
        for copy in copies_in(slot):
            copy.wait()

        def sink(_, cols, key_grad, value_grad):
            grads[slot, 0, :, cols] = key_grad.astype(BF16)
            grads[slot, 1, :, cols] = value_grad.astype(BF16)

        units = [
            Unit([token_rows(z, slot)], [slot], k, [lens[slot]], [factors[slot]]) for k in range(z.kv_heads)
        ]
        attend(z, units, q, og, kv, prefix.at[slot], out, own, sink, True)
        for copy in copies_out(slot):
            copy.start()
        return 0

    lax.fori_loop(0, z.count, unit, 0)

    def end(slot, _):
        for copy in copies_out(slot):
            copy.wait()
        return 0

    lax.fori_loop(0, z.count, end, 0)


def far_shards(z, prompt_kv, resp_q, resp_kv, out_grad, rewards, resp_prompt, resp_len):
    assert z.slots == 1
    count, n_dp = z.count, z.n_dp
    one = (2, z.prefix_len, z.width)
    smem = pl.BlockSpec(memory_space=pltpu.SMEM)
    q_out, self_out, per_resp = pl.pallas_call(
        functools.partial(far_kernel, z),
        out_shape=[
            jax.ShapeDtypeStruct(resp_q.shape, BF16),
            jax.ShapeDtypeStruct(resp_kv.shape, BF16),
            jax.ShapeDtypeStruct((count,) + one, BF16),
        ],
        in_specs=[smem] * 3 + [ANYWHERE] * 4,
        out_specs=[ANYWHERE] * 3,
        scratch_shapes=[
            pltpu.SMEM((n_dp,), F32),
            pltpu.SMEM((count,), jnp.int32),
            pltpu.SMEM((count,), F32),
            pltpu.VMEM(resp_q.shape, BF16),
            pltpu.VMEM(resp_q.shape, BF16),
            pltpu.VMEM(resp_kv.shape, BF16),
            pltpu.VMEM((count,) + one, BF16),
            pltpu.VMEM((count, z.tokens, z.lanes), BF16),
            pltpu.VMEM((count, 2, z.tokens, z.width), BF16),
            pltpu.VMEM((count,) + one, BF16),
            pltpu.SemaphoreType.DMA((count, 4)),
            pltpu.SemaphoreType.DMA((count,)),
            pltpu.SemaphoreType.DMA((count, 4)),
        ],
        compiler_params=pltpu.CompilerParams(vmem_limit_bytes=VMEM_BYTES),
        name="far_grads",
    )(
        resp_prompt,
        resp_len,
        lax.all_gather(rewards, "dp", axis=0, tiled=True),
        resp_q,
        out_grad,
        resp_kv,
        lax.all_gather(prompt_kv, "dp", axis=0),
    )
    my_prompts = lax.dynamic_slice_in_dim(resp_prompt, lax.axis_index("dp") * count, count)
    route = (jnp.arange(n_dp, dtype=jnp.int32)[:, None] == my_prompts[None, :]).astype(BF16)
    outgoing = jnp.dot(route, per_resp.reshape(count, -1), preferred_element_type=F32).astype(BF16)
    outgoing = outgoing.reshape((n_dp,) + one)
    incoming = lax.all_to_all(outgoing, "dp", split_axis=0, concat_axis=0, tiled=True)
    prefix_out = jnp.sum(incoming, axis=0, dtype=F32).astype(BF16)
    return (q_out, self_out, prefix_out)


def shards(prompt_kv, resp_q, resp_kv, out_grad, rewards, resp_prompt, resp_len):
    n_dp = lax.axis_size("dp")
    count = rewards.shape[0]
    prefix_len, width = prompt_kv.shape[1:]
    slots = (count + n_dp - 1) // n_dp
    z = Sizes(
        n_dp, count, slots, width // HD, resp_q.shape[1] // width, resp_q.shape[0] // count, prefix_len
    )
    part = near_shards if count // slots == n_dp else far_shards
    return part(z, prompt_kv, resp_q, resp_kv, out_grad, rewards, resp_prompt, resp_len)


def solution(mesh):
    in_specs = (
        P(None, ("groups", "dp"), "tensor"),
        P(("groups", "dp"), "tensor"),
        P(None, ("groups", "dp"), "tensor"),
        P(("groups", "dp"), "tensor"),
        P(("groups", "dp")),
        P("groups"),
        P(("groups", "dp")),
    )
    out_specs = (
        P(("groups", "dp"), "tensor"),
        P(None, ("groups", "dp"), "tensor"),
        P(None, ("groups", "dp"), "tensor"),
    )
    return jax.shard_map(shards, mesh=mesh, in_specs=in_specs, out_specs=out_specs, check_vma=False)
```

```python
import functools
import math
from typing import NamedTuple

import jax
import jax.numpy as jnp
from jax import lax
from jax.experimental import pallas as pl
from jax.experimental.pallas import tpu as pltpu
from jax.sharding import PartitionSpec as P

HD = 128
NEG = -1e30
TAIL = 16
F32 = jnp.float32
BF16 = jnp.bfloat16
PAIR = 2
FAR = 3
VMEM_BYTES = 63 * 1024 * 1024
GROUP_BYTES = 53 * 1024 * 1024
FINISH_BYTES = 24 * 1024 * 1024
ANYWHERE = pl.BlockSpec(memory_space=pl.ANY)


class Sizes(NamedTuple):
    n_dp: int
    count: int
    slots: int
    kv_heads: int
    group_size: int
    tokens: int
    prefix_len: int

    @property
    def width(self):
        return self.kv_heads * HD

    @property
    def lanes(self):
        return self.kv_heads * self.group_size * HD


def dot(a, b, dims):
    return lax.dot_general(a, b, (dims, ((), ())), preferred_element_type=F32)


NN = ((1,), (0,))
NT = ((1,), (1,))


class Bag:
    pass


class Unit(NamedTuple):
    at: list
    places: list
    k: object
    lens: list
    factors: list


def attend(z, units, q, og, kv, prefix, out, own_out, sink, apart, fine=False):
    tokens, prefix_len, group_size = z.tokens, z.prefix_len, z.group_size
    scale = 1.0 / math.sqrt(HD)
    log_scale = scale * math.log2(math.e)
    whole = group_size - group_size % 2
    most = max(whole, 2) * tokens
    assert tokens & (tokens - 1) == 0
    token = lax.broadcasted_iota(jnp.int32, (1, most), 1) & (tokens - 1)
    key = lax.broadcasted_iota(jnp.int32, (tokens, most), 0)
    causal = key <= (lax.broadcasted_iota(jnp.int32, (tokens, most), 1) & (tokens - 1))
    left = lax.broadcasted_iota(jnp.int32, (1, 2 * tokens), 1) < tokens

    def columns(index):
        if isinstance(index, int):
            return slice(index * HD, (index + 1) * HD)
        return pl.ds(pl.multiple_of(index * HD, HD), HD)

    def head(k, h):
        return columns(k * group_size + h)

    def rows(ref, c):
        return jnp.concatenate([ref[c.t.at[n], head(c.t.k, h)] for n, h in c.blocks], axis=0)

    def halves(part):
        none = jnp.zeros_like(part)
        return [jnp.where(left, part, none), jnp.where(left, none, part)]

    def over_keys(combine, *parts):
        reduce = jnp.max if combine is jnp.maximum else jnp.sum
        eights = [reduce(part.reshape(-1, 8, part.shape[1]), axis=0) for part in parts]
        return reduce(functools.reduce(combine, eights), axis=0, keepdims=True)

    def own_half(both):
        return jnp.where(left, both[:tokens], both[tokens:])

    def rounded(*parts):
        return jnp.concatenate([part.astype(BF16) for part in parts], axis=0)

    chunks = []
    for unit in units:
        t = Bag()
        t.at, t.places, t.k, t.lens, t.factors = unit
        t.single = len(t.at) == 1
        t.members = range(len(t.at))
        sides = (0, 0) if t.single else (0, 1)
        t.cols = columns(t.k)
        t.key_p, t.value_p = prefix[0, :, t.cols], prefix[1, :, t.cols]
        t.keys = [kv[0, t.at[n], t.cols] for n in sides]
        t.values = [kv[1, t.at[n], t.cols] for n in sides]
        t.key_pair = jnp.concatenate(t.keys, axis=0)
        t.value_pair = jnp.concatenate(t.values, axis=0)
        t.key_t = jnp.concatenate([t.key_p.T, t.key_pair.T], axis=1)
        t.prefix_sums = {n: [] for n in t.members}
        t.self_sums = {n: [] for n in t.members}
        mine = []
        for n in t.members:
            c = Bag()
            c.t, c.side, c.blocks = t, n, [(n, h) for h in range(whole)]
            mine.append(c)
        if group_size % 2:
            c = Bag()
            c.t, c.side, c.blocks = t, None, [(n, group_size - 1) for n in sides]
            mine.append(c)
        t.left_over = len(mine)
        chunks += mine

    def products(c):
        t = c.t
        if c.side is None:
            key_s, value_s = t.key_pair, t.value_pair
        else:
            key_s, value_s = t.keys[c.side], t.values[c.side]
        c.scores = dot(jnp.concatenate([t.key_p, key_s], axis=0), rows(q, c), NT)
        c.gw = dot(jnp.concatenate([t.value_p, value_s], axis=0), rows(og, c), NT)

    def weigh(c):
        scores_p, scores_s = c.scores[:prefix_len], c.scores[prefix_len:]
        c.gw_p, c.gw_s = c.gw[:prefix_len], c.gw[prefix_len:]
        if c.side is None:
            scores_s, c.gw_s = own_half(scores_s), own_half(c.gw_s)
        scores_s = jnp.where(causal[:, : scores_s.shape[1]], scores_s, NEG)
        top = over_keys(jnp.maximum, scores_p, scores_s)
        c.e_p = jnp.exp2((scores_p - top) * log_scale)
        c.e_s = jnp.exp2((scores_s - top) * log_scale)

    def totals(c):
        total = over_keys(jnp.add, c.e_p, c.e_s)
        weighted = over_keys(jnp.add, c.e_p * c.gw_p, c.e_s * c.gw_s)
        if c.side is None:
            length = jnp.where(left, c.t.lens[0], 0 if c.t.single else c.t.lens[1])
            gain = jnp.where(left, c.t.factors[0], c.t.factors[-1])
        else:
            length, gain = c.t.lens[c.side], c.t.factors[c.side]
        inverse = 1.0 / total
        c.delta = weighted * inverse
        c.gain = inverse * jnp.where(token[:, : total.shape[1]] < length, gain, 0.0)

    def gradients(c):
        w_p, w_s = c.e_p * c.gain, c.e_s * c.gain
        d_p, d_s = w_p * (c.gw_p - c.delta), w_s * (c.gw_s - c.delta)
        if c.side is None:
            d_s, w_s = halves(d_s), halves(w_s)
            c.d_wide = rounded(d_p, *d_s)
            c.d_all = rounded(*halves(d_p), *d_s) if apart else c.d_wide
            c.w_all = rounded(*(halves(w_p) if apart else [w_p]), *w_s)
        else:
            empty = jnp.zeros_like(d_s)
            c.d_wide = rounded(*([d_p, empty, d_s] if c.side else [d_p, d_s, empty]))
            c.d_all = rounded(d_p, d_s)
            c.w_all = rounded(w_p, w_s)

    def outgoing(c):
        t = c.t
        q_grad = (dot(t.key_t, c.d_wide, NN) * scale).astype(BF16).T
        kg = dot(c.d_all, rows(q, c), NN)
        vg = dot(c.w_all, rows(og, c), NN)
        targets = t.members if c.side is None else [c.side]
        for place, (n, h) in enumerate(c.blocks):
            if c.side is not None or place < len(targets):
                out[t.places[n], :, head(t.k, h)] = q_grad[place * tokens : (place + 1) * tokens]
        many = 2 if c.side is None and apart else 1
        for place, n in enumerate(targets):
            if place < many:
                rows_p = slice(place * prefix_len, (place + 1) * prefix_len)
                t.prefix_sums[n if apart else 0].append((kg[rows_p], vg[rows_p]))
            start = many * prefix_len + place * tokens
            rows_s = slice(start, start + tokens)
            t.self_sums[n].append((kg[rows_s], vg[rows_s]))
        t.left_over -= 1
        if t.left_over == 0:
            for n in t.members:
                keys, values = zip(*t.self_sums[n])
                own_out[t.places[n], 0, :, t.cols] = (sum(keys) * scale).astype(BF16)
                own_out[t.places[n], 1, :, t.cols] = sum(values).astype(BF16)
                if apart or n == 0:
                    keys, values = zip(*t.prefix_sums[n])
                    sink(t.places[n], t.cols, sum(keys) * scale, sum(values))

    def weigh_and_totals(c):
        weigh(c)
        totals(c)

    if fine:
        stages = (products, weigh, totals, gradients, outgoing)
    else:
        stages = (products, weigh_and_totals, gradients, outgoing)
    for step in range(len(chunks) + len(stages) - 1):
        for late, stage in enumerate(stages):
            if 0 <= step - late < len(chunks):
                stage(chunks[step - late])


def token_rows(z, i):
    return pl.ds(pl.multiple_of(i * z.tokens, z.tokens), z.tokens)


def find_responses(z, me, turns, resp_prompt, order):
    for t, turn in enumerate(turns):
        prompt = me ^ turn
        found = t * z.slots
        for i in range(z.count):
            order[found] = i
            found = found + (resp_prompt[me * z.count + i] == prompt).astype(jnp.int32)


def prompt_total(z, me, prompt, resp_prompt, tails, far_rewards):
    sums = jnp.zeros((1, z.width), F32)
    for s in range(tails.shape[0]):
        tail = tails[s].astype(F32)
        sums += tail[0:1] + tail[1:2] + tail[2:3]
    lane = lax.broadcasted_iota(jnp.int32, sums.shape, 1)
    total = jnp.sum(jnp.where(lane == prompt, sums, 0.0))
    for i in range(z.count):
        total += jnp.where(resp_prompt[(me ^ FAR) * z.count + i] == prompt, far_rewards[i], 0.0)
    return total


def reward_factor(z, reward, total, length):
    return (reward - total / z.count) * (z.tokens / length.astype(F32))


def pack_kernel(z, prompt_hbm, rewards_hbm, resp_prompt_hbm, payload, rewards, resp_prompt, staged, sems):
    me = lax.axis_index("dp")
    small = [
        pltpu.make_async_copy(rewards_hbm, rewards, sems.at[0]),
        pltpu.make_async_copy(resp_prompt_hbm, resp_prompt, sems.at[1]),
    ]
    large = [
        pltpu.make_async_copy(
            prompt_hbm.at[n], staged.at[pl.ds(n * z.prefix_len, z.prefix_len)], sems.at[2 + n]
        )
        for n in range(2)
    ]
    for copy in small + large:
        copy.start()
    for copy in small:
        copy.wait()
    lane = lax.broadcasted_iota(jnp.int32, (1, z.width), 1)
    sums = jnp.zeros((1, z.width), F32)
    for i in range(z.count):
        sums += jnp.where(lane == resp_prompt[me * z.count + i], rewards[i], 0.0)
    high = sums.astype(BF16).astype(F32)
    middle = (sums - high).astype(BF16).astype(F32)
    low = sums - high - middle
    row = lax.broadcasted_iota(jnp.int32, (TAIL, z.width), 0)
    pieces = jnp.where(row == 0, high, jnp.where(row == 1, middle, jnp.where(row == 2, low, 0.0)))
    staged[2 * z.prefix_len :, :] = pieces.astype(BF16)
    for copy in large:
        copy.wait()
    last = pltpu.make_async_copy(staged, payload, sems.at[0])
    last.start()
    last.wait()


def tail_copies(z, payloads, tails, sems):
    return [
        pltpu.make_async_copy(payload.at[pl.ds(2 * z.prefix_len, TAIL)], tails.at[n], sems.at[n])
        for n, payload in enumerate(payloads)
    ]


def row_copies(here, there, at_here, at_there, sems):
    (q0, og0, kv0), (q1, og1, kv1) = here, there
    return (
        pltpu.make_async_copy(q0.at[at_here], q1.at[at_there], sems.at[0]),
        pltpu.make_async_copy(og0.at[at_here], og1.at[at_there], sems.at[1]),
        pltpu.make_async_copy(kv0.at[:, at_here], kv1.at[:, at_there], sems.at[2]),
    )


def result_copies(out, own, q_out, self_out, place, at, sems, back=False):
    pairs = [
        (out.at[place], q_out.at[at]),
        (own.at[place], self_out.at[:, at]),
    ]
    return [
        pltpu.make_async_copy(*(reversed(pair) if back else pair), sems.at[place, n])
        for n, pair in enumerate(pairs)
    ]


def group_kernel(z, turns, raw, body, ahead, n_tails, aliased, *refs):
    small_hbm, given = refs[:4], refs[4:7]
    tail_hbm, prompts = refs[7 : 7 + n_tails], refs[7 + n_tails : 7 + n_tails + len(turns)]
    refs = refs[7 + n_tails + len(turns) :]
    if raw:
        (q_out, self_out), grads_out, in_order, refs = refs[:2], refs[2:3], refs[3:5], refs[5:]
    else:
        in_order, refs = refs[:2], refs[2 + aliased :]
        (q_out, self_out), grads_out, refs = refs[:2], refs[2 : 2 + len(turns)], refs[2 + len(turns) :]
    in_order = (in_order[0].at[0], in_order[0].at[1], in_order[1])
    (resp_prompt, resp_len, rewards, far_rewards, order, q, og, kv, prefix, tails, acc, out, own, grads,
     sem_small, sem_tails, sem_prefix, sem_in, sem_out, sem_grads, sem_order) = refs
    me = lax.axis_index("dp")
    n_slots = len(turns) * z.slots
    span = z.slots * z.tokens

    small = [
        pltpu.make_async_copy(src, dst, sem_small.at[n])
        for n, (src, dst) in enumerate(zip(small_hbm, (resp_prompt, resp_len, rewards, far_rewards)))
    ]
    prefix_copies = [
        pltpu.make_async_copy(
            prompts[t].at[pl.ds(n * z.prefix_len, z.prefix_len)], prefix.at[t, n], sem_prefix.at[t, n]
        )
        for t in range(len(turns))
        for n in range(2)
    ]
    late = tail_copies(z, tail_hbm, tails, sem_tails)
    first_rows = []
    if not raw:
        first_rows = row_copies(in_order, (q, og, kv), pl.ds(ahead * span, span), pl.ds(0, span), sem_order.at[0])
    for copy in [*small, *first_rows, *prefix_copies, *late]:
        copy.start()
    small[0].wait()
    ordered = [*turns, *ahead] if raw else turns
    find_responses(z, me, ordered, resp_prompt, order)

    def copies_in(slot):
        return row_copies(
            given, (q, og, kv), token_rows(z, order[slot]), token_rows(z, slot), sem_in.at[slot]
        )

    def copies_out(slot):
        return result_copies(out, own, q_out, self_out, slot, token_rows(z, order[slot]), sem_out)

    def copies_ordered(slot):
        rows = token_rows(z, slot - n_slots)
        return row_copies((q, og, kv), in_order, token_rows(z, slot), rows, sem_order.at[slot - n_slots])

    for slot in range(0 if raw else z.slots, len(ordered) * z.slots):
        for copy in copies_in(slot):
            copy.start()
    for copy in small[1:] + late:
        copy.wait()
    if not raw:
        acc[...] = jnp.zeros(acc.shape, F32)
    for copy in prefix_copies:
        copy.wait()

    pairs_in_body = body
    steps_per_turn = z.slots // PAIR // pairs_in_body

    def step(u, _):
        t = u // steps_per_turn
        first = u * pairs_in_body * PAIR
        mine = range(pairs_in_body * PAIR)

        def wait_for_slots():
            for n in mine:
                for copy in copies_in(first + n):
                    copy.wait()

        if raw:
            wait_for_slots()
        else:

            @pl.when(u == 0)
            def _():
                for copy in first_rows:
                    copy.wait()

            if len(turns) > 1:
                pl.when(u >= steps_per_turn)(wait_for_slots)

        def sink(place, cols, key_grad, value_grad):
            if raw:
                grads[place, 0, :, cols] = key_grad.astype(BF16)
                grads[place, 1, :, cols] = value_grad.astype(BF16)
            else:
                acc[t, 0, :, cols] += key_grad
                acc[t, 1, :, cols] += value_grad

        turn = turns[0]
        for n, other in enumerate(turns[1:], 1):
            turn = jnp.where(t == n, other, turn)
        total = None if raw else prompt_total(z, me, me ^ turn, resp_prompt, tails, far_rewards)
        lens, factors = {}, {}
        for n in mine:
            i = order[first + n]
            lens[n] = resp_len[i]
            factors[n] = 1.0 if raw else reward_factor(z, rewards[i], total, resp_len[i])
        units = []
        for pair in range(pairs_in_body):
            places = [first + pair * PAIR + n for n in range(PAIR)]
            own_places = range(pair * PAIR, (pair + 1) * PAIR)
            at = [token_rows(z, n) for n in places]
            for k in range(z.kv_heads):
                units.append(Unit(at, places, k, [lens[n] for n in own_places], [factors[n] for n in own_places]))
        attend(z, units, q, og, kv, prefix.at[t], out, own, sink, raw, len(turns) > 1)
        for n in mine:
            for copy in copies_out(first + n):
                copy.start()
        if raw:

            @pl.when(u == 0)
            def _():
                def pass_on(slot, _):
                    for copy in copies_in(slot):
                        copy.wait()
                    for copy in copies_ordered(slot):
                        copy.start()
                    return 0

                lax.fori_loop(n_slots, len(ordered) * z.slots, pass_on, 0)

        return 0

    lax.fori_loop(0, len(turns) * steps_per_turn, step, 0)
    if raw:
        last = [pltpu.make_async_copy(grads, grads_out[0], sem_grads.at[0])]
    else:
        grads[...] = acc[...].astype(BF16)
        last = [
            pltpu.make_async_copy(grads.at[t], grads_out[t], sem_grads.at[t]) for t in range(len(turns))
        ]
    for copy in last:
        copy.start()
    for slot in range(n_slots):
        for copy in copies_out(slot):
            copy.wait()
    if raw:
        for slot in range(n_slots, len(ordered) * z.slots):
            for copy in copies_ordered(slot):
                copy.wait()
    for copy in last:
        copy.wait()


def finish_kernel(z, n_tails, n_come, *refs):
    small_hbm, tail_hbm = refs[:4], refs[4 : 4 + n_tails]
    per_resp_hbm, come_hbm = refs[4 + n_tails], refs[5 + n_tails : 5 + n_tails + n_come]
    q_out, self_out, grads_out = refs[7 + n_tails + n_come : 10 + n_tails + n_come]
    (resp_prompt, resp_len, rewards, far_rewards, order, tails, out, own, per_resp, come, grads,
     sem_small, sem_tails, sem_come, sem_in, sem_out) = refs[10 + n_tails + n_come :]
    me = lax.axis_index("dp")
    small = [
        pltpu.make_async_copy(src, dst, sem_small.at[n])
        for n, (src, dst) in enumerate(zip(small_hbm, (resp_prompt, resp_len, rewards, far_rewards)))
    ]
    late = tail_copies(z, tail_hbm, tails, sem_tails)
    late += [pltpu.make_async_copy(src, come.at[n], sem_come.at[n]) for n, src in enumerate(come_hbm)]
    late += [pltpu.make_async_copy(per_resp_hbm, per_resp, sem_come.at[n_come])]
    for copy in small + late:
        copy.start()
    small[0].wait()
    find_responses(z, me, (0,), resp_prompt, order)

    def moves(slot, back):
        sems = sem_in if back else sem_out
        return result_copies(out, own, q_out, self_out, slot, token_rows(z, order[slot]), sems, back)

    for slot in range(z.slots):
        for copy in moves(slot, True):
            copy.start()
    for copy in small[1:] + late:
        copy.wait()
    total = prompt_total(z, me, me, resp_prompt, tails, far_rewards)
    summed = come[0].astype(F32)
    for n in range(1, n_come):
        summed += come[n].astype(F32)
    factors = [reward_factor(z, rewards[order[n]], total, resp_len[order[n]]) for n in range(z.slots)]
    for slot in range(z.slots):
        summed += per_resp[slot].astype(F32) * factors[slot]
    grads[...] = summed
    last = pltpu.make_async_copy(grads, grads_out, sem_small.at[0])
    last.start()
    for slot in range(z.slots):
        for copy in moves(slot, True):
            copy.wait()
        out[slot] = (out[slot].astype(F32) * factors[slot]).astype(BF16)
        own[slot] = (own[slot].astype(F32) * factors[slot]).astype(BF16)
        for copy in moves(slot, False):
            copy.start()
    for slot in range(z.slots):
        for copy in moves(slot, False):
            copy.wait()
    last.wait()


def near_shards(z, prompt_kv, resp_q, resp_kv, out_grad, rewards, resp_prompt, resp_len):
    n_dp = z.n_dp
    assert z.slots % PAIR == 0
    shape = jax.ShapeDtypeStruct
    one = (2, z.prefix_len, z.width)
    params = pltpu.CompilerParams(vmem_limit_bytes=VMEM_BYTES)
    cost = pl.CostEstimate(flops=0, bytes_accessed=0, transcendentals=0)
    payload = pl.pallas_call(
        functools.partial(pack_kernel, z),
        out_shape=jax.ShapeDtypeStruct((2 * z.prefix_len + TAIL, z.width), BF16),
        in_specs=[ANYWHERE] * 3,
        out_specs=ANYWHERE,
        scratch_shapes=[
            pltpu.SMEM(rewards.shape, F32),
            pltpu.SMEM(resp_prompt.shape, jnp.int32),
            pltpu.VMEM((2 * z.prefix_len + TAIL, z.width), BF16),
            pltpu.SemaphoreType.DMA((4,)),
        ],
        compiler_params=pltpu.CompilerParams(vmem_limit_bytes=VMEM_BYTES),
        name="pack",
    )(prompt_kv, rewards, resp_prompt)

    assert n_dp == FAR + 1

    def swap(x, s):
        return lax.ppermute(x, "dp", [(i, i ^ s) for i in range(n_dp)])

    payloads = {0: payload, 2: swap(payload, 2), 1: swap(payload, 1)}
    tails = [payloads[s] for s in range(FAR)]
    small = (resp_prompt, resp_len, rewards)
    far_rewards = swap(rewards, FAR)
    smem = [pltpu.SMEM(x.shape, x.dtype) for x in (*small, rewards)]
    slots = z.slots

    def grads_of(turns, raw, body, ahead, in_order=(), written=()):
        n_slots, n_turns = len(turns) * slots, len(turns)
        n_ahead = len(ahead) * slots if raw else 0
        n_held = n_slots + n_ahead
        used_tails = [] if raw else tails
        used_small = (*small, rewards if raw else far_rewards)
        prompts = [payloads[turn] for turn in turns]
        operands = [*used_small, resp_q, out_grad, resp_kv, *used_tails, *prompts, *in_order, *written]
        grads_shapes = [(slots,) + one] if raw else [one] * n_turns
        ordered_shapes = [(2, n_ahead * z.tokens, z.lanes), (2, n_ahead * z.tokens, z.width)] if raw else []
        return pl.pallas_call(
            functools.partial(group_kernel, z, turns, raw, body, ahead, len(used_tails), len(written)),
            out_shape=[shape(resp_q.shape, BF16), shape(resp_kv.shape, BF16)]
            + [shape(x, BF16) for x in grads_shapes + ordered_shapes],
            in_specs=[ANYWHERE] * len(operands),
            out_specs=[ANYWHERE] * (2 + len(grads_shapes) + len(ordered_shapes)),
            input_output_aliases={len(operands) - 2: 0, len(operands) - 1: 1} if written else {},
            scratch_shapes=[
                *smem,
                pltpu.SMEM((n_held + 1,), jnp.int32),
                pltpu.VMEM((n_held * z.tokens, z.lanes), BF16),
                pltpu.VMEM((n_held * z.tokens, z.lanes), BF16),
                pltpu.VMEM((2, n_held * z.tokens, z.width), BF16),
                pltpu.VMEM((n_turns,) + one, BF16),
                pltpu.VMEM((FAR, TAIL, z.width), BF16),
                pltpu.VMEM((n_turns,) + one, F32),
                pltpu.VMEM((n_slots, z.tokens, z.lanes), BF16),
                pltpu.VMEM((n_slots, 2, z.tokens, z.width), BF16),
                pltpu.VMEM(grads_shapes[0] if raw else (n_turns,) + one, BF16),
                pltpu.SemaphoreType.DMA((len(smem),)),
                pltpu.SemaphoreType.DMA((FAR,)),
                pltpu.SemaphoreType.DMA((n_turns, 2)),
                pltpu.SemaphoreType.DMA((n_held, 3)),
                pltpu.SemaphoreType.DMA((n_slots, 2)),
                pltpu.SemaphoreType.DMA((n_turns,)),
                pltpu.SemaphoreType.DMA((max(n_ahead, 1), 3)),
            ],
            compiler_params=params if raw else pltpu.CompilerParams(vmem_limit_bytes=GROUP_BYTES),
            cost_estimate=cost,
            name="raw_grads" if raw else "group_grads",
        )(*operands)

    *written, per_resp, rows_ahead, kv_ahead = grads_of((0,), True, 1, (2, FAR))
    in_order = (rows_ahead, kv_ahead)
    onward, per_resp, far_rewards = lax.optimization_barrier((payloads[2], per_resp, far_rewards))
    payloads[FAR] = swap(onward, 1)
    *written, for_2 = grads_of((2,), False, slots // PAIR, 0, in_order, written)
    come = [swap(for_2, 2)]
    *written, for_far, for_1 = grads_of((FAR, 1), False, slots // PAIR, 1, in_order, written)
    last = [swap(for_far, FAR), swap(for_1, 1)]
    operands = [*small, far_rewards, *tails, per_resp, *come, *written]
    q_out, self_out, own_grads = pl.pallas_call(
        functools.partial(finish_kernel, z, len(tails), len(come)),
        out_shape=[shape(resp_q.shape, BF16), shape(resp_kv.shape, BF16), shape(one, F32)],
        in_specs=[ANYWHERE] * len(operands),
        out_specs=[ANYWHERE] * 3,
        input_output_aliases={len(operands) - 2: 0, len(operands) - 1: 1},
        scratch_shapes=[
            *smem,
            pltpu.SMEM((slots + 1,), jnp.int32),
            pltpu.VMEM((FAR, TAIL, z.width), BF16),
            pltpu.VMEM((slots, z.tokens, z.lanes), BF16),
            pltpu.VMEM((slots, 2, z.tokens, z.width), BF16),
            pltpu.VMEM((slots,) + one, BF16),
            pltpu.VMEM((len(come),) + one, BF16),
            pltpu.VMEM(one, F32),
            pltpu.SemaphoreType.DMA((len(smem),)),
            pltpu.SemaphoreType.DMA((FAR,)),
            pltpu.SemaphoreType.DMA((len(come) + 1,)),
            pltpu.SemaphoreType.DMA((slots, 3)),
            pltpu.SemaphoreType.DMA((slots, 3)),
        ],
        compiler_params=pltpu.CompilerParams(vmem_limit_bytes=FINISH_BYTES),
        cost_estimate=cost,
        name="finish_own",
    )(*operands)
    prefix_out = (own_grads + sum(part.astype(F32) for part in last)).astype(BF16)
    return (q_out, self_out, prefix_out)


def far_kernel(z, *refs):
    (resp_prompt, resp_len, rewards, q_hbm, og_hbm, kv_hbm, prompts, q_out, self_out, prefix_outs,
     totals, lens, factors, q, og, kv, prefix, out, own, grads, sem_in, sem_prefix, sem_out) = refs
    me = lax.axis_index("dp")

    for p in range(z.n_dp):
        totals[p] = 0.0

    def copies_in(slot):
        rows = token_rows(z, slot)
        prompt = resp_prompt[me * z.count + slot]
        return (
            *row_copies((q_hbm, og_hbm, kv_hbm), (q, og, kv), rows, rows, sem_in.at[slot]),
            pltpu.make_async_copy(prompts.at[prompt], prefix.at[slot], sem_prefix.at[slot]),
        )

    def copies_out(slot):
        rows = token_rows(z, slot)
        return (
            *result_copies(out, own, q_out, self_out, slot, rows, sem_out),
            pltpu.make_async_copy(grads.at[slot], prefix_outs.at[slot], sem_out.at[slot, 3]),
        )

    def start(slot, _):
        for copy in copies_in(slot):
            copy.start()
        return 0

    lax.fori_loop(0, z.count, start, 0)

    def add(i, _):
        prompt = resp_prompt[i]
        totals[prompt] = totals[prompt] + rewards[i]
        return 0

    lax.fori_loop(0, z.n_dp * z.count, add, 0)

    def find_factor(slot, _):
        place = me * z.count + slot
        lens[slot] = resp_len[slot]
        factors[slot] = reward_factor(z, rewards[place], totals[resp_prompt[place]], resp_len[slot])
        return 0

    lax.fori_loop(0, z.count, find_factor, 0)

    def unit(slot, _):
        for copy in copies_in(slot):
            copy.wait()

        def sink(_, cols, key_grad, value_grad):
            grads[slot, 0, :, cols] = key_grad.astype(BF16)
            grads[slot, 1, :, cols] = value_grad.astype(BF16)

        units = [
            Unit([token_rows(z, slot)], [slot], k, [lens[slot]], [factors[slot]]) for k in range(z.kv_heads)
        ]
        attend(z, units, q, og, kv, prefix.at[slot], out, own, sink, True)
        for copy in copies_out(slot):
            copy.start()
        return 0

    lax.fori_loop(0, z.count, unit, 0)

    def end(slot, _):
        for copy in copies_out(slot):
            copy.wait()
        return 0

    lax.fori_loop(0, z.count, end, 0)


def far_shards(z, prompt_kv, resp_q, resp_kv, out_grad, rewards, resp_prompt, resp_len):
    assert z.slots == 1
    count, n_dp = z.count, z.n_dp
    one = (2, z.prefix_len, z.width)
    smem = pl.BlockSpec(memory_space=pltpu.SMEM)
    q_out, self_out, per_resp = pl.pallas_call(
        functools.partial(far_kernel, z),
        out_shape=[
            jax.ShapeDtypeStruct(resp_q.shape, BF16),
            jax.ShapeDtypeStruct(resp_kv.shape, BF16),
            jax.ShapeDtypeStruct((count,) + one, BF16),
        ],
        in_specs=[smem] * 3 + [ANYWHERE] * 4,
        out_specs=[ANYWHERE] * 3,
        scratch_shapes=[
            pltpu.SMEM((n_dp,), F32),
            pltpu.SMEM((count,), jnp.int32),
            pltpu.SMEM((count,), F32),
            pltpu.VMEM(resp_q.shape, BF16),
            pltpu.VMEM(resp_q.shape, BF16),
            pltpu.VMEM(resp_kv.shape, BF16),
            pltpu.VMEM((count,) + one, BF16),
            pltpu.VMEM((count, z.tokens, z.lanes), BF16),
            pltpu.VMEM((count, 2, z.tokens, z.width), BF16),
            pltpu.VMEM((count,) + one, BF16),
            pltpu.SemaphoreType.DMA((count, 4)),
            pltpu.SemaphoreType.DMA((count,)),
            pltpu.SemaphoreType.DMA((count, 4)),
        ],
        compiler_params=pltpu.CompilerParams(vmem_limit_bytes=VMEM_BYTES),
        name="far_grads",
    )(
        resp_prompt,
        resp_len,
        lax.all_gather(rewards, "dp", axis=0, tiled=True),
        resp_q,
        out_grad,
        resp_kv,
        lax.all_gather(prompt_kv, "dp", axis=0),
    )
    my_prompts = lax.dynamic_slice_in_dim(resp_prompt, lax.axis_index("dp") * count, count)
    route = (jnp.arange(n_dp, dtype=jnp.int32)[:, None] == my_prompts[None, :]).astype(BF16)
    outgoing = jnp.dot(route, per_resp.reshape(count, -1), preferred_element_type=F32).astype(BF16)
    outgoing = outgoing.reshape((n_dp,) + one)
    incoming = lax.all_to_all(outgoing, "dp", split_axis=0, concat_axis=0, tiled=True)
    prefix_out = jnp.sum(incoming, axis=0, dtype=F32).astype(BF16)
    return (q_out, self_out, prefix_out)


def shards(prompt_kv, resp_q, resp_kv, out_grad, rewards, resp_prompt, resp_len):
    n_dp = lax.axis_size("dp")
    count = rewards.shape[0]
    prefix_len, width = prompt_kv.shape[1:]
    slots = (count + n_dp - 1) // n_dp
    z = Sizes(
        n_dp, count, slots, width // HD, resp_q.shape[1] // width, resp_q.shape[0] // count, prefix_len
    )
    part = near_shards if count // slots == n_dp else far_shards
    return part(z, prompt_kv, resp_q, resp_kv, out_grad, rewards, resp_prompt, resp_len)


def solution(mesh):
    in_specs = (
        P(None, ("groups", "dp"), "tensor"),
        P(("groups", "dp"), "tensor"),
        P(None, ("groups", "dp"), "tensor"),
        P(("groups", "dp"), "tensor"),
        P(("groups", "dp")),
        P("groups"),
        P(("groups", "dp")),
    )
    out_specs = (
        P(("groups", "dp"), "tensor"),
        P(None, ("groups", "dp"), "tensor"),
        P(None, ("groups", "dp"), "tensor"),
    )
    return jax.shard_map(shards, mesh=mesh, in_specs=in_specs, out_specs=out_specs, check_vma=False)
```

```python
import functools
import math
from typing import NamedTuple

import jax
import jax.numpy as jnp
from jax import lax
from jax.experimental import pallas as pl
from jax.experimental.pallas import tpu as pltpu
from jax.sharding import PartitionSpec as P

HD = 128
NEG = -1e30
TAIL = 16
F32 = jnp.float32
BF16 = jnp.bfloat16
PAIR = 2
FAR = 3
STRAIGHT = (2,)
VMEM_BYTES = 63 * 1024 * 1024
GROUP_BYTES = 53 * 1024 * 1024
FINISH_BYTES = 24 * 1024 * 1024
ANYWHERE = pl.BlockSpec(memory_space=pl.ANY)


class Sizes(NamedTuple):
    n_dp: int
    count: int
    slots: int
    kv_heads: int
    group_size: int
    tokens: int
    prefix_len: int

    @property
    def width(self):
        return self.kv_heads * HD

    @property
    def lanes(self):
        return self.kv_heads * self.group_size * HD


def dot(a, b, dims):
    return lax.dot_general(a, b, (dims, ((), ())), preferred_element_type=F32)


NN = ((1,), (0,))
NT = ((1,), (1,))
TN = ((0,), (0,))


class Bag:
    pass


class Unit(NamedTuple):
    at: list
    places: list
    k: object
    lens: list
    factors: list


def attend(z, units, q, og, kv, prefix, out, own_out, sink, apart, straight=False):
    tokens, prefix_len, group_size = z.tokens, z.prefix_len, z.group_size
    scale = 1.0 / math.sqrt(HD)
    log_scale = scale * math.log2(math.e)
    whole = group_size - group_size % 2
    most = max(whole, 2) * tokens
    assert tokens & (tokens - 1) == 0
    token = lax.broadcasted_iota(jnp.int32, (1, most), 1) & (tokens - 1)
    key = lax.broadcasted_iota(jnp.int32, (tokens, most), 0)
    causal = key <= (lax.broadcasted_iota(jnp.int32, (tokens, most), 1) & (tokens - 1))
    left = lax.broadcasted_iota(jnp.int32, (1, 2 * tokens), 1) < tokens

    def columns(index):
        if isinstance(index, int):
            return slice(index * HD, (index + 1) * HD)
        return pl.ds(pl.multiple_of(index * HD, HD), HD)

    def head(k, h):
        return columns(k * group_size + h)

    def rows(ref, c):
        return jnp.concatenate([ref[c.t.at[n], head(c.t.k, h)] for n, h in c.blocks], axis=0)

    def halves(part):
        none = jnp.zeros_like(part)
        return [jnp.where(left, part, none), jnp.where(left, none, part)]

    def over_keys(combine, *parts):
        reduce = jnp.max if combine is jnp.maximum else jnp.sum
        eights = [reduce(part.reshape(-1, 8, part.shape[1]), axis=0) for part in parts]
        return reduce(functools.reduce(combine, eights), axis=0, keepdims=True)

    def own_half(both):
        return jnp.where(left, both[:tokens], both[tokens:])

    def rounded(*parts):
        return jnp.concatenate([part.astype(BF16) for part in parts], axis=0)

    chunks = []
    for unit in units:
        t = Bag()
        t.at, t.places, t.k, t.lens, t.factors = unit
        t.single = len(t.at) == 1
        t.members = range(len(t.at))
        sides = (0, 0) if t.single else (0, 1)
        t.cols = columns(t.k)
        t.key_p, t.value_p = prefix[0, :, t.cols], prefix[1, :, t.cols]
        t.keys = [kv[0, t.at[n], t.cols] for n in sides]
        t.values = [kv[1, t.at[n], t.cols] for n in sides]
        t.key_pair = jnp.concatenate(t.keys, axis=0)
        t.value_pair = jnp.concatenate(t.values, axis=0)
        if straight:
            t.key_all = jnp.concatenate([t.key_p, t.key_pair], axis=0)
        else:
            t.key_t = jnp.concatenate([t.key_p.T, t.key_pair.T], axis=1)
        t.prefix_sums = {n: [] for n in t.members}
        t.self_sums = {n: [] for n in t.members}
        mine = []
        for n in t.members:
            c = Bag()
            c.t, c.side, c.blocks = t, n, [(n, h) for h in range(whole)]
            mine.append(c)
        if group_size % 2:
            c = Bag()
            c.t, c.side, c.blocks = t, None, [(n, group_size - 1) for n in sides]
            mine.append(c)
        t.left_over = len(mine)
        chunks += mine

    def products(c):
        t = c.t
        c.q_rows, c.g_rows = rows(q, c), rows(og, c)
        if c.side is None:
            key_s, value_s = t.key_pair, t.value_pair
        else:
            key_s, value_s = t.keys[c.side], t.values[c.side]
        c.scores = dot(jnp.concatenate([t.key_p, key_s], axis=0), c.q_rows, NT)
        c.gw = dot(jnp.concatenate([t.value_p, value_s], axis=0), c.g_rows, NT)

    def weigh(c):
        scores_p, scores_s = c.scores[:prefix_len], c.scores[prefix_len:]
        c.gw_p, c.gw_s = c.gw[:prefix_len], c.gw[prefix_len:]
        if c.side is None:
            scores_s, c.gw_s = own_half(scores_s), own_half(c.gw_s)
        scores_s = jnp.where(causal[:, : scores_s.shape[1]], scores_s, NEG)
        top = over_keys(jnp.maximum, scores_p, scores_s)
        c.e_p = jnp.exp2((scores_p - top) * log_scale)
        c.e_s = jnp.exp2((scores_s - top) * log_scale)
        total = over_keys(jnp.add, c.e_p, c.e_s)
        weighted = over_keys(jnp.add, c.e_p * c.gw_p, c.e_s * c.gw_s)
        if c.side is None:
            length = jnp.where(left, c.t.lens[0], 0 if c.t.single else c.t.lens[1])
            gain = jnp.where(left, c.t.factors[0], c.t.factors[-1])
        else:
            length, gain = c.t.lens[c.side], c.t.factors[c.side]
        inverse = 1.0 / total
        c.delta = weighted * inverse
        c.gain = inverse * jnp.where(token[:, : total.shape[1]] < length, gain, 0.0)

    def gradients(c):
        w_p, w_s = c.e_p * c.gain, c.e_s * c.gain
        d_p, d_s = w_p * (c.gw_p - c.delta), w_s * (c.gw_s - c.delta)
        if c.side is None:
            d_s, w_s = halves(d_s), halves(w_s)
            c.d_wide = rounded(d_p, *d_s)
            c.d_all = rounded(*halves(d_p), *d_s) if apart else c.d_wide
            c.w_all = rounded(*(halves(w_p) if apart else [w_p]), *w_s)
        else:
            empty = jnp.zeros_like(d_s)
            c.d_wide = rounded(*([d_p, empty, d_s] if c.side else [d_p, d_s, empty]))
            c.d_all = rounded(d_p, d_s)
            c.w_all = rounded(w_p, w_s)

    def outgoing(c):
        t = c.t
        if straight:
            q_grad = (dot(c.d_wide, t.key_all, TN) * scale).astype(BF16)
        else:
            q_grad = (dot(t.key_t, c.d_wide, NN) * scale).astype(BF16).T
        kg = dot(c.d_all, c.q_rows, NN)
        vg = dot(c.w_all, c.g_rows, NN)
        targets = t.members if c.side is None else [c.side]
        for place, (n, h) in enumerate(c.blocks):
            if c.side is not None or place < len(targets):
                out[t.places[n], :, head(t.k, h)] = q_grad[place * tokens : (place + 1) * tokens]
        many = 2 if c.side is None and apart else 1
        for place, n in enumerate(targets):
            if place < many:
                rows_p = slice(place * prefix_len, (place + 1) * prefix_len)
                t.prefix_sums[n if apart else 0].append((kg[rows_p], vg[rows_p]))
            start = many * prefix_len + place * tokens
            rows_s = slice(start, start + tokens)
            t.self_sums[n].append((kg[rows_s], vg[rows_s]))
        t.left_over -= 1
        if t.left_over == 0:
            for n in t.members:
                keys, values = zip(*t.self_sums[n])
                own_out[t.places[n], 0, :, t.cols] = (sum(keys) * scale).astype(BF16)
                own_out[t.places[n], 1, :, t.cols] = sum(values).astype(BF16)
                if apart or n == 0:
                    keys, values = zip(*t.prefix_sums[n])
                    sink(t.places[n], t.cols, sum(keys) * scale, sum(values))

    stages = (products, weigh, gradients, outgoing)
    for step in range(len(chunks) + len(stages) - 1):
        for late, stage in enumerate(stages):
            if 0 <= step - late < len(chunks):
                stage(chunks[step - late])


def token_rows(z, i):
    return pl.ds(pl.multiple_of(i * z.tokens, z.tokens), z.tokens)


def find_responses(z, me, turns, resp_prompt, order):
    for t, turn in enumerate(turns):
        prompt = me ^ turn
        found = t * z.slots
        for i in range(z.count):
            order[found] = i
            found = found + (resp_prompt[me * z.count + i] == prompt).astype(jnp.int32)


def prompt_total(z, me, prompt, resp_prompt, tails, far_rewards):
    sums = jnp.zeros((1, z.width), F32)
    for s in range(tails.shape[0]):
        tail = tails[s].astype(F32)
        sums += tail[0:1] + tail[1:2] + tail[2:3]
    lane = lax.broadcasted_iota(jnp.int32, sums.shape, 1)
    total = jnp.sum(jnp.where(lane == prompt, sums, 0.0))
    for i in range(z.count):
        total += jnp.where(resp_prompt[(me ^ FAR) * z.count + i] == prompt, far_rewards[i], 0.0)
    return total


def reward_factor(z, reward, total, length):
    return (reward - total / z.count) * (z.tokens / length.astype(F32))


def pack_kernel(z, prompt_hbm, rewards_hbm, resp_prompt_hbm, payload, rewards, resp_prompt, staged, sems):
    me = lax.axis_index("dp")
    small = [
        pltpu.make_async_copy(rewards_hbm, rewards, sems.at[0]),
        pltpu.make_async_copy(resp_prompt_hbm, resp_prompt, sems.at[1]),
    ]
    large = [
        pltpu.make_async_copy(
            prompt_hbm.at[n], staged.at[pl.ds(n * z.prefix_len, z.prefix_len)], sems.at[2 + n]
        )
        for n in range(2)
    ]
    for copy in small + large:
        copy.start()
    for copy in small:
        copy.wait()
    lane = lax.broadcasted_iota(jnp.int32, (1, z.width), 1)
    sums = jnp.zeros((1, z.width), F32)
    for i in range(z.count):
        sums += jnp.where(lane == resp_prompt[me * z.count + i], rewards[i], 0.0)
    high = sums.astype(BF16).astype(F32)
    middle = (sums - high).astype(BF16).astype(F32)
    low = sums - high - middle
    row = lax.broadcasted_iota(jnp.int32, (TAIL, z.width), 0)
    pieces = jnp.where(row == 0, high, jnp.where(row == 1, middle, jnp.where(row == 2, low, 0.0)))
    staged[2 * z.prefix_len :, :] = pieces.astype(BF16)
    for copy in large:
        copy.wait()
    last = pltpu.make_async_copy(staged, payload, sems.at[0])
    last.start()
    last.wait()


def tail_copies(z, payloads, tails, sems):
    return [
        pltpu.make_async_copy(payload.at[pl.ds(2 * z.prefix_len, TAIL)], tails.at[n], sems.at[n])
        for n, payload in enumerate(payloads)
    ]


def row_copies(here, there, at_here, at_there, sems):
    (q0, og0, kv0), (q1, og1, kv1) = here, there
    return (
        pltpu.make_async_copy(q0.at[at_here], q1.at[at_there], sems.at[0]),
        pltpu.make_async_copy(og0.at[at_here], og1.at[at_there], sems.at[1]),
        pltpu.make_async_copy(kv0.at[:, at_here], kv1.at[:, at_there], sems.at[2]),
    )


def result_copies(out, own, q_out, self_out, place, at, sems, back=False):
    pairs = [
        (out.at[place], q_out.at[at]),
        (own.at[place], self_out.at[:, at]),
    ]
    return [
        pltpu.make_async_copy(*(reversed(pair) if back else pair), sems.at[place, n])
        for n, pair in enumerate(pairs)
    ]


def group_kernel(z, turns, raw, body, ahead, n_tails, aliased, *refs):
    small_hbm, given = refs[:4], refs[4:7]
    tail_hbm, prompts = refs[7 : 7 + n_tails], refs[7 + n_tails : 7 + n_tails + len(turns)]
    refs = refs[7 + n_tails + len(turns) :]
    if raw:
        (q_out, self_out), grads_out, in_order, refs = refs[:2], refs[2:3], refs[3:5], refs[5:]
    else:
        in_order, refs = refs[:2], refs[2 + aliased :]
        (q_out, self_out), grads_out, refs = refs[:2], refs[2 : 2 + len(turns)], refs[2 + len(turns) :]
    in_order = (in_order[0].at[0], in_order[0].at[1], in_order[1])
    (resp_prompt, resp_len, rewards, far_rewards, order, q, og, kv, prefix, tails, acc, out, own, grads,
     sem_small, sem_tails, sem_prefix, sem_in, sem_out, sem_grads, sem_order) = refs
    me = lax.axis_index("dp")
    n_slots = len(turns) * z.slots
    span = z.slots * z.tokens

    small = [
        pltpu.make_async_copy(src, dst, sem_small.at[n])
        for n, (src, dst) in enumerate(zip(small_hbm, (resp_prompt, resp_len, rewards, far_rewards)))
    ]
    prefix_copies = [
        pltpu.make_async_copy(
            prompts[t].at[pl.ds(n * z.prefix_len, z.prefix_len)], prefix.at[t, n], sem_prefix.at[t, n]
        )
        for t in range(len(turns))
        for n in range(2)
    ]
    late = tail_copies(z, tail_hbm, tails, sem_tails)
    first_rows = []
    if not raw:
        first_rows = row_copies(in_order, (q, og, kv), pl.ds(ahead * span, span), pl.ds(0, span), sem_order.at[0])
    for copy in [*small, *first_rows, *prefix_copies, *late]:
        copy.start()
    small[0].wait()
    ordered = [*turns, *ahead] if raw else turns
    find_responses(z, me, ordered, resp_prompt, order)

    def copies_in(slot):
        return row_copies(
            given, (q, og, kv), token_rows(z, order[slot]), token_rows(z, slot), sem_in.at[slot]
        )

    def copies_out(slot):
        return result_copies(out, own, q_out, self_out, slot, token_rows(z, order[slot]), sem_out)

    def copies_ordered(slot):
        rows = token_rows(z, slot - n_slots)
        return row_copies((q, og, kv), in_order, token_rows(z, slot), rows, sem_order.at[slot - n_slots])

    for slot in range(0 if raw else z.slots, len(ordered) * z.slots):
        for copy in copies_in(slot):
            copy.start()
    for copy in small[1:] + late:
        copy.wait()
    if not raw:
        acc[...] = jnp.zeros(acc.shape, F32)
    for copy in prefix_copies:
        copy.wait()

    pairs_in_body = body
    steps_per_turn = z.slots // PAIR // pairs_in_body

    def step(u, _):
        t = u // steps_per_turn
        first = u * pairs_in_body * PAIR
        mine = range(pairs_in_body * PAIR)

        def wait_for_slots():
            for n in mine:
                for copy in copies_in(first + n):
                    copy.wait()

        if raw:
            wait_for_slots()
        else:

            @pl.when(u == 0)
            def _():
                for copy in first_rows:
                    copy.wait()

            if len(turns) > 1:
                pl.when(u >= steps_per_turn)(wait_for_slots)

        def sink(place, cols, key_grad, value_grad):
            if raw:
                grads[place, 0, :, cols] = key_grad.astype(BF16)
                grads[place, 1, :, cols] = value_grad.astype(BF16)
            else:
                acc[t, 0, :, cols] += key_grad
                acc[t, 1, :, cols] += value_grad

        turn = turns[0]
        for n, other in enumerate(turns[1:], 1):
            turn = jnp.where(t == n, other, turn)
        total = None if raw else prompt_total(z, me, me ^ turn, resp_prompt, tails, far_rewards)
        lens, factors = {}, {}
        for n in mine:
            i = order[first + n]
            lens[n] = resp_len[i]
            factors[n] = 1.0 if raw else reward_factor(z, rewards[i], total, resp_len[i])
        units = []
        for pair in range(pairs_in_body):
            places = [first + pair * PAIR + n for n in range(PAIR)]
            own_places = range(pair * PAIR, (pair + 1) * PAIR)
            at = [token_rows(z, n) for n in places]
            for k in range(z.kv_heads):
                units.append(Unit(at, places, k, [lens[n] for n in own_places], [factors[n] for n in own_places]))
        attend(z, units, q, og, kv, prefix.at[t], out, own, sink, raw, turns == STRAIGHT)
        for n in mine:
            for copy in copies_out(first + n):
                copy.start()
        if raw:

            @pl.when(u == 0)
            def _():
                def pass_on(slot, _):
                    for copy in copies_in(slot):
                        copy.wait()
                    for copy in copies_ordered(slot):
                        copy.start()
                    return 0

                lax.fori_loop(n_slots, len(ordered) * z.slots, pass_on, 0)

        return 0

    lax.fori_loop(0, len(turns) * steps_per_turn, step, 0)
    if raw:
        last = [pltpu.make_async_copy(grads, grads_out[0], sem_grads.at[0])]
    else:
        grads[...] = acc[...].astype(BF16)
        last = [
            pltpu.make_async_copy(grads.at[t], grads_out[t], sem_grads.at[t]) for t in range(len(turns))
        ]
    for copy in last:
        copy.start()
    for slot in range(n_slots):
        for copy in copies_out(slot):
            copy.wait()
    if raw:
        for slot in range(n_slots, len(ordered) * z.slots):
            for copy in copies_ordered(slot):
                copy.wait()
    for copy in last:
        copy.wait()


def finish_kernel(z, n_tails, n_come, *refs):
    small_hbm, tail_hbm = refs[:4], refs[4 : 4 + n_tails]
    per_resp_hbm, come_hbm = refs[4 + n_tails], refs[5 + n_tails : 5 + n_tails + n_come]
    q_out, self_out, grads_out = refs[7 + n_tails + n_come : 10 + n_tails + n_come]
    (resp_prompt, resp_len, rewards, far_rewards, order, tails, out, own, per_resp, come, grads,
     sem_small, sem_tails, sem_come, sem_in, sem_out) = refs[10 + n_tails + n_come :]
    me = lax.axis_index("dp")
    small = [
        pltpu.make_async_copy(src, dst, sem_small.at[n])
        for n, (src, dst) in enumerate(zip(small_hbm, (resp_prompt, resp_len, rewards, far_rewards)))
    ]
    late = tail_copies(z, tail_hbm, tails, sem_tails)
    late += [pltpu.make_async_copy(src, come.at[n], sem_come.at[n]) for n, src in enumerate(come_hbm)]
    late += [pltpu.make_async_copy(per_resp_hbm, per_resp, sem_come.at[n_come])]
    for copy in small + late:
        copy.start()
    small[0].wait()
    find_responses(z, me, (0,), resp_prompt, order)

    def moves(slot, back):
        sems = sem_in if back else sem_out
        return result_copies(out, own, q_out, self_out, slot, token_rows(z, order[slot]), sems, back)

    for slot in range(z.slots):
        for copy in moves(slot, True):
            copy.start()
    for copy in small[1:] + late:
        copy.wait()
    total = prompt_total(z, me, me, resp_prompt, tails, far_rewards)
    summed = come[0].astype(F32)
    for n in range(1, n_come):
        summed += come[n].astype(F32)
    factors = [reward_factor(z, rewards[order[n]], total, resp_len[order[n]]) for n in range(z.slots)]
    for slot in range(z.slots):
        summed += per_resp[slot].astype(F32) * factors[slot]
    grads[...] = summed
    last = pltpu.make_async_copy(grads, grads_out, sem_small.at[0])
    last.start()
    for slot in range(z.slots):
        for copy in moves(slot, True):
            copy.wait()
        out[slot] = (out[slot].astype(F32) * factors[slot]).astype(BF16)
        own[slot] = (own[slot].astype(F32) * factors[slot]).astype(BF16)
        for copy in moves(slot, False):
            copy.start()
    for slot in range(z.slots):
        for copy in moves(slot, False):
            copy.wait()
    last.wait()


def near_shards(z, prompt_kv, resp_q, resp_kv, out_grad, rewards, resp_prompt, resp_len):
    n_dp = z.n_dp
    assert z.slots % PAIR == 0
    shape = jax.ShapeDtypeStruct
    one = (2, z.prefix_len, z.width)
    params = pltpu.CompilerParams(vmem_limit_bytes=VMEM_BYTES)
    cost = pl.CostEstimate(flops=0, bytes_accessed=0, transcendentals=0)
    payload = pl.pallas_call(
        functools.partial(pack_kernel, z),
        out_shape=jax.ShapeDtypeStruct((2 * z.prefix_len + TAIL, z.width), BF16),
        in_specs=[ANYWHERE] * 3,
        out_specs=ANYWHERE,
        scratch_shapes=[
            pltpu.SMEM(rewards.shape, F32),
            pltpu.SMEM(resp_prompt.shape, jnp.int32),
            pltpu.VMEM((2 * z.prefix_len + TAIL, z.width), BF16),
            pltpu.SemaphoreType.DMA((4,)),
        ],
        compiler_params=pltpu.CompilerParams(vmem_limit_bytes=VMEM_BYTES),
        name="pack",
    )(prompt_kv, rewards, resp_prompt)

    assert n_dp == FAR + 1

    def swap(x, s):
        return lax.ppermute(x, "dp", [(i, i ^ s) for i in range(n_dp)])

    payloads = {0: payload, 2: swap(payload, 2), 1: swap(payload, 1)}
    tails = [payloads[s] for s in range(FAR)]
    small = (resp_prompt, resp_len, rewards)
    far_rewards = swap(rewards, FAR)
    smem = [pltpu.SMEM(x.shape, x.dtype) for x in (*small, rewards)]
    slots = z.slots

    def grads_of(turns, raw, body, ahead, in_order=(), written=()):
        n_slots, n_turns = len(turns) * slots, len(turns)
        n_ahead = len(ahead) * slots if raw else 0
        n_held = n_slots + n_ahead
        used_tails = [] if raw else tails
        used_small = (*small, rewards if raw else far_rewards)
        prompts = [payloads[turn] for turn in turns]
        operands = [*used_small, resp_q, out_grad, resp_kv, *used_tails, *prompts, *in_order, *written]
        grads_shapes = [(slots,) + one] if raw else [one] * n_turns
        ordered_shapes = [(2, n_ahead * z.tokens, z.lanes), (2, n_ahead * z.tokens, z.width)] if raw else []
        return pl.pallas_call(
            functools.partial(group_kernel, z, turns, raw, body, ahead, len(used_tails), len(written)),
            out_shape=[shape(resp_q.shape, BF16), shape(resp_kv.shape, BF16)]
            + [shape(x, BF16) for x in grads_shapes + ordered_shapes],
            in_specs=[ANYWHERE] * len(operands),
            out_specs=[ANYWHERE] * (2 + len(grads_shapes) + len(ordered_shapes)),
            input_output_aliases={len(operands) - 2: 0, len(operands) - 1: 1} if written else {},
            scratch_shapes=[
                *smem,
                pltpu.SMEM((n_held + 1,), jnp.int32),
                pltpu.VMEM((n_held * z.tokens, z.lanes), BF16),
                pltpu.VMEM((n_held * z.tokens, z.lanes), BF16),
                pltpu.VMEM((2, n_held * z.tokens, z.width), BF16),
                pltpu.VMEM((n_turns,) + one, BF16),
                pltpu.VMEM((FAR, TAIL, z.width), BF16),
                pltpu.VMEM((n_turns,) + one, F32),
                pltpu.VMEM((n_slots, z.tokens, z.lanes), BF16),
                pltpu.VMEM((n_slots, 2, z.tokens, z.width), BF16),
                pltpu.VMEM(grads_shapes[0] if raw else (n_turns,) + one, BF16),
                pltpu.SemaphoreType.DMA((len(smem),)),
                pltpu.SemaphoreType.DMA((FAR,)),
                pltpu.SemaphoreType.DMA((n_turns, 2)),
                pltpu.SemaphoreType.DMA((n_held, 3)),
                pltpu.SemaphoreType.DMA((n_slots, 2)),
                pltpu.SemaphoreType.DMA((n_turns,)),
                pltpu.SemaphoreType.DMA((max(n_ahead, 1), 3)),
            ],
            compiler_params=params if raw else pltpu.CompilerParams(
                vmem_limit_bytes=GROUP_BYTES, fuse_transposed_lhs_in_matmul=turns == STRAIGHT
            ),
            cost_estimate=cost,
            name="raw_grads" if raw else "group_grads",
        )(*operands)

    *written, per_resp, rows_ahead, kv_ahead = grads_of((0,), True, 1, (2, FAR))
    in_order = (rows_ahead, kv_ahead)
    onward, per_resp, far_rewards = lax.optimization_barrier((payloads[2], per_resp, far_rewards))
    payloads[FAR] = swap(onward, 1)
    *written, for_2 = grads_of((2,), False, slots // PAIR, 0, in_order, written)
    come = [swap(for_2, 2)]
    *written, for_far, for_1 = grads_of((FAR, 1), False, slots // PAIR, 1, in_order, written)
    last = [swap(for_far, FAR), swap(for_1, 1)]
    operands = [*small, far_rewards, *tails, per_resp, *come, *written]
    q_out, self_out, own_grads = pl.pallas_call(
        functools.partial(finish_kernel, z, len(tails), len(come)),
        out_shape=[shape(resp_q.shape, BF16), shape(resp_kv.shape, BF16), shape(one, F32)],
        in_specs=[ANYWHERE] * len(operands),
        out_specs=[ANYWHERE] * 3,
        input_output_aliases={len(operands) - 2: 0, len(operands) - 1: 1},
        scratch_shapes=[
            *smem,
            pltpu.SMEM((slots + 1,), jnp.int32),
            pltpu.VMEM((FAR, TAIL, z.width), BF16),
            pltpu.VMEM((slots, z.tokens, z.lanes), BF16),
            pltpu.VMEM((slots, 2, z.tokens, z.width), BF16),
            pltpu.VMEM((slots,) + one, BF16),
            pltpu.VMEM((len(come),) + one, BF16),
            pltpu.VMEM(one, F32),
            pltpu.SemaphoreType.DMA((len(smem),)),
            pltpu.SemaphoreType.DMA((FAR,)),
            pltpu.SemaphoreType.DMA((len(come) + 1,)),
            pltpu.SemaphoreType.DMA((slots, 3)),
            pltpu.SemaphoreType.DMA((slots, 3)),
        ],
        compiler_params=pltpu.CompilerParams(vmem_limit_bytes=FINISH_BYTES),
        cost_estimate=cost,
        name="finish_own",
    )(*operands)
    prefix_out = (own_grads + sum(part.astype(F32) for part in last)).astype(BF16)
    return (q_out, self_out, prefix_out)


def far_kernel(z, *refs):
    (resp_prompt, resp_len, rewards, q_hbm, og_hbm, kv_hbm, prompts, q_out, self_out, prefix_outs,
     totals, lens, factors, q, og, kv, prefix, out, own, grads, sem_in, sem_prefix, sem_out) = refs
    me = lax.axis_index("dp")

    for p in range(z.n_dp):
        totals[p] = 0.0

    def copies_in(slot):
        rows = token_rows(z, slot)
        prompt = resp_prompt[me * z.count + slot]
        return (
            *row_copies((q_hbm, og_hbm, kv_hbm), (q, og, kv), rows, rows, sem_in.at[slot]),
            pltpu.make_async_copy(prompts.at[prompt], prefix.at[slot], sem_prefix.at[slot]),
        )

    def copies_out(slot):
        rows = token_rows(z, slot)
        return (
            *result_copies(out, own, q_out, self_out, slot, rows, sem_out),
            pltpu.make_async_copy(grads.at[slot], prefix_outs.at[slot], sem_out.at[slot, 3]),
        )

    def start(slot, _):
        for copy in copies_in(slot):
            copy.start()
        return 0

    lax.fori_loop(0, z.count, start, 0)

    def add(i, _):
        prompt = resp_prompt[i]
        totals[prompt] = totals[prompt] + rewards[i]
        return 0

    lax.fori_loop(0, z.n_dp * z.count, add, 0)

    def find_factor(slot, _):
        place = me * z.count + slot
        lens[slot] = resp_len[slot]
        factors[slot] = reward_factor(z, rewards[place], totals[resp_prompt[place]], resp_len[slot])
        return 0

    lax.fori_loop(0, z.count, find_factor, 0)

    def unit(slot, _):
        for copy in copies_in(slot):
            copy.wait()

        def sink(_, cols, key_grad, value_grad):
            grads[slot, 0, :, cols] = key_grad.astype(BF16)
            grads[slot, 1, :, cols] = value_grad.astype(BF16)

        units = [
            Unit([token_rows(z, slot)], [slot], k, [lens[slot]], [factors[slot]]) for k in range(z.kv_heads)
        ]
        attend(z, units, q, og, kv, prefix.at[slot], out, own, sink, True)
        for copy in copies_out(slot):
            copy.start()
        return 0

    lax.fori_loop(0, z.count, unit, 0)

    def end(slot, _):
        for copy in copies_out(slot):
            copy.wait()
        return 0

    lax.fori_loop(0, z.count, end, 0)


def far_shards(z, prompt_kv, resp_q, resp_kv, out_grad, rewards, resp_prompt, resp_len):
    assert z.slots == 1
    count, n_dp = z.count, z.n_dp
    one = (2, z.prefix_len, z.width)
    smem = pl.BlockSpec(memory_space=pltpu.SMEM)
    q_out, self_out, per_resp = pl.pallas_call(
        functools.partial(far_kernel, z),
        out_shape=[
            jax.ShapeDtypeStruct(resp_q.shape, BF16),
            jax.ShapeDtypeStruct(resp_kv.shape, BF16),
            jax.ShapeDtypeStruct((count,) + one, BF16),
        ],
        in_specs=[smem] * 3 + [ANYWHERE] * 4,
        out_specs=[ANYWHERE] * 3,
        scratch_shapes=[
            pltpu.SMEM((n_dp,), F32),
            pltpu.SMEM((count,), jnp.int32),
            pltpu.SMEM((count,), F32),
            pltpu.VMEM(resp_q.shape, BF16),
            pltpu.VMEM(resp_q.shape, BF16),
            pltpu.VMEM(resp_kv.shape, BF16),
            pltpu.VMEM((count,) + one, BF16),
            pltpu.VMEM((count, z.tokens, z.lanes), BF16),
            pltpu.VMEM((count, 2, z.tokens, z.width), BF16),
            pltpu.VMEM((count,) + one, BF16),
            pltpu.SemaphoreType.DMA((count, 4)),
            pltpu.SemaphoreType.DMA((count,)),
            pltpu.SemaphoreType.DMA((count, 4)),
        ],
        compiler_params=pltpu.CompilerParams(vmem_limit_bytes=VMEM_BYTES),
        name="far_grads",
    )(
        resp_prompt,
        resp_len,
        lax.all_gather(rewards, "dp", axis=0, tiled=True),
        resp_q,
        out_grad,
        resp_kv,
        lax.all_gather(prompt_kv, "dp", axis=0),
    )
    my_prompts = lax.dynamic_slice_in_dim(resp_prompt, lax.axis_index("dp") * count, count)
    route = (jnp.arange(n_dp, dtype=jnp.int32)[:, None] == my_prompts[None, :]).astype(BF16)
    outgoing = jnp.dot(route, per_resp.reshape(count, -1), preferred_element_type=F32).astype(BF16)
    outgoing = outgoing.reshape((n_dp,) + one)
    incoming = lax.all_to_all(outgoing, "dp", split_axis=0, concat_axis=0, tiled=True)
    prefix_out = jnp.sum(incoming, axis=0, dtype=F32).astype(BF16)
    return (q_out, self_out, prefix_out)


def shards(prompt_kv, resp_q, resp_kv, out_grad, rewards, resp_prompt, resp_len):
    n_dp = lax.axis_size("dp")
    count = rewards.shape[0]
    prefix_len, width = prompt_kv.shape[1:]
    slots = (count + n_dp - 1) // n_dp
    z = Sizes(
        n_dp, count, slots, width // HD, resp_q.shape[1] // width, resp_q.shape[0] // count, prefix_len
    )
    part = near_shards if count // slots == n_dp else far_shards
    return part(z, prompt_kv, resp_q, resp_kv, out_grad, rewards, resp_prompt, resp_len)


def solution(mesh):
    in_specs = (
        P(None, ("groups", "dp"), "tensor"),
        P(("groups", "dp"), "tensor"),
        P(None, ("groups", "dp"), "tensor"),
        P(("groups", "dp"), "tensor"),
        P(("groups", "dp")),
        P("groups"),
        P(("groups", "dp")),
    )
    out_specs = (
        P(("groups", "dp"), "tensor"),
        P(None, ("groups", "dp"), "tensor"),
        P(None, ("groups", "dp"), "tensor"),
    )
    return jax.shard_map(shards, mesh=mesh, in_specs=in_specs, out_specs=out_specs, check_vma=False)
```

```python
import functools
import math
from typing import NamedTuple

import jax
import jax.numpy as jnp
from jax import lax
from jax.experimental import pallas as pl
from jax.experimental.pallas import tpu as pltpu
from jax.sharding import PartitionSpec as P

HD = 128
NEG = -1e30
TAIL = 16
F32 = jnp.float32
BF16 = jnp.bfloat16
PAIR = 2
FAR = 3
VMEM_BYTES = 63 * 1024 * 1024
GROUP_BYTES = 53 * 1024 * 1024
FINISH_BYTES = 24 * 1024 * 1024
ANYWHERE = pl.BlockSpec(memory_space=pl.ANY)


class Sizes(NamedTuple):
    n_dp: int
    count: int
    slots: int
    kv_heads: int
    group_size: int
    tokens: int
    prefix_len: int

    @property
    def width(self):
        return self.kv_heads * HD

    @property
    def lanes(self):
        return self.kv_heads * self.group_size * HD


def dot(a, b, dims):
    return lax.dot_general(a, b, (dims, ((), ())), preferred_element_type=F32)


NN = ((1,), (0,))
NT = ((1,), (1,))


class Bag:
    pass


class Unit(NamedTuple):
    at: list
    places: list
    k: object
    lens: list
    factors: list


def attend(z, units, q, og, kv, prefix, out, own_out, sink, apart, by_product=False):
    tokens, prefix_len, group_size = z.tokens, z.prefix_len, z.group_size
    scale = 1.0 / math.sqrt(HD)
    log_scale = scale * math.log2(math.e)
    whole = group_size - group_size % 2
    most = max(whole, 2) * tokens
    assert tokens & (tokens - 1) == 0
    token = lax.broadcasted_iota(jnp.int32, (1, most), 1) & (tokens - 1)
    key = lax.broadcasted_iota(jnp.int32, (tokens, most), 0)
    causal = key <= (lax.broadcasted_iota(jnp.int32, (tokens, most), 1) & (tokens - 1))
    left = lax.broadcasted_iota(jnp.int32, (1, 2 * tokens), 1) < tokens

    identity = (
        lax.broadcasted_iota(jnp.int32, (most, most), 0) == lax.broadcasted_iota(jnp.int32, (most, most), 1)
    ).astype(F32).astype(BF16)

    def columns(index):
        if isinstance(index, int):
            return slice(index * HD, (index + 1) * HD)
        return pl.ds(pl.multiple_of(index * HD, HD), HD)

    def head(k, h):
        return columns(k * group_size + h)

    def rows(ref, c):
        return jnp.concatenate([ref[c.t.at[n], head(c.t.k, h)] for n, h in c.blocks], axis=0)

    def halves(part):
        none = jnp.zeros_like(part)
        return [jnp.where(left, part, none), jnp.where(left, none, part)]

    def over_keys(combine, *parts):
        reduce = jnp.max if combine is jnp.maximum else jnp.sum
        eights = [reduce(part.reshape(-1, 8, part.shape[1]), axis=0) for part in parts]
        return reduce(functools.reduce(combine, eights), axis=0, keepdims=True)

    def own_half(both):
        return jnp.where(left, both[:tokens], both[tokens:])

    def rounded(*parts):
        return jnp.concatenate([part.astype(BF16) for part in parts], axis=0)

    chunks = []
    for unit in units:
        t = Bag()
        t.at, t.places, t.k, t.lens, t.factors = unit
        t.single = len(t.at) == 1
        t.members = range(len(t.at))
        sides = (0, 0) if t.single else (0, 1)
        t.cols = columns(t.k)
        t.key_p, t.value_p = prefix[0, :, t.cols], prefix[1, :, t.cols]
        t.keys = [kv[0, t.at[n], t.cols] for n in sides]
        t.values = [kv[1, t.at[n], t.cols] for n in sides]
        t.key_pair = jnp.concatenate(t.keys, axis=0)
        t.value_pair = jnp.concatenate(t.values, axis=0)
        t.key_t = jnp.concatenate([t.key_p.T, t.key_pair.T], axis=1)
        t.prefix_sums = {n: [] for n in t.members}
        t.self_sums = {n: [] for n in t.members}
        mine = []
        for n in t.members:
            c = Bag()
            c.t, c.side, c.blocks = t, n, [(n, h) for h in range(whole)]
            mine.append(c)
        if group_size % 2:
            c = Bag()
            c.t, c.side, c.blocks = t, None, [(n, group_size - 1) for n in sides]
            mine.append(c)
        t.left_over = len(mine)
        chunks += mine

    def products(c):
        t = c.t
        c.q_rows, c.g_rows = rows(q, c), rows(og, c)
        if c.side is None:
            key_s, value_s = t.key_pair, t.value_pair
        else:
            key_s, value_s = t.keys[c.side], t.values[c.side]
        c.scores = dot(jnp.concatenate([t.key_p, key_s], axis=0), c.q_rows, NT)
        c.gw = dot(jnp.concatenate([t.value_p, value_s], axis=0), c.g_rows, NT)

    def weigh(c):
        scores_p, scores_s = c.scores[:prefix_len], c.scores[prefix_len:]
        c.gw_p, c.gw_s = c.gw[:prefix_len], c.gw[prefix_len:]
        if c.side is None:
            scores_s, c.gw_s = own_half(scores_s), own_half(c.gw_s)
        scores_s = jnp.where(causal[:, : scores_s.shape[1]], scores_s, NEG)
        top = over_keys(jnp.maximum, scores_p, scores_s)
        c.e_p = jnp.exp2((scores_p - top) * log_scale)
        c.e_s = jnp.exp2((scores_s - top) * log_scale)
        total = over_keys(jnp.add, c.e_p, c.e_s)
        weighted = over_keys(jnp.add, c.e_p * c.gw_p, c.e_s * c.gw_s)
        if c.side is None:
            length = jnp.where(left, c.t.lens[0], 0 if c.t.single else c.t.lens[1])
            gain = jnp.where(left, c.t.factors[0], c.t.factors[-1])
        else:
            length, gain = c.t.lens[c.side], c.t.factors[c.side]
        inverse = 1.0 / total
        c.delta = weighted * inverse
        c.gain = inverse * jnp.where(token[:, : total.shape[1]] < length, gain, 0.0)

    def gradients(c):
        w_p, w_s = c.e_p * c.gain, c.e_s * c.gain
        d_p, d_s = w_p * (c.gw_p - c.delta), w_s * (c.gw_s - c.delta)
        if c.side is None:
            d_s, w_s = halves(d_s), halves(w_s)
            c.d_wide = rounded(d_p, *d_s)
            c.d_all = rounded(*halves(d_p), *d_s) if apart else c.d_wide
            c.w_all = rounded(*(halves(w_p) if apart else [w_p]), *w_s)
        else:
            empty = jnp.zeros_like(d_s)
            c.d_wide = rounded(*([d_p, empty, d_s] if c.side else [d_p, d_s, empty]))
            c.d_all = rounded(d_p, d_s)
            c.w_all = rounded(w_p, w_s)

    def outgoing(c):
        t = c.t
        q_grad = (dot(t.key_t, c.d_wide, NN) * scale).astype(BF16)
        if by_product:
            lanes = q_grad.shape[1]
            q_grad = dot(identity[:lanes, :lanes], q_grad, NT).astype(BF16)
        else:
            q_grad = q_grad.T
        kg = dot(c.d_all, c.q_rows, NN)
        vg = dot(c.w_all, c.g_rows, NN)
        targets = t.members if c.side is None else [c.side]
        for place, (n, h) in enumerate(c.blocks):
            if c.side is not None or place < len(targets):
                out[t.places[n], :, head(t.k, h)] = q_grad[place * tokens : (place + 1) * tokens]
        many = 2 if c.side is None and apart else 1
        for place, n in enumerate(targets):
            if place < many:
                rows_p = slice(place * prefix_len, (place + 1) * prefix_len)
                t.prefix_sums[n if apart else 0].append((kg[rows_p], vg[rows_p]))
            start = many * prefix_len + place * tokens
            rows_s = slice(start, start + tokens)
            t.self_sums[n].append((kg[rows_s], vg[rows_s]))
        t.left_over -= 1
        if t.left_over == 0:
            for n in t.members:
                keys, values = zip(*t.self_sums[n])
                own_out[t.places[n], 0, :, t.cols] = (sum(keys) * scale).astype(BF16)
                own_out[t.places[n], 1, :, t.cols] = sum(values).astype(BF16)
                if apart or n == 0:
                    keys, values = zip(*t.prefix_sums[n])
                    sink(t.places[n], t.cols, sum(keys) * scale, sum(values))

    stages = (products, weigh, gradients, outgoing)
    for step in range(len(chunks) + len(stages) - 1):
        for late, stage in enumerate(stages):
            if 0 <= step - late < len(chunks):
                stage(chunks[step - late])


def token_rows(z, i):
    return pl.ds(pl.multiple_of(i * z.tokens, z.tokens), z.tokens)


def find_responses(z, me, turns, resp_prompt, order):
    for t, turn in enumerate(turns):
        prompt = me ^ turn
        found = t * z.slots
        for i in range(z.count):
            order[found] = i
            found = found + (resp_prompt[me * z.count + i] == prompt).astype(jnp.int32)


def prompt_total(z, me, prompt, resp_prompt, tails, far_rewards):
    sums = jnp.zeros((1, z.width), F32)
    for s in range(tails.shape[0]):
        tail = tails[s].astype(F32)
        sums += tail[0:1] + tail[1:2] + tail[2:3]
    lane = lax.broadcasted_iota(jnp.int32, sums.shape, 1)
    total = jnp.sum(jnp.where(lane == prompt, sums, 0.0))
    for i in range(z.count):
        total += jnp.where(resp_prompt[(me ^ FAR) * z.count + i] == prompt, far_rewards[i], 0.0)
    return total


def reward_factor(z, reward, total, length):
    return (reward - total / z.count) * (z.tokens / length.astype(F32))


def pack_kernel(z, prompt_hbm, rewards_hbm, resp_prompt_hbm, payload, rewards, resp_prompt, staged, sems):
    me = lax.axis_index("dp")
    small = [
        pltpu.make_async_copy(rewards_hbm, rewards, sems.at[0]),
        pltpu.make_async_copy(resp_prompt_hbm, resp_prompt, sems.at[1]),
    ]
    large = [
        pltpu.make_async_copy(
            prompt_hbm.at[n], staged.at[pl.ds(n * z.prefix_len, z.prefix_len)], sems.at[2 + n]
        )
        for n in range(2)
    ]
    for copy in small + large:
        copy.start()
    for copy in small:
        copy.wait()
    lane = lax.broadcasted_iota(jnp.int32, (1, z.width), 1)
    sums = jnp.zeros((1, z.width), F32)
    for i in range(z.count):
        sums += jnp.where(lane == resp_prompt[me * z.count + i], rewards[i], 0.0)
    high = sums.astype(BF16).astype(F32)
    middle = (sums - high).astype(BF16).astype(F32)
    low = sums - high - middle
    row = lax.broadcasted_iota(jnp.int32, (TAIL, z.width), 0)
    pieces = jnp.where(row == 0, high, jnp.where(row == 1, middle, jnp.where(row == 2, low, 0.0)))
    staged[2 * z.prefix_len :, :] = pieces.astype(BF16)
    for copy in large:
        copy.wait()
    last = pltpu.make_async_copy(staged, payload, sems.at[0])
    last.start()
    last.wait()


def tail_copies(z, payloads, tails, sems):
    return [
        pltpu.make_async_copy(payload.at[pl.ds(2 * z.prefix_len, TAIL)], tails.at[n], sems.at[n])
        for n, payload in enumerate(payloads)
    ]


def row_copies(here, there, at_here, at_there, sems):
    (q0, og0, kv0), (q1, og1, kv1) = here, there
    return (
        pltpu.make_async_copy(q0.at[at_here], q1.at[at_there], sems.at[0]),
        pltpu.make_async_copy(og0.at[at_here], og1.at[at_there], sems.at[1]),
        pltpu.make_async_copy(kv0.at[:, at_here], kv1.at[:, at_there], sems.at[2]),
    )


def result_copies(out, own, q_out, self_out, place, at, sems, back=False):
    pairs = [
        (out.at[place], q_out.at[at]),
        (own.at[place], self_out.at[:, at]),
    ]
    return [
        pltpu.make_async_copy(*(reversed(pair) if back else pair), sems.at[place, n])
        for n, pair in enumerate(pairs)
    ]


def group_kernel(z, turns, raw, body, ahead, n_tails, aliased, *refs):
    small_hbm, given = refs[:4], refs[4:7]
    tail_hbm, prompts = refs[7 : 7 + n_tails], refs[7 + n_tails : 7 + n_tails + len(turns)]
    refs = refs[7 + n_tails + len(turns) :]
    if raw:
        (q_out, self_out), grads_out, in_order, refs = refs[:2], refs[2:3], refs[3:5], refs[5:]
    else:
        in_order, refs = refs[:2], refs[2 + aliased :]
        (q_out, self_out), grads_out, refs = refs[:2], refs[2 : 2 + len(turns)], refs[2 + len(turns) :]
    in_order = (in_order[0].at[0], in_order[0].at[1], in_order[1])
    (resp_prompt, resp_len, rewards, far_rewards, order, q, og, kv, prefix, tails, acc, out, own, grads,
     sem_small, sem_tails, sem_prefix, sem_in, sem_out, sem_grads, sem_order) = refs
    me = lax.axis_index("dp")
    n_slots = len(turns) * z.slots
    span = z.slots * z.tokens

    small = [
        pltpu.make_async_copy(src, dst, sem_small.at[n])
        for n, (src, dst) in enumerate(zip(small_hbm, (resp_prompt, resp_len, rewards, far_rewards)))
    ]
    prefix_copies = [
        pltpu.make_async_copy(
            prompts[t].at[pl.ds(n * z.prefix_len, z.prefix_len)], prefix.at[t, n], sem_prefix.at[t, n]
        )
        for t in range(len(turns))
        for n in range(2)
    ]
    late = tail_copies(z, tail_hbm, tails, sem_tails)
    first_rows = []
    if not raw:
        first_rows = row_copies(in_order, (q, og, kv), pl.ds(ahead * span, span), pl.ds(0, span), sem_order.at[0])
    for copy in [*small, *first_rows, *prefix_copies, *late]:
        copy.start()
    small[0].wait()
    ordered = [*turns, *ahead] if raw else turns
    find_responses(z, me, ordered, resp_prompt, order)

    def copies_in(slot):
        return row_copies(
            given, (q, og, kv), token_rows(z, order[slot]), token_rows(z, slot), sem_in.at[slot]
        )

    def copies_out(slot):
        return result_copies(out, own, q_out, self_out, slot, token_rows(z, order[slot]), sem_out)

    def copies_ordered(slot):
        rows = token_rows(z, slot - n_slots)
        return row_copies((q, og, kv), in_order, token_rows(z, slot), rows, sem_order.at[slot - n_slots])

    for slot in range(0 if raw else z.slots, len(ordered) * z.slots):
        for copy in copies_in(slot):
            copy.start()
    for copy in small[1:] + late:
        copy.wait()
    if not raw:
        acc[...] = jnp.zeros(acc.shape, F32)
    for copy in prefix_copies:
        copy.wait()

    pairs_in_body = body
    steps_per_turn = z.slots // PAIR // pairs_in_body

    def step(u, _):
        t = u // steps_per_turn
        first = u * pairs_in_body * PAIR
        mine = range(pairs_in_body * PAIR)

        def wait_for_slots():
            for n in mine:
                for copy in copies_in(first + n):
                    copy.wait()

        if raw:
            wait_for_slots()
        else:

            @pl.when(u == 0)
            def _():
                for copy in first_rows:
                    copy.wait()

            if len(turns) > 1:
                pl.when(u >= steps_per_turn)(wait_for_slots)

        def sink(place, cols, key_grad, value_grad):
            if raw:
                grads[place, 0, :, cols] = key_grad.astype(BF16)
                grads[place, 1, :, cols] = value_grad.astype(BF16)
            else:
                acc[t, 0, :, cols] += key_grad
                acc[t, 1, :, cols] += value_grad

        turn = turns[0]
        for n, other in enumerate(turns[1:], 1):
            turn = jnp.where(t == n, other, turn)
        total = None if raw else prompt_total(z, me, me ^ turn, resp_prompt, tails, far_rewards)
        lens, factors = {}, {}
        for n in mine:
            i = order[first + n]
            lens[n] = resp_len[i]
            factors[n] = 1.0 if raw else reward_factor(z, rewards[i], total, resp_len[i])
        units = []
        for pair in range(pairs_in_body):
            places = [first + pair * PAIR + n for n in range(PAIR)]
            own_places = range(pair * PAIR, (pair + 1) * PAIR)
            at = [token_rows(z, n) for n in places]
            for k in range(z.kv_heads):
                units.append(Unit(at, places, k, [lens[n] for n in own_places], [factors[n] for n in own_places]))
        attend(z, units, q, og, kv, prefix.at[t], out, own, sink, raw, turns == (2,))
        for n in mine:
            for copy in copies_out(first + n):
                copy.start()
        if raw:

            @pl.when(u == 0)
            def _():
                def pass_on(slot, _):
                    for copy in copies_in(slot):
                        copy.wait()
                    for copy in copies_ordered(slot):
                        copy.start()
                    return 0

                lax.fori_loop(n_slots, len(ordered) * z.slots, pass_on, 0)

        return 0

    lax.fori_loop(0, len(turns) * steps_per_turn, step, 0)
    if raw:
        last = [pltpu.make_async_copy(grads, grads_out[0], sem_grads.at[0])]
    else:
        grads[...] = acc[...].astype(BF16)
        last = [
            pltpu.make_async_copy(grads.at[t], grads_out[t], sem_grads.at[t]) for t in range(len(turns))
        ]
    for copy in last:
        copy.start()
    for slot in range(n_slots):
        for copy in copies_out(slot):
            copy.wait()
    if raw:
        for slot in range(n_slots, len(ordered) * z.slots):
            for copy in copies_ordered(slot):
                copy.wait()
    for copy in last:
        copy.wait()


def finish_kernel(z, n_tails, n_come, *refs):
    small_hbm, tail_hbm = refs[:4], refs[4 : 4 + n_tails]
    per_resp_hbm, come_hbm = refs[4 + n_tails], refs[5 + n_tails : 5 + n_tails + n_come]
    q_out, self_out, grads_out = refs[7 + n_tails + n_come : 10 + n_tails + n_come]
    (resp_prompt, resp_len, rewards, far_rewards, order, tails, out, own, per_resp, come, grads,
     sem_small, sem_tails, sem_come, sem_in, sem_out) = refs[10 + n_tails + n_come :]
    me = lax.axis_index("dp")
    small = [
        pltpu.make_async_copy(src, dst, sem_small.at[n])
        for n, (src, dst) in enumerate(zip(small_hbm, (resp_prompt, resp_len, rewards, far_rewards)))
    ]
    late = tail_copies(z, tail_hbm, tails, sem_tails)
    late += [pltpu.make_async_copy(src, come.at[n], sem_come.at[n]) for n, src in enumerate(come_hbm)]
    late += [pltpu.make_async_copy(per_resp_hbm, per_resp, sem_come.at[n_come])]
    for copy in small + late:
        copy.start()
    small[0].wait()
    find_responses(z, me, (0,), resp_prompt, order)

    def moves(slot, back):
        sems = sem_in if back else sem_out
        return result_copies(out, own, q_out, self_out, slot, token_rows(z, order[slot]), sems, back)

    for slot in range(z.slots):
        for copy in moves(slot, True):
            copy.start()
    for copy in small[1:] + late:
        copy.wait()
    total = prompt_total(z, me, me, resp_prompt, tails, far_rewards)
    summed = come[0].astype(F32)
    for n in range(1, n_come):
        summed += come[n].astype(F32)
    factors = [reward_factor(z, rewards[order[n]], total, resp_len[order[n]]) for n in range(z.slots)]
    for slot in range(z.slots):
        summed += per_resp[slot].astype(F32) * factors[slot]
    grads[...] = summed
    last = pltpu.make_async_copy(grads, grads_out, sem_small.at[0])
    last.start()
    for slot in range(z.slots):
        for copy in moves(slot, True):
            copy.wait()
        out[slot] = (out[slot].astype(F32) * factors[slot]).astype(BF16)
        own[slot] = (own[slot].astype(F32) * factors[slot]).astype(BF16)
        for copy in moves(slot, False):
            copy.start()
    for slot in range(z.slots):
        for copy in moves(slot, False):
            copy.wait()
    last.wait()


def near_shards(z, prompt_kv, resp_q, resp_kv, out_grad, rewards, resp_prompt, resp_len):
    n_dp = z.n_dp
    assert z.slots % PAIR == 0
    shape = jax.ShapeDtypeStruct
    one = (2, z.prefix_len, z.width)
    params = pltpu.CompilerParams(vmem_limit_bytes=VMEM_BYTES)
    cost = pl.CostEstimate(flops=0, bytes_accessed=0, transcendentals=0)
    payload = pl.pallas_call(
        functools.partial(pack_kernel, z),
        out_shape=jax.ShapeDtypeStruct((2 * z.prefix_len + TAIL, z.width), BF16),
        in_specs=[ANYWHERE] * 3,
        out_specs=ANYWHERE,
        scratch_shapes=[
            pltpu.SMEM(rewards.shape, F32),
            pltpu.SMEM(resp_prompt.shape, jnp.int32),
            pltpu.VMEM((2 * z.prefix_len + TAIL, z.width), BF16),
            pltpu.SemaphoreType.DMA((4,)),
        ],
        compiler_params=pltpu.CompilerParams(vmem_limit_bytes=VMEM_BYTES),
        name="pack",
    )(prompt_kv, rewards, resp_prompt)

    assert n_dp == FAR + 1

    def swap(x, s):
        return lax.ppermute(x, "dp", [(i, i ^ s) for i in range(n_dp)])

    payloads = {0: payload, 2: swap(payload, 2), 1: swap(payload, 1)}
    tails = [payloads[s] for s in range(FAR)]
    small = (resp_prompt, resp_len, rewards)
    far_rewards = swap(rewards, FAR)
    smem = [pltpu.SMEM(x.shape, x.dtype) for x in (*small, rewards)]
    slots = z.slots

    def grads_of(turns, raw, body, ahead, in_order=(), written=()):
        n_slots, n_turns = len(turns) * slots, len(turns)
        n_ahead = len(ahead) * slots if raw else 0
        n_held = n_slots + n_ahead
        used_tails = [] if raw else tails
        used_small = (*small, rewards if raw else far_rewards)
        prompts = [payloads[turn] for turn in turns]
        operands = [*used_small, resp_q, out_grad, resp_kv, *used_tails, *prompts, *in_order, *written]
        grads_shapes = [(slots,) + one] if raw else [one] * n_turns
        ordered_shapes = [(2, n_ahead * z.tokens, z.lanes), (2, n_ahead * z.tokens, z.width)] if raw else []
        return pl.pallas_call(
            functools.partial(group_kernel, z, turns, raw, body, ahead, len(used_tails), len(written)),
            out_shape=[shape(resp_q.shape, BF16), shape(resp_kv.shape, BF16)]
            + [shape(x, BF16) for x in grads_shapes + ordered_shapes],
            in_specs=[ANYWHERE] * len(operands),
            out_specs=[ANYWHERE] * (2 + len(grads_shapes) + len(ordered_shapes)),
            input_output_aliases={len(operands) - 2: 0, len(operands) - 1: 1} if written else {},
            scratch_shapes=[
                *smem,
                pltpu.SMEM((n_held + 1,), jnp.int32),
                pltpu.VMEM((n_held * z.tokens, z.lanes), BF16),
                pltpu.VMEM((n_held * z.tokens, z.lanes), BF16),
                pltpu.VMEM((2, n_held * z.tokens, z.width), BF16),
                pltpu.VMEM((n_turns,) + one, BF16),
                pltpu.VMEM((FAR, TAIL, z.width), BF16),
                pltpu.VMEM((n_turns,) + one, F32),
                pltpu.VMEM((n_slots, z.tokens, z.lanes), BF16),
                pltpu.VMEM((n_slots, 2, z.tokens, z.width), BF16),
                pltpu.VMEM(grads_shapes[0] if raw else (n_turns,) + one, BF16),
                pltpu.SemaphoreType.DMA((len(smem),)),
                pltpu.SemaphoreType.DMA((FAR,)),
                pltpu.SemaphoreType.DMA((n_turns, 2)),
                pltpu.SemaphoreType.DMA((n_held, 3)),
                pltpu.SemaphoreType.DMA((n_slots, 2)),
                pltpu.SemaphoreType.DMA((n_turns,)),
                pltpu.SemaphoreType.DMA((max(n_ahead, 1), 3)),
            ],
            compiler_params=params if raw else pltpu.CompilerParams(vmem_limit_bytes=GROUP_BYTES),
            cost_estimate=cost,
            name="raw_grads" if raw else "group_grads",
        )(*operands)

    *written, per_resp, rows_ahead, kv_ahead = grads_of((0,), True, 1, (2, FAR))
    in_order = (rows_ahead, kv_ahead)
    onward, per_resp, far_rewards = lax.optimization_barrier((payloads[2], per_resp, far_rewards))
    payloads[FAR] = swap(onward, 1)
    *written, for_2 = grads_of((2,), False, slots // PAIR, 0, in_order, written)
    come = [swap(for_2, 2)]
    *written, for_far, for_1 = grads_of((FAR, 1), False, slots // PAIR, 1, in_order, written)
    last = [swap(for_far, FAR), swap(for_1, 1)]
    operands = [*small, far_rewards, *tails, per_resp, *come, *written]
    q_out, self_out, own_grads = pl.pallas_call(
        functools.partial(finish_kernel, z, len(tails), len(come)),
        out_shape=[shape(resp_q.shape, BF16), shape(resp_kv.shape, BF16), shape(one, F32)],
        in_specs=[ANYWHERE] * len(operands),
        out_specs=[ANYWHERE] * 3,
        input_output_aliases={len(operands) - 2: 0, len(operands) - 1: 1},
        scratch_shapes=[
            *smem,
            pltpu.SMEM((slots + 1,), jnp.int32),
            pltpu.VMEM((FAR, TAIL, z.width), BF16),
            pltpu.VMEM((slots, z.tokens, z.lanes), BF16),
            pltpu.VMEM((slots, 2, z.tokens, z.width), BF16),
            pltpu.VMEM((slots,) + one, BF16),
            pltpu.VMEM((len(come),) + one, BF16),
            pltpu.VMEM(one, F32),
            pltpu.SemaphoreType.DMA((len(smem),)),
            pltpu.SemaphoreType.DMA((FAR,)),
            pltpu.SemaphoreType.DMA((len(come) + 1,)),
            pltpu.SemaphoreType.DMA((slots, 3)),
            pltpu.SemaphoreType.DMA((slots, 3)),
        ],
        compiler_params=pltpu.CompilerParams(vmem_limit_bytes=FINISH_BYTES),
        cost_estimate=cost,
        name="finish_own",
    )(*operands)
    prefix_out = (own_grads + sum(part.astype(F32) for part in last)).astype(BF16)
    return (q_out, self_out, prefix_out)


def far_kernel(z, *refs):
    (resp_prompt, resp_len, rewards, q_hbm, og_hbm, kv_hbm, prompts, q_out, self_out, prefix_outs,
     totals, lens, factors, q, og, kv, prefix, out, own, grads, sem_in, sem_prefix, sem_out) = refs
    me = lax.axis_index("dp")

    for p in range(z.n_dp):
        totals[p] = 0.0

    def copies_in(slot):
        rows = token_rows(z, slot)
        prompt = resp_prompt[me * z.count + slot]
        return (
            *row_copies((q_hbm, og_hbm, kv_hbm), (q, og, kv), rows, rows, sem_in.at[slot]),
            pltpu.make_async_copy(prompts.at[prompt], prefix.at[slot], sem_prefix.at[slot]),
        )

    def copies_out(slot):
        rows = token_rows(z, slot)
        return (
            *result_copies(out, own, q_out, self_out, slot, rows, sem_out),
            pltpu.make_async_copy(grads.at[slot], prefix_outs.at[slot], sem_out.at[slot, 3]),
        )

    def start(slot, _):
        for copy in copies_in(slot):
            copy.start()
        return 0

    lax.fori_loop(0, z.count, start, 0)

    def add(i, _):
        prompt = resp_prompt[i]
        totals[prompt] = totals[prompt] + rewards[i]
        return 0

    lax.fori_loop(0, z.n_dp * z.count, add, 0)

    def find_factor(slot, _):
        place = me * z.count + slot
        lens[slot] = resp_len[slot]
        factors[slot] = reward_factor(z, rewards[place], totals[resp_prompt[place]], resp_len[slot])
        return 0

    lax.fori_loop(0, z.count, find_factor, 0)

    def unit(slot, _):
        for copy in copies_in(slot):
            copy.wait()

        def sink(_, cols, key_grad, value_grad):
            grads[slot, 0, :, cols] = key_grad.astype(BF16)
            grads[slot, 1, :, cols] = value_grad.astype(BF16)

        units = [
            Unit([token_rows(z, slot)], [slot], k, [lens[slot]], [factors[slot]]) for k in range(z.kv_heads)
        ]
        attend(z, units, q, og, kv, prefix.at[slot], out, own, sink, True)
        for copy in copies_out(slot):
            copy.start()
        return 0

    lax.fori_loop(0, z.count, unit, 0)

    def end(slot, _):
        for copy in copies_out(slot):
            copy.wait()
        return 0

    lax.fori_loop(0, z.count, end, 0)


def far_shards(z, prompt_kv, resp_q, resp_kv, out_grad, rewards, resp_prompt, resp_len):
    assert z.slots == 1
    count, n_dp = z.count, z.n_dp
    one = (2, z.prefix_len, z.width)
    smem = pl.BlockSpec(memory_space=pltpu.SMEM)
    q_out, self_out, per_resp = pl.pallas_call(
        functools.partial(far_kernel, z),
        out_shape=[
            jax.ShapeDtypeStruct(resp_q.shape, BF16),
            jax.ShapeDtypeStruct(resp_kv.shape, BF16),
            jax.ShapeDtypeStruct((count,) + one, BF16),
        ],
        in_specs=[smem] * 3 + [ANYWHERE] * 4,
        out_specs=[ANYWHERE] * 3,
        scratch_shapes=[
            pltpu.SMEM((n_dp,), F32),
            pltpu.SMEM((count,), jnp.int32),
            pltpu.SMEM((count,), F32),
            pltpu.VMEM(resp_q.shape, BF16),
            pltpu.VMEM(resp_q.shape, BF16),
            pltpu.VMEM(resp_kv.shape, BF16),
            pltpu.VMEM((count,) + one, BF16),
            pltpu.VMEM((count, z.tokens, z.lanes), BF16),
            pltpu.VMEM((count, 2, z.tokens, z.width), BF16),
            pltpu.VMEM((count,) + one, BF16),
            pltpu.SemaphoreType.DMA((count, 4)),
            pltpu.SemaphoreType.DMA((count,)),
            pltpu.SemaphoreType.DMA((count, 4)),
        ],
        compiler_params=pltpu.CompilerParams(vmem_limit_bytes=VMEM_BYTES),
        name="far_grads",
    )(
        resp_prompt,
        resp_len,
        lax.all_gather(rewards, "dp", axis=0, tiled=True),
        resp_q,
        out_grad,
        resp_kv,
        lax.all_gather(prompt_kv, "dp", axis=0),
    )
    my_prompts = lax.dynamic_slice_in_dim(resp_prompt, lax.axis_index("dp") * count, count)
    route = (jnp.arange(n_dp, dtype=jnp.int32)[:, None] == my_prompts[None, :]).astype(BF16)
    outgoing = jnp.dot(route, per_resp.reshape(count, -1), preferred_element_type=F32).astype(BF16)
    outgoing = outgoing.reshape((n_dp,) + one)
    incoming = lax.all_to_all(outgoing, "dp", split_axis=0, concat_axis=0, tiled=True)
    prefix_out = jnp.sum(incoming, axis=0, dtype=F32).astype(BF16)
    return (q_out, self_out, prefix_out)


def shards(prompt_kv, resp_q, resp_kv, out_grad, rewards, resp_prompt, resp_len):
    n_dp = lax.axis_size("dp")
    count = rewards.shape[0]
    prefix_len, width = prompt_kv.shape[1:]
    slots = (count + n_dp - 1) // n_dp
    z = Sizes(
        n_dp, count, slots, width // HD, resp_q.shape[1] // width, resp_q.shape[0] // count, prefix_len
    )
    part = near_shards if count // slots == n_dp else far_shards
    return part(z, prompt_kv, resp_q, resp_kv, out_grad, rewards, resp_prompt, resp_len)


def solution(mesh):
    in_specs = (
        P(None, ("groups", "dp"), "tensor"),
        P(("groups", "dp"), "tensor"),
        P(None, ("groups", "dp"), "tensor"),
        P(("groups", "dp"), "tensor"),
        P(("groups", "dp")),
        P("groups"),
        P(("groups", "dp")),
    )
    out_specs = (
        P(("groups", "dp"), "tensor"),
        P(None, ("groups", "dp"), "tensor"),
        P(None, ("groups", "dp"), "tensor"),
    )
    return jax.shard_map(shards, mesh=mesh, in_specs=in_specs, out_specs=out_specs, check_vma=False)
```

```python
import functools
import math
from typing import NamedTuple

import jax
import jax.numpy as jnp
from jax import lax
from jax.experimental import pallas as pl
from jax.experimental.pallas import tpu as pltpu
from jax.sharding import PartitionSpec as P

HD = 128
NEG = -1e30
F32 = jnp.float32
BF16 = jnp.bfloat16
PAIR = 2
FAR = 3
VMEM_BYTES = 63 * 1024 * 1024
GROUP_BYTES = 54528 * 1024
ANYWHERE = pl.BlockSpec(memory_space=pl.ANY)


class Sizes(NamedTuple):
    n_dp: int
    count: int
    slots: int
    kv_heads: int
    group_size: int
    tokens: int
    prefix_len: int

    @property
    def width(self):
        return self.kv_heads * HD

    @property
    def lanes(self):
        return self.kv_heads * self.group_size * HD


def dot(a, b, dims):
    return lax.dot_general(a, b, (dims, ((), ())), preferred_element_type=F32)


NN = ((1,), (0,))
NT = ((1,), (1,))


class Bag:
    pass


class Unit(NamedTuple):
    at: list
    places: list
    k: object
    lens: list
    factors: list


def attend(z, units, q, og, kv, prefix, out, own_out, sink, apart):
    tokens, prefix_len, group_size = z.tokens, z.prefix_len, z.group_size
    scale = 1.0 / math.sqrt(HD)
    log_scale = scale * math.log2(math.e)
    whole = group_size - group_size % 2
    most = max(whole, 2) * tokens
    assert tokens & (tokens - 1) == 0
    token = lax.broadcasted_iota(jnp.int32, (1, most), 1) & (tokens - 1)
    key = lax.broadcasted_iota(jnp.int32, (tokens, most), 0)
    causal = key <= (lax.broadcasted_iota(jnp.int32, (tokens, most), 1) & (tokens - 1))
    left = lax.broadcasted_iota(jnp.int32, (1, 2 * tokens), 1) < tokens

    def columns(index):
        if isinstance(index, int):
            return slice(index * HD, (index + 1) * HD)
        return pl.ds(pl.multiple_of(index * HD, HD), HD)

    def head(k, h):
        return columns(k * group_size + h)

    def rows(ref, c):
        return jnp.concatenate([ref[c.t.at[n], head(c.t.k, h)] for n, h in c.blocks], axis=0)

    def halves(part):
        none = jnp.zeros_like(part)
        return [jnp.where(left, part, none), jnp.where(left, none, part)]

    def over_keys(combine, *parts):
        reduce = jnp.max if combine is jnp.maximum else jnp.sum
        eights = [reduce(part.reshape(-1, 8, part.shape[1]), axis=0) for part in parts]
        return reduce(functools.reduce(combine, eights), axis=0, keepdims=True)

    def own_half(both):
        return jnp.where(left, both[:tokens], both[tokens:])

    def rounded(*parts):
        return jnp.concatenate([part.astype(BF16) for part in parts], axis=0)

    chunks = []
    for unit in units:
        t = Bag()
        t.at, t.places, t.k, t.lens, t.factors = unit
        t.single = len(t.at) == 1
        t.members = range(len(t.at))
        sides = (0, 0) if t.single else (0, 1)
        t.cols = columns(t.k)
        t.key_p, t.value_p = prefix[0, :, t.cols], prefix[1, :, t.cols]
        t.keys = [kv[0, t.at[n], t.cols] for n in sides]
        t.values = [kv[1, t.at[n], t.cols] for n in sides]
        t.key_pair = jnp.concatenate(t.keys, axis=0)
        t.value_pair = jnp.concatenate(t.values, axis=0)
        t.key_t = jnp.concatenate([t.key_p.T, t.key_pair.T], axis=1)
        t.prefix_sums = {n: [] for n in t.members}
        t.self_sums = {n: [] for n in t.members}
        mine = []
        for n in t.members:
            c = Bag()
            c.t, c.side, c.blocks = t, n, [(n, h) for h in range(whole)]
            mine.append(c)
        if group_size % 2:
            c = Bag()
            c.t, c.side, c.blocks = t, None, [(n, group_size - 1) for n in sides]
            mine.append(c)
        t.left_over = len(mine)
        chunks += mine

    def products(c):
        t = c.t
        c.q_rows, c.g_rows = rows(q, c), rows(og, c)
        if c.side is None:
            key_s, value_s = t.key_pair, t.value_pair
        else:
            key_s, value_s = t.keys[c.side], t.values[c.side]
        c.scores = dot(jnp.concatenate([t.key_p, key_s], axis=0), c.q_rows, NT)
        c.gw = dot(jnp.concatenate([t.value_p, value_s], axis=0), c.g_rows, NT)

    def weigh(c):
        scores_p, scores_s = c.scores[:prefix_len], c.scores[prefix_len:]
        c.gw_p, c.gw_s = c.gw[:prefix_len], c.gw[prefix_len:]
        if c.side is None:
            scores_s, c.gw_s = own_half(scores_s), own_half(c.gw_s)
        scores_s = jnp.where(causal[:, : scores_s.shape[1]], scores_s, NEG)
        top = over_keys(jnp.maximum, scores_p, scores_s)
        c.e_p = jnp.exp2((scores_p - top) * log_scale)
        c.e_s = jnp.exp2((scores_s - top) * log_scale)
        total = over_keys(jnp.add, c.e_p, c.e_s)
        weighted = over_keys(jnp.add, c.e_p * c.gw_p, c.e_s * c.gw_s)
        if c.side is None:
            length = jnp.where(left, c.t.lens[0], 0 if c.t.single else c.t.lens[1])
            gain = jnp.where(left, c.t.factors[0], c.t.factors[-1])
        else:
            length, gain = c.t.lens[c.side], c.t.factors[c.side]
        inverse = 1.0 / total
        c.delta = weighted * inverse
        c.gain = inverse * jnp.where(token[:, : total.shape[1]] < length, gain, 0.0)

    def gradients(c):
        w_p, w_s = c.e_p * c.gain, c.e_s * c.gain
        d_p, d_s = w_p * (c.gw_p - c.delta), w_s * (c.gw_s - c.delta)
        if c.side is None:
            d_s, w_s = halves(d_s), halves(w_s)
            c.d_wide = rounded(d_p, *d_s)
            c.d_all = rounded(*halves(d_p), *d_s) if apart else c.d_wide
            c.w_all = rounded(*(halves(w_p) if apart else [w_p]), *w_s)
        else:
            empty = jnp.zeros_like(d_s)
            c.d_wide = rounded(*([d_p, empty, d_s] if c.side else [d_p, d_s, empty]))
            c.d_all = rounded(d_p, d_s)
            c.w_all = rounded(w_p, w_s)

    def outgoing(c):
        t = c.t
        q_grad = (dot(t.key_t, c.d_wide, NN) * scale).astype(BF16).T
        kg = dot(c.d_all, c.q_rows, NN)
        vg = dot(c.w_all, c.g_rows, NN)
        targets = t.members if c.side is None else [c.side]
        for place, (n, h) in enumerate(c.blocks):
            if c.side is not None or place < len(targets):
                out[t.places[n], :, head(t.k, h)] = q_grad[place * tokens : (place + 1) * tokens]
        many = 2 if c.side is None and apart else 1
        for place, n in enumerate(targets):
            if place < many:
                rows_p = slice(place * prefix_len, (place + 1) * prefix_len)
                t.prefix_sums[n if apart else 0].append((kg[rows_p], vg[rows_p]))
            start = many * prefix_len + place * tokens
            rows_s = slice(start, start + tokens)
            t.self_sums[n].append((kg[rows_s], vg[rows_s]))
        t.left_over -= 1
        if t.left_over == 0:
            for n in t.members:
                keys, values = zip(*t.self_sums[n])
                own_out[t.places[n], 0, :, t.cols] = (sum(keys) * scale).astype(BF16)
                own_out[t.places[n], 1, :, t.cols] = sum(values).astype(BF16)
                if apart or n == 0:
                    keys, values = zip(*t.prefix_sums[n])
                    sink(t.places[n], t.cols, sum(keys) * scale, sum(values))

    stages = (products, weigh, gradients, outgoing)
    for step in range(len(chunks) + len(stages) - 1):
        for late, stage in enumerate(stages):
            if 0 <= step - late < len(chunks):
                stage(chunks[step - late])


def token_rows(z, i):
    return pl.ds(pl.multiple_of(i * z.tokens, z.tokens), z.tokens)


def find_responses(z, me, turns, resp_prompt, order):
    for t, turn in enumerate(turns):
        prompt = me ^ turn
        found = t * z.slots
        for i in range(z.count):
            order[found] = i
            found = found + (resp_prompt[me * z.count + i] == prompt).astype(jnp.int32)


def prompt_total(z, me, prompt, resp_prompt, rewards):
    total = jnp.float32(0.0)
    for s in range(z.n_dp):
        for i in range(z.count):
            total += jnp.where(resp_prompt[(me ^ s) * z.count + i] == prompt, rewards[s][i], 0.0)
    return total


def reward_factor(z, reward, total, length):
    return (reward - total / z.count) * (z.tokens / length.astype(F32))


def row_copies(here, there, at_here, at_there, sems):
    (q0, og0, kv0), (q1, og1, kv1) = here, there
    return (
        pltpu.make_async_copy(q0.at[at_here], q1.at[at_there], sems.at[0]),
        pltpu.make_async_copy(og0.at[at_here], og1.at[at_there], sems.at[1]),
        pltpu.make_async_copy(kv0.at[:, at_here], kv1.at[:, at_there], sems.at[2]),
    )


def result_copies(out, own, q_out, self_out, place, at, sems, back=False):
    pairs = [
        (out.at[place], q_out.at[at]),
        (own.at[place], self_out.at[:, at]),
    ]
    return [
        pltpu.make_async_copy(*(reversed(pair) if back else pair), sems.at[place, n])
        for n, pair in enumerate(pairs)
    ]


def sort_kernel(z, ahead, resp_prompt_hbm, q_hbm, og_hbm, kv_hbm, both_out, kv_out, *scratch):
    resp_prompt, order, q, og, kv, sem_small, sem_in, sem_out = scratch
    me = lax.axis_index("dp")
    small = pltpu.make_async_copy(resp_prompt_hbm, resp_prompt, sem_small)
    small.start()
    small.wait()
    find_responses(z, me, ahead, resp_prompt, order)
    held, in_order = (q, og, kv), (both_out.at[0], both_out.at[1], kv_out)
    slots = range(len(ahead) * z.slots)

    def copies_in(slot):
        return row_copies(
            (q_hbm, og_hbm, kv_hbm), held, token_rows(z, order[slot]), token_rows(z, slot), sem_in.at[slot]
        )

    def copies_out(slot):
        rows = token_rows(z, slot)
        return row_copies(held, in_order, rows, rows, sem_out.at[slot])

    for slot in slots:
        for copy in copies_in(slot):
            copy.start()
    for slot in slots:
        for copy in copies_in(slot):
            copy.wait()
        for copy in copies_out(slot):
            copy.start()
    for slot in slots:
        for copy in copies_out(slot):
            copy.wait()


def group_kernel(z, turns, ahead, n_come, aliased, *refs):
    n_small = 2 + z.n_dp
    small_hbm, given, refs = refs[:n_small], refs[n_small : n_small + 3], refs[n_small + 3 :]
    prompts, refs = refs[: len(turns)], refs[len(turns) :]
    come_hbm, refs = refs[:n_come], refs[n_come:]
    if ahead is not None:
        (both, kv_ordered), refs = refs[:2], refs[2:]
    (q_out, self_out), refs = refs[aliased : aliased + 2], refs[aliased + 2 :]
    grads_out, refs = refs[: len(turns)], refs[len(turns) :]
    resp_prompt, resp_len, *rewards = refs[:n_small]
    (order, lens, factors, q, og, kv, prefix, come, acc, out, own, grads,
     sem_small, sem_prefix, sem_come, sem_in, sem_out, sem_grads, sem_first) = refs[n_small:]
    me = lax.axis_index("dp")
    n_slots = len(turns) * z.slots
    span = z.slots * z.tokens

    small = [
        pltpu.make_async_copy(src, dst, sem_small.at[n])
        for n, (src, dst) in enumerate(zip(small_hbm, (resp_prompt, resp_len, *rewards)))
    ]
    first_rows = ()
    if ahead is not None:
        first_rows = row_copies(
            (both.at[0], both.at[1], kv_ordered), (q, og, kv), pl.ds(ahead * span, span), pl.ds(0, span), sem_first
        )
    prefix_copies = [
        pltpu.make_async_copy(prompts[t], prefix.at[t], sem_prefix.at[t]) for t in range(len(turns))
    ]
    late = [pltpu.make_async_copy(src, come, sem_come) for src in come_hbm]
    for copy in [*small, *first_rows, *prefix_copies, *late]:
        copy.start()
    small[0].wait()
    find_responses(z, me, turns, resp_prompt, order)

    def copies_in(slot):
        return row_copies(
            given, (q, og, kv), token_rows(z, order[slot]), token_rows(z, slot), sem_in.at[slot]
        )

    def copies_out(slot):
        return result_copies(out, own, q_out, self_out, slot, token_rows(z, order[slot]), sem_out)

    for slot in range(0 if ahead is None else z.slots, n_slots):
        for copy in copies_in(slot):
            copy.start()
    for copy in small[1:] + late:
        copy.wait()
    for t, turn in enumerate(turns):
        total = prompt_total(z, me, me ^ turn, resp_prompt, rewards)
        for slot in range(t * z.slots, (t + 1) * z.slots):
            i = order[slot]
            lens[slot] = resp_len[i]
            factors[slot] = reward_factor(z, rewards[0][i], total, resp_len[i])
    if n_come:
        acc[0] = come[...].astype(F32)
    else:
        acc[...] = jnp.zeros(acc.shape, F32)
    for copy in prefix_copies:
        copy.wait()

    def step(t, _):
        slots = [t * z.slots + n for n in range(z.slots)]

        def wait_for_slots():
            for slot in slots:
                for copy in copies_in(slot):
                    copy.wait()

        if ahead is None:
            wait_for_slots()
        else:

            @pl.when(t == 0)
            def _():
                for copy in first_rows:
                    copy.wait()

            if len(turns) > 1:
                pl.when(t > 0)(wait_for_slots)

        def sink(_, cols, key_grad, value_grad):
            acc[t, 0, :, cols] += key_grad
            acc[t, 1, :, cols] += value_grad

        units = []
        for pair in range(0, z.slots, PAIR):
            places = slots[pair : pair + PAIR]
            at = [token_rows(z, n) for n in places]
            for k in range(z.kv_heads):
                units.append(Unit(at, places, k, [lens[n] for n in places], [factors[n] for n in places]))
        attend(z, units, q, og, kv, prefix.at[t], out, own, sink, False)
        for slot in slots:
            for copy in copies_out(slot):
                copy.start()
        return 0

    lax.fori_loop(0, len(turns), step, 0)
    grads[...] = acc[...].astype(grads.dtype)
    last = [pltpu.make_async_copy(grads.at[t], grads_out[t], sem_grads.at[t]) for t in range(len(turns))]
    for copy in last:
        copy.start()
    for slot in range(n_slots):
        for copy in copies_out(slot):
            copy.wait()
    for copy in last:
        copy.wait()


def near_shards(z, prompt_kv, resp_q, resp_kv, out_grad, rewards, resp_prompt, resp_len):
    n_dp = z.n_dp
    assert z.slots % PAIR == 0
    shape = jax.ShapeDtypeStruct
    one = (2, z.prefix_len, z.width)
    params = pltpu.CompilerParams(vmem_limit_bytes=VMEM_BYTES)
    cost = pl.CostEstimate(flops=0, bytes_accessed=0, transcendentals=0)
    assert n_dp == FAR + 1

    def swap(x, s):
        return lax.ppermute(x, "dp", [(i, i ^ s) for i in range(n_dp)])

    prompts = {0: prompt_kv, 2: swap(prompt_kv, 2), 1: swap(prompt_kv, 1)}
    others = [swap(rewards, s) for s in range(1, n_dp)]
    small = (resp_prompt, resp_len)
    smem = [pltpu.SMEM(x.shape, x.dtype) for x in (*small, rewards, *others)]
    slots = z.slots
    given = (resp_q, out_grad, resp_kv)
    n_ahead = 2 * slots * z.tokens
    in_order = pl.pallas_call(
        functools.partial(sort_kernel, z, (2, FAR)),
        out_shape=[shape((2, n_ahead, z.lanes), BF16), shape((2, n_ahead, z.width), BF16)],
        in_specs=[ANYWHERE] * 4,
        out_specs=[ANYWHERE] * 2,
        scratch_shapes=[
            smem[0],
            pltpu.SMEM((2 * slots + 1,), jnp.int32),
            pltpu.VMEM((n_ahead, z.lanes), BF16),
            pltpu.VMEM((n_ahead, z.lanes), BF16),
            pltpu.VMEM((2, n_ahead, z.width), BF16),
            pltpu.SemaphoreType.DMA,
            pltpu.SemaphoreType.DMA((2 * slots, 3)),
            pltpu.SemaphoreType.DMA((2 * slots, 3)),
        ],
        compiler_params=params,
        cost_estimate=cost,
        name="sort_rows",
    )(resp_prompt, *given)
    onward, *barred = lax.optimization_barrier((prompts[2], *others, *in_order))
    others, in_order = barred[: n_dp - 1], barred[n_dp - 1 :]
    prompts[FAR] = swap(onward, 1)

    def grads_of(turns, ahead, written, come=(), kind=BF16):
        n_slots, n_turns = len(turns) * slots, len(turns)
        rows = () if ahead is None else in_order
        used_prompts = [prompts[turn] for turn in turns]
        operands = [*small, rewards, *others, *given, *used_prompts, *come, *rows, *written]
        return pl.pallas_call(
            functools.partial(group_kernel, z, turns, ahead, len(come), len(written)),
            out_shape=[shape(resp_q.shape, BF16), shape(resp_kv.shape, BF16)] + [shape(one, kind)] * n_turns,
            in_specs=[ANYWHERE] * len(operands),
            out_specs=[ANYWHERE] * (2 + n_turns),
            input_output_aliases={len(operands) - 2: 0, len(operands) - 1: 1} if written else {},
            scratch_shapes=[
                *smem,
                pltpu.SMEM((n_slots + 1,), jnp.int32),
                pltpu.SMEM((n_slots,), jnp.int32),
                pltpu.SMEM((n_slots,), F32),
                pltpu.VMEM((n_slots * z.tokens, z.lanes), BF16),
                pltpu.VMEM((n_slots * z.tokens, z.lanes), BF16),
                pltpu.VMEM((2, n_slots * z.tokens, z.width), BF16),
                pltpu.VMEM((n_turns,) + one, BF16),
                pltpu.VMEM(one, BF16),
                pltpu.VMEM((n_turns,) + one, F32),
                pltpu.VMEM((n_slots, z.tokens, z.lanes), BF16),
                pltpu.VMEM((n_slots, 2, z.tokens, z.width), BF16),
                pltpu.VMEM((n_turns,) + one, kind),
                pltpu.SemaphoreType.DMA((len(smem),)),
                pltpu.SemaphoreType.DMA((n_turns,)),
                pltpu.SemaphoreType.DMA,
                pltpu.SemaphoreType.DMA((n_slots, 3)),
                pltpu.SemaphoreType.DMA((n_slots, 2)),
                pltpu.SemaphoreType.DMA((n_turns,)),
                pltpu.SemaphoreType.DMA((3,)),
            ],
            compiler_params=pltpu.CompilerParams(vmem_limit_bytes=GROUP_BYTES),
            cost_estimate=cost,
            name="group_grads" if turns[0] else "own_grads",
        )(*operands)

    *written, for_2 = grads_of((2,), 0, ())
    come = [swap(for_2, 2)]
    *written, for_far, for_1 = grads_of((FAR, 1), 1, written)
    last = [swap(for_far, FAR), swap(for_1, 1)]
    q_out, self_out, summed = grads_of((0,), None, written, come, F32)
    prefix_out = (summed + sum(part.astype(F32) for part in last)).astype(BF16)
    return (q_out, self_out, prefix_out)


def far_kernel(z, *refs):
    (resp_prompt, resp_len, rewards, q_hbm, og_hbm, kv_hbm, prompts, q_out, self_out, prefix_outs,
     totals, lens, factors, q, og, kv, prefix, out, own, grads, sem_in, sem_prefix, sem_out) = refs
    me = lax.axis_index("dp")

    for p in range(z.n_dp):
        totals[p] = 0.0

    def copies_in(slot):
        rows = token_rows(z, slot)
        prompt = resp_prompt[me * z.count + slot]
        return (
            *row_copies((q_hbm, og_hbm, kv_hbm), (q, og, kv), rows, rows, sem_in.at[slot]),
            pltpu.make_async_copy(prompts.at[prompt], prefix.at[slot], sem_prefix.at[slot]),
        )

    def copies_out(slot):
        rows = token_rows(z, slot)
        return (
            *result_copies(out, own, q_out, self_out, slot, rows, sem_out),
            pltpu.make_async_copy(grads.at[slot], prefix_outs.at[slot], sem_out.at[slot, 3]),
        )

    def start(slot, _):
        for copy in copies_in(slot):
            copy.start()
        return 0

    lax.fori_loop(0, z.count, start, 0)

    def add(i, _):
        prompt = resp_prompt[i]
        totals[prompt] = totals[prompt] + rewards[i]
        return 0

    lax.fori_loop(0, z.n_dp * z.count, add, 0)

    def find_factor(slot, _):
        place = me * z.count + slot
        lens[slot] = resp_len[slot]
        factors[slot] = reward_factor(z, rewards[place], totals[resp_prompt[place]], resp_len[slot])
        return 0

    lax.fori_loop(0, z.count, find_factor, 0)

    def unit(slot, _):
        for copy in copies_in(slot):
            copy.wait()

        def sink(_, cols, key_grad, value_grad):
            grads[slot, 0, :, cols] = key_grad.astype(BF16)
            grads[slot, 1, :, cols] = value_grad.astype(BF16)

        units = [
            Unit([token_rows(z, slot)], [slot], k, [lens[slot]], [factors[slot]]) for k in range(z.kv_heads)
        ]
        attend(z, units, q, og, kv, prefix.at[slot], out, own, sink, True)
        for copy in copies_out(slot):
            copy.start()
        return 0

    lax.fori_loop(0, z.count, unit, 0)

    def end(slot, _):
        for copy in copies_out(slot):
            copy.wait()
        return 0

    lax.fori_loop(0, z.count, end, 0)


def far_shards(z, prompt_kv, resp_q, resp_kv, out_grad, rewards, resp_prompt, resp_len):
    assert z.slots == 1
    count, n_dp = z.count, z.n_dp
    one = (2, z.prefix_len, z.width)
    smem = pl.BlockSpec(memory_space=pltpu.SMEM)
    q_out, self_out, per_resp = pl.pallas_call(
        functools.partial(far_kernel, z),
        out_shape=[
            jax.ShapeDtypeStruct(resp_q.shape, BF16),
            jax.ShapeDtypeStruct(resp_kv.shape, BF16),
            jax.ShapeDtypeStruct((count,) + one, BF16),
        ],
        in_specs=[smem] * 3 + [ANYWHERE] * 4,
        out_specs=[ANYWHERE] * 3,
        scratch_shapes=[
            pltpu.SMEM((n_dp,), F32),
            pltpu.SMEM((count,), jnp.int32),
            pltpu.SMEM((count,), F32),
            pltpu.VMEM(resp_q.shape, BF16),
            pltpu.VMEM(resp_q.shape, BF16),
            pltpu.VMEM(resp_kv.shape, BF16),
            pltpu.VMEM((count,) + one, BF16),
            pltpu.VMEM((count, z.tokens, z.lanes), BF16),
            pltpu.VMEM((count, 2, z.tokens, z.width), BF16),
            pltpu.VMEM((count,) + one, BF16),
            pltpu.SemaphoreType.DMA((count, 4)),
            pltpu.SemaphoreType.DMA((count,)),
            pltpu.SemaphoreType.DMA((count, 4)),
        ],
        compiler_params=pltpu.CompilerParams(vmem_limit_bytes=VMEM_BYTES),
        name="far_grads",
    )(
        resp_prompt,
        resp_len,
        lax.all_gather(rewards, "dp", axis=0, tiled=True),
        resp_q,
        out_grad,
        resp_kv,
        lax.all_gather(prompt_kv, "dp", axis=0),
    )
    my_prompts = lax.dynamic_slice_in_dim(resp_prompt, lax.axis_index("dp") * count, count)
    route = (jnp.arange(n_dp, dtype=jnp.int32)[:, None] == my_prompts[None, :]).astype(BF16)
    outgoing = jnp.dot(route, per_resp.reshape(count, -1), preferred_element_type=F32).astype(BF16)
    outgoing = outgoing.reshape((n_dp,) + one)
    incoming = lax.all_to_all(outgoing, "dp", split_axis=0, concat_axis=0, tiled=True)
    prefix_out = jnp.sum(incoming, axis=0, dtype=F32).astype(BF16)
    return (q_out, self_out, prefix_out)


def shards(prompt_kv, resp_q, resp_kv, out_grad, rewards, resp_prompt, resp_len):
    n_dp = lax.axis_size("dp")
    count = rewards.shape[0]
    prefix_len, width = prompt_kv.shape[1:]
    slots = (count + n_dp - 1) // n_dp
    z = Sizes(
        n_dp, count, slots, width // HD, resp_q.shape[1] // width, resp_q.shape[0] // count, prefix_len
    )
    part = near_shards if count // slots == n_dp else far_shards
    return part(z, prompt_kv, resp_q, resp_kv, out_grad, rewards, resp_prompt, resp_len)


def solution(mesh):
    in_specs = (
        P(None, ("groups", "dp"), "tensor"),
        P(("groups", "dp"), "tensor"),
        P(None, ("groups", "dp"), "tensor"),
        P(("groups", "dp"), "tensor"),
        P(("groups", "dp")),
        P("groups"),
        P(("groups", "dp")),
    )
    out_specs = (
        P(("groups", "dp"), "tensor"),
        P(None, ("groups", "dp"), "tensor"),
        P(None, ("groups", "dp"), "tensor"),
    )
    return jax.shard_map(shards, mesh=mesh, in_specs=in_specs, out_specs=out_specs, check_vma=False)
```

```python
import functools
import math
from typing import NamedTuple

import jax
import jax.numpy as jnp
from jax import lax
from jax.experimental import pallas as pl
from jax.experimental.pallas import tpu as pltpu
from jax.sharding import PartitionSpec as P

HD = 128
NEG = -1e30
F32 = jnp.float32
BF16 = jnp.bfloat16
PAIR = 2
FAR = 3
VMEM_BYTES = 63 * 1024 * 1024
GROUP_BYTES = 54528 * 1024
ANYWHERE = pl.BlockSpec(memory_space=pl.ANY)


class Sizes(NamedTuple):
    n_dp: int
    count: int
    slots: int
    kv_heads: int
    group_size: int
    tokens: int
    prefix_len: int

    @property
    def width(self):
        return self.kv_heads * HD

    @property
    def lanes(self):
        return self.kv_heads * self.group_size * HD


def dot(a, b, dims):
    return lax.dot_general(a, b, (dims, ((), ())), preferred_element_type=F32)


NN = ((1,), (0,))
NT = ((1,), (1,))


class Bag:
    pass


class Unit(NamedTuple):
    at: list
    places: list
    k: object
    lens: list
    factors: list


def attend(z, units, q, og, kv, prefix, out, own_out, sink, apart):
    tokens, prefix_len, group_size = z.tokens, z.prefix_len, z.group_size
    scale = 1.0 / math.sqrt(HD)
    log_scale = scale * math.log2(math.e)
    whole = group_size - group_size % 2
    most = max(whole, 2) * tokens
    assert tokens & (tokens - 1) == 0
    token = lax.broadcasted_iota(jnp.int32, (1, most), 1) & (tokens - 1)
    key = lax.broadcasted_iota(jnp.int32, (tokens, most), 0)
    causal = key <= (lax.broadcasted_iota(jnp.int32, (tokens, most), 1) & (tokens - 1))
    left = lax.broadcasted_iota(jnp.int32, (1, 2 * tokens), 1) < tokens

    def columns(index):
        if isinstance(index, int):
            return slice(index * HD, (index + 1) * HD)
        return pl.ds(pl.multiple_of(index * HD, HD), HD)

    def head(k, h):
        return columns(k * group_size + h)

    def rows(ref, c):
        return jnp.concatenate([ref[c.t.at[n], head(c.t.k, h)] for n, h in c.blocks], axis=0)

    def halves(part):
        none = jnp.zeros_like(part)
        return [jnp.where(left, part, none), jnp.where(left, none, part)]

    def over_keys(combine, *parts):
        reduce = jnp.max if combine is jnp.maximum else jnp.sum
        eights = [reduce(part.reshape(-1, 8, part.shape[1]), axis=0) for part in parts]
        return reduce(functools.reduce(combine, eights), axis=0, keepdims=True)

    def own_half(both):
        return jnp.where(left, both[:tokens], both[tokens:])

    def rounded(*parts):
        return jnp.concatenate([part.astype(BF16) for part in parts], axis=0)

    chunks = []
    for unit in units:
        t = Bag()
        t.at, t.places, t.k, t.lens, t.factors = unit
        t.single = len(t.at) == 1
        t.members = range(len(t.at))
        sides = (0, 0) if t.single else (0, 1)
        t.cols = columns(t.k)
        t.key_p, t.value_p = prefix[0, :, t.cols], prefix[1, :, t.cols]
        t.keys = [kv[0, t.at[n], t.cols] for n in sides]
        t.values = [kv[1, t.at[n], t.cols] for n in sides]
        t.key_pair = jnp.concatenate(t.keys, axis=0)
        t.value_pair = jnp.concatenate(t.values, axis=0)
        t.key_t = jnp.concatenate([t.key_p.T, t.key_pair.T], axis=1)
        t.prefix_sums = {n: [] for n in t.members}
        t.self_sums = {n: [] for n in t.members}
        mine = []
        for n in t.members:
            c = Bag()
            c.t, c.side, c.blocks = t, n, [(n, h) for h in range(whole)]
            mine.append(c)
        if group_size % 2:
            c = Bag()
            c.t, c.side, c.blocks = t, None, [(n, group_size - 1) for n in sides]
            mine.append(c)
        t.left_over = len(mine)
        chunks += mine

    def products(c):
        t = c.t
        c.q_rows, c.g_rows = rows(q, c), rows(og, c)
        if c.side is None:
            key_s, value_s = t.key_pair, t.value_pair
        else:
            key_s, value_s = t.keys[c.side], t.values[c.side]
        c.scores = dot(jnp.concatenate([t.key_p, key_s], axis=0), c.q_rows, NT)
        c.gw = dot(jnp.concatenate([t.value_p, value_s], axis=0), c.g_rows, NT)

    def weigh(c):
        scores_p, scores_s = c.scores[:prefix_len], c.scores[prefix_len:]
        c.gw_p, c.gw_s = c.gw[:prefix_len], c.gw[prefix_len:]
        if c.side is None:
            scores_s, c.gw_s = own_half(scores_s), own_half(c.gw_s)
        scores_s = jnp.where(causal[:, : scores_s.shape[1]], scores_s, NEG)
        top = over_keys(jnp.maximum, scores_p, scores_s)
        c.e_p = jnp.exp2((scores_p - top) * log_scale)
        c.e_s = jnp.exp2((scores_s - top) * log_scale)
        total = over_keys(jnp.add, c.e_p, c.e_s)
        weighted = over_keys(jnp.add, c.e_p * c.gw_p, c.e_s * c.gw_s)
        if c.side is None:
            length = jnp.where(left, c.t.lens[0], 0 if c.t.single else c.t.lens[1])
            gain = jnp.where(left, c.t.factors[0], c.t.factors[-1])
        else:
            length, gain = c.t.lens[c.side], c.t.factors[c.side]
        inverse = 1.0 / total
        c.delta = weighted * inverse
        c.gain = inverse * jnp.where(token[:, : total.shape[1]] < length, gain, 0.0)

    def gradients(c):
        w_p, w_s = c.e_p * c.gain, c.e_s * c.gain
        d_p, d_s = w_p * (c.gw_p - c.delta), w_s * (c.gw_s - c.delta)
        if c.side is None:
            d_s, w_s = halves(d_s), halves(w_s)
            c.d_wide = rounded(d_p, *d_s)
            c.d_all = rounded(*halves(d_p), *d_s) if apart else c.d_wide
            c.w_all = rounded(*(halves(w_p) if apart else [w_p]), *w_s)
        else:
            empty = jnp.zeros_like(d_s)
            c.d_wide = rounded(*([d_p, empty, d_s] if c.side else [d_p, d_s, empty]))
            c.d_all = rounded(d_p, d_s)
            c.w_all = rounded(w_p, w_s)

    def outgoing(c):
        t = c.t
        q_grad = (dot(t.key_t, c.d_wide, NN) * scale).astype(BF16).T
        kg = dot(c.d_all, c.q_rows, NN)
        vg = dot(c.w_all, c.g_rows, NN)
        targets = t.members if c.side is None else [c.side]
        for place, (n, h) in enumerate(c.blocks):
            if c.side is not None or place < len(targets):
                out[t.places[n], :, head(t.k, h)] = q_grad[place * tokens : (place + 1) * tokens]
        many = 2 if c.side is None and apart else 1
        for place, n in enumerate(targets):
            if place < many:
                rows_p = slice(place * prefix_len, (place + 1) * prefix_len)
                t.prefix_sums[n if apart else 0].append((kg[rows_p], vg[rows_p]))
            start = many * prefix_len + place * tokens
            rows_s = slice(start, start + tokens)
            t.self_sums[n].append((kg[rows_s], vg[rows_s]))
        t.left_over -= 1
        if t.left_over == 0:
            for n in t.members:
                keys, values = zip(*t.self_sums[n])
                own_out[t.places[n], 0, :, t.cols] = (sum(keys) * scale).astype(BF16)
                own_out[t.places[n], 1, :, t.cols] = sum(values).astype(BF16)
                if apart or n == 0:
                    keys, values = zip(*t.prefix_sums[n])
                    sink(t.places[n], t.cols, sum(keys) * scale, sum(values))

    stages = (products, weigh, gradients, outgoing)
    for step in range(len(chunks) + len(stages) - 1):
        for late, stage in enumerate(stages):
            if 0 <= step - late < len(chunks):
                stage(chunks[step - late])


def token_rows(z, i):
    return pl.ds(pl.multiple_of(i * z.tokens, z.tokens), z.tokens)


def find_responses(z, me, turns, resp_prompt, order):
    for t, turn in enumerate(turns):
        prompt = me ^ turn
        found = t * z.slots
        for i in range(z.count):
            order[found] = i
            found = found + (resp_prompt[me * z.count + i] == prompt).astype(jnp.int32)


def prompt_total(z, me, prompt, resp_prompt, rewards):
    own, near, two = rewards
    total = jnp.float32(0.0)
    for s, (held, start) in enumerate([(own, 0), (near, 0), (two, 0), (two, z.count)]):
        for i in range(z.count):
            total += jnp.where(resp_prompt[(me ^ s) * z.count + i] == prompt, held[start + i], 0.0)
    return total


def reward_factor(z, reward, total, length):
    return (reward - total / z.count) * (z.tokens / length.astype(F32))


def row_copies(here, there, at_here, at_there, sems):
    (q0, og0, kv0), (q1, og1, kv1) = here, there
    return (
        pltpu.make_async_copy(q0.at[at_here], q1.at[at_there], sems.at[0]),
        pltpu.make_async_copy(og0.at[at_here], og1.at[at_there], sems.at[1]),
        pltpu.make_async_copy(kv0.at[:, at_here], kv1.at[:, at_there], sems.at[2]),
    )


def result_copies(out, own, q_out, self_out, place, at, sems, back=False):
    pairs = [
        (out.at[place], q_out.at[at]),
        (own.at[place], self_out.at[:, at]),
    ]
    return [
        pltpu.make_async_copy(*(reversed(pair) if back else pair), sems.at[place, n])
        for n, pair in enumerate(pairs)
    ]


def sort_kernel(z, ahead, resp_prompt_hbm, q_hbm, og_hbm, kv_hbm, both_out, kv_out, *scratch):
    resp_prompt, order, q, og, kv, sem_small, sem_in, sem_out = scratch
    me = lax.axis_index("dp")
    small = pltpu.make_async_copy(resp_prompt_hbm, resp_prompt, sem_small)
    small.start()
    small.wait()
    find_responses(z, me, ahead, resp_prompt, order)
    held, in_order = (q, og, kv), (both_out.at[0], both_out.at[1], kv_out)
    slots = range(len(ahead) * z.slots)

    def copies_in(slot):
        return row_copies(
            (q_hbm, og_hbm, kv_hbm), held, token_rows(z, order[slot]), token_rows(z, slot), sem_in.at[slot]
        )

    def copies_out(slot):
        rows = token_rows(z, slot)
        return row_copies(held, in_order, rows, rows, sem_out.at[slot])

    for slot in slots:
        for copy in copies_in(slot):
            copy.start()
    for slot in slots:
        for copy in copies_in(slot):
            copy.wait()
        for copy in copies_out(slot):
            copy.start()
    for slot in slots:
        for copy in copies_out(slot):
            copy.wait()


def group_kernel(z, turns, ahead, n_come, aliased, *refs):
    n_small = 5
    small_hbm, given, refs = refs[:n_small], refs[n_small : n_small + 3], refs[n_small + 3 :]
    prompts, refs = refs[: len(turns)], refs[len(turns) :]
    come_hbm, refs = refs[:n_come], refs[n_come:]
    if ahead is not None:
        (both, kv_ordered), refs = refs[:2], refs[2:]
    (q_out, self_out), refs = refs[aliased : aliased + 2], refs[aliased + 2 :]
    grads_out, refs = refs[: len(turns)], refs[len(turns) :]
    resp_prompt, resp_len, *rewards = refs[:n_small]
    (order, lens, factors, q, og, kv, prefix, come, acc, out, own, grads,
     sem_small, sem_prefix, sem_come, sem_in, sem_out, sem_grads, sem_first) = refs[n_small:]
    me = lax.axis_index("dp")
    n_slots = len(turns) * z.slots
    span = z.slots * z.tokens

    small = [
        pltpu.make_async_copy(src, dst, sem_small.at[n])
        for n, (src, dst) in enumerate(zip(small_hbm, (resp_prompt, resp_len, *rewards)))
    ]
    first_rows = ()
    if ahead is not None:
        first_rows = row_copies(
            (both.at[0], both.at[1], kv_ordered), (q, og, kv), pl.ds(ahead * span, span), pl.ds(0, span), sem_first
        )
    prefix_copies = [
        pltpu.make_async_copy(prompts[t], prefix.at[t], sem_prefix.at[t]) for t in range(len(turns))
    ]
    late = [pltpu.make_async_copy(src, come, sem_come) for src in come_hbm]
    for copy in [*small, *first_rows, *prefix_copies, *late]:
        copy.start()
    small[0].wait()
    find_responses(z, me, turns, resp_prompt, order)

    def copies_in(slot):
        return row_copies(
            given, (q, og, kv), token_rows(z, order[slot]), token_rows(z, slot), sem_in.at[slot]
        )

    def copies_out(slot):
        return result_copies(out, own, q_out, self_out, slot, token_rows(z, order[slot]), sem_out)

    for slot in range(0 if ahead is None else z.slots, n_slots):
        for copy in copies_in(slot):
            copy.start()
    for copy in small[1:] + late:
        copy.wait()
    for t, turn in enumerate(turns):
        total = prompt_total(z, me, me ^ turn, resp_prompt, rewards)
        for slot in range(t * z.slots, (t + 1) * z.slots):
            i = order[slot]
            lens[slot] = resp_len[i]
            factors[slot] = reward_factor(z, rewards[0][i], total, resp_len[i])
    if n_come:
        acc[0] = come[...].astype(F32)
    else:
        acc[...] = jnp.zeros(acc.shape, F32)
    for copy in prefix_copies:
        copy.wait()

    def step(t, _):
        slots = [t * z.slots + n for n in range(z.slots)]

        def wait_for_slots():
            for slot in slots:
                for copy in copies_in(slot):
                    copy.wait()

        if ahead is None:
            wait_for_slots()
        else:

            @pl.when(t == 0)
            def _():
                for copy in first_rows:
                    copy.wait()

            if len(turns) > 1:
                pl.when(t > 0)(wait_for_slots)

        def sink(_, cols, key_grad, value_grad):
            acc[t, 0, :, cols] += key_grad
            acc[t, 1, :, cols] += value_grad

        units = []
        for pair in range(0, z.slots, PAIR):
            places = slots[pair : pair + PAIR]
            at = [token_rows(z, n) for n in places]
            for k in range(z.kv_heads):
                units.append(Unit(at, places, k, [lens[n] for n in places], [factors[n] for n in places]))
        attend(z, units, q, og, kv, prefix.at[t], out, own, sink, False)
        for slot in slots:
            for copy in copies_out(slot):
                copy.start()
        return 0

    lax.fori_loop(0, len(turns), step, 0)
    grads[...] = acc[...].astype(grads.dtype)
    last = [pltpu.make_async_copy(grads.at[t], grads_out[t], sem_grads.at[t]) for t in range(len(turns))]
    for copy in last:
        copy.start()
    for slot in range(n_slots):
        for copy in copies_out(slot):
            copy.wait()
    for copy in last:
        copy.wait()


def near_shards(z, prompt_kv, resp_q, resp_kv, out_grad, rewards, resp_prompt, resp_len):
    n_dp = z.n_dp
    assert z.slots % PAIR == 0
    shape = jax.ShapeDtypeStruct
    one = (2, z.prefix_len, z.width)
    params = pltpu.CompilerParams(vmem_limit_bytes=VMEM_BYTES)
    cost = pl.CostEstimate(flops=0, bytes_accessed=0, transcendentals=0)
    assert n_dp == FAR + 1

    def swap(x, s):
        return lax.ppermute(x, "dp", [(i, i ^ s) for i in range(n_dp)])

    prompts = {0: prompt_kv, 2: swap(prompt_kv, 2), 1: swap(prompt_kv, 1)}
    near_rewards = swap(rewards, 1)
    others = [near_rewards, swap(jnp.concatenate([rewards, near_rewards]), 2)]
    small = (resp_prompt, resp_len)
    smem = [pltpu.SMEM(x.shape, x.dtype) for x in (*small, rewards, *others)]
    slots = z.slots
    given = (resp_q, out_grad, resp_kv)
    n_ahead = 2 * slots * z.tokens
    in_order = pl.pallas_call(
        functools.partial(sort_kernel, z, (2, FAR)),
        out_shape=[shape((2, n_ahead, z.lanes), BF16), shape((2, n_ahead, z.width), BF16)],
        in_specs=[ANYWHERE] * 4,
        out_specs=[ANYWHERE] * 2,
        scratch_shapes=[
            smem[0],
            pltpu.SMEM((2 * slots + 1,), jnp.int32),
            pltpu.VMEM((n_ahead, z.lanes), BF16),
            pltpu.VMEM((n_ahead, z.lanes), BF16),
            pltpu.VMEM((2, n_ahead, z.width), BF16),
            pltpu.SemaphoreType.DMA,
            pltpu.SemaphoreType.DMA((2 * slots, 3)),
            pltpu.SemaphoreType.DMA((2 * slots, 3)),
        ],
        compiler_params=params,
        cost_estimate=cost,
        name="sort_rows",
    )(resp_prompt, *given)
    onward, *barred = lax.optimization_barrier((prompts[2], *others, *in_order))
    others, in_order = barred[: len(others)], barred[len(others) :]
    prompts[FAR] = swap(onward, 1)

    def grads_of(turns, ahead, written, come=(), kind=BF16):
        n_slots, n_turns = len(turns) * slots, len(turns)
        rows = () if ahead is None else in_order
        used_prompts = [prompts[turn] for turn in turns]
        operands = [*small, rewards, *others, *given, *used_prompts, *come, *rows, *written]
        return pl.pallas_call(
            functools.partial(group_kernel, z, turns, ahead, len(come), len(written)),
            out_shape=[shape(resp_q.shape, BF16), shape(resp_kv.shape, BF16)] + [shape(one, kind)] * n_turns,
            in_specs=[ANYWHERE] * len(operands),
            out_specs=[ANYWHERE] * (2 + n_turns),
            input_output_aliases={len(operands) - 2: 0, len(operands) - 1: 1} if written else {},
            scratch_shapes=[
                *smem,
                pltpu.SMEM((n_slots + 1,), jnp.int32),
                pltpu.SMEM((n_slots,), jnp.int32),
                pltpu.SMEM((n_slots,), F32),
                pltpu.VMEM((n_slots * z.tokens, z.lanes), BF16),
                pltpu.VMEM((n_slots * z.tokens, z.lanes), BF16),
                pltpu.VMEM((2, n_slots * z.tokens, z.width), BF16),
                pltpu.VMEM((n_turns,) + one, BF16),
                pltpu.VMEM(one, BF16),
                pltpu.VMEM((n_turns,) + one, F32),
                pltpu.VMEM((n_slots, z.tokens, z.lanes), BF16),
                pltpu.VMEM((n_slots, 2, z.tokens, z.width), BF16),
                pltpu.VMEM((n_turns,) + one, kind),
                pltpu.SemaphoreType.DMA((len(smem),)),
                pltpu.SemaphoreType.DMA((n_turns,)),
                pltpu.SemaphoreType.DMA,
                pltpu.SemaphoreType.DMA((n_slots, 3)),
                pltpu.SemaphoreType.DMA((n_slots, 2)),
                pltpu.SemaphoreType.DMA((n_turns,)),
                pltpu.SemaphoreType.DMA((3,)),
            ],
            compiler_params=pltpu.CompilerParams(vmem_limit_bytes=GROUP_BYTES),
            cost_estimate=cost,
            name="group_grads" if turns[0] else "own_grads",
        )(*operands)

    *written, for_2 = grads_of((2,), 0, ())
    come = [swap(for_2, 2)]
    *written, for_far, for_1 = grads_of((FAR, 1), 1, written)
    last = [swap(for_far, FAR), swap(for_1, 1)]
    q_out, self_out, summed = grads_of((0,), None, written, come, F32)
    prefix_out = (summed + sum(part.astype(F32) for part in last)).astype(BF16)
    return (q_out, self_out, prefix_out)


def far_kernel(z, *refs):
    (resp_prompt, resp_len, rewards, q_hbm, og_hbm, kv_hbm, prompts, q_out, self_out, prefix_outs,
     totals, lens, factors, q, og, kv, prefix, out, own, grads, sem_in, sem_prefix, sem_out) = refs
    me = lax.axis_index("dp")

    for p in range(z.n_dp):
        totals[p] = 0.0

    def copies_in(slot):
        rows = token_rows(z, slot)
        prompt = resp_prompt[me * z.count + slot]
        return (
            *row_copies((q_hbm, og_hbm, kv_hbm), (q, og, kv), rows, rows, sem_in.at[slot]),
            pltpu.make_async_copy(prompts.at[prompt], prefix.at[slot], sem_prefix.at[slot]),
        )

    def copies_out(slot):
        rows = token_rows(z, slot)
        return (
            *result_copies(out, own, q_out, self_out, slot, rows, sem_out),
            pltpu.make_async_copy(grads.at[slot], prefix_outs.at[slot], sem_out.at[slot, 3]),
        )

    def start(slot, _):
        for copy in copies_in(slot):
            copy.start()
        return 0

    lax.fori_loop(0, z.count, start, 0)

    def add(i, _):
        prompt = resp_prompt[i]
        totals[prompt] = totals[prompt] + rewards[i]
        return 0

    lax.fori_loop(0, z.n_dp * z.count, add, 0)

    def find_factor(slot, _):
        place = me * z.count + slot
        lens[slot] = resp_len[slot]
        factors[slot] = reward_factor(z, rewards[place], totals[resp_prompt[place]], resp_len[slot])
        return 0

    lax.fori_loop(0, z.count, find_factor, 0)

    def unit(slot, _):
        for copy in copies_in(slot):
            copy.wait()

        def sink(_, cols, key_grad, value_grad):
            grads[slot, 0, :, cols] = key_grad.astype(BF16)
            grads[slot, 1, :, cols] = value_grad.astype(BF16)

        units = [
            Unit([token_rows(z, slot)], [slot], k, [lens[slot]], [factors[slot]]) for k in range(z.kv_heads)
        ]
        attend(z, units, q, og, kv, prefix.at[slot], out, own, sink, True)
        for copy in copies_out(slot):
            copy.start()
        return 0

    lax.fori_loop(0, z.count, unit, 0)

    def end(slot, _):
        for copy in copies_out(slot):
            copy.wait()
        return 0

    lax.fori_loop(0, z.count, end, 0)


def far_shards(z, prompt_kv, resp_q, resp_kv, out_grad, rewards, resp_prompt, resp_len):
    assert z.slots == 1
    count, n_dp = z.count, z.n_dp
    one = (2, z.prefix_len, z.width)
    smem = pl.BlockSpec(memory_space=pltpu.SMEM)
    q_out, self_out, per_resp = pl.pallas_call(
        functools.partial(far_kernel, z),
        out_shape=[
            jax.ShapeDtypeStruct(resp_q.shape, BF16),
            jax.ShapeDtypeStruct(resp_kv.shape, BF16),
            jax.ShapeDtypeStruct((count,) + one, BF16),
        ],
        in_specs=[smem] * 3 + [ANYWHERE] * 4,
        out_specs=[ANYWHERE] * 3,
        scratch_shapes=[
            pltpu.SMEM((n_dp,), F32),
            pltpu.SMEM((count,), jnp.int32),
            pltpu.SMEM((count,), F32),
            pltpu.VMEM(resp_q.shape, BF16),
            pltpu.VMEM(resp_q.shape, BF16),
            pltpu.VMEM(resp_kv.shape, BF16),
            pltpu.VMEM((count,) + one, BF16),
            pltpu.VMEM((count, z.tokens, z.lanes), BF16),
            pltpu.VMEM((count, 2, z.tokens, z.width), BF16),
            pltpu.VMEM((count,) + one, BF16),
            pltpu.SemaphoreType.DMA((count, 4)),
            pltpu.SemaphoreType.DMA((count,)),
            pltpu.SemaphoreType.DMA((count, 4)),
        ],
        compiler_params=pltpu.CompilerParams(vmem_limit_bytes=VMEM_BYTES),
        name="far_grads",
    )(
        resp_prompt,
        resp_len,
        lax.all_gather(rewards, "dp", axis=0, tiled=True),
        resp_q,
        out_grad,
        resp_kv,
        lax.all_gather(prompt_kv, "dp", axis=0),
    )
    my_prompts = lax.dynamic_slice_in_dim(resp_prompt, lax.axis_index("dp") * count, count)
    route = (jnp.arange(n_dp, dtype=jnp.int32)[:, None] == my_prompts[None, :]).astype(BF16)
    outgoing = jnp.dot(route, per_resp.reshape(count, -1), preferred_element_type=F32).astype(BF16)
    outgoing = outgoing.reshape((n_dp,) + one)
    incoming = lax.all_to_all(outgoing, "dp", split_axis=0, concat_axis=0, tiled=True)
    prefix_out = jnp.sum(incoming, axis=0, dtype=F32).astype(BF16)
    return (q_out, self_out, prefix_out)


def shards(prompt_kv, resp_q, resp_kv, out_grad, rewards, resp_prompt, resp_len):
    n_dp = lax.axis_size("dp")
    count = rewards.shape[0]
    prefix_len, width = prompt_kv.shape[1:]
    slots = (count + n_dp - 1) // n_dp
    z = Sizes(
        n_dp, count, slots, width // HD, resp_q.shape[1] // width, resp_q.shape[0] // count, prefix_len
    )
    part = near_shards if count // slots == n_dp else far_shards
    return part(z, prompt_kv, resp_q, resp_kv, out_grad, rewards, resp_prompt, resp_len)


def solution(mesh):
    in_specs = (
        P(None, ("groups", "dp"), "tensor"),
        P(("groups", "dp"), "tensor"),
        P(None, ("groups", "dp"), "tensor"),
        P(("groups", "dp"), "tensor"),
        P(("groups", "dp")),
        P("groups"),
        P(("groups", "dp")),
    )
    out_specs = (
        P(("groups", "dp"), "tensor"),
        P(None, ("groups", "dp"), "tensor"),
        P(None, ("groups", "dp"), "tensor"),
    )
    return jax.shard_map(shards, mesh=mesh, in_specs=in_specs, out_specs=out_specs, check_vma=False)
```

```python
import functools
import math
from typing import NamedTuple

import jax
import jax.numpy as jnp
from jax import lax
from jax.experimental import pallas as pl
from jax.experimental.pallas import tpu as pltpu
from jax.sharding import PartitionSpec as P

HD = 128
NEG = -1e30
F32 = jnp.float32
BF16 = jnp.bfloat16
PAIR = 2
FAR = 3
VMEM_BYTES = 63 * 1024 * 1024
GROUP_BYTES = 54528 * 1024
FIRST_BYTES = 54784 * 1024
ANYWHERE = pl.BlockSpec(memory_space=pl.ANY)


class Sizes(NamedTuple):
    n_dp: int
    count: int
    slots: int
    kv_heads: int
    group_size: int
    tokens: int
    prefix_len: int

    @property
    def width(self):
        return self.kv_heads * HD

    @property
    def lanes(self):
        return self.kv_heads * self.group_size * HD


def dot(a, b, dims):
    return lax.dot_general(a, b, (dims, ((), ())), preferred_element_type=F32)


NN = ((1,), (0,))
NT = ((1,), (1,))


class Bag:
    pass


class Unit(NamedTuple):
    at: list
    places: list
    k: object
    lens: list
    factors: list


def attend(z, units, q, og, kv, prefix, out, own_out, sink, apart):
    tokens, prefix_len, group_size = z.tokens, z.prefix_len, z.group_size
    scale = 1.0 / math.sqrt(HD)
    log_scale = scale * math.log2(math.e)
    whole = group_size - group_size % 2
    most = max(whole, 2) * tokens
    assert tokens & (tokens - 1) == 0
    token = lax.broadcasted_iota(jnp.int32, (1, most), 1) & (tokens - 1)
    key = lax.broadcasted_iota(jnp.int32, (tokens, most), 0)
    causal = key <= (lax.broadcasted_iota(jnp.int32, (tokens, most), 1) & (tokens - 1))
    left = lax.broadcasted_iota(jnp.int32, (1, 2 * tokens), 1) < tokens

    def columns(index):
        if isinstance(index, int):
            return slice(index * HD, (index + 1) * HD)
        return pl.ds(pl.multiple_of(index * HD, HD), HD)

    def head(k, h):
        return columns(k * group_size + h)

    def rows(ref, c):
        return jnp.concatenate([ref[c.t.at[n], head(c.t.k, h)] for n, h in c.blocks], axis=0)

    def halves(part):
        none = jnp.zeros_like(part)
        return [jnp.where(left, part, none), jnp.where(left, none, part)]

    def over_keys(combine, *parts):
        reduce = jnp.max if combine is jnp.maximum else jnp.sum
        eights = [reduce(part.reshape(-1, 8, part.shape[1]), axis=0) for part in parts]
        return reduce(functools.reduce(combine, eights), axis=0, keepdims=True)

    def own_half(both):
        return jnp.where(left, both[:tokens], both[tokens:])

    def rounded(*parts):
        return jnp.concatenate([part.astype(BF16) for part in parts], axis=0)

    chunks = []
    for unit in units:
        t = Bag()
        t.at, t.places, t.k, t.lens, t.factors = unit
        t.single = len(t.at) == 1
        t.members = range(len(t.at))
        sides = (0, 0) if t.single else (0, 1)
        t.cols = columns(t.k)
        t.key_p, t.value_p = prefix[0, :, t.cols], prefix[1, :, t.cols]
        t.keys = [kv[0, t.at[n], t.cols] for n in sides]
        t.values = [kv[1, t.at[n], t.cols] for n in sides]
        t.key_pair = jnp.concatenate(t.keys, axis=0)
        t.value_pair = jnp.concatenate(t.values, axis=0)
        t.key_t = jnp.concatenate([t.key_p.T, t.key_pair.T], axis=1)
        t.prefix_sums = {n: [] for n in t.members}
        t.self_sums = {n: [] for n in t.members}
        mine = []
        for n in t.members:
            c = Bag()
            c.t, c.side, c.blocks = t, n, [(n, h) for h in range(whole)]
            mine.append(c)
        if group_size % 2:
            c = Bag()
            c.t, c.side, c.blocks = t, None, [(n, group_size - 1) for n in sides]
            mine.append(c)
        t.left_over = len(mine)
        chunks += mine

    def products(c):
        t = c.t
        c.q_rows, c.g_rows = rows(q, c), rows(og, c)
        if c.side is None:
            key_s, value_s = t.key_pair, t.value_pair
        else:
            key_s, value_s = t.keys[c.side], t.values[c.side]
        c.scores = dot(jnp.concatenate([t.key_p, key_s], axis=0), c.q_rows, NT)
        c.gw = dot(jnp.concatenate([t.value_p, value_s], axis=0), c.g_rows, NT)

    def weigh(c):
        scores_p, scores_s = c.scores[:prefix_len], c.scores[prefix_len:]
        c.gw_p, c.gw_s = c.gw[:prefix_len], c.gw[prefix_len:]
        if c.side is None:
            scores_s, c.gw_s = own_half(scores_s), own_half(c.gw_s)
        scores_s = jnp.where(causal[:, : scores_s.shape[1]], scores_s, NEG)
        top = over_keys(jnp.maximum, scores_p, scores_s)
        c.e_p = jnp.exp2((scores_p - top) * log_scale)
        c.e_s = jnp.exp2((scores_s - top) * log_scale)
        total = over_keys(jnp.add, c.e_p, c.e_s)
        weighted = over_keys(jnp.add, c.e_p * c.gw_p, c.e_s * c.gw_s)
        if c.side is None:
            length = jnp.where(left, c.t.lens[0], 0 if c.t.single else c.t.lens[1])
            gain = jnp.where(left, c.t.factors[0], c.t.factors[-1])
        else:
            length, gain = c.t.lens[c.side], c.t.factors[c.side]
        inverse = 1.0 / total
        c.delta = weighted * inverse
        c.gain = inverse * jnp.where(token[:, : total.shape[1]] < length, gain, 0.0)

    def gradients(c):
        w_p, w_s = c.e_p * c.gain, c.e_s * c.gain
        d_p, d_s = w_p * (c.gw_p - c.delta), w_s * (c.gw_s - c.delta)
        if c.side is None:
            d_s, w_s = halves(d_s), halves(w_s)
            c.d_wide = rounded(d_p, *d_s)
            c.d_all = rounded(*halves(d_p), *d_s) if apart else c.d_wide
            c.w_all = rounded(*(halves(w_p) if apart else [w_p]), *w_s)
        else:
            empty = jnp.zeros_like(d_s)
            c.d_wide = rounded(*([d_p, empty, d_s] if c.side else [d_p, d_s, empty]))
            c.d_all = rounded(d_p, d_s)
            c.w_all = rounded(w_p, w_s)

    def outgoing(c):
        t = c.t
        q_grad = (dot(t.key_t, c.d_wide, NN) * scale).astype(BF16).T
        kg = dot(c.d_all, c.q_rows, NN)
        vg = dot(c.w_all, c.g_rows, NN)
        targets = t.members if c.side is None else [c.side]
        for place, (n, h) in enumerate(c.blocks):
            if c.side is not None or place < len(targets):
                out[t.places[n], :, head(t.k, h)] = q_grad[place * tokens : (place + 1) * tokens]
        many = 2 if c.side is None and apart else 1
        for place, n in enumerate(targets):
            if place < many:
                rows_p = slice(place * prefix_len, (place + 1) * prefix_len)
                t.prefix_sums[n if apart else 0].append((kg[rows_p], vg[rows_p]))
            start = many * prefix_len + place * tokens
            rows_s = slice(start, start + tokens)
            t.self_sums[n].append((kg[rows_s], vg[rows_s]))
        t.left_over -= 1
        if t.left_over == 0:
            for n in t.members:
                keys, values = zip(*t.self_sums[n])
                own_out[t.places[n], 0, :, t.cols] = (sum(keys) * scale).astype(BF16)
                own_out[t.places[n], 1, :, t.cols] = sum(values).astype(BF16)
                if apart or n == 0:
                    keys, values = zip(*t.prefix_sums[n])
                    sink(t.places[n], t.cols, sum(keys) * scale, sum(values))

    stages = (products, weigh, gradients, outgoing)
    for step in range(len(chunks) + len(stages) - 1):
        for late, stage in enumerate(stages):
            if 0 <= step - late < len(chunks):
                stage(chunks[step - late])


def token_rows(z, i):
    return pl.ds(pl.multiple_of(i * z.tokens, z.tokens), z.tokens)


def find_responses(z, me, turns, resp_prompt, order):
    for t, turn in enumerate(turns):
        prompt = me ^ turn
        found = t * z.slots
        for i in range(z.count):
            order[found] = i
            found = found + (resp_prompt[me * z.count + i] == prompt).astype(jnp.int32)


def prompt_total(z, me, prompt, resp_prompt, rewards):
    total = jnp.float32(0.0)
    for s in range(z.n_dp):
        for i in range(z.count):
            total += jnp.where(resp_prompt[(me ^ s) * z.count + i] == prompt, rewards[s][i], 0.0)
    return total


def reward_factor(z, reward, total, length):
    return (reward - total / z.count) * (z.tokens / length.astype(F32))


def row_copies(here, there, at_here, at_there, sems):
    (q0, og0, kv0), (q1, og1, kv1) = here, there
    return (
        pltpu.make_async_copy(q0.at[at_here], q1.at[at_there], sems.at[0]),
        pltpu.make_async_copy(og0.at[at_here], og1.at[at_there], sems.at[1]),
        pltpu.make_async_copy(kv0.at[:, at_here], kv1.at[:, at_there], sems.at[2]),
    )


def result_copies(out, own, q_out, self_out, place, at, sems, back=False):
    pairs = [
        (out.at[place], q_out.at[at]),
        (own.at[place], self_out.at[:, at]),
    ]
    return [
        pltpu.make_async_copy(*(reversed(pair) if back else pair), sems.at[place, n])
        for n, pair in enumerate(pairs)
    ]


def sort_kernel(z, ahead, resp_prompt_hbm, q_hbm, og_hbm, kv_hbm, both_out, kv_out, *scratch):
    resp_prompt, order, q, og, kv, sem_small, sem_in, sem_out = scratch
    me = lax.axis_index("dp")
    small = pltpu.make_async_copy(resp_prompt_hbm, resp_prompt, sem_small)
    small.start()
    small.wait()
    find_responses(z, me, ahead, resp_prompt, order)
    held, in_order = (q, og, kv), (both_out.at[0], both_out.at[1], kv_out)
    slots = range(len(ahead) * z.slots)

    def copies_in(slot):
        return row_copies(
            (q_hbm, og_hbm, kv_hbm), held, token_rows(z, order[slot]), token_rows(z, slot), sem_in.at[slot]
        )

    def copies_out(slot):
        rows = token_rows(z, slot)
        return row_copies(held, in_order, rows, rows, sem_out.at[slot])

    for slot in slots:
        for copy in copies_in(slot):
            copy.start()
    for slot in slots:
        for copy in copies_in(slot):
            copy.wait()
        for copy in copies_out(slot):
            copy.start()
    for slot in slots:
        for copy in copies_out(slot):
            copy.wait()


def group_kernel(z, turns, ahead, stage, n_come, aliased, *refs):
    n_small = 2 + z.n_dp
    small_hbm, given, refs = refs[:n_small], refs[n_small : n_small + 3], refs[n_small + 3 :]
    prompts, refs = refs[: len(turns)], refs[len(turns) :]
    come_hbm, refs = refs[:n_come], refs[n_come:]
    if ahead:
        (both, kv_ordered), refs = refs[:2], refs[2:]
    (q_out, self_out), refs = refs[aliased : aliased + 2], refs[aliased + 2 :]
    grads_out, refs = refs[: len(turns)], refs[len(turns) :]
    if stage is not None:
        (next_both, next_kv), refs = refs[:2], refs[2:]
    resp_prompt, resp_len, *rewards = refs[:n_small]
    (order, lens, factors, q, og, kv, prefix, come, acc, out, own, grads,
     sem_small, sem_prefix, sem_come, sem_in, sem_out, sem_grads, sem_first, sem_stage) = refs[n_small:]
    me = lax.axis_index("dp")
    n_slots = len(turns) * z.slots
    span = z.slots * z.tokens

    small = [
        pltpu.make_async_copy(src, dst, sem_small.at[n])
        for n, (src, dst) in enumerate(zip(small_hbm, (resp_prompt, resp_len, *rewards)))
    ]
    first_rows = ()
    if ahead:
        first_rows = row_copies(
            (both.at[0], both.at[1], kv_ordered), (q, og, kv), pl.ds(0, span), pl.ds(0, span), sem_first
        )
    prefix_copies = [
        pltpu.make_async_copy(prompts[t], prefix.at[t], sem_prefix.at[t]) for t in range(len(turns))
    ]
    late = [pltpu.make_async_copy(src, come, sem_come) for src in come_hbm]
    for copy in [*small, *first_rows, *prefix_copies, *late]:
        copy.start()
    small[0].wait()
    staged = range(n_slots, n_slots + (0 if stage is None else z.slots))
    find_responses(z, me, [*turns, *([] if stage is None else [stage])], resp_prompt, order)

    def copies_in(slot):
        return row_copies(
            given, (q, og, kv), token_rows(z, order[slot]), token_rows(z, slot), sem_in.at[slot]
        )

    def copies_out(slot):
        return result_copies(out, own, q_out, self_out, slot, token_rows(z, order[slot]), sem_out)

    def copies_staged(slot):
        return row_copies(
            (q, og, kv),
            (next_both.at[0], next_both.at[1], next_kv),
            token_rows(z, slot),
            token_rows(z, slot - n_slots),
            sem_stage.at[slot - n_slots],
        )

    for slot in [*range(z.slots if ahead else 0, n_slots), *staged]:
        for copy in copies_in(slot):
            copy.start()
    for copy in small[1:] + late:
        copy.wait()
    for t, turn in enumerate(turns):
        total = prompt_total(z, me, me ^ turn, resp_prompt, rewards)
        for slot in range(t * z.slots, (t + 1) * z.slots):
            i = order[slot]
            lens[slot] = resp_len[i]
            factors[slot] = reward_factor(z, rewards[0][i], total, resp_len[i])
    if n_come:
        acc[0] = come[...].astype(F32)
    else:
        acc[...] = jnp.zeros(acc.shape, F32)
    for copy in prefix_copies:
        copy.wait()

    def step(t, _):
        slots = [t * z.slots + n for n in range(z.slots)]

        def wait_for_slots():
            for slot in slots:
                for copy in copies_in(slot):
                    copy.wait()

        if not ahead:
            wait_for_slots()
        else:

            @pl.when(t == 0)
            def _():
                for copy in first_rows:
                    copy.wait()

            if len(turns) > 1:
                pl.when(t > 0)(wait_for_slots)

        def sink(_, cols, key_grad, value_grad):
            acc[t, 0, :, cols] += key_grad
            acc[t, 1, :, cols] += value_grad

        units = []
        for pair in range(0, z.slots, PAIR):
            places = slots[pair : pair + PAIR]
            at = [token_rows(z, n) for n in places]
            for k in range(z.kv_heads):
                units.append(Unit(at, places, k, [lens[n] for n in places], [factors[n] for n in places]))
        attend(z, units, q, og, kv, prefix.at[t], out, own, sink, False)
        for slot in slots:
            for copy in copies_out(slot):
                copy.start()
        return 0

    lax.fori_loop(0, len(turns), step, 0)
    grads[...] = acc[...].astype(grads.dtype)
    last = [pltpu.make_async_copy(grads.at[t], grads_out[t], sem_grads.at[t]) for t in range(len(turns))]
    for copy in last:
        copy.start()
    for slot in staged:
        for copy in copies_in(slot):
            copy.wait()
        for copy in copies_staged(slot):
            copy.start()
    for slot in range(n_slots):
        for copy in copies_out(slot):
            copy.wait()
    for slot in staged:
        for copy in copies_staged(slot):
            copy.wait()
    for copy in last:
        copy.wait()


def near_shards(z, prompt_kv, resp_q, resp_kv, out_grad, rewards, resp_prompt, resp_len):
    n_dp = z.n_dp
    assert z.slots % PAIR == 0
    shape = jax.ShapeDtypeStruct
    one = (2, z.prefix_len, z.width)
    params = pltpu.CompilerParams(vmem_limit_bytes=VMEM_BYTES)
    cost = pl.CostEstimate(flops=0, bytes_accessed=0, transcendentals=0)
    assert n_dp == FAR + 1

    def swap(x, s):
        return lax.ppermute(x, "dp", [(i, i ^ s) for i in range(n_dp)])

    prompts = {0: prompt_kv, 2: swap(prompt_kv, 2), 1: swap(prompt_kv, 1)}
    others = [swap(rewards, s) for s in range(1, n_dp)]
    small = (resp_prompt, resp_len)
    smem = [pltpu.SMEM(x.shape, x.dtype) for x in (*small, rewards, *others)]
    slots = z.slots
    given = (resp_q, out_grad, resp_kv)
    n_ahead = slots * z.tokens
    in_order = pl.pallas_call(
        functools.partial(sort_kernel, z, (2,)),
        out_shape=[shape((2, n_ahead, z.lanes), BF16), shape((2, n_ahead, z.width), BF16)],
        in_specs=[ANYWHERE] * 4,
        out_specs=[ANYWHERE] * 2,
        scratch_shapes=[
            smem[0],
            pltpu.SMEM((slots + 1,), jnp.int32),
            pltpu.VMEM((n_ahead, z.lanes), BF16),
            pltpu.VMEM((n_ahead, z.lanes), BF16),
            pltpu.VMEM((2, n_ahead, z.width), BF16),
            pltpu.SemaphoreType.DMA,
            pltpu.SemaphoreType.DMA((slots, 3)),
            pltpu.SemaphoreType.DMA((slots, 3)),
        ],
        compiler_params=params,
        cost_estimate=cost,
        name="sort_rows",
    )(resp_prompt, *given)
    onward, *barred = lax.optimization_barrier((prompts[2], *others, *in_order))
    others, in_order = barred[: n_dp - 1], barred[n_dp - 1 :]
    prompts[FAR] = swap(onward, 1)

    def grads_of(turns, rows, stage, written, come=(), kind=BF16):
        n_slots, n_turns = len(turns) * slots, len(turns)
        n_held = n_slots + (0 if stage is None else slots)
        next_shapes = [] if stage is None else [(2, n_ahead, z.lanes), (2, n_ahead, z.width)]
        used_prompts = [prompts[turn] for turn in turns]
        operands = [*small, rewards, *others, *given, *used_prompts, *come, *rows, *written]
        return pl.pallas_call(
            functools.partial(group_kernel, z, turns, bool(rows), stage, len(come), len(written)),
            out_shape=[shape(resp_q.shape, BF16), shape(resp_kv.shape, BF16)]
            + [shape(one, kind)] * n_turns
            + [shape(x, BF16) for x in next_shapes],
            in_specs=[ANYWHERE] * len(operands),
            out_specs=[ANYWHERE] * (2 + n_turns + len(next_shapes)),
            input_output_aliases={len(operands) - 2: 0, len(operands) - 1: 1} if written else {},
            scratch_shapes=[
                *smem,
                pltpu.SMEM((n_held + 1,), jnp.int32),
                pltpu.SMEM((n_slots,), jnp.int32),
                pltpu.SMEM((n_slots,), F32),
                pltpu.VMEM((n_held * z.tokens, z.lanes), BF16),
                pltpu.VMEM((n_held * z.tokens, z.lanes), BF16),
                pltpu.VMEM((2, n_held * z.tokens, z.width), BF16),
                pltpu.VMEM((n_turns,) + one, BF16),
                pltpu.VMEM(one, BF16),
                pltpu.VMEM((n_turns,) + one, F32),
                pltpu.VMEM((n_slots, z.tokens, z.lanes), BF16),
                pltpu.VMEM((n_slots, 2, z.tokens, z.width), BF16),
                pltpu.VMEM((n_turns,) + one, kind),
                pltpu.SemaphoreType.DMA((len(smem),)),
                pltpu.SemaphoreType.DMA((n_turns,)),
                pltpu.SemaphoreType.DMA,
                pltpu.SemaphoreType.DMA((n_held, 3)),
                pltpu.SemaphoreType.DMA((n_slots, 2)),
                pltpu.SemaphoreType.DMA((n_turns,)),
                pltpu.SemaphoreType.DMA((3,)),
                pltpu.SemaphoreType.DMA((slots, 3)),
            ],
            compiler_params=pltpu.CompilerParams(vmem_limit_bytes=GROUP_BYTES if stage is None else FIRST_BYTES),
            cost_estimate=cost,
            name="group_grads" if turns[0] else "own_grads",
        )(*operands)

    *written, for_2, next_both, next_kv = grads_of((2,), in_order, FAR, ())
    come = [swap(for_2, 2)]
    *written, for_far, for_1 = grads_of((FAR, 1), (next_both, next_kv), None, written)
    last = [swap(for_far, FAR), swap(for_1, 1)]
    q_out, self_out, summed = grads_of((0,), (), None, written, come, F32)
    prefix_out = (summed + sum(part.astype(F32) for part in last)).astype(BF16)
    return (q_out, self_out, prefix_out)


def far_kernel(z, *refs):
    (resp_prompt, resp_len, rewards, q_hbm, og_hbm, kv_hbm, prompts, q_out, self_out, prefix_outs,
     totals, lens, factors, q, og, kv, prefix, out, own, grads, sem_in, sem_prefix, sem_out) = refs
    me = lax.axis_index("dp")

    for p in range(z.n_dp):
        totals[p] = 0.0

    def copies_in(slot):
        rows = token_rows(z, slot)
        prompt = resp_prompt[me * z.count + slot]
        return (
            *row_copies((q_hbm, og_hbm, kv_hbm), (q, og, kv), rows, rows, sem_in.at[slot]),
            pltpu.make_async_copy(prompts.at[prompt], prefix.at[slot], sem_prefix.at[slot]),
        )

    def copies_out(slot):
        rows = token_rows(z, slot)
        return (
            *result_copies(out, own, q_out, self_out, slot, rows, sem_out),
            pltpu.make_async_copy(grads.at[slot], prefix_outs.at[slot], sem_out.at[slot, 3]),
        )

    def start(slot, _):
        for copy in copies_in(slot):
            copy.start()
        return 0

    lax.fori_loop(0, z.count, start, 0)

    def add(i, _):
        prompt = resp_prompt[i]
        totals[prompt] = totals[prompt] + rewards[i]
        return 0

    lax.fori_loop(0, z.n_dp * z.count, add, 0)

    def find_factor(slot, _):
        place = me * z.count + slot
        lens[slot] = resp_len[slot]
        factors[slot] = reward_factor(z, rewards[place], totals[resp_prompt[place]], resp_len[slot])
        return 0

    lax.fori_loop(0, z.count, find_factor, 0)

    def unit(slot, _):
        for copy in copies_in(slot):
            copy.wait()

        def sink(_, cols, key_grad, value_grad):
            grads[slot, 0, :, cols] = key_grad.astype(BF16)
            grads[slot, 1, :, cols] = value_grad.astype(BF16)

        units = [
            Unit([token_rows(z, slot)], [slot], k, [lens[slot]], [factors[slot]]) for k in range(z.kv_heads)
        ]
        attend(z, units, q, og, kv, prefix.at[slot], out, own, sink, True)
        for copy in copies_out(slot):
            copy.start()
        return 0

    lax.fori_loop(0, z.count, unit, 0)

    def end(slot, _):
        for copy in copies_out(slot):
            copy.wait()
        return 0

    lax.fori_loop(0, z.count, end, 0)


def far_shards(z, prompt_kv, resp_q, resp_kv, out_grad, rewards, resp_prompt, resp_len):
    assert z.slots == 1
    count, n_dp = z.count, z.n_dp
    one = (2, z.prefix_len, z.width)
    smem = pl.BlockSpec(memory_space=pltpu.SMEM)
    q_out, self_out, per_resp = pl.pallas_call(
        functools.partial(far_kernel, z),
        out_shape=[
            jax.ShapeDtypeStruct(resp_q.shape, BF16),
            jax.ShapeDtypeStruct(resp_kv.shape, BF16),
            jax.ShapeDtypeStruct((count,) + one, BF16),
        ],
        in_specs=[smem] * 3 + [ANYWHERE] * 4,
        out_specs=[ANYWHERE] * 3,
        scratch_shapes=[
            pltpu.SMEM((n_dp,), F32),
            pltpu.SMEM((count,), jnp.int32),
            pltpu.SMEM((count,), F32),
            pltpu.VMEM(resp_q.shape, BF16),
            pltpu.VMEM(resp_q.shape, BF16),
            pltpu.VMEM(resp_kv.shape, BF16),
            pltpu.VMEM((count,) + one, BF16),
            pltpu.VMEM((count, z.tokens, z.lanes), BF16),
            pltpu.VMEM((count, 2, z.tokens, z.width), BF16),
            pltpu.VMEM((count,) + one, BF16),
            pltpu.SemaphoreType.DMA((count, 4)),
            pltpu.SemaphoreType.DMA((count,)),
            pltpu.SemaphoreType.DMA((count, 4)),
        ],
        compiler_params=pltpu.CompilerParams(vmem_limit_bytes=VMEM_BYTES),
        name="far_grads",
    )(
        resp_prompt,
        resp_len,
        lax.all_gather(rewards, "dp", axis=0, tiled=True),
        resp_q,
        out_grad,
        resp_kv,
        lax.all_gather(prompt_kv, "dp", axis=0),
    )
    my_prompts = lax.dynamic_slice_in_dim(resp_prompt, lax.axis_index("dp") * count, count)
    route = (jnp.arange(n_dp, dtype=jnp.int32)[:, None] == my_prompts[None, :]).astype(BF16)
    outgoing = jnp.dot(route, per_resp.reshape(count, -1), preferred_element_type=F32).astype(BF16)
    outgoing = outgoing.reshape((n_dp,) + one)
    incoming = lax.all_to_all(outgoing, "dp", split_axis=0, concat_axis=0, tiled=True)
    prefix_out = jnp.sum(incoming, axis=0, dtype=F32).astype(BF16)
    return (q_out, self_out, prefix_out)


def shards(prompt_kv, resp_q, resp_kv, out_grad, rewards, resp_prompt, resp_len):
    n_dp = lax.axis_size("dp")
    count = rewards.shape[0]
    prefix_len, width = prompt_kv.shape[1:]
    slots = (count + n_dp - 1) // n_dp
    z = Sizes(
        n_dp, count, slots, width // HD, resp_q.shape[1] // width, resp_q.shape[0] // count, prefix_len
    )
    part = near_shards if count // slots == n_dp else far_shards
    return part(z, prompt_kv, resp_q, resp_kv, out_grad, rewards, resp_prompt, resp_len)


def solution(mesh):
    in_specs = (
        P(None, ("groups", "dp"), "tensor"),
        P(("groups", "dp"), "tensor"),
        P(None, ("groups", "dp"), "tensor"),
        P(("groups", "dp"), "tensor"),
        P(("groups", "dp")),
        P("groups"),
        P(("groups", "dp")),
    )
    out_specs = (
        P(("groups", "dp"), "tensor"),
        P(None, ("groups", "dp"), "tensor"),
        P(None, ("groups", "dp"), "tensor"),
    )
    return jax.shard_map(shards, mesh=mesh, in_specs=in_specs, out_specs=out_specs, check_vma=False)
```

```python
import functools
import math
from typing import NamedTuple

import jax
import jax.numpy as jnp
from jax import lax
from jax.experimental import pallas as pl
from jax.experimental.pallas import tpu as pltpu
from jax.sharding import PartitionSpec as P

HD = 128
NEG = -1e30
F32 = jnp.float32
BF16 = jnp.bfloat16
PAIR = 2
FAR = 3
VMEM_BYTES = 63 * 1024 * 1024
GROUP_BYTES = 54528 * 1024
ANYWHERE = pl.BlockSpec(memory_space=pl.ANY)


class Sizes(NamedTuple):
    n_dp: int
    count: int
    slots: int
    kv_heads: int
    group_size: int
    tokens: int
    prefix_len: int

    @property
    def width(self):
        return self.kv_heads * HD

    @property
    def lanes(self):
        return self.kv_heads * self.group_size * HD


def dot(a, b, dims):
    return lax.dot_general(a, b, (dims, ((), ())), preferred_element_type=F32)


NN = ((1,), (0,))
NT = ((1,), (1,))


class Bag:
    pass


class Unit(NamedTuple):
    at: list
    places: list
    k: object
    lens: list
    factors: list


def attend(z, units, q, og, kv, prefix, out, own_out, sink, apart):
    tokens, prefix_len, group_size = z.tokens, z.prefix_len, z.group_size
    scale = 1.0 / math.sqrt(HD)
    log_scale = scale * math.log2(math.e)
    whole = group_size - group_size % 2
    most = max(whole, 2) * tokens
    assert tokens & (tokens - 1) == 0
    token = lax.broadcasted_iota(jnp.int32, (1, most), 1) & (tokens - 1)
    key = lax.broadcasted_iota(jnp.int32, (tokens, most), 0)
    causal = key <= (lax.broadcasted_iota(jnp.int32, (tokens, most), 1) & (tokens - 1))
    left = lax.broadcasted_iota(jnp.int32, (1, 2 * tokens), 1) < tokens

    def columns(index):
        if isinstance(index, int):
            return slice(index * HD, (index + 1) * HD)
        return pl.ds(pl.multiple_of(index * HD, HD), HD)

    def head(k, h):
        return columns(k * group_size + h)

    def rows(ref, c):
        return jnp.concatenate([ref[c.t.at[n], head(c.t.k, h)] for n, h in c.blocks], axis=0)

    def halves(part):
        none = jnp.zeros_like(part)
        return [jnp.where(left, part, none), jnp.where(left, none, part)]

    def over_keys(combine, *parts):
        reduce = jnp.max if combine is jnp.maximum else jnp.sum
        eights = [reduce(part.reshape(-1, 8, part.shape[1]), axis=0) for part in parts]
        return reduce(functools.reduce(combine, eights), axis=0, keepdims=True)

    def own_half(both):
        return jnp.where(left, both[:tokens], both[tokens:])

    def rounded(*parts):
        return jnp.concatenate([part.astype(BF16) for part in parts], axis=0)

    chunks = []
    for unit in units:
        t = Bag()
        t.at, t.places, t.k, t.lens, t.factors = unit
        t.single = len(t.at) == 1
        t.members = range(len(t.at))
        sides = (0, 0) if t.single else (0, 1)
        t.cols = columns(t.k)
        t.key_p, t.value_p = prefix[0, :, t.cols], prefix[1, :, t.cols]
        t.keys = [kv[0, t.at[n], t.cols] for n in sides]
        t.values = [kv[1, t.at[n], t.cols] for n in sides]
        t.key_pair = jnp.concatenate(t.keys, axis=0)
        t.value_pair = jnp.concatenate(t.values, axis=0)
        t.key_t = jnp.concatenate([t.key_p.T, t.key_pair.T], axis=1)
        t.prefix_sums = {n: [] for n in t.members}
        t.self_sums = {n: [] for n in t.members}
        mine = []
        for n in t.members:
            c = Bag()
            c.t, c.side, c.blocks = t, n, [(n, h) for h in range(whole)]
            mine.append(c)
        if group_size % 2:
            c = Bag()
            c.t, c.side, c.blocks = t, None, [(n, group_size - 1) for n in sides]
            mine.append(c)
        t.left_over = len(mine)
        chunks += mine

    def products(c):
        t = c.t
        c.q_rows, c.g_rows = rows(q, c), rows(og, c)
        if c.side is None:
            key_s, value_s = t.key_pair, t.value_pair
        else:
            key_s, value_s = t.keys[c.side], t.values[c.side]
        c.scores = dot(jnp.concatenate([t.key_p, key_s], axis=0), c.q_rows, NT)
        c.gw = dot(jnp.concatenate([t.value_p, value_s], axis=0), c.g_rows, NT)

    def weigh(c):
        scores_p, scores_s = c.scores[:prefix_len], c.scores[prefix_len:]
        c.gw_p, c.gw_s = c.gw[:prefix_len], c.gw[prefix_len:]
        if c.side is None:
            scores_s, c.gw_s = own_half(scores_s), own_half(c.gw_s)
        scores_s = jnp.where(causal[:, : scores_s.shape[1]], scores_s, NEG)
        top = over_keys(jnp.maximum, scores_p, scores_s)
        c.e_p = jnp.exp2((scores_p - top) * log_scale)
        c.e_s = jnp.exp2((scores_s - top) * log_scale)
        total = over_keys(jnp.add, c.e_p, c.e_s)
        weighted = over_keys(jnp.add, c.e_p * c.gw_p, c.e_s * c.gw_s)
        if c.side is None:
            length = jnp.where(left, c.t.lens[0], 0 if c.t.single else c.t.lens[1])
            gain = jnp.where(left, c.t.factors[0], c.t.factors[-1])
        else:
            length, gain = c.t.lens[c.side], c.t.factors[c.side]
        inverse = 1.0 / total
        c.delta = weighted * inverse
        c.gain = inverse * jnp.where(token[:, : total.shape[1]] < length, gain, 0.0)

    def gradients(c):
        w_p, w_s = c.e_p * c.gain, c.e_s * c.gain
        d_p, d_s = w_p * (c.gw_p - c.delta), w_s * (c.gw_s - c.delta)
        if c.side is None:
            d_s, w_s = halves(d_s), halves(w_s)
            c.d_wide = rounded(d_p, *d_s)
            c.d_all = rounded(*halves(d_p), *d_s) if apart else c.d_wide
            c.w_all = rounded(*(halves(w_p) if apart else [w_p]), *w_s)
        else:
            empty = jnp.zeros_like(d_s)
            c.d_wide = rounded(*([d_p, empty, d_s] if c.side else [d_p, d_s, empty]))
            c.d_all = rounded(d_p, d_s)
            c.w_all = rounded(w_p, w_s)

    def outgoing(c):
        t = c.t
        q_grad = (dot(t.key_t, c.d_wide, NN) * scale).astype(BF16).T
        kg = dot(c.d_all, c.q_rows, NN)
        vg = dot(c.w_all, c.g_rows, NN)
        targets = t.members if c.side is None else [c.side]
        for place, (n, h) in enumerate(c.blocks):
            if c.side is not None or place < len(targets):
                out[t.places[n], :, head(t.k, h)] = q_grad[place * tokens : (place + 1) * tokens]
        many = 2 if c.side is None and apart else 1
        for place, n in enumerate(targets):
            if place < many:
                rows_p = slice(place * prefix_len, (place + 1) * prefix_len)
                t.prefix_sums[n if apart else 0].append((kg[rows_p], vg[rows_p]))
            start = many * prefix_len + place * tokens
            rows_s = slice(start, start + tokens)
            t.self_sums[n].append((kg[rows_s], vg[rows_s]))
        t.left_over -= 1
        if t.left_over == 0:
            for n in t.members:
                keys, values = zip(*t.self_sums[n])
                own_out[t.places[n], 0, :, t.cols] = (sum(keys) * scale).astype(BF16)
                own_out[t.places[n], 1, :, t.cols] = sum(values).astype(BF16)
                if apart or n == 0:
                    keys, values = zip(*t.prefix_sums[n])
                    sink(t.places[n], t.cols, sum(keys) * scale, sum(values))

    stages = (products, weigh, gradients, outgoing)
    for step in range(len(chunks) + len(stages) - 1):
        for late, stage in enumerate(stages):
            if 0 <= step - late < len(chunks):
                stage(chunks[step - late])


def token_rows(z, i):
    return pl.ds(pl.multiple_of(i * z.tokens, z.tokens), z.tokens)


def find_responses(z, me, turns, resp_prompt, order):
    for t, turn in enumerate(turns):
        prompt = me ^ turn
        found = t * z.slots
        for i in range(z.count):
            order[found] = i
            found = found + (resp_prompt[me * z.count + i] == prompt).astype(jnp.int32)


def prompt_total(z, me, prompt, resp_prompt, rewards):
    total = jnp.float32(0.0)
    for s in range(z.n_dp):
        for i in range(z.count):
            total += jnp.where(resp_prompt[(me ^ s) * z.count + i] == prompt, rewards[s][i], 0.0)
    return total


def reward_factor(z, reward, total, length):
    return (reward - total / z.count) * (z.tokens / length.astype(F32))


def row_copies(here, there, at_here, at_there, sems):
    (q0, og0, kv0), (q1, og1, kv1) = here, there
    return (
        pltpu.make_async_copy(q0.at[at_here], q1.at[at_there], sems.at[0]),
        pltpu.make_async_copy(og0.at[at_here], og1.at[at_there], sems.at[1]),
        pltpu.make_async_copy(kv0.at[:, at_here], kv1.at[:, at_there], sems.at[2]),
    )


def result_copies(out, own, q_out, self_out, place, at, sems, back=False):
    pairs = [
        (out.at[place], q_out.at[at]),
        (own.at[place], self_out.at[:, at]),
    ]
    return [
        pltpu.make_async_copy(*(reversed(pair) if back else pair), sems.at[place, n])
        for n, pair in enumerate(pairs)
    ]


def sort_kernel(z, ahead, resp_prompt_hbm, q_hbm, og_hbm, kv_hbm, both_out, kv_out, *scratch):
    resp_prompt, order, q, og, kv, sem_small, sem_in, sem_out = scratch
    me = lax.axis_index("dp")
    small = pltpu.make_async_copy(resp_prompt_hbm, resp_prompt, sem_small)
    small.start()
    small.wait()
    find_responses(z, me, ahead, resp_prompt, order)
    held, in_order = (q, og, kv), (both_out.at[0], both_out.at[1], kv_out)
    slots = range(len(ahead) * z.slots)

    def copies_in(slot):
        return row_copies(
            (q_hbm, og_hbm, kv_hbm), held, token_rows(z, order[slot]), token_rows(z, slot), sem_in.at[slot]
        )

    def copies_out(slot):
        rows = token_rows(z, slot)
        return row_copies(held, in_order, rows, rows, sem_out.at[slot])

    for slot in slots:
        for copy in copies_in(slot):
            copy.start()
    for slot in slots:
        for copy in copies_in(slot):
            copy.wait()
        for copy in copies_out(slot):
            copy.start()
    for slot in slots:
        for copy in copies_out(slot):
            copy.wait()


def group_kernel(z, turns, ahead, n_come, aliased, *refs):
    n_small = 2 + z.n_dp
    small_hbm, given, refs = refs[:n_small], refs[n_small : n_small + 3], refs[n_small + 3 :]
    prompts, refs = refs[: len(turns)], refs[len(turns) :]
    come_hbm, refs = refs[:n_come], refs[n_come:]
    if ahead is not None:
        (both, kv_ordered), refs = refs[:2], refs[2:]
    (q_out, self_out), refs = refs[aliased : aliased + 2], refs[aliased + 2 :]
    grads_out, refs = refs[: len(turns)], refs[len(turns) :]
    resp_prompt, resp_len, *rewards = refs[:n_small]
    (order, lens, factors, q, og, kv, prefix, come, acc, out, own, grads,
     sem_small, sem_prefix, sem_come, sem_in, sem_out, sem_grads, sem_first) = refs[n_small:]
    me = lax.axis_index("dp")
    n_slots = len(turns) * z.slots
    span = z.slots * z.tokens

    small = [
        pltpu.make_async_copy(src, dst, sem_small.at[n])
        for n, (src, dst) in enumerate(zip(small_hbm, (resp_prompt, resp_len, *rewards)))
    ]
    first_rows = ()
    if ahead is not None:
        first_rows = row_copies(
            (both.at[0], both.at[1], kv_ordered), (q, og, kv), pl.ds(ahead * span, span), pl.ds(0, span), sem_first
        )
    prefix_copies = [
        pltpu.make_async_copy(prompts[t], prefix.at[t], sem_prefix.at[t]) for t in range(len(turns))
    ]
    late = [pltpu.make_async_copy(src, come, sem_come) for src in come_hbm]
    for copy in [*small, *first_rows, *prefix_copies, *late]:
        copy.start()
    small[0].wait()
    find_responses(z, me, turns, resp_prompt, order)

    def copies_in(slot):
        return row_copies(
            given, (q, og, kv), token_rows(z, order[slot]), token_rows(z, slot), sem_in.at[slot]
        )

    def copies_out(slot):
        return result_copies(out, own, q_out, self_out, slot, token_rows(z, order[slot]), sem_out)

    for slot in range(0 if ahead is None else z.slots, n_slots):
        for copy in copies_in(slot):
            copy.start()
    for copy in small[1:] + late:
        copy.wait()
    for t, turn in enumerate(turns):
        total = prompt_total(z, me, me ^ turn, resp_prompt, rewards)
        for slot in range(t * z.slots, (t + 1) * z.slots):
            i = order[slot]
            lens[slot] = resp_len[i]
            factors[slot] = reward_factor(z, rewards[0][i], total, resp_len[i])
    if n_come:
        acc[0] = come[...].astype(F32)
    else:
        acc[...] = jnp.zeros(acc.shape, F32)
    for copy in prefix_copies:
        copy.wait()

    def step(t, _):
        slots = [t * z.slots + n for n in range(z.slots)]

        def wait_for_slots():
            for slot in slots:
                for copy in copies_in(slot):
                    copy.wait()

        if ahead is None:
            wait_for_slots()
        else:

            @pl.when(t == 0)
            def _():
                for copy in first_rows:
                    copy.wait()

            if len(turns) > 1:
                pl.when(t > 0)(wait_for_slots)

        def sink(_, cols, key_grad, value_grad):
            acc[t, 0, :, cols] += key_grad
            acc[t, 1, :, cols] += value_grad

        units = []
        for pair in range(0, z.slots, PAIR):
            places = slots[pair : pair + PAIR]
            at = [token_rows(z, n) for n in places]
            for k in range(z.kv_heads):
                units.append(Unit(at, places, k, [lens[n] for n in places], [factors[n] for n in places]))
        attend(z, units, q, og, kv, prefix.at[t], out, own, sink, False)
        for slot in slots:
            for copy in copies_out(slot):
                copy.start()
        return 0

    lax.fori_loop(0, len(turns), step, 0)
    grads[...] = acc[...].astype(grads.dtype)
    last = [pltpu.make_async_copy(grads.at[t], grads_out[t], sem_grads.at[t]) for t in range(len(turns))]
    for copy in last:
        copy.start()
    for slot in range(n_slots):
        for copy in copies_out(slot):
            copy.wait()
    for copy in last:
        copy.wait()


def near_shards(z, prompt_kv, resp_q, resp_kv, out_grad, rewards, resp_prompt, resp_len):
    n_dp = z.n_dp
    assert z.slots % PAIR == 0
    shape = jax.ShapeDtypeStruct
    one = (2, z.prefix_len, z.width)
    params = pltpu.CompilerParams(vmem_limit_bytes=VMEM_BYTES)
    cost = pl.CostEstimate(flops=0, bytes_accessed=0, transcendentals=0)
    assert n_dp == FAR + 1

    def swap(x, s):
        return lax.ppermute(x, "dp", [(i, i ^ s) for i in range(n_dp)])

    prompts = {0: prompt_kv, 2: swap(prompt_kv, 2), 1: swap(prompt_kv, 1)}
    others = [swap(rewards, s) for s in range(1, n_dp)]
    small = (resp_prompt, resp_len)
    smem = [pltpu.SMEM(x.shape, x.dtype) for x in (*small, rewards, *others)]
    slots = z.slots
    given = (resp_q, out_grad, resp_kv)
    n_ahead = 2 * slots * z.tokens
    in_order = pl.pallas_call(
        functools.partial(sort_kernel, z, (2, FAR)),
        out_shape=[shape((2, n_ahead, z.lanes), BF16), shape((2, n_ahead, z.width), BF16)],
        in_specs=[ANYWHERE] * 4,
        out_specs=[ANYWHERE] * 2,
        scratch_shapes=[
            smem[0],
            pltpu.SMEM((2 * slots + 1,), jnp.int32),
            pltpu.VMEM((n_ahead, z.lanes), BF16),
            pltpu.VMEM((n_ahead, z.lanes), BF16),
            pltpu.VMEM((2, n_ahead, z.width), BF16),
            pltpu.SemaphoreType.DMA,
            pltpu.SemaphoreType.DMA((2 * slots, 3)),
            pltpu.SemaphoreType.DMA((2 * slots, 3)),
        ],
        compiler_params=params,
        cost_estimate=cost,
        name="sort_rows",
    )(resp_prompt, *given)
    onward, *barred = lax.optimization_barrier((prompts[2], *others, *in_order))
    others, in_order = barred[: n_dp - 1], barred[n_dp - 1 :]
    prompts[FAR] = swap(onward, 1)

    def grads_of(turns, ahead, written, come=(), kind=BF16):
        n_slots, n_turns = len(turns) * slots, len(turns)
        rows = () if ahead is None else in_order
        used_prompts = [prompts[turn] for turn in turns]
        operands = [*small, rewards, *others, *given, *used_prompts, *come, *rows, *written]
        return pl.pallas_call(
            functools.partial(group_kernel, z, turns, ahead, len(come), len(written)),
            out_shape=[shape(resp_q.shape, BF16), shape(resp_kv.shape, BF16)] + [shape(one, kind)] * n_turns,
            in_specs=[ANYWHERE] * len(operands),
            out_specs=[ANYWHERE] * (2 + n_turns),
            input_output_aliases={len(operands) - 2: 0, len(operands) - 1: 1} if written else {},
            scratch_shapes=[
                *smem,
                pltpu.SMEM((n_slots + 1,), jnp.int32),
                pltpu.SMEM((n_slots,), jnp.int32),
                pltpu.SMEM((n_slots,), F32),
                pltpu.VMEM((n_slots * z.tokens, z.lanes), BF16),
                pltpu.VMEM((n_slots * z.tokens, z.lanes), BF16),
                pltpu.VMEM((2, n_slots * z.tokens, z.width), BF16),
                pltpu.VMEM((n_turns,) + one, BF16),
                pltpu.VMEM(one, BF16),
                pltpu.VMEM((n_turns,) + one, F32),
                pltpu.VMEM((n_slots, z.tokens, z.lanes), BF16),
                pltpu.VMEM((n_slots, 2, z.tokens, z.width), BF16),
                pltpu.VMEM((n_turns,) + one, kind),
                pltpu.SemaphoreType.DMA((len(smem),)),
                pltpu.SemaphoreType.DMA((n_turns,)),
                pltpu.SemaphoreType.DMA,
                pltpu.SemaphoreType.DMA((n_slots, 3)),
                pltpu.SemaphoreType.DMA((n_slots, 2)),
                pltpu.SemaphoreType.DMA((n_turns,)),
                pltpu.SemaphoreType.DMA((3,)),
            ],
            compiler_params=pltpu.CompilerParams(vmem_limit_bytes=GROUP_BYTES),
            cost_estimate=cost,
            name="group_grads" if turns[0] else "own_grads",
        )(*operands)

    *written, for_2 = grads_of((2,), 0, ())
    come = [swap(for_2, 2)]
    *written, for_far, for_1 = grads_of((FAR, 1), 1, written)
    last = [swap(for_1, 1), swap(for_far, FAR)]
    q_out, self_out, summed = grads_of((0,), None, written, come, F32)
    prefix_out = (summed + sum(part.astype(F32) for part in last)).astype(BF16)
    return (q_out, self_out, prefix_out)


def far_kernel(z, *refs):
    (resp_prompt, resp_len, rewards, q_hbm, og_hbm, kv_hbm, prompts, q_out, self_out, prefix_outs,
     totals, lens, factors, q, og, kv, prefix, out, own, grads, sem_in, sem_prefix, sem_out) = refs
    me = lax.axis_index("dp")

    for p in range(z.n_dp):
        totals[p] = 0.0

    def copies_in(slot):
        rows = token_rows(z, slot)
        prompt = resp_prompt[me * z.count + slot]
        return (
            *row_copies((q_hbm, og_hbm, kv_hbm), (q, og, kv), rows, rows, sem_in.at[slot]),
            pltpu.make_async_copy(prompts.at[prompt], prefix.at[slot], sem_prefix.at[slot]),
        )

    def copies_out(slot):
        rows = token_rows(z, slot)
        return (
            *result_copies(out, own, q_out, self_out, slot, rows, sem_out),
            pltpu.make_async_copy(grads.at[slot], prefix_outs.at[slot], sem_out.at[slot, 3]),
        )

    def start(slot, _):
        for copy in copies_in(slot):
            copy.start()
        return 0

    lax.fori_loop(0, z.count, start, 0)

    def add(i, _):
        prompt = resp_prompt[i]
        totals[prompt] = totals[prompt] + rewards[i]
        return 0

    lax.fori_loop(0, z.n_dp * z.count, add, 0)

    def find_factor(slot, _):
        place = me * z.count + slot
        lens[slot] = resp_len[slot]
        factors[slot] = reward_factor(z, rewards[place], totals[resp_prompt[place]], resp_len[slot])
        return 0

    lax.fori_loop(0, z.count, find_factor, 0)

    def unit(slot, _):
        for copy in copies_in(slot):
            copy.wait()

        def sink(_, cols, key_grad, value_grad):
            grads[slot, 0, :, cols] = key_grad.astype(BF16)
            grads[slot, 1, :, cols] = value_grad.astype(BF16)

        units = [
            Unit([token_rows(z, slot)], [slot], k, [lens[slot]], [factors[slot]]) for k in range(z.kv_heads)
        ]
        attend(z, units, q, og, kv, prefix.at[slot], out, own, sink, True)
        for copy in copies_out(slot):
            copy.start()
        return 0

    lax.fori_loop(0, z.count, unit, 0)

    def end(slot, _):
        for copy in copies_out(slot):
            copy.wait()
        return 0

    lax.fori_loop(0, z.count, end, 0)


def far_shards(z, prompt_kv, resp_q, resp_kv, out_grad, rewards, resp_prompt, resp_len):
    assert z.slots == 1
    count, n_dp = z.count, z.n_dp
    one = (2, z.prefix_len, z.width)
    smem = pl.BlockSpec(memory_space=pltpu.SMEM)
    q_out, self_out, per_resp = pl.pallas_call(
        functools.partial(far_kernel, z),
        out_shape=[
            jax.ShapeDtypeStruct(resp_q.shape, BF16),
            jax.ShapeDtypeStruct(resp_kv.shape, BF16),
            jax.ShapeDtypeStruct((count,) + one, BF16),
        ],
        in_specs=[smem] * 3 + [ANYWHERE] * 4,
        out_specs=[ANYWHERE] * 3,
        scratch_shapes=[
            pltpu.SMEM((n_dp,), F32),
            pltpu.SMEM((count,), jnp.int32),
            pltpu.SMEM((count,), F32),
            pltpu.VMEM(resp_q.shape, BF16),
            pltpu.VMEM(resp_q.shape, BF16),
            pltpu.VMEM(resp_kv.shape, BF16),
            pltpu.VMEM((count,) + one, BF16),
            pltpu.VMEM((count, z.tokens, z.lanes), BF16),
            pltpu.VMEM((count, 2, z.tokens, z.width), BF16),
            pltpu.VMEM((count,) + one, BF16),
            pltpu.SemaphoreType.DMA((count, 4)),
            pltpu.SemaphoreType.DMA((count,)),
            pltpu.SemaphoreType.DMA((count, 4)),
        ],
        compiler_params=pltpu.CompilerParams(vmem_limit_bytes=VMEM_BYTES),
        name="far_grads",
    )(
        resp_prompt,
        resp_len,
        lax.all_gather(rewards, "dp", axis=0, tiled=True),
        resp_q,
        out_grad,
        resp_kv,
        lax.all_gather(prompt_kv, "dp", axis=0),
    )
    my_prompts = lax.dynamic_slice_in_dim(resp_prompt, lax.axis_index("dp") * count, count)
    route = (jnp.arange(n_dp, dtype=jnp.int32)[:, None] == my_prompts[None, :]).astype(BF16)
    outgoing = jnp.dot(route, per_resp.reshape(count, -1), preferred_element_type=F32).astype(BF16)
    outgoing = outgoing.reshape((n_dp,) + one)
    incoming = lax.all_to_all(outgoing, "dp", split_axis=0, concat_axis=0, tiled=True)
    prefix_out = jnp.sum(incoming, axis=0, dtype=F32).astype(BF16)
    return (q_out, self_out, prefix_out)


def shards(prompt_kv, resp_q, resp_kv, out_grad, rewards, resp_prompt, resp_len):
    n_dp = lax.axis_size("dp")
    count = rewards.shape[0]
    prefix_len, width = prompt_kv.shape[1:]
    slots = (count + n_dp - 1) // n_dp
    z = Sizes(
        n_dp, count, slots, width // HD, resp_q.shape[1] // width, resp_q.shape[0] // count, prefix_len
    )
    part = near_shards if count // slots == n_dp else far_shards
    return part(z, prompt_kv, resp_q, resp_kv, out_grad, rewards, resp_prompt, resp_len)


def solution(mesh):
    in_specs = (
        P(None, ("groups", "dp"), "tensor"),
        P(("groups", "dp"), "tensor"),
        P(None, ("groups", "dp"), "tensor"),
        P(("groups", "dp"), "tensor"),
        P(("groups", "dp")),
        P("groups"),
        P(("groups", "dp")),
    )
    out_specs = (
        P(("groups", "dp"), "tensor"),
        P(None, ("groups", "dp"), "tensor"),
        P(None, ("groups", "dp"), "tensor"),
    )
    return jax.shard_map(shards, mesh=mesh, in_specs=in_specs, out_specs=out_specs, check_vma=False)
```

```python
import functools
import math
from typing import NamedTuple

import jax
import jax.numpy as jnp
from jax import lax
from jax.experimental import pallas as pl
from jax.experimental.pallas import tpu as pltpu
from jax.sharding import PartitionSpec as P

HD = 128
NEG = -1e30
F32 = jnp.float32
BF16 = jnp.bfloat16
PAIR = 2
FAR = 3
VMEM_BYTES = 63 * 1024 * 1024
GROUP_BYTES = 54528 * 1024
ANYWHERE = pl.BlockSpec(memory_space=pl.ANY)


class Sizes(NamedTuple):
    n_dp: int
    count: int
    slots: int
    kv_heads: int
    group_size: int
    tokens: int
    prefix_len: int

    @property
    def width(self):
        return self.kv_heads * HD

    @property
    def lanes(self):
        return self.kv_heads * self.group_size * HD


def dot(a, b, dims):
    return lax.dot_general(a, b, (dims, ((), ())), preferred_element_type=F32)


NN = ((1,), (0,))
NT = ((1,), (1,))


class Bag:
    pass


class Unit(NamedTuple):
    at: list
    places: list
    k: object
    lens: list
    factors: list


def attend(z, units, q, og, kv, prefix, out, own_out, sink, apart):
    tokens, prefix_len, group_size = z.tokens, z.prefix_len, z.group_size
    scale = 1.0 / math.sqrt(HD)
    log_scale = scale * math.log2(math.e)
    whole = group_size - group_size % 2
    most = max(whole, 2) * tokens
    assert tokens & (tokens - 1) == 0
    token = lax.broadcasted_iota(jnp.int32, (1, most), 1) & (tokens - 1)
    key = lax.broadcasted_iota(jnp.int32, (tokens, most), 0)
    causal = key <= (lax.broadcasted_iota(jnp.int32, (tokens, most), 1) & (tokens - 1))
    left = lax.broadcasted_iota(jnp.int32, (1, 2 * tokens), 1) < tokens

    def columns(index):
        if isinstance(index, int):
            return slice(index * HD, (index + 1) * HD)
        return pl.ds(pl.multiple_of(index * HD, HD), HD)

    def head(k, h):
        return columns(k * group_size + h)

    def rows(ref, c):
        return jnp.concatenate([ref[c.t.at[n], head(c.t.k, h)] for n, h in c.blocks], axis=0)

    def halves(part):
        none = jnp.zeros_like(part)
        return [jnp.where(left, part, none), jnp.where(left, none, part)]

    def over_keys(combine, *parts):
        reduce = jnp.max if combine is jnp.maximum else jnp.sum
        eights = [reduce(part.reshape(-1, 8, part.shape[1]), axis=0) for part in parts]
        return reduce(functools.reduce(combine, eights), axis=0, keepdims=True)

    def own_half(both):
        return jnp.where(left, both[:tokens], both[tokens:])

    def rounded(*parts):
        return jnp.concatenate([part.astype(BF16) for part in parts], axis=0)

    chunks = []
    for unit in units:
        t = Bag()
        t.at, t.places, t.k, t.lens, t.factors = unit
        t.single = len(t.at) == 1
        t.members = range(len(t.at))
        sides = (0, 0) if t.single else (0, 1)
        t.cols = columns(t.k)
        t.key_p, t.value_p = prefix[0, :, t.cols], prefix[1, :, t.cols]
        t.keys = [kv[0, t.at[n], t.cols] for n in sides]
        t.values = [kv[1, t.at[n], t.cols] for n in sides]
        t.key_pair = jnp.concatenate(t.keys, axis=0)
        t.value_pair = jnp.concatenate(t.values, axis=0)
        t.key_t = jnp.concatenate([t.key_p.T, t.key_pair.T], axis=1)
        t.prefix_sums = {n: [] for n in t.members}
        t.self_sums = {n: [] for n in t.members}
        mine = []
        for n in t.members:
            c = Bag()
            c.t, c.side, c.blocks = t, n, [(n, h) for h in range(whole)]
            mine.append(c)
        if group_size % 2:
            c = Bag()
            c.t, c.side, c.blocks = t, None, [(n, group_size - 1) for n in sides]
            mine.append(c)
        t.left_over = len(mine)
        chunks += mine

    def products(c):
        t = c.t
        c.q_rows, c.g_rows = rows(q, c), rows(og, c)
        if c.side is None:
            key_s, value_s = t.key_pair, t.value_pair
        else:
            key_s, value_s = t.keys[c.side], t.values[c.side]
        c.scores = dot(jnp.concatenate([t.key_p, key_s], axis=0), c.q_rows, NT)
        c.gw = dot(jnp.concatenate([t.value_p, value_s], axis=0), c.g_rows, NT)

    def weigh(c):
        scores_p, scores_s = c.scores[:prefix_len], c.scores[prefix_len:]
        c.gw_p, c.gw_s = c.gw[:prefix_len], c.gw[prefix_len:]
        if c.side is None:
            scores_s, c.gw_s = own_half(scores_s), own_half(c.gw_s)
        scores_s = jnp.where(causal[:, : scores_s.shape[1]], scores_s, NEG)
        top = over_keys(jnp.maximum, scores_p, scores_s)
        c.e_p = jnp.exp2((scores_p - top) * log_scale)
        c.e_s = jnp.exp2((scores_s - top) * log_scale)
        total = over_keys(jnp.add, c.e_p, c.e_s)
        weighted = over_keys(jnp.add, c.e_p * c.gw_p, c.e_s * c.gw_s)
        if c.side is None:
            length = jnp.where(left, c.t.lens[0], 0 if c.t.single else c.t.lens[1])
            gain = jnp.where(left, c.t.factors[0], c.t.factors[-1])
        else:
            length, gain = c.t.lens[c.side], c.t.factors[c.side]
        inverse = 1.0 / total
        c.delta = weighted * inverse
        c.gain = inverse * jnp.where(token[:, : total.shape[1]] < length, gain, 0.0)

    def gradients(c):
        w_p, w_s = c.e_p * c.gain, c.e_s * c.gain
        d_p, d_s = w_p * (c.gw_p - c.delta), w_s * (c.gw_s - c.delta)
        if c.side is None:
            d_s, w_s = halves(d_s), halves(w_s)
            c.d_wide = rounded(d_p, *d_s)
            c.d_all = rounded(*halves(d_p), *d_s) if apart else c.d_wide
            c.w_all = rounded(*(halves(w_p) if apart else [w_p]), *w_s)
        else:
            empty = jnp.zeros_like(d_s)
            c.d_wide = rounded(*([d_p, empty, d_s] if c.side else [d_p, d_s, empty]))
            c.d_all = rounded(d_p, d_s)
            c.w_all = rounded(w_p, w_s)

    def outgoing(c):
        t = c.t
        q_grad = (dot(t.key_t, c.d_wide, NN) * scale).astype(BF16).T
        kg = dot(c.d_all, c.q_rows, NN)
        vg = dot(c.w_all, c.g_rows, NN)
        targets = t.members if c.side is None else [c.side]
        for place, (n, h) in enumerate(c.blocks):
            if c.side is not None or place < len(targets):
                out[t.places[n], :, head(t.k, h)] = q_grad[place * tokens : (place + 1) * tokens]
        many = 2 if c.side is None and apart else 1
        for place, n in enumerate(targets):
            if place < many:
                rows_p = slice(place * prefix_len, (place + 1) * prefix_len)
                t.prefix_sums[n if apart else 0].append((kg[rows_p], vg[rows_p]))
            start = many * prefix_len + place * tokens
            rows_s = slice(start, start + tokens)
            t.self_sums[n].append((kg[rows_s], vg[rows_s]))
        t.left_over -= 1
        if t.left_over == 0:
            for n in t.members:
                keys, values = zip(*t.self_sums[n])
                own_out[t.places[n], 0, :, t.cols] = (sum(keys) * scale).astype(BF16)
                own_out[t.places[n], 1, :, t.cols] = sum(values).astype(BF16)
                if apart or n == 0:
                    keys, values = zip(*t.prefix_sums[n])
                    sink(t.places[n], t.cols, sum(keys) * scale, sum(values))

    stages = (products, weigh, gradients, outgoing)
    for step in range(len(chunks) + len(stages) - 1):
        for late, stage in enumerate(stages):
            if 0 <= step - late < len(chunks):
                stage(chunks[step - late])


def token_rows(z, i):
    return pl.ds(pl.multiple_of(i * z.tokens, z.tokens), z.tokens)


def find_responses(z, me, turns, resp_prompt, order):
    for t, turn in enumerate(turns):
        prompt = me ^ turn
        found = t * z.slots
        for i in range(z.count):
            order[found] = i
            found = found + (resp_prompt[me * z.count + i] == prompt).astype(jnp.int32)


def prompt_total(z, me, prompt, resp_prompt, rewards):
    total = jnp.float32(0.0)
    for s in range(z.n_dp):
        for i in range(z.count):
            total += jnp.where(resp_prompt[(me ^ s) * z.count + i] == prompt, rewards[s][i], 0.0)
    return total


def reward_factor(z, reward, total, length):
    return (reward - total / z.count) * (z.tokens / length.astype(F32))


def row_copies(here, there, at_here, at_there, sems):
    (q0, og0, kv0), (q1, og1, kv1) = here, there
    return (
        pltpu.make_async_copy(q0.at[at_here], q1.at[at_there], sems.at[0]),
        pltpu.make_async_copy(og0.at[at_here], og1.at[at_there], sems.at[1]),
        pltpu.make_async_copy(kv0.at[:, at_here], kv1.at[:, at_there], sems.at[2]),
    )


def result_copies(out, own, q_out, self_out, place, at, sems, back=False):
    pairs = [
        (out.at[place], q_out.at[at]),
        (own.at[place], self_out.at[:, at]),
    ]
    return [
        pltpu.make_async_copy(*(reversed(pair) if back else pair), sems.at[place, n])
        for n, pair in enumerate(pairs)
    ]


def sort_kernel(z, ahead, resp_prompt_hbm, q_hbm, og_hbm, kv_hbm, both_out, kv_out, *scratch):
    resp_prompt, order, q, og, kv, sem_small, sem_in, sem_out = scratch
    me = lax.axis_index("dp")
    small = pltpu.make_async_copy(resp_prompt_hbm, resp_prompt, sem_small)
    small.start()
    small.wait()
    find_responses(z, me, ahead, resp_prompt, order)
    held, in_order = (q, og, kv), (both_out.at[0], both_out.at[1], kv_out)
    slots = range(len(ahead) * z.slots)

    def copies_in(slot):
        return row_copies(
            (q_hbm, og_hbm, kv_hbm), held, token_rows(z, order[slot]), token_rows(z, slot), sem_in.at[slot]
        )

    def copies_out(slot):
        rows = token_rows(z, slot)
        return row_copies(held, in_order, rows, rows, sem_out.at[slot])

    for slot in slots:
        for copy in copies_in(slot):
            copy.start()
    for slot in slots:
        for copy in copies_in(slot):
            copy.wait()
        for copy in copies_out(slot):
            copy.start()
    for slot in slots:
        for copy in copies_out(slot):
            copy.wait()


def group_kernel(z, turns, ahead, n_come, aliased, *refs):
    n_small = 2 + z.n_dp
    small_hbm, given, refs = refs[:n_small], refs[n_small : n_small + 3], refs[n_small + 3 :]
    prompts, refs = refs[: len(turns)], refs[len(turns) :]
    come_hbm, refs = refs[:n_come], refs[n_come:]
    if ahead is not None:
        (both, kv_ordered), refs = refs[:2], refs[2:]
    (q_out, self_out), refs = refs[aliased : aliased + 2], refs[aliased + 2 :]
    grads_out, refs = refs[: len(turns)], refs[len(turns) :]
    resp_prompt, resp_len, *rewards = refs[:n_small]
    (order, lens, factors, q, og, kv, prefix, come, acc, out, own, grads,
     sem_small, sem_prefix, sem_come, sem_in, sem_out, sem_grads, sem_first) = refs[n_small:]
    me = lax.axis_index("dp")
    n_slots = len(turns) * z.slots
    span = z.slots * z.tokens

    small = [
        pltpu.make_async_copy(src, dst, sem_small.at[n])
        for n, (src, dst) in enumerate(zip(small_hbm, (resp_prompt, resp_len, *rewards)))
    ]
    first_rows = ()
    if ahead is not None:
        first_rows = row_copies(
            (both.at[0], both.at[1], kv_ordered), (q, og, kv), pl.ds(ahead * span, span), pl.ds(0, span), sem_first
        )
    prefix_copies = [
        pltpu.make_async_copy(prompts[t], prefix.at[t], sem_prefix.at[t]) for t in range(len(turns))
    ]
    late = [pltpu.make_async_copy(src, come, sem_come) for src in come_hbm]
    for copy in [*small, *first_rows, *prefix_copies, *late]:
        copy.start()
    small[0].wait()
    find_responses(z, me, turns, resp_prompt, order)

    def copies_in(slot):
        return row_copies(
            given, (q, og, kv), token_rows(z, order[slot]), token_rows(z, slot), sem_in.at[slot]
        )

    def copies_out(slot):
        return result_copies(out, own, q_out, self_out, slot, token_rows(z, order[slot]), sem_out)

    for slot in range(0 if ahead is None else z.slots, n_slots):
        for copy in copies_in(slot):
            copy.start()
    for copy in small[1:] + late:
        copy.wait()
    for t, turn in enumerate(turns):
        total = prompt_total(z, me, me ^ turn, resp_prompt, rewards)
        for slot in range(t * z.slots, (t + 1) * z.slots):
            i = order[slot]
            lens[slot] = resp_len[i]
            factors[slot] = reward_factor(z, rewards[0][i], total, resp_len[i])
    if n_come:
        acc[0] = come[...].astype(F32)
    else:
        acc[...] = jnp.zeros(acc.shape, F32)
    for copy in prefix_copies:
        copy.wait()

    def step(t, _):
        slots = [t * z.slots + n for n in range(z.slots)]

        def wait_for_slots():
            for slot in slots:
                for copy in copies_in(slot):
                    copy.wait()

        if ahead is None:
            wait_for_slots()
        else:

            @pl.when(t == 0)
            def _():
                for copy in first_rows:
                    copy.wait()

            if len(turns) > 1:
                pl.when(t > 0)(wait_for_slots)

        def sink(_, cols, key_grad, value_grad):
            acc[t, 0, :, cols] += key_grad
            acc[t, 1, :, cols] += value_grad

        units = []
        for pair in range(0, z.slots, PAIR):
            places = slots[pair : pair + PAIR]
            at = [token_rows(z, n) for n in places]
            for k in range(z.kv_heads):
                units.append(Unit(at, places, k, [lens[n] for n in places], [factors[n] for n in places]))
        attend(z, units, q, og, kv, prefix.at[t], out, own, sink, False)
        for slot in slots:
            for copy in copies_out(slot):
                copy.start()
        return 0

    lax.fori_loop(0, len(turns), step, 0)
    grads[...] = acc[...].astype(grads.dtype)
    last = [pltpu.make_async_copy(grads.at[t], grads_out[t], sem_grads.at[t]) for t in range(len(turns))]
    for copy in last:
        copy.start()
    for slot in range(n_slots):
        for copy in copies_out(slot):
            copy.wait()
    for copy in last:
        copy.wait()


def near_shards(z, prompt_kv, resp_q, resp_kv, out_grad, rewards, resp_prompt, resp_len):
    n_dp = z.n_dp
    assert z.slots % PAIR == 0
    shape = jax.ShapeDtypeStruct
    one = (2, z.prefix_len, z.width)
    params = pltpu.CompilerParams(vmem_limit_bytes=VMEM_BYTES)
    cost = pl.CostEstimate(flops=0, bytes_accessed=0, transcendentals=0)
    assert n_dp == FAR + 1

    def swap(x, s):
        return lax.ppermute(x, "dp", [(i, i ^ s) for i in range(n_dp)])

    prompts = {0: prompt_kv, 2: swap(prompt_kv, 2), 1: swap(prompt_kv, 1)}
    others = [swap(rewards, s) for s in range(1, n_dp)]
    small = (resp_prompt, resp_len)
    smem = [pltpu.SMEM(x.shape, x.dtype) for x in (*small, rewards, *others)]
    slots = z.slots
    given = (resp_q, out_grad, resp_kv)
    n_ahead = 2 * slots * z.tokens
    in_order = pl.pallas_call(
        functools.partial(sort_kernel, z, (2, FAR)),
        out_shape=[shape((2, n_ahead, z.lanes), BF16), shape((2, n_ahead, z.width), BF16)],
        in_specs=[ANYWHERE] * 4,
        out_specs=[ANYWHERE] * 2,
        scratch_shapes=[
            smem[0],
            pltpu.SMEM((2 * slots + 1,), jnp.int32),
            pltpu.VMEM((n_ahead, z.lanes), BF16),
            pltpu.VMEM((n_ahead, z.lanes), BF16),
            pltpu.VMEM((2, n_ahead, z.width), BF16),
            pltpu.SemaphoreType.DMA,
            pltpu.SemaphoreType.DMA((2 * slots, 3)),
            pltpu.SemaphoreType.DMA((2 * slots, 3)),
        ],
        compiler_params=params,
        cost_estimate=cost,
        name="sort_rows",
    )(resp_prompt, *given)
    onward, *barred = lax.optimization_barrier((prompts[2], *others[::-1], *in_order))
    others, in_order = barred[: n_dp - 1][::-1], barred[n_dp - 1 :]
    prompts[FAR] = swap(onward, 1)

    def grads_of(turns, ahead, written, come=(), kind=BF16):
        n_slots, n_turns = len(turns) * slots, len(turns)
        rows = () if ahead is None else in_order
        used_prompts = [prompts[turn] for turn in turns]
        operands = [*small, rewards, *others, *given, *used_prompts, *come, *rows, *written]
        return pl.pallas_call(
            functools.partial(group_kernel, z, turns, ahead, len(come), len(written)),
            out_shape=[shape(resp_q.shape, BF16), shape(resp_kv.shape, BF16)] + [shape(one, kind)] * n_turns,
            in_specs=[ANYWHERE] * len(operands),
            out_specs=[ANYWHERE] * (2 + n_turns),
            input_output_aliases={len(operands) - 2: 0, len(operands) - 1: 1} if written else {},
            scratch_shapes=[
                *smem,
                pltpu.SMEM((n_slots + 1,), jnp.int32),
                pltpu.SMEM((n_slots,), jnp.int32),
                pltpu.SMEM((n_slots,), F32),
                pltpu.VMEM((n_slots * z.tokens, z.lanes), BF16),
                pltpu.VMEM((n_slots * z.tokens, z.lanes), BF16),
                pltpu.VMEM((2, n_slots * z.tokens, z.width), BF16),
                pltpu.VMEM((n_turns,) + one, BF16),
                pltpu.VMEM(one, BF16),
                pltpu.VMEM((n_turns,) + one, F32),
                pltpu.VMEM((n_slots, z.tokens, z.lanes), BF16),
                pltpu.VMEM((n_slots, 2, z.tokens, z.width), BF16),
                pltpu.VMEM((n_turns,) + one, kind),
                pltpu.SemaphoreType.DMA((len(smem),)),
                pltpu.SemaphoreType.DMA((n_turns,)),
                pltpu.SemaphoreType.DMA,
                pltpu.SemaphoreType.DMA((n_slots, 3)),
                pltpu.SemaphoreType.DMA((n_slots, 2)),
                pltpu.SemaphoreType.DMA((n_turns,)),
                pltpu.SemaphoreType.DMA((3,)),
            ],
            compiler_params=pltpu.CompilerParams(vmem_limit_bytes=GROUP_BYTES),
            cost_estimate=cost,
            name="group_grads" if turns[0] else "own_grads",
        )(*operands)

    *written, for_2 = grads_of((2,), 0, ())
    come = [swap(for_2, 2)]
    *written, for_far, for_1 = grads_of((FAR, 1), 1, written)
    last = [swap(for_far, FAR), swap(for_1, 1)]
    q_out, self_out, summed = grads_of((0,), None, written, come, F32)
    prefix_out = (summed + sum(part.astype(F32) for part in last)).astype(BF16)
    return (q_out, self_out, prefix_out)


def far_kernel(z, *refs):
    (resp_prompt, resp_len, rewards, q_hbm, og_hbm, kv_hbm, prompts, q_out, self_out, prefix_outs,
     totals, lens, factors, q, og, kv, prefix, out, own, grads, sem_in, sem_prefix, sem_out) = refs
    me = lax.axis_index("dp")

    for p in range(z.n_dp):
        totals[p] = 0.0

    def copies_in(slot):
        rows = token_rows(z, slot)
        prompt = resp_prompt[me * z.count + slot]
        return (
            *row_copies((q_hbm, og_hbm, kv_hbm), (q, og, kv), rows, rows, sem_in.at[slot]),
            pltpu.make_async_copy(prompts.at[prompt], prefix.at[slot], sem_prefix.at[slot]),
        )

    def copies_out(slot):
        rows = token_rows(z, slot)
        return (
            *result_copies(out, own, q_out, self_out, slot, rows, sem_out),
            pltpu.make_async_copy(grads.at[slot], prefix_outs.at[slot], sem_out.at[slot, 3]),
        )

    def start(slot, _):
        for copy in copies_in(slot):
            copy.start()
        return 0

    lax.fori_loop(0, z.count, start, 0)

    def add(i, _):
        prompt = resp_prompt[i]
        totals[prompt] = totals[prompt] + rewards[i]
        return 0

    lax.fori_loop(0, z.n_dp * z.count, add, 0)

    def find_factor(slot, _):
        place = me * z.count + slot
        lens[slot] = resp_len[slot]
        factors[slot] = reward_factor(z, rewards[place], totals[resp_prompt[place]], resp_len[slot])
        return 0

    lax.fori_loop(0, z.count, find_factor, 0)

    def unit(slot, _):
        for copy in copies_in(slot):
            copy.wait()

        def sink(_, cols, key_grad, value_grad):
            grads[slot, 0, :, cols] = key_grad.astype(BF16)
            grads[slot, 1, :, cols] = value_grad.astype(BF16)

        units = [
            Unit([token_rows(z, slot)], [slot], k, [lens[slot]], [factors[slot]]) for k in range(z.kv_heads)
        ]
        attend(z, units, q, og, kv, prefix.at[slot], out, own, sink, True)
        for copy in copies_out(slot):
            copy.start()
        return 0

    lax.fori_loop(0, z.count, unit, 0)

    def end(slot, _):
        for copy in copies_out(slot):
            copy.wait()
        return 0

    lax.fori_loop(0, z.count, end, 0)


def far_shards(z, prompt_kv, resp_q, resp_kv, out_grad, rewards, resp_prompt, resp_len):
    assert z.slots == 1
    count, n_dp = z.count, z.n_dp
    one = (2, z.prefix_len, z.width)
    smem = pl.BlockSpec(memory_space=pltpu.SMEM)
    q_out, self_out, per_resp = pl.pallas_call(
        functools.partial(far_kernel, z),
        out_shape=[
            jax.ShapeDtypeStruct(resp_q.shape, BF16),
            jax.ShapeDtypeStruct(resp_kv.shape, BF16),
            jax.ShapeDtypeStruct((count,) + one, BF16),
        ],
        in_specs=[smem] * 3 + [ANYWHERE] * 4,
        out_specs=[ANYWHERE] * 3,
        scratch_shapes=[
            pltpu.SMEM((n_dp,), F32),
            pltpu.SMEM((count,), jnp.int32),
            pltpu.SMEM((count,), F32),
            pltpu.VMEM(resp_q.shape, BF16),
            pltpu.VMEM(resp_q.shape, BF16),
            pltpu.VMEM(resp_kv.shape, BF16),
            pltpu.VMEM((count,) + one, BF16),
            pltpu.VMEM((count, z.tokens, z.lanes), BF16),
            pltpu.VMEM((count, 2, z.tokens, z.width), BF16),
            pltpu.VMEM((count,) + one, BF16),
            pltpu.SemaphoreType.DMA((count, 4)),
            pltpu.SemaphoreType.DMA((count,)),
            pltpu.SemaphoreType.DMA((count, 4)),
        ],
        compiler_params=pltpu.CompilerParams(vmem_limit_bytes=VMEM_BYTES),
        name="far_grads",
    )(
        resp_prompt,
        resp_len,
        lax.all_gather(rewards, "dp", axis=0, tiled=True),
        resp_q,
        out_grad,
        resp_kv,
        lax.all_gather(prompt_kv, "dp", axis=0),
    )
    my_prompts = lax.dynamic_slice_in_dim(resp_prompt, lax.axis_index("dp") * count, count)
    route = (jnp.arange(n_dp, dtype=jnp.int32)[:, None] == my_prompts[None, :]).astype(BF16)
    outgoing = jnp.dot(route, per_resp.reshape(count, -1), preferred_element_type=F32).astype(BF16)
    outgoing = outgoing.reshape((n_dp,) + one)
    incoming = lax.all_to_all(outgoing, "dp", split_axis=0, concat_axis=0, tiled=True)
    prefix_out = jnp.sum(incoming, axis=0, dtype=F32).astype(BF16)
    return (q_out, self_out, prefix_out)


def shards(prompt_kv, resp_q, resp_kv, out_grad, rewards, resp_prompt, resp_len):
    n_dp = lax.axis_size("dp")
    count = rewards.shape[0]
    prefix_len, width = prompt_kv.shape[1:]
    slots = (count + n_dp - 1) // n_dp
    z = Sizes(
        n_dp, count, slots, width // HD, resp_q.shape[1] // width, resp_q.shape[0] // count, prefix_len
    )
    part = near_shards if count // slots == n_dp else far_shards
    return part(z, prompt_kv, resp_q, resp_kv, out_grad, rewards, resp_prompt, resp_len)


def solution(mesh):
    in_specs = (
        P(None, ("groups", "dp"), "tensor"),
        P(("groups", "dp"), "tensor"),
        P(None, ("groups", "dp"), "tensor"),
        P(("groups", "dp"), "tensor"),
        P(("groups", "dp")),
        P("groups"),
        P(("groups", "dp")),
    )
    out_specs = (
        P(("groups", "dp"), "tensor"),
        P(None, ("groups", "dp"), "tensor"),
        P(None, ("groups", "dp"), "tensor"),
    )
    return jax.shard_map(shards, mesh=mesh, in_specs=in_specs, out_specs=out_specs, check_vma=False)
```
